32 devices in a mesh: seq: 4 (over x, core), fsdp: 8 (over z, y).
Axes of the slice: x: 2, y: 2, z: 4, core: 2. Of those that a mesh axis runs over, the one named last changes fastest.
Arguments:
- inputs: bfloat16 [8, 4096, 1024], P('fsdp', 'seq'), may hold values from -6 to 6
- g_attn: bfloat16 [1024], P('fsdp'), may hold values from 0.5 to 1.5
- w_query: bfloat16 [1024, 1024], P('fsdp'), may hold values from -0.1875 to 0.1875
- w_key: bfloat16 [1024, 1024], P('fsdp'), may hold values from -0.1875 to 0.1875
- w_value: bfloat16 [1024, 1024], P('fsdp'), may hold values from -0.1875 to 0.1875
- w_beta: bfloat16 [1024, 8], P('fsdp'), may hold values from -0.1875 to 0.1875
- conv_taps: bfloat16 [4, 3072], P(None, 'fsdp'), may hold values from -3 to 3
- o_gain: bfloat16 [128], P('fsdp'), may hold values from 0.5 to 1.5
- w_out: bfloat16 [1024, 1024], P('fsdp'), may hold values from -0.1875 to 0.1875
- g_mlp: bfloat16 [1024], P('fsdp'), may hold values from 0.5 to 1.5
- w_gate: bfloat16 [1024, 2816], P('fsdp'), may hold values from -0.1875 to 0.1875
- w_up: bfloat16 [1024, 2816], P('fsdp'), may hold values from -0.1875 to 0.1875
- w_down: bfloat16 [2816, 1024], P(None, 'fsdp'), may hold values from -0.109375 to 0.109375
- cotangent: bfloat16 [8, 4096, 1024], P('fsdp', 'seq'), may hold values from -6 to 6
Outputs:
- layer_out: bfloat16 [8, 4096, 1024], P('fsdp', 'seq')
- grad_inputs: float32 [8, 4096, 1024], P('fsdp', 'seq')
- grad_g_attn: float32 [1024], P('fsdp')
- grad_w_query: float32 [1024, 1024], P('fsdp')
- grad_w_key: float32 [1024, 1024], P('fsdp')
- grad_w_value: float32 [1024, 1024], P('fsdp')
- grad_w_beta: float32 [1024, 8], P('fsdp')
- grad_conv_taps: float32 [4, 3072], P(None, 'fsdp')
- grad_o_gain: float32 [128], P('fsdp')
- grad_w_out: float32 [1024, 1024], P('fsdp')
- grad_g_mlp: float32 [1024], P('fsdp')
- grad_w_gate: float32 [1024, 2816], P('fsdp')
- grad_w_up: float32 [1024, 2816], P('fsdp')
- grad_w_down: float32 [2816, 1024], P(None, 'fsdp')
The draws below stay inside these ranges and needn't reach their ends.
All inputs are finite; a program needn't handle non-finite values.
Results may differ from the reference program's by a relative error of at most 0.017.
Values may be sent and summed in bfloat16 or wider, within the bound.
A program may use at most 256 MiB of HBM per device.

```python
import jax
import jax.numpy as jnp
from jax import lax

D = 1024
H = 8
DK = 128
FF = 2816
KCONV = 4
BLOCK = 64
SEQ_LEN = 4096
SEQS = 8


def block_scale(own_key, dims, split, low, largest):
    level = 1.0
    for position, blocks in split:
        heights = jax.random.uniform(jax.random.fold_in(jax.random.fold_in(own_key, 6), position), (blocks,), jnp.float32, low / len(split), largest / len(split))
        level = level * jnp.repeat(jnp.exp(heights), dims[position] // blocks).reshape((-1,) + (1,) * (len(dims) - 1 - position))
    return level


def noise(own_key, shape, deviation, bound, split=(), kind=jnp.bfloat16):
    values = jax.random.normal(own_key, shape, jnp.float32) * deviation
    if len(split) > 0:
        values = block_scale(own_key, shape, split, -0.22, 0.18) * values
    return jnp.clip(values, min=-bound, max=bound).astype(kind)


def setup_inputs(seed: int = 0) -> dict:
    key_of = jax.random.split(jax.random.key(seed), 15)
    return {
        "inputs": noise(key_of[0], (SEQS, SEQ_LEN, D), 1.0, 6.0, ((0, 8), (1, 4))),
        "g_attn": jnp.clip(1.0 + 0.1 * jax.random.normal(key_of[1], (D,), jnp.float32), 0.5, 1.5).astype(jnp.bfloat16),
        "w_query": noise(key_of[2], (D, D), D ** -0.5, 0.1875, ((0, 8),)),
        "w_key": noise(key_of[3], (D, D), D ** -0.5, 0.1875, ((0, 8),)),
        "w_value": noise(key_of[4], (D, D), D ** -0.5, 0.1875, ((0, 8),)),
        "w_beta": noise(key_of[5], (D, H), D ** -0.5, 0.1875, ((0, 8),)),
        "conv_taps": noise(key_of[6], (KCONV, 3 * D), KCONV ** -0.5, 3.0, ((1, 8),)),
        "o_gain": jnp.clip(1.0 + 0.1 * jax.random.normal(key_of[7], (DK,), jnp.float32), 0.5, 1.5).astype(jnp.bfloat16),
        "w_out": noise(key_of[8], (D, D), D ** -0.5, 0.1875, ((0, 8),)),
        "g_mlp": jnp.clip(1.0 + 0.1 * jax.random.normal(key_of[9], (D,), jnp.float32), 0.5, 1.5).astype(jnp.bfloat16),
        "w_gate": noise(key_of[10], (D, FF), D ** -0.5, 0.1875, ((0, 8),)),
        "w_up": noise(key_of[11], (D, FF), D ** -0.5, 0.1875, ((0, 8),)),
        "w_down": noise(key_of[12], (FF, D), FF ** -0.5, 0.109375, ((1, 8),)),
        "cotangent": noise(key_of[13], (SEQS, SEQ_LEN, D), 1.0, 6.0, ((0, 8), (1, 4))),
    }


@jax.custom_vjp
def low(v):
    return lax.optimization_barrier(v.astype(jnp.bfloat16)).astype(jnp.float32)

@jax.custom_vjp
def low_back(v):
    return v

def low_keep(v):
    return (low(v), None)

def low_pass(kept, grad):
    return (grad,)

def back_keep(v):
    return (v, None)

def back_low(kept, grad):
    return (low(grad),)
low.defvjp(low_keep, low_pass)
low_back.defvjp(back_keep, back_low)
highest = lax.Precision.HIGHEST
epsilon = 1e-06

def matmul(left_side, right_side):
    return jnp.dot(left_side, right_side, precision=highest, preferred_element_type=jnp.float32)

def rms_scale(values, gain_vec):
    return values * lax.rsqrt(lax.optimization_barrier(jnp.mean(values * values, axis=-1, keepdims=True)) + epsilon) * gain_vec

def unit_inverse(strict_lower):
    width_all = strict_lower.shape[-1]
    identity = jnp.eye(width_all, dtype=jnp.float32)
    result = identity - strict_lower
    powered = strict_lower
    for doubling in range(1, (width_all - 1).bit_length()):
        powered = jnp.einsum('gij,gjk->gik', powered, powered, precision=highest)
        result = jnp.einsum('gij,gjk->gik', result, identity + powered, precision=highest)
    return result

def causal_conv(signal, conv_weights):
    length = signal.shape[0]
    padded = jnp.pad(signal, ((conv_weights.shape[0] - 1, 0), (0, 0), (0, 0)))
    summed_taps = conv_weights[0] * padded[0:length]
    for offset in range(1, conv_weights.shape[0]):
        summed_taps = summed_taps + conv_weights[offset] * padded[offset:offset + length]
    return jax.nn.silu(summed_taps)

def block_step(memory, pieces):
    queries, key_rows, values, beta_rates = pieces
    scaling = queries.shape[-1] ** (-0.5)
    keys_rated = key_rows * beta_rates[..., None]
    values_rated = values * beta_rates[..., None]
    products = beta_rates[..., None] * jnp.einsum('gie,gje->gij', key_rows, key_rows, precision=highest)
    inverse = unit_inverse(jnp.tril(products, -1))
    weights_wy = jnp.einsum('gij,gje->gie', inverse, keys_rated, precision=highest)
    targets = jnp.einsum('gij,gje->gie', inverse, values_rated, precision=highest)
    fresh = targets - jnp.einsum('gie,gef->gif', weights_wy, memory, precision=highest)
    scores = jnp.tril(jnp.einsum('gie,gje->gij', queries, key_rows, precision=highest))
    output = scaling * (jnp.einsum('gie,gef->gif', queries, memory, precision=highest) + jnp.einsum('gij,gjf->gif', scores, fresh, precision=highest))
    memory = memory + jnp.einsum('gie,gif->gef', key_rows, fresh, precision=highest)
    return (memory, output)

def mixer(queries, key_rows, values, logits, conv_weights, gain_vec):
    length, head_count, head_size = queries.shape
    queries = causal_conv(queries, conv_weights[:, 0])
    key_rows = causal_conv(key_rows, conv_weights[:, 1])
    values = causal_conv(values, conv_weights[:, 2])
    queries = queries * lax.rsqrt(lax.optimization_barrier(jnp.sum(queries * queries, axis=-1, keepdims=True)) + epsilon)
    key_rows = key_rows * lax.rsqrt(lax.optimization_barrier(jnp.sum(key_rows * key_rows, axis=-1, keepdims=True)) + epsilon)
    queries = low(queries)
    key_rows = low(key_rows)
    values = low(values)
    beta_rates = jax.nn.sigmoid(logits)
    block_count = length // BLOCK

    def blocks(array):
        return jnp.moveaxis(array.reshape((block_count, BLOCK) + array.shape[1:]), 2, 1)
    initial = jnp.zeros((head_count, head_size, head_size), jnp.float32)
    final_memory, outputs = lax.scan(jax.checkpoint(block_step), initial, (blocks(queries), blocks(key_rows), blocks(values), blocks(beta_rates)))
    outputs = jnp.moveaxis(outputs, 1, 2).reshape(length, head_count, head_size)
    return rms_scale(outputs, gain_vec)

def layer(params, inputs):
    gain_attn, query_matrix, key_matrix, value_matrix, beta_matrix, conv_weights, gain_out, out_matrix, gain_mlp, gate_matrix, up_matrix, down_matrix = params
    length = inputs.shape[0]
    normed = low(rms_scale(inputs, gain_attn))

    def project(matrix):
        return low_back(low(matmul(normed, matrix))).reshape(length, H, DK)
    queries = project(query_matrix)
    key_rows = project(key_matrix)
    values = project(value_matrix)
    logits = low_back(low(matmul(normed, beta_matrix)))
    mixed_heads = mixer(queries, key_rows, values, logits, conv_weights.reshape(KCONV, 3, H, DK), gain_out)
    head_rows = low_back(low(mixed_heads.reshape(length, D)))
    attended = inputs + low_back(matmul(head_rows, out_matrix))
    normed_ff = low(rms_scale(attended, gain_mlp))
    gated = low_back(matmul(normed_ff, gate_matrix))
    upward = low_back(matmul(normed_ff, up_matrix))
    hidden = low(jax.nn.silu(gated) * upward)
    return attended + matmul(hidden, down_matrix)

def reference(inputs, g_attn, w_query, w_key, w_value, w_beta, conv_taps, o_gain, w_out, g_mlp, w_gate, w_up, w_down, cotangent):
    params = tuple((matrix.astype(jnp.float32) for matrix in (g_attn, w_query, w_key, w_value, w_beta, conv_taps, o_gain, w_out, g_mlp, w_gate, w_up, w_down)))

    def sequence_step(totals, pieces):
        sequence_in, sequence_grad = pieces
        result, pull_back = jax.vjp(layer, params, sequence_in.astype(jnp.float32))
        param_grads, input_grad = pull_back(sequence_grad.astype(jnp.float32))
        totals = tuple((first + second for first, second in zip(totals, param_grads)))
        return (totals, (result.astype(jnp.bfloat16), input_grad))
    initial = tuple((jnp.zeros_like(matrix) for matrix in params))
    grads, (layer_out, grad_inputs) = lax.scan(sequence_step, initial, (inputs, cotangent))
    return (layer_out, grad_inputs, grads[0], grads[1], grads[2], grads[3], grads[4], grads[5], grads[6], grads[7], grads[8], grads[9], grads[10], grads[11])
```

```python
import functools

import jax
import jax.numpy as jnp
from jax import lax
from jax.experimental import pallas as pl
from jax.experimental.pallas import tpu as pltpu
from jax.sharding import PartitionSpec as P

CHUNK = 256
HALO = 16
TAPS = 4
MIB = 1024 * 1024

highest = lax.Precision.HIGHEST
epsilon = 1e-06
f32 = jnp.float32
bf16 = jnp.bfloat16


def nn(left_side, right_side):
    return lax.dot_general(
        left_side, right_side, (((1,), (0,)), ((), ())), preferred_element_type=f32
    )


def nt(left_side, right_side):
    return lax.dot_general(
        left_side, right_side, (((1,), (1,)), ((), ())), preferred_element_type=f32
    )


def tn(left_side, right_side):
    return lax.dot_general(
        left_side, right_side, (((0,), (0,)), ((), ())), preferred_element_type=f32
    )


def rms_scale(values, gain_vec):
    return (
        values * lax.rsqrt(jnp.mean(values * values, axis=-1, keepdims=True) + epsilon) * gain_vec
    )


def norm_backward(values, gain_vec, grad_out):
    scaling = lax.rsqrt(jnp.mean(values * values, axis=-1, keepdims=True) + epsilon)
    unit_rows = values * scaling
    gain_grad = jnp.sum(grad_out * unit_rows, axis=0)
    scaled_grad = grad_out * gain_vec
    input_grad = scaling * (
        scaled_grad - unit_rows * jnp.mean(scaled_grad * unit_rows, axis=-1, keepdims=True)
    )
    return (input_grad, gain_grad)


MESH = pl.DeviceIdType.MESH


class Place:
    def __init__(self, count):
        self.count = count
        self.sides = 2 if count % 2 == 0 else 1
        self.length = count // self.sides
        self.position = lax.axis_index("seq")
        self.index = lax.axis_index("fsdp")
        self.core = lax.rem(self.position, 2)
        self.side = lax.rem(self.index, self.sides)
        self.spot = lax.div(self.index, self.sides)

    def sibling(self):
        return {"seq": self.position + 1 - 2 * self.core, "fsdp": self.index}

    def across(self):
        return {"seq": lax.rem(self.position + 2, 4), "fsdp": self.index}

    def partner(self):
        return {"seq": self.position, "fsdp": self.spot * 2 + 1 - self.side}

    def ahead(self, step):
        spot = lax.rem(self.spot + step, self.length)
        return {"seq": self.position, "fsdp": spot * self.sides + self.side}

    def shard(self, spot, side):
        return spot * self.sides + side

    def behind(self, step):
        return lax.rem(self.spot + self.length - step, self.length)

    def greet(self, across):
        barrier = pltpu.get_barrier_semaphore()
        total = self.length

        def signal(device):
            pl.semaphore_signal(barrier, inc=1, device_id=device, device_id_type=MESH)

        def one(step, carry):
            signal(self.ahead(step))
            return carry

        lax.fori_loop(1, self.length, one, 0)
        signal(self.sibling())
        if self.sides == 2:
            signal(self.partner())
            total += 1
        if across:
            signal(self.across())
            total += 1
        pl.semaphore_wait(barrier, total)


def remote(source, target, send, recv, device):
    return pltpu.make_async_remote_copy(
        src_ref=source,
        dst_ref=target,
        send_sem=send,
        recv_sem=recv,
        device_id=device,
        device_id_type=MESH,
    )


def steps(first, last, body):
    def one(step, carry):
        body(step)
        return carry

    lax.fori_loop(first, last, one, 0)


class Gather:
    def __init__(self, count, shards, outs, sems):
        self.place = Place(count)
        self.shards, self.outs = shards, outs
        (
            self.line_send,
            self.line_recv,
            self.side_send,
            self.side_recv,
            self.core_send,
            self.core_recv,
            self.own,
        ) = sems

    @staticmethod
    def scratch(arrays, count):
        length = count // 2 if count % 2 == 0 else count
        return [
            pltpu.SemaphoreType.DMA((arrays, length)),
            pltpu.SemaphoreType.DMA((arrays, length)),
            pltpu.SemaphoreType.DMA((arrays, length)),
            pltpu.SemaphoreType.DMA((arrays, length)),
            pltpu.SemaphoreType.DMA((arrays, 2 * length)),
            pltpu.SemaphoreType.DMA((arrays, 2 * length)),
            pltpu.SemaphoreType.DMA((arrays,)),
        ]

    def half(self, a, core):
        width = self.shards[a].shape[1] // 2
        return pl.ds(pl.multiple_of(core * width, 128), width)

    def spot(self, a, shard, core):
        depth = self.shards[a].shape[0]
        return self.outs[a].at[
            pl.ds(pl.multiple_of(shard * depth, depth), depth), self.half(a, core)
        ]

    def line(self, a, step, arriving):
        p = self.place
        shard = p.shard(p.behind(step), p.side) if arriving else p.index
        target = self.spot(a, shard, p.core)
        source = target if arriving else self.shards[a].at[:, self.half(a, p.core)]
        return remote(
            source, target, self.line_send.at[a, step], self.line_recv.at[a, step], p.ahead(step)
        )

    def side(self, a, step, arriving):
        p = self.place
        shard = p.shard(p.behind(step), 1 - p.side if arriving else p.side)
        target = self.spot(a, shard, p.core)
        return remote(
            target, target, self.side_send.at[a, step], self.side_recv.at[a, step], p.partner()
        )

    def side_own(self, a):
        p = self.place
        return remote(
            self.shards[a].at[:, self.half(a, p.core)],
            self.spot(a, p.index, p.core),
            self.side_send.at[a, 0],
            self.side_recv.at[a, 0],
            p.partner(),
        )

    def core(self, a, step, other, arriving):
        p = self.place
        shard = p.shard(p.behind(step), 1 - p.side if other else p.side)
        target = self.spot(a, shard, 1 - p.core if arriving else p.core)
        slot = 2 * step + (1 if other else 0)
        return remote(
            target, target, self.core_send.at[a, slot], self.core_recv.at[a, slot], p.sibling()
        )

    def keep(self, a):
        depth = self.shards[a].shape[0]
        rows = pl.ds(pl.multiple_of(self.place.index * depth, depth), depth)
        return pltpu.make_async_copy(self.shards[a], self.outs[a].at[rows, :], self.own.at[a])

    def start(self, a):
        if self.place.sides == 2:
            self.side_own(a).start()
        steps(1, self.place.length, lambda step: self.line(a, step, False).start())
        self.keep(a).start()

    def forward(self, a):
        def one(step):
            self.line(a, step, True).wait_recv()
            if self.place.sides == 2:
                self.side(a, step, False).start()
            self.core(a, step, False, False).start()

        steps(1, self.place.length, one)

    def spread(self, a):
        def one(step):
            self.side(a, step, True).wait_recv()
            self.core(a, step, True, False).start()

        if self.place.sides == 2:
            steps(0, self.place.length, one)

    def finish(self, a):
        p = self.place
        self.keep(a).wait()

        def own(step):
            self.line(a, step, False).wait_send()
            self.core(a, step, False, False).wait_send()
            self.core(a, step, False, True).wait_recv()

        steps(1, p.length, own)
        if p.sides == 2:
            self.side_own(a).wait_send()
            steps(1, p.length, lambda step: self.side(a, step, False).wait_send())

            def other(step):
                self.core(a, step, True, False).wait_send()
                self.core(a, step, True, True).wait_recv()

            steps(0, p.length, other)


def gather_kernel(arrays, count, *refs):
    gather = Gather(count, refs[:arrays], refs[arrays : 2 * arrays], refs[2 * arrays :])
    gather.place.greet(False)
    for a in range(arrays):
        gather.start(a)
    for a in range(arrays + 1):
        if a < arrays:
            gather.forward(a)
        if a > 0:
            gather.spread(a - 1)
    for a in range(arrays):
        gather.finish(a)


def gather_all(shards, collective_id):
    count = lax.axis_size("fsdp")
    arrays = len(shards)
    anywhere = pl.BlockSpec(memory_space=pl.ANY)
    return pl.pallas_call(
        functools.partial(gather_kernel, arrays, count),
        in_specs=[anywhere] * arrays,
        out_specs=[anywhere] * arrays,
        out_shape=[
            jax.ShapeDtypeStruct((count * s.shape[0], s.shape[1]), s.dtype) for s in shards
        ],
        scratch_shapes=Gather.scratch(arrays, count),
        compiler_params=pltpu.CompilerParams(collective_id=collective_id, has_side_effects=True),
    )(*shards)


class Reduce:
    def __init__(self, count, pieces, sources, outs, buffers, sems):
        self.place = Place(count)
        self.pieces, self.sources, self.outs = pieces, sources, outs
        self.total, self.core_in, self.side_in, self.line_in, self.across_in, self.done = buffers
        (
            self.core_sem,
            self.load_sem,
            self.side_sem,
            self.line_sem,
            self.across_sem,
            self.last_sem,
            self.store_sem,
        ) = sems

    @staticmethod
    def plan(widths, limit):
        pieces = []
        for a, width in enumerate(widths):
            tiles = width // 256
            parts = -(-tiles * 128 // limit)
            offset = 0
            for part in range(parts):
                wide = (tiles // parts + (1 if part < tiles % parts else 0)) * 128
                pieces.append((a, offset, wide))
                offset += wide
        return pieces

    @staticmethod
    def scratch(count, pieces, depths):
        sides = 2 if count % 2 == 0 else 1
        length = count // sides
        pairs = [(depths[a], wide) for a, _, wide in pieces]
        number = len(pieces)

        def stack(lead):
            return [pltpu.VMEM(lead + pair, bf16) for pair in pairs]

        shapes = (
            stack((count,)) + stack((count,)) + stack((length,)) + stack((length,))
            + stack(()) + stack(())
        )
        sems = [
            pltpu.SemaphoreType.DMA((number, 2)),
            pltpu.SemaphoreType.DMA((number,)),
            pltpu.SemaphoreType.DMA((number, 2, length)),
            pltpu.SemaphoreType.DMA((number, 2, length)),
            pltpu.SemaphoreType.DMA((number, 2)),
            pltpu.SemaphoreType.DMA((number, 2)),
            pltpu.SemaphoreType.DMA((number,)),
        ]
        return shapes + sems

    @staticmethod
    def split(refs, number):
        buffers = [refs[i * number : (i + 1) * number] for i in range(6)]
        return buffers, refs[6 * number :]

    def columns(self, p, core):
        a, offset, wide = self.pieces[p]
        width = self.sources[a].shape[2] // 2
        return a, pl.ds(pl.multiple_of(core * width + offset, 128), wide)

    def to_sibling(self, p):
        a, columns = self.columns(p, 1 - self.place.core)
        return remote(
            self.sources[a].at[:, :, columns],
            self.core_in[p],
            self.core_sem.at[p, 0],
            self.core_sem.at[p, 1],
            self.place.sibling(),
        )

    def load(self, p):
        a, columns = self.columns(p, self.place.core)
        return pltpu.make_async_copy(
            self.sources[a].at[:, :, columns], self.total[p], self.load_sem.at[p]
        )

    def to_side(self, p, spot):
        place = self.place
        return remote(
            self.total[p].at[place.shard(spot, 1 - place.side)],
            self.side_in[p].at[spot],
            self.side_sem.at[p, 0, spot],
            self.side_sem.at[p, 1, spot],
            place.partner(),
        )

    def to_line(self, p, step):
        place = self.place
        spot = lax.rem(place.spot + step, place.length)
        return remote(
            self.total[p].at[place.shard(spot, place.side)],
            self.line_in[p].at[step],
            self.line_sem.at[p, 0, step],
            self.line_sem.at[p, 1, step],
            place.ahead(step),
        )

    def to_across(self, p):
        return remote(
            self.done[p],
            self.across_in[p],
            self.across_sem.at[p, 0],
            self.across_sem.at[p, 1],
            self.place.across(),
        )

    def target(self, p, core):
        a, columns = self.columns(p, core)
        return self.outs[a].at[:, columns]

    def to_result(self, p, arriving):
        core = 1 - self.place.core if arriving else self.place.core
        return remote(
            self.across_in[p],
            self.target(p, core),
            self.last_sem.at[p, 0],
            self.last_sem.at[p, 1],
            self.place.sibling(),
        )

    def store(self, p):
        return pltpu.make_async_copy(
            self.across_in[p], self.target(p, self.place.core), self.store_sem.at[p]
        )

    def start(self, p):
        self.to_sibling(p).start()
        self.load(p).start()

    def stage_core(self, p):
        place = self.place
        self.load(p).wait()
        self.to_sibling(p).wait_recv()
        if place.sides == 2:

            def one(step):
                spot = lax.rem(place.spot + step, place.length)
                shard = place.shard(spot, 1 - place.side)
                self.total[p][shard] = (
                    self.total[p][shard].astype(f32) + self.core_in[p][shard].astype(f32)
                ).astype(bf16)
                self.to_side(p, spot).start()

            steps(1, place.length + 1, one)

    def stage_side(self, p):
        place = self.place

        def one(step):
            spot = lax.rem(place.spot + step, place.length)
            shard = place.shard(spot, place.side)
            total = self.total[p][shard].astype(f32) + self.core_in[p][shard].astype(f32)
            if place.sides == 2:
                self.to_side(p, spot).wait_recv()
                total = total + self.side_in[p][spot].astype(f32)
            self.total[p][shard] = total.astype(bf16)

        def send(step):
            one(step)
            self.to_line(p, step).start()

        steps(1, place.length, send)
        one(0)

    def stage_line(self, p):
        place = self.place
        self.done[p][...] = self.total[p][place.index]

        def one(step):
            self.to_line(p, step).wait_recv()

        steps(1, place.length, one)
        total = self.total[p][place.index].astype(f32)
        if place.length <= 8:
            for step in range(1, place.length):
                total = total + self.line_in[p][step].astype(f32)
        else:
            total = lax.fori_loop(
                1,
                place.length,
                lambda step, carry: carry + self.line_in[p][step].astype(f32),
                total,
            )
        self.done[p][...] = total.astype(bf16)
        self.to_across(p).start()

    def stage_across(self, p):
        copy = self.to_across(p)
        copy.wait_recv()
        self.across_in[p][...] = (
            self.across_in[p][...].astype(f32) + self.done[p][...].astype(f32)
        ).astype(bf16)
        self.to_result(p, False).start()
        self.store(p).start()

    def finish(self, p):
        place = self.place
        self.to_sibling(p).wait_send()
        if place.sides == 2:
            steps(0, place.length, lambda spot: self.to_side(p, spot).wait_send())
        steps(1, place.length, lambda step: self.to_line(p, step).wait_send())
        self.to_across(p).wait_send()
        self.to_result(p, False).wait_send()
        self.to_result(p, True).wait_recv()
        self.store(p).wait()


def reduce_kernel(arrays, count, pieces, *refs):
    buffers, sems = Reduce.split(refs[2 * arrays :], len(pieces))
    reduce = Reduce(count, pieces, refs[:arrays], refs[arrays : 2 * arrays], buffers, sems)
    reduce.place.greet(True)
    number = len(pieces)
    for p in range(number):
        reduce.start(p)
    stages = (reduce.stage_core, reduce.stage_side, reduce.stage_line, reduce.stage_across)
    for turn in range(number + len(stages) - 1):
        for behind, stage in enumerate(stages):
            if 0 <= turn - behind < number:
                stage(turn - behind)
    for p in range(number):
        reduce.finish(p)


def reduce_all(sources, collective_id, limit=768):
    count = lax.axis_size("fsdp")
    arrays = len(sources)
    views = [s.reshape(count, s.shape[0] // count, s.shape[1]) for s in sources]
    pieces = Reduce.plan([s.shape[1] for s in sources], limit)
    anywhere = pl.BlockSpec(memory_space=pl.ANY)
    return pl.pallas_call(
        functools.partial(reduce_kernel, arrays, count, pieces),
        in_specs=[anywhere] * arrays,
        out_specs=[anywhere] * arrays,
        out_shape=[jax.ShapeDtypeStruct(v.shape[1:], bf16) for v in views],
        scratch_shapes=Reduce.scratch(count, pieces, [v.shape[1] for v in views]),
        compiler_params=pltpu.CompilerParams(
            collective_id=collective_id, has_side_effects=True, vmem_limit_bytes=60 * MIB
        ),
    )(*views)


PACK = (16, 256)


def pack_shard(parts):
    flat = jnp.concatenate([part.reshape(-1).astype(bf16) for part in parts])
    return jnp.pad(flat, (0, PACK[0] * PACK[1] - flat.shape[0])).reshape(PACK)


def pack_shards(parts):
    count = parts[0].shape[0]
    flat = jnp.concatenate([part.reshape(count, -1).astype(bf16) for part in parts], axis=1)
    flat = jnp.pad(flat, ((0, 0), (0, PACK[0] * PACK[1] - flat.shape[1])))
    return flat.reshape(count * PACK[0], PACK[1])


def unpack(flat, shapes):
    parts, offset = [], 0
    for shape in shapes:
        size = 1
        for extent in shape:
            size *= extent
        parts.append(flat[:, offset : offset + size].reshape((flat.shape[0],) + tuple(shape)))
        offset += size
    return parts


def grid_indices():
    row = lax.broadcasted_iota(jnp.int32, (CHUNK, CHUNK), 0)
    col = lax.broadcasted_iota(jnp.int32, (CHUNK, CHUNK), 1)
    return row, col


def conv_pre(wide_ref, taps, rows):
    total = None
    for offset in range(TAPS):
        term = taps[offset : offset + 1, :] * wide_ref[pl.ds(HALO - TAPS + 1 + offset, rows), :]
        total = term if total is None else total + term
    return total


def sigmoid(values):
    return 1.0 / (1.0 + jnp.exp(-values))


def head_column(table, head):
    lane = lax.broadcasted_iota(jnp.int32, table.shape, 1)
    return jnp.sum(jnp.where(lane == head, table, 0.0), axis=1, keepdims=True)


def forward_kernel(
    q_ref,
    k_ref,
    v_ref,
    logit_ref,
    taps_ref,
    out_ref,
    carry_ref,
    fresh_ref,
    inverse_ref,
    starts_ref,
    final_ref,
    wide,
    level_masks,
):
    head = pl.program_id(0)
    rows = out_ref.shape[0]
    size = out_ref.shape[1]
    chunks = rows // CHUNK
    levels = CHUNK.bit_length() - 1
    row, col = grid_indices()

    @pl.when(head == 0)
    def _():
        for level in range(levels):
            same = (row >> (level + 1)) == (col >> (level + 1))
            below = ((row >> level) & 1 == 1) & ((col >> level) & 1 == 0)
            level_masks[level] = jnp.where(same & below, 1.0, 0.0).astype(bf16)

    lows = []
    for which, ref in enumerate((q_ref, k_ref, v_ref)):
        wide[...] = ref[...].astype(f32)
        pre = conv_pre(wide, taps_ref[0, which].astype(f32), rows)
        act = pre * sigmoid(pre)
        if which < 2:
            act = act * lax.rsqrt(jnp.sum(act * act, axis=1, keepdims=True) + epsilon)
        lows.append(act.astype(bf16))
    queries, keys, values = lows
    rates = sigmoid(head_column(logit_ref[...].astype(f32), head))
    scaling = size ** (-0.5)
    eye = jnp.where(row == col, 1.0, 0.0)
    lower = row >= col

    parts = [slice(chunk * CHUNK, (chunk + 1) * CHUNK) for chunk in range(chunks)]
    stricts = [(rates[p] * nt(keys[p], keys[p])).astype(bf16) for p in parts]
    results = [eye - (strict * level_masks[0]).astype(f32) for strict in stricts]
    scores = [jnp.where(lower, nt(queries[p], keys[p]), 0.0).astype(bf16) for p in parts]
    for level in range(1, levels):
        mask = level_masks[level]
        lows = [result.astype(bf16) for result in results]
        inners = [nn(low, strict * mask).astype(bf16) for low, strict in zip(lows, stricts)]
        results = [
            result - nn(inner, low) for result, inner, low in zip(results, inners, lows)
        ]
    inverses = [result.astype(bf16) for result in results]
    for part, inverse in zip(parts, inverses):
        inverse_ref[part, :] = inverse

    srow = lax.broadcasted_iota(jnp.int32, (size, size), 0)
    scol = lax.broadcasted_iota(jnp.int32, (size, size), 1)
    memory = jnp.concatenate(
        [jnp.zeros((size, size), f32), jnp.where(srow == scol, 1.0, 0.0)], axis=1
    )
    for chunk in range(chunks):
        part = slice(chunk * CHUNK, (chunk + 1) * CHUNK)
        key_part, query_part, rate_part = keys[part], queries[part], rates[part]
        low_memory = memory.astype(bf16)
        starts_ref[0, chunk] = low_memory
        seen = nn(key_part, low_memory)
        aim = jnp.concatenate([values[part].astype(f32), jnp.zeros((CHUNK, size), f32)], axis=1)
        aim = (rate_part * (aim - seen)).astype(bf16)
        fresh = nn(inverses[chunk], aim).astype(bf16)
        fresh_ref[part, :] = fresh
        both = scaling * (nn(query_part, low_memory) + nn(scores[chunk], fresh))
        out_ref[part, :] = both[:, :size]
        carry_ref[part, :] = both[:, size:].astype(bf16)
        memory = memory + tn(key_part, fresh)
    final_ref[0] = memory


def delta_forward(queries, keys, values, logits, taps):
    wide_rows, width = queries.shape
    heads = logits.shape[1]
    size = width // heads
    rows = wide_rows - HALO
    chunks = rows // CHUNK
    column = pl.BlockSpec((wide_rows, size), lambda h: (0, h))
    plain = pl.BlockSpec((rows, size), lambda h: (0, h))
    return pl.pallas_call(
        forward_kernel,
        grid=(heads,),
        in_specs=[
            column,
            column,
            column,
            pl.BlockSpec((rows, heads), lambda h: (0, 0)),
            pl.BlockSpec((1, 3, TAPS, size), lambda h: (h, 0, 0, 0)),
        ],
        out_specs=[
            plain,
            plain,
            pl.BlockSpec((rows, 2 * size), lambda h: (0, h)),
            pl.BlockSpec((rows, CHUNK), lambda h: (0, h)),
            pl.BlockSpec((1, chunks, size, 2 * size), lambda h: (h, 0, 0, 0)),
            pl.BlockSpec((1, size, 2 * size), lambda h: (h, 0, 0)),
        ],
        out_shape=[
            jax.ShapeDtypeStruct((rows, width), f32),
            jax.ShapeDtypeStruct((rows, width), bf16),
            jax.ShapeDtypeStruct((rows, 2 * width), bf16),
            jax.ShapeDtypeStruct((rows, heads * CHUNK), bf16),
            jax.ShapeDtypeStruct((heads, chunks, size, 2 * size), bf16),
            jax.ShapeDtypeStruct((heads, size, 2 * size), f32),
        ],
        scratch_shapes=[
            pltpu.VMEM((wide_rows, size), f32),
            pltpu.VMEM((CHUNK.bit_length() - 1, CHUNK, CHUNK), bf16),
        ],
        compiler_params=pltpu.CompilerParams(vmem_limit_bytes=48 * MIB),
    )(queries, keys, values, logits, taps)


def mix_kernel(out_ref, carry_ref, state_ref, gain_ref, mixed_ref):
    output = out_ref[...] + nn(carry_ref[...], state_ref[0].astype(bf16))
    gain = gain_ref[...].astype(f32)
    mixed_ref[...] = rms_scale(output, gain).astype(bf16)


def mix(outputs, carries, states, gain):
    rows, width = outputs.shape
    heads, size, _ = states.shape
    plain = pl.BlockSpec((rows, size), lambda h: (0, h))
    return pl.pallas_call(
        mix_kernel,
        grid=(heads,),
        in_specs=[
            plain,
            plain,
            pl.BlockSpec((1, size, size), lambda h: (h, 0, 0)),
            pl.BlockSpec((1, size), lambda h: (0, 0)),
        ],
        out_specs=plain,
        out_shape=jax.ShapeDtypeStruct((rows, width), bf16),
        compiler_params=pltpu.CompilerParams(vmem_limit_bytes=32 * MIB),
    )(outputs, carries, states, gain)


def unmix_kernel(
    out_ref, carry_ref, state_ref, gain_ref, grad_ref, grad_out_ref, grad_state_ref, grad_gain_ref
):
    output = out_ref[...] + nn(carry_ref[...], state_ref[0].astype(bf16))
    gain = gain_ref[...].astype(f32)
    grad = grad_ref[...].astype(f32)
    scaling = lax.rsqrt(jnp.mean(output * output, axis=1, keepdims=True) + epsilon)
    unit_rows = output * scaling

    @pl.when(pl.program_id(0) == 0)
    def _():
        grad_gain_ref[...] = jnp.zeros_like(grad_gain_ref)

    grad_gain_ref[...] += jnp.sum(grad * unit_rows, axis=0, keepdims=True)
    scaled = grad * gain
    grad_out = scaling * (scaled - unit_rows * jnp.mean(scaled * unit_rows, axis=1, keepdims=True))
    low_grad = grad_out.astype(bf16)
    grad_state_ref[0] = tn(carry_ref[...], low_grad)
    grad_out_ref[...] = (grad_out * output.shape[1] ** (-0.5)).astype(bf16)


def unmix(outputs, carries, states, gain, grad_heads):
    rows, width = outputs.shape
    heads, size, _ = states.shape
    plain = pl.BlockSpec((rows, size), lambda h: (0, h))
    state = pl.BlockSpec((1, size, size), lambda h: (h, 0, 0))
    vector = pl.BlockSpec((1, size), lambda h: (0, 0))
    return pl.pallas_call(
        unmix_kernel,
        grid=(heads,),
        in_specs=[plain, plain, state, vector, plain],
        out_specs=[plain, state, vector],
        out_shape=[
            jax.ShapeDtypeStruct((rows, width), bf16),
            jax.ShapeDtypeStruct((heads, size, size), f32),
            jax.ShapeDtypeStruct((1, size), f32),
        ],
        compiler_params=pltpu.CompilerParams(vmem_limit_bytes=32 * MIB),
    )(outputs, carries, states, gain, grad_heads)


def backward_kernel(
    q_ref,
    k_ref,
    v_ref,
    logit_ref,
    taps_ref,
    grad_ref,
    fresh_ref,
    inverse_ref,
    starts_ref,
    state_ref,
    grad_state_ref,
    grad_q_ref,
    grad_k_ref,
    grad_v_ref,
    tails_ref,
    heads_ref,
    grad_taps_ref,
    grad_logit_ref,
    wides,
    pres,
    grads,
    padded,
):
    head = pl.program_id(0)
    rows, size = grad_ref.shape
    chunks = rows // CHUNK
    row, col = grid_indices()
    lower, upper = row >= col, row <= col

    lows, scales = [], []
    for which, ref in enumerate((q_ref, k_ref, v_ref)):
        wides[which] = ref[...].astype(f32)
        pre = conv_pre(wides.at[which], taps_ref[0, which].astype(f32), rows)
        pres[which] = pre
        act = pre * sigmoid(pre)
        if which < 2:
            scale = lax.rsqrt(jnp.sum(act * act, axis=1, keepdims=True) + epsilon)
            act = act * scale
            scales.append(scale)
        lows.append(act.astype(bf16))
    queries, keys, values = lows
    rates = sigmoid(head_column(logit_ref[...].astype(f32), head))

    state_in = state_ref[0].astype(bf16)
    pairs = fresh_ref[...]
    fresh_all = (pairs[:, :size].astype(f32) + nn(pairs[:, size:], state_in)).astype(bf16)

    grad_memory = grad_state_ref[0]
    grad_rates = [None] * chunks
    for chunk in reversed(range(chunks)):
        part = slice(chunk * CHUNK, (chunk + 1) * CHUNK)
        key, query, rate = keys[part], queries[part], rates[part]
        value = values[part]
        grad_out = grad_ref[part, :]
        fresh = fresh_all[part]
        start = starts_ref[0, chunk]
        memory = (start[:, :size].astype(f32) + nn(start[:, size:], state_in)).astype(bf16)
        low_grad = grad_memory.astype(bf16)
        key_f = key.astype(f32)
        rated = (rate * key_f).astype(bf16)

        scores_t = jnp.where(upper, nt(key, query), 0.0).astype(bf16)
        grad_fresh = (nn(scores_t, grad_out) + nn(key, low_grad)).astype(bf16)
        aim = tn(inverse_ref[part, :], grad_fresh)
        low_aim = aim.astype(bf16)
        grad_memory = grad_memory + tn(query, grad_out) - tn(rated, low_aim)

        grad_scores = jnp.where(lower, nt(grad_out, fresh), 0.0).astype(bf16)
        grad_scores_t = jnp.where(upper, nt(fresh, grad_out), 0.0).astype(bf16)
        grad_strict = jnp.where(row > col, nt(low_aim, fresh), 0.0).astype(bf16)
        grad_strict_t = jnp.where(row < col, nt(fresh, low_aim), 0.0).astype(bf16)

        grad_query = nt(grad_out, memory) + nn(grad_scores, key)
        inner = -(nn(grad_strict, key) + nt(low_aim, memory))
        grad_rates[chunk] = jnp.sum(key_f * inner + value.astype(f32) * aim, axis=1, keepdims=True)
        grad_key = (
            rate * inner
            - nn(grad_strict_t, rated)
            + nn(grad_scores_t, query)
            + nt(fresh, low_grad)
        )
        grads[0, part, :] = grad_query
        grads[1, part, :] = grad_key
        grads[2, part, :] = rate * aim

    grad_rate = jnp.concatenate(grad_rates, axis=0)
    grad_logit = grad_rate * rates * (1.0 - rates)
    lane = lax.broadcasted_iota(jnp.int32, grad_logit_ref.shape, 1)

    @pl.when(head == 0)
    def _():
        grad_logit_ref[...] = jnp.zeros_like(grad_logit_ref)
        padded[...] = jnp.zeros_like(padded)

    grad_logit_ref[...] = jnp.where(lane == head, grad_logit, grad_logit_ref[...])

    for which, ref in enumerate((grad_q_ref, grad_k_ref, grad_v_ref)):
        taps = taps_ref[0, which].astype(f32)
        pre = pres[which]
        sig = sigmoid(pre)
        grad_act = grads[which]
        if which < 2:
            scale = scales[which]
            unit_rows = pre * sig * scale
            grad_act = scale * (
                grad_act - unit_rows * jnp.sum(grad_act * unit_rows, axis=1, keepdims=True)
            )
        grad_pre = grad_act * sig * (1.0 + pre * (1.0 - sig))
        padded[pl.ds(HALO, rows), :] = grad_pre
        for offset in range(TAPS):
            shifted = wides[which, pl.ds(HALO - TAPS + 1 + offset, rows), :]
            grad_taps_ref[0, which, pl.ds(offset, 1), :] = jnp.sum(
                grad_pre * shifted, axis=0, keepdims=True
            )

        def back(start, count):
            total = None
            for offset in range(TAPS):
                term = (
                    taps[offset : offset + 1, :]
                    * padded[pl.ds(start + TAPS - 1 - offset, count), :]
                )
                total = term if total is None else total + term
            return total

        grad_signal = back(HALO, rows)
        ref[...] = grad_signal.astype(bf16)
        tails_ref[0, which] = grad_signal[rows - HALO :]
        heads_ref[0, which] = back(0, HALO)


def delta_backward(
    queries, keys, values, logits, taps, grad_out, fresh, inverses, starts, state, grad_state
):
    wide_rows, width = queries.shape
    heads = logits.shape[1]
    size = width // heads
    rows = wide_rows - HALO
    chunks = rows // CHUNK
    column = pl.BlockSpec((wide_rows, size), lambda h: (0, h))
    plain = pl.BlockSpec((rows, size), lambda h: (0, h))
    whole = pl.BlockSpec((rows, heads), lambda h: (0, 0))
    tap = pl.BlockSpec((1, 3, TAPS, size), lambda h: (h, 0, 0, 0))
    state_spec = pl.BlockSpec((1, size, size), lambda h: (h, 0, 0))
    edge = pl.BlockSpec((1, 3, HALO, size), lambda h: (h, 0, 0, 0))
    return pl.pallas_call(
        backward_kernel,
        grid=(heads,),
        in_specs=[
            column,
            column,
            column,
            whole,
            tap,
            plain,
            pl.BlockSpec((rows, 2 * size), lambda h: (0, h)),
            pl.BlockSpec((rows, CHUNK), lambda h: (0, h)),
            pl.BlockSpec((1, chunks, size, 2 * size), lambda h: (h, 0, 0, 0)),
            state_spec,
            state_spec,
        ],
        out_specs=[plain, plain, plain, edge, edge, tap, whole],
        out_shape=[
            jax.ShapeDtypeStruct((rows, width), bf16),
            jax.ShapeDtypeStruct((rows, width), bf16),
            jax.ShapeDtypeStruct((rows, width), bf16),
            jax.ShapeDtypeStruct((heads, 3, HALO, size), f32),
            jax.ShapeDtypeStruct((heads, 3, HALO, size), f32),
            jax.ShapeDtypeStruct((heads, 3, TAPS, size), f32),
            jax.ShapeDtypeStruct((rows, heads), f32),
        ],
        scratch_shapes=[
            pltpu.VMEM((3, wide_rows, size), f32),
            pltpu.VMEM((3, rows, size), f32),
            pltpu.VMEM((3, rows, size), f32),
            pltpu.VMEM((rows + 2 * HALO, size), f32),
        ],
        compiler_params=pltpu.CompilerParams(vmem_limit_bytes=56 * MIB),
    )(
        queries,
        keys,
        values,
        logits,
        taps,
        grad_out,
        fresh,
        inverses,
        starts,
        state,
        grad_state,
    )


def batched(left_side, right_side, transpose_left=False):
    return lax.dot_general(
        left_side,
        right_side,
        (((1 if transpose_left else 2,), (1,)), ((0,), (0,))),
        precision=highest,
        preferred_element_type=f32,
    )


def local(
    inputs,
    g_attn,
    w_query,
    w_key,
    w_value,
    w_beta,
    conv_taps,
    o_gain,
    w_out,
    g_mlp,
    w_gate,
    w_up,
    w_down,
    cotangent,
):
    count = lax.axis_size("fsdp")
    small = (g_attn.shape, g_mlp.shape, o_gain.shape, conv_taps.shape, w_beta.shape)
    packed = pack_shard((g_attn, g_mlp, o_gain, conv_taps, w_beta))
    packed, w_query, w_key, w_value, w_out = gather_all(
        (packed, w_query, w_key, w_value, w_out), 0
    )
    w_gate, w_up, w_down_t = gather_all((w_gate, w_up, jnp.transpose(w_down)), 1)
    g_attn, g_mlp, o_gain, conv_taps, w_beta = unpack(packed.reshape(count, -1), small)
    g_attn, g_mlp, o_gain = g_attn.reshape(-1), g_mlp.reshape(-1), o_gain.reshape(-1)
    conv_taps = jnp.transpose(conv_taps, (1, 0, 2)).reshape(conv_taps.shape[1], -1)
    w_beta = w_beta.reshape(-1, w_beta.shape[2])

    groups = lax.axis_size("seq")
    position = lax.axis_index("seq")
    forward_pairs = [(index, index + 1) for index in range(groups - 1)]
    backward_pairs = [(index + 1, index) for index in range(groups - 1)]
    tokens_low = inputs[0]
    rows, width = tokens_low.shape
    heads = w_beta.shape[1]
    size = o_gain.shape[0]
    halo = lax.ppermute(tokens_low[rows - HALO :], "seq", forward_pairs)
    gain_attn = g_attn.astype(f32)
    wide_tokens = jnp.concatenate([halo, tokens_low], axis=0).astype(f32)
    tokens = tokens_low.astype(f32)
    wide_normed = rms_scale(wide_tokens, gain_attn).astype(bf16)
    normed = wide_normed[HALO:]

    queries = nn(wide_normed, w_query).astype(bf16)
    keys = nn(wide_normed, w_key).astype(bf16)
    values = nn(wide_normed, w_value).astype(bf16)
    logits = nn(normed, w_beta).astype(bf16)
    taps = jnp.transpose(conv_taps.reshape(TAPS, 3, heads, size), (2, 1, 0, 3))

    outputs, carries, fresh, inverses, starts, finals = delta_forward(
        queries, keys, values, logits, taps
    )

    finals_all = lax.all_gather(finals, "seq", axis=0)
    state = jnp.zeros((heads, size, size), f32)
    states = [state]
    for index in range(groups - 1):
        state = finals_all[index, :, :, :size] + batched(finals_all[index, :, :, size:], state)
        states.append(state)
    state_in = lax.dynamic_index_in_dim(jnp.stack(states), position, 0, keepdims=False)

    gain_out = o_gain.reshape(1, size)
    head_rows = mix(outputs, carries, state_in, gain_out)
    attended = tokens + nn(head_rows, w_out)
    gain_mlp = g_mlp.astype(f32)
    normed_ff = rms_scale(attended, gain_mlp).astype(bf16)
    gated = nn(normed_ff, w_gate)
    upward = nn(normed_ff, w_up)
    sigmoid_gate = jax.nn.sigmoid(gated)
    activated = gated * sigmoid_gate
    hidden = (activated * upward).astype(bf16)
    layer_out = (attended + nt(hidden, w_down_t)).astype(bf16)

    grad_out = cotangent[0]
    grad_down_t = tn(grad_out, hidden).astype(bf16)
    grad_hidden = nn(grad_out, w_down_t)
    grad_gate = (grad_hidden * upward * sigmoid_gate * (1.0 + gated * (1.0 - sigmoid_gate))).astype(
        bf16
    )
    grad_upward = (grad_hidden * activated).astype(bf16)
    grad_gate_matrix = tn(normed_ff, grad_gate).astype(bf16)
    grad_up_matrix = tn(normed_ff, grad_upward).astype(bf16)
    grad_normed_ff = nt(grad_gate, w_gate) + nt(grad_upward, w_up)
    grad_from_ff, grad_gain_mlp = norm_backward(attended, gain_mlp, grad_normed_ff)
    grad_attended = grad_out.astype(f32) + grad_from_ff

    grad_mixed = grad_attended.astype(bf16)
    grad_out_matrix = tn(head_rows, grad_mixed).astype(bf16)
    grad_heads = nt(grad_mixed, w_out).astype(bf16)
    grad_delta, grad_starts, grad_gain_out = unmix(
        outputs, carries, state_in, gain_out, grad_heads
    )
    grads_all = lax.all_gather(grad_starts, "seq", axis=0)
    grad_state = jnp.zeros((heads, size, size), f32)
    grad_states = [grad_state]
    for index in reversed(range(1, groups)):
        grad_state = grads_all[index] + batched(
            finals_all[index, :, :, size:], grad_state, transpose_left=True
        )
        grad_states.append(grad_state)
    grad_states.reverse()
    grad_final = lax.dynamic_index_in_dim(jnp.stack(grad_states), position, 0, keepdims=False)

    grad_q, grad_k, grad_v, tails, firsts, grad_taps, grad_logits = delta_backward(
        queries,
        keys,
        values,
        logits,
        taps,
        grad_delta,
        fresh,
        inverses,
        starts,
        state_in,
        grad_final,
    )
    received = lax.ppermute(firsts, "seq", backward_pairs)
    fixed = jnp.transpose((tails + received).astype(bf16), (1, 2, 0, 3)).reshape(3, HALO, width)
    grad_q = lax.dynamic_update_slice(grad_q, fixed[0], (rows - HALO, 0))
    grad_k = lax.dynamic_update_slice(grad_k, fixed[1], (rows - HALO, 0))
    grad_v = lax.dynamic_update_slice(grad_v, fixed[2], (rows - HALO, 0))
    grad_logits = grad_logits.astype(bf16)

    grad_query_matrix = tn(normed, grad_q).astype(bf16)
    grad_key_matrix = tn(normed, grad_k).astype(bf16)
    grad_value_matrix = tn(normed, grad_v).astype(bf16)
    grad_beta_matrix = tn(normed, grad_logits)
    grad_normed = (
        nt(grad_q, w_query) + nt(grad_k, w_key) + nt(grad_v, w_value) + nt(grad_logits, w_beta)
    )
    grad_from_attn, grad_gain_attn = norm_backward(tokens, gain_attn, grad_normed)
    grad_inputs = (grad_attended + grad_from_attn)[None]
    grad_taps = jnp.transpose(grad_taps, (2, 1, 0, 3)).reshape(TAPS, count, -1)
    packed = pack_shards(
        (
            grad_gain_attn.reshape(count, -1),
            grad_gain_mlp.reshape(count, -1),
            grad_gain_out.reshape(count, -1),
            jnp.transpose(grad_taps, (1, 0, 2)),
            grad_beta_matrix.reshape(count, -1),
        )
    )
    grad_gate_matrix, grad_up_matrix, grad_down_t = reduce_all(
        (grad_gate_matrix, grad_up_matrix, grad_down_t), 2
    )
    packed, grad_query_matrix, grad_key_matrix, grad_value_matrix, grad_out_matrix = reduce_all(
        (packed, grad_query_matrix, grad_key_matrix, grad_value_matrix, grad_out_matrix), 3
    )
    parts = [part[0].astype(f32) for part in unpack(packed.reshape(1, -1), small)]
    grad_gain_attn, grad_gain_mlp, grad_gain_out, grad_taps, grad_beta_matrix = parts
    return (
        layer_out[None],
        grad_inputs,
        grad_gain_attn,
        grad_query_matrix.astype(f32),
        grad_key_matrix.astype(f32),
        grad_value_matrix.astype(f32),
        grad_beta_matrix,
        grad_taps,
        grad_gain_out,
        grad_out_matrix.astype(f32),
        grad_gain_mlp,
        grad_gate_matrix.astype(f32),
        grad_up_matrix.astype(f32),
        jnp.transpose(grad_down_t).astype(f32),
    )


def solution(mesh):
    vector = P("fsdp")
    rows = P("fsdp", None)
    columns = P(None, "fsdp")
    tokens = P("fsdp", "seq", None)
    return jax.shard_map(
        local,
        mesh=mesh,
        in_specs=(
            tokens,
            vector,
            rows,
            rows,
            rows,
            rows,
            columns,
            vector,
            rows,
            vector,
            rows,
            rows,
            columns,
            tokens,
        ),
        out_specs=(
            tokens,
            tokens,
            vector,
            rows,
            rows,
            rows,
            rows,
            columns,
            vector,
            rows,
            vector,
            rows,
            rows,
            columns,
        ),
        check_vma=False,
    )
```

```python
import functools

import jax
import jax.numpy as jnp
from jax import lax
from jax.experimental import pallas as pl
from jax.experimental.pallas import tpu as pltpu
from jax.sharding import PartitionSpec as P

CHUNK = 256
HALO = 16
TAPS = 4
MIB = 1024 * 1024

highest = lax.Precision.HIGHEST
epsilon = 1e-06
f32 = jnp.float32
bf16 = jnp.bfloat16


def nn(left_side, right_side):
    return lax.dot_general(
        left_side, right_side, (((1,), (0,)), ((), ())), preferred_element_type=f32
    )


def nt(left_side, right_side):
    return lax.dot_general(
        left_side, right_side, (((1,), (1,)), ((), ())), preferred_element_type=f32
    )


def tn(left_side, right_side):
    return lax.dot_general(
        left_side, right_side, (((0,), (0,)), ((), ())), preferred_element_type=f32
    )


def rms_scale(values, gain_vec):
    return (
        values * lax.rsqrt(jnp.mean(values * values, axis=-1, keepdims=True) + epsilon) * gain_vec
    )


def norm_backward(values, gain_vec, grad_out):
    scaling = lax.rsqrt(jnp.mean(values * values, axis=-1, keepdims=True) + epsilon)
    unit_rows = values * scaling
    gain_grad = jnp.sum(grad_out * unit_rows, axis=0)
    scaled_grad = grad_out * gain_vec
    input_grad = scaling * (
        scaled_grad - unit_rows * jnp.mean(scaled_grad * unit_rows, axis=-1, keepdims=True)
    )
    return (input_grad, gain_grad)


MESH = pl.DeviceIdType.MESH


class Place:
    def __init__(self, count):
        self.count = count
        self.sides = 2 if count % 2 == 0 else 1
        self.length = count // self.sides
        self.position = lax.axis_index("seq")
        self.index = lax.axis_index("fsdp")
        self.core = lax.rem(self.position, 2)
        self.chip = lax.div(self.position, 2)
        self.side = lax.rem(self.index, self.sides)
        self.spot = lax.div(self.index, self.sides)

    def sibling(self):
        return {"seq": self.position + 1 - 2 * self.core, "fsdp": self.index}

    def across(self):
        return {"seq": lax.rem(self.position + 2, 4), "fsdp": self.index}

    def partner(self):
        return {"seq": self.position, "fsdp": self.spot * 2 + 1 - self.side}

    def ahead(self, step):
        spot = lax.rem(self.spot + step, self.length)
        return {"seq": self.position, "fsdp": spot * self.sides + self.side}

    def shard(self, spot, side):
        return spot * self.sides + side

    def behind(self, step):
        return lax.rem(self.spot + self.length - step, self.length)

    def greet_all(self):
        self.greet(False, True)

    def greet(self, across, sequence=False):
        barrier = pltpu.get_barrier_semaphore()
        total = self.length - 1

        def signal(device):
            pl.semaphore_signal(barrier, inc=1, device_id=device, device_id_type=MESH)

        def one(step, carry):
            signal(self.ahead(step))
            return carry

        lax.fori_loop(1, self.length, one, 0)
        if sequence:
            for hop in range(1, 4):
                signal({"seq": lax.rem(self.position + hop, 4), "fsdp": self.index})
            total += 3
        else:
            signal(self.sibling())
            total += 1
        if self.sides == 2:
            signal(self.partner())
            total += 1
        if across:
            signal(self.across())
            total += 1
        pl.semaphore_wait(barrier, total)


def remote(source, target, send, recv, device):
    return pltpu.make_async_remote_copy(
        src_ref=source,
        dst_ref=target,
        send_sem=send,
        recv_sem=recv,
        device_id=device,
        device_id_type=MESH,
    )


def steps(first, last, body):
    def one(step, carry):
        body(step)
        return carry

    lax.fori_loop(first, last, one, 0)


class Reduce:
    def __init__(self, count, pieces, sources, outs, buffers, sems):
        self.place = Place(count)
        self.pieces, self.sources, self.outs = pieces, sources, outs
        self.total, self.core_in, self.side_in, self.line_in, self.across_in, self.done = buffers
        (
            self.core_sem,
            self.load_sem,
            self.side_sem,
            self.line_sem,
            self.across_sem,
            self.last_sem,
            self.store_sem,
        ) = sems

    @staticmethod
    def plan(widths, limit):
        pieces = []
        for a, width in enumerate(widths):
            tiles = max(width // 256, 1)
            parts = -(-tiles * 128 // limit)
            offset = 0
            for part in range(parts):
                wide = (tiles // parts + (1 if part < tiles % parts else 0)) * 128
                pieces.append((a, offset, wide))
                offset += wide
        return pieces

    @staticmethod
    def scratch(count, pieces, depths):
        sides = 2 if count % 2 == 0 else 1
        length = count // sides
        pairs = [(depths[a], wide) for a, _, wide in pieces]
        number = len(pieces)

        def stack(lead):
            return [pltpu.VMEM(lead + pair, bf16) for pair in pairs]

        shapes = (
            stack((count,)) + stack((count,)) + stack((length,)) + stack((length,))
            + stack(()) + stack(())
        )
        sems = [
            pltpu.SemaphoreType.DMA((number, 2)),
            pltpu.SemaphoreType.DMA((number,)),
            pltpu.SemaphoreType.DMA((number, 2, length)),
            pltpu.SemaphoreType.DMA((number, 2, length)),
            pltpu.SemaphoreType.DMA((number, 2)),
            pltpu.SemaphoreType.DMA((number, 2)),
            pltpu.SemaphoreType.DMA((number,)),
        ]
        return shapes + sems

    @staticmethod
    def split(refs, number):
        buffers = [refs[i * number : (i + 1) * number] for i in range(6)]
        return buffers, refs[6 * number :]

    def columns(self, p, core):
        a, offset, wide = self.pieces[p]
        width = self.sources[a].shape[2] // 2
        return a, pl.ds(pl.multiple_of(core * width + offset, 128), wide)

    def to_sibling(self, p):
        a, columns = self.columns(p, 1 - self.place.core)
        return remote(
            self.sources[a].at[:, :, columns],
            self.core_in[p],
            self.core_sem.at[p, 0],
            self.core_sem.at[p, 1],
            self.place.sibling(),
        )

    def load(self, p):
        a, columns = self.columns(p, self.place.core)
        return pltpu.make_async_copy(
            self.sources[a].at[:, :, columns], self.total[p], self.load_sem.at[p]
        )

    def to_side(self, p, spot):
        place = self.place
        return remote(
            self.total[p].at[place.shard(spot, 1 - place.side)],
            self.side_in[p].at[spot],
            self.side_sem.at[p, 0, spot],
            self.side_sem.at[p, 1, spot],
            place.partner(),
        )

    def to_line(self, p, step):
        place = self.place
        spot = lax.rem(place.spot + step, place.length)
        return remote(
            self.total[p].at[place.shard(spot, place.side)],
            self.line_in[p].at[step],
            self.line_sem.at[p, 0, step],
            self.line_sem.at[p, 1, step],
            place.ahead(step),
        )

    def to_across(self, p):
        return remote(
            self.done[p],
            self.across_in[p],
            self.across_sem.at[p, 0],
            self.across_sem.at[p, 1],
            self.place.across(),
        )

    def target(self, p, core):
        a, columns = self.columns(p, core)
        return self.outs[a].at[:, columns]

    def to_result(self, p, arriving):
        core = 1 - self.place.core if arriving else self.place.core
        return remote(
            self.across_in[p],
            self.target(p, core),
            self.last_sem.at[p, 0],
            self.last_sem.at[p, 1],
            self.place.sibling(),
        )

    def store(self, p):
        return pltpu.make_async_copy(
            self.across_in[p], self.target(p, self.place.core), self.store_sem.at[p]
        )

    def start(self, p):
        self.to_sibling(p).start()
        self.load(p).start()

    def stage_core(self, p):
        place = self.place
        self.load(p).wait()
        self.to_sibling(p).wait_recv()
        if place.sides == 2:

            def one(step):
                spot = lax.rem(place.spot + step, place.length)
                shard = place.shard(spot, 1 - place.side)
                self.total[p][shard] = (
                    self.total[p][shard].astype(f32) + self.core_in[p][shard].astype(f32)
                ).astype(bf16)
                self.to_side(p, spot).start()

            steps(1, place.length + 1, one)

    def stage_side(self, p):
        place = self.place

        def one(step):
            spot = lax.rem(place.spot + step, place.length)
            shard = place.shard(spot, place.side)
            total = self.total[p][shard].astype(f32) + self.core_in[p][shard].astype(f32)
            if place.sides == 2:
                self.to_side(p, spot).wait_recv()
                total = total + self.side_in[p][spot].astype(f32)
            self.total[p][shard] = total.astype(bf16)

        def send(step):
            one(step)
            self.to_line(p, step).start()

        steps(1, place.length, send)
        one(0)

    def stage_line(self, p):
        place = self.place
        self.done[p][...] = self.total[p][place.index]

        def one(step):
            self.to_line(p, step).wait_recv()

        steps(1, place.length, one)
        total = self.total[p][place.index].astype(f32)
        if place.length <= 8:
            for step in range(1, place.length):
                total = total + self.line_in[p][step].astype(f32)
        else:
            total = lax.fori_loop(
                1,
                place.length,
                lambda step, carry: carry + self.line_in[p][step].astype(f32),
                total,
            )
        self.done[p][...] = total.astype(bf16)
        self.to_across(p).start()

    def stage_across(self, p):
        copy = self.to_across(p)
        copy.wait_recv()
        self.across_in[p][...] = (
            self.across_in[p][...].astype(f32) + self.done[p][...].astype(f32)
        ).astype(bf16)
        self.to_result(p, False).start()
        self.store(p).start()

    def finish(self, p):
        place = self.place
        self.to_sibling(p).wait_send()
        if place.sides == 2:
            steps(0, place.length, lambda spot: self.to_side(p, spot).wait_send())
        steps(1, place.length, lambda step: self.to_line(p, step).wait_send())
        self.to_across(p).wait_send()
        self.to_result(p, False).wait_send()
        self.to_result(p, True).wait_recv()
        self.store(p).wait()


def reduce_kernel(arrays, count, pieces, *refs):
    buffers, sems = Reduce.split(refs[2 * arrays :], len(pieces))
    reduce = Reduce(count, pieces, refs[:arrays], refs[arrays : 2 * arrays], buffers, sems)
    reduce.place.greet(True)
    number = len(pieces)
    for p in range(number):
        reduce.start(p)
    stages = (reduce.stage_core, reduce.stage_side, reduce.stage_line, reduce.stage_across)
    for turn in range(number + len(stages) - 1):
        for behind, stage in enumerate(stages):
            if 0 <= turn - behind < number:
                stage(turn - behind)
    for p in range(number):
        reduce.finish(p)


def reduce_all(sources, collective_id, limit=768):
    count = lax.axis_size("fsdp")
    arrays = len(sources)
    views = [s.reshape(count, s.shape[0] // count, s.shape[1]) for s in sources]
    pieces = Reduce.plan([s.shape[1] for s in sources], limit)
    anywhere = pl.BlockSpec(memory_space=pl.ANY)
    return pl.pallas_call(
        functools.partial(reduce_kernel, arrays, count, pieces),
        in_specs=[anywhere] * arrays,
        out_specs=[anywhere] * arrays,
        out_shape=[jax.ShapeDtypeStruct(v.shape[1:], bf16) for v in views],
        scratch_shapes=Reduce.scratch(count, pieces, [v.shape[1] for v in views]),
        compiler_params=pltpu.CompilerParams(
            collective_id=collective_id, has_side_effects=True, vmem_limit_bytes=60 * MIB
        ),
    )(*views)


class Gather:
    SEMS = 6

    def __init__(self, count, pieces, shards, outs, sems):
        self.place = Place(count)
        self.pieces, self.shards, self.outs = pieces, shards, outs
        self.line_sem, self.side_sem, self.core_sem, self.across_sem, self.relay_sem, self.own = (
            sems
        )

    @staticmethod
    def scratch(pieces, count):
        length = count // 2 if count % 2 == 0 else count
        number = len(pieces)
        slots = 2 * length if max(piece[3] for piece in pieces) > 1 else 1
        return [
            pltpu.SemaphoreType.DMA((number, 2, length)),
            pltpu.SemaphoreType.DMA((number, 2, length)),
            pltpu.SemaphoreType.DMA((number, 2, slots)),
            pltpu.SemaphoreType.DMA((number, 2, slots)),
            pltpu.SemaphoreType.DMA((number, 2, slots)),
            pltpu.SemaphoreType.DMA((number,)),
        ]

    def portion(self, k, core, chip):
        parts = self.pieces[k][3]
        if parts == 1:
            return 0
        return core if parts == 2 else 2 * chip + core

    def region(self, k, shard, core, chip):
        a, offset, width, parts = self.pieces[k]
        depth = self.shards[a].shape[0]
        rows = depth // parts
        first = shard * depth + self.portion(k, core, chip) * rows
        return self.outs[a].at[pl.ds(pl.multiple_of(first, 16), rows), pl.ds(offset, width)]

    def source(self, k):
        p = self.place
        a, offset, width, parts = self.pieces[k]
        rows = self.shards[a].shape[0] // parts
        first = self.portion(k, p.core, p.chip) * rows
        return self.shards[a].at[pl.ds(pl.multiple_of(first, 16), rows), pl.ds(offset, width)]

    def line(self, k, step, arriving=False):
        p = self.place
        shard = p.shard(p.behind(step), p.side) if arriving else p.index
        target = self.region(k, shard, p.core, p.chip)
        return remote(
            target if arriving else self.source(k),
            target,
            self.line_sem.at[k, 0, step],
            self.line_sem.at[k, 1, step],
            p.ahead(step),
        )

    def side(self, k, step, arriving=False, own=False):
        p = self.place
        shard = p.shard(p.behind(step), 1 - p.side if arriving else p.side)
        target = self.region(k, shard, p.core, p.chip)
        return remote(
            self.source(k) if own else target,
            target,
            self.side_sem.at[k, 0, step],
            self.side_sem.at[k, 1, step],
            p.partner(),
        )

    def cross(self, k, step, other, sems, core, chip, device):
        p = self.place
        shard = p.shard(p.behind(step), 1 - p.side if other else p.side)
        target = self.region(k, shard, core, chip)
        slot = 2 * step + (1 if other else 0)
        return remote(target, target, sems.at[k, 0, slot], sems.at[k, 1, slot], device)

    def core(self, k, step, other, arriving=False):
        p = self.place
        core = 1 - p.core if arriving else p.core
        return self.cross(k, step, other, self.core_sem, core, p.chip, p.sibling())

    def across(self, k, step, other, arriving=False):
        p = self.place
        chip = 1 - p.chip if arriving else p.chip
        return self.cross(k, step, other, self.across_sem, p.core, chip, p.across())

    def relay(self, k, step, other, arriving=False):
        p = self.place
        core = 1 - p.core if arriving else p.core
        return self.cross(k, step, other, self.relay_sem, core, 1 - p.chip, p.sibling())

    def keep(self, k):
        a, offset, width, _ = self.pieces[k]
        depth = self.shards[a].shape[0]
        rows = pl.ds(pl.multiple_of(self.place.index * depth, 16), depth)
        columns = pl.ds(offset, width)
        return pltpu.make_async_copy(
            self.shards[a].at[:, columns], self.outs[a].at[rows, columns], self.own.at[k]
        )

    def hand(self, k, step, other):
        parts = self.pieces[k][3]
        if parts == 4:
            self.across(k, step, other).start()
        if parts > 1:
            self.core(k, step, other).start()

    def start(self, k):
        steps(1, self.place.length, lambda step: self.line(k, step).start())
        if self.place.sides == 2:
            self.side(k, 0, own=True).start()
        self.keep(k).start()

    def forward(self, k):
        def one(step):
            self.line(k, step, True).wait_recv()
            if self.place.sides == 2:
                self.side(k, step).start()
            self.hand(k, step, False)

        steps(1, self.place.length, one)

    def spread(self, k):
        def one(step):
            self.side(k, step, True).wait_recv()
            self.hand(k, step, True)

        if self.place.sides == 2:
            steps(0, self.place.length, one)

    def each(self, body):
        steps(1, self.place.length, lambda step: body(step, False))
        if self.place.sides == 2:
            steps(0, self.place.length, lambda step: body(step, True))

    def exchange(self, k):
        def one(step, other):
            self.across(k, step, other, True).wait_recv()
            self.relay(k, step, other).start()

        if self.pieces[k][3] == 4:
            self.each(one)

    def arrive(self, k):
        parts = self.pieces[k][3]

        def one(step, other):
            self.core(k, step, other, True).wait_recv()
            if parts == 4:
                self.relay(k, step, other, True).wait_recv()

        self.keep(k).wait()
        if parts > 1:
            self.each(one)

    def sent(self, k):
        parts = self.pieces[k][3]

        def one(step, other):
            self.core(k, step, other).wait_send()
            if parts == 4:
                self.across(k, step, other).wait_send()
                self.relay(k, step, other).wait_send()

        steps(1, self.place.length, lambda step: self.line(k, step).wait_send())
        if self.place.sides == 2:
            steps(0, self.place.length, lambda step: self.side(k, step).wait_send())
        if parts > 1:
            self.each(one)

    def events(self, tiles, urgent, ahead=3):
        made = []
        line = side = across = 0.0
        hop = 8.0
        number = len(self.pieces)
        for k in range(number):
            parts = self.pieces[k][3]
            margin = 8.0 if k < urgent else 30.0
            load = tiles[k] * (2 if parts == 4 else 4)
            line = line + load
            side = max(side + load, line + load / 4 + hop)
            last = side
            made.append((line + hop, k, 0))
            made.append((side + hop, k, 1))
            if parts == 4:
                across = max(across + 3.5 * tiles[k], side + tiles[k] / 2 + hop)
                last = across
                made.append((across + hop + margin, k, 2))
            wait = 0.0 if k < urgent else 2 * margin
            made.append((last + 2 * hop + wait + (margin if parts == 4 else 0.0), k, 3))
        made.sort()

        def action(k, kind):
            if kind == 0:
                self.forward(k)
                if k + ahead < number:
                    self.start(k + ahead)
            else:
                (self.spread, self.exchange, self.arrive)[kind - 1](k)

        return [(when, k, kind, functools.partial(action, k, kind)) for when, k, kind in made]


PACK = (16, 512)


def pack_small(gains, taps):
    count = taps.shape[0]

    def fit(values, rows):
        values = values.reshape(count, -1, values.shape[-1]).astype(bf16)
        return jnp.pad(
            values, ((0, 0), (0, rows - values.shape[1]), (0, PACK[1] - values.shape[2]))
        )

    rows = [fit(gains[0], 1), fit(gains[1], 1), fit(gains[2], 2), fit(taps, PACK[0] - 4)]
    return jnp.concatenate(rows, axis=1).reshape(count * PACK[0], PACK[1])


def unpack_small(packed, shapes):
    packed = packed.reshape(-1, PACK[0], PACK[1])
    gains = [packed[:, row, : shape[0]] for row, shape in enumerate(shapes[:3])]
    return gains + [packed[:, 4 : 4 + shapes[3][0], : shapes[3][1]]]


def place_rows(packed, count, width):
    if width % 128 == 0:
        return jnp.concatenate(
            [packed[s * PACK[0] : (s + 1) * PACK[0], :width] for s in range(count)], axis=1
        )
    total = count * width
    row = lax.broadcasted_iota(jnp.int32, (PACK[1], total), 0)
    col = lax.broadcasted_iota(jnp.int32, (PACK[1], total), 1)
    pick = jnp.where(lax.rem(col, width) == row, 1.0, 0.0).astype(bf16)
    wide = nn(packed.astype(bf16), pick)
    row = lax.broadcasted_iota(jnp.int32, wide.shape, 0)
    col = lax.broadcasted_iota(jnp.int32, wide.shape, 1)
    wide = jnp.where(lax.div(row, PACK[0]) == lax.div(col, width), wide, 0.0).astype(bf16)
    row = lax.broadcasted_iota(jnp.int32, (PACK[0], count * PACK[0]), 0)
    col = lax.broadcasted_iota(jnp.int32, (PACK[0], count * PACK[0]), 1)
    fold = jnp.where(lax.rem(col, PACK[0]) == row, 1.0, 0.0).astype(bf16)
    return nn(fold, wide)


GROUP = 2
BACK = 1


def grid_indices():
    row = lax.broadcasted_iota(jnp.int32, (CHUNK, CHUNK), 0)
    col = lax.broadcasted_iota(jnp.int32, (CHUNK, CHUNK), 1)
    return row, col


def conv_pre(wide_ref, taps, rows):
    total = None
    for offset in range(TAPS):
        term = taps[offset : offset + 1, :] * wide_ref[pl.ds(HALO - TAPS + 1 + offset, rows), :]
        total = term if total is None else total + term
    return total


def sigmoid(values):
    return 1.0 / (1.0 + jnp.exp(-values))


def head_column(table, head):
    lane = lax.broadcasted_iota(jnp.int32, table.shape, 1)
    return jnp.sum(jnp.where(lane == head, table, 0.0), axis=1, keepdims=True)


ARRAYS = 7


def forward_kernel(count, pieces, mixed, heads, tap_width, *refs):
    tokens_ref = refs[0]
    shards, refs = refs[1 : 1 + ARRAYS], refs[1 + ARRAYS :]
    gathered, refs = refs[:ARRAYS], refs[ARRAYS:]
    (
        finals_ref,
        normed_ref,
        signals_ref,
        logit_ref,
        taps_ref,
        out_ref,
        carry_ref,
        fresh_ref,
        inverse_ref,
        starts_ref,
    ), refs = refs[:10], refs[10:]
    (
        tokens,
        weights,
        rates_weight,
        packed,
        all_taps,
        wide,
        level_masks,
        final,
        halo_sem,
        token_sem,
        load_sem,
        final_sem,
        *sems,
    ) = refs
    group = pl.program_id(0)
    groups = heads // GROUP
    rows = out_ref.shape[0]
    size = out_ref.shape[1] // GROUP
    span = GROUP * size
    chunks = rows // CHUNK
    levels = CHUNK.bit_length() - 1
    row, col = grid_indices()
    gather = Gather(count, pieces, shards, gathered, sems)
    place = gather.place
    tiles = [piece[2] / 128 * shards[piece[0]].shape[0] / 128 for piece in pieces]
    events = gather.events(tiles, 2 + groups)

    def halo(arriving):
        return remote(
            tokens_ref.at[pl.ds(rows - HALO, HALO), :],
            tokens.at[pl.ds(0, HALO), :],
            halo_sem.at[0],
            halo_sem.at[1],
            {"seq": lax.rem(place.position + 1, 4), "fsdp": place.index},
        )

    def load(step, slot):
        return pltpu.make_async_copy(
            gathered[mixed].at[:, pl.ds(pl.multiple_of(step * 3 * span, 128), 3 * span)],
            weights.at[slot],
            load_sem.at[slot],
        )

    per_step = 9
    plan = {}
    mark = 0
    for step in range(groups):
        for spot in range(per_step):
            now = 60.0 + (step * per_step + spot) * 5.0
            upto = mark
            for index in range(mark, len(events)):
                when, k, kind, _ = events[index]
                if spot == 0 and kind == 3 and (k == 2 + step or (step == 0 and k < 2)):
                    upto = index + 1
                elif when <= now and upto == index:
                    upto = index + 1
            plan[step, spot] = (mark, upto)
            mark = upto
    remaining = (mark, len(events))

    def run(bounds):
        for _, _, _, action in events[bounds[0] : bounds[1]]:
            action()

    def spot(number):
        for step in range(groups):
            bounds = plan[step, number]
            if bounds[1] > bounds[0]:

                @pl.when(group == step)
                def _():
                    run(bounds)

    @pl.when(group == 0)
    def _():
        own = pltpu.make_async_copy(tokens_ref, tokens.at[pl.ds(HALO, rows), :], token_sem.at[0])
        own.start()
        place.greet_all()

        @pl.when(place.position < 3)
        def _():
            halo(False).start()

        gather.start(0)
        gather.start(1)
        gather.start(2)

        @pl.when(place.position == 0)
        def _():
            tokens[pl.ds(0, HALO), :] = jnp.zeros((HALO, tokens.shape[1]), bf16)

        for level in range(levels):
            same = (row >> (level + 1)) == (col >> (level + 1))
            below = ((row >> level) & 1 == 1) & ((col >> level) & 1 == 0)
            level_masks[level] = jnp.where(same & below, 1.0, 0.0).astype(bf16)

        limit = max(i for i, event in enumerate(events) if event[1] == 0) + 1
        run((0, limit))
        copy = pltpu.make_async_copy(gathered[0], packed, token_sem.at[1])
        copy.start()
        copy.wait()
        small = packed[...].astype(f32)
        gain = place_rows(small, count, tokens.shape[1] // count)[0:1, :]
        all_taps[...] = place_rows(small, count, tap_width)[4 : 4 + TAPS, :]
        own.wait()

        @pl.when(place.position > 0)
        def _():
            halo(True).wait_recv()

        block = 208 if tokens.shape[0] % 208 == 0 else HALO

        def norm(index):
            part = pl.ds(pl.multiple_of(index * block, HALO), block)
            normed_ref[part, :] = rms_scale(tokens[part, :].astype(f32), gain).astype(bf16)

        steps(0, tokens.shape[0] // block, norm)
        run((limit, plan[0, 0][1]))
        copy = pltpu.make_async_copy(gathered[1], rates_weight, token_sem.at[1])
        copy.start()
        load(0, 0).start()
        copy.wait()
        logit_ref[...] = nn(normed_ref[pl.ds(HALO, rows), :], rates_weight[...]).astype(bf16)
        load(0, 0).wait()

    for step in range(1, groups):
        bounds = plan[step, 0]

        @pl.when(group == step)
        def _():
            run(bounds)
            load(step, 0).start()
            load(step, 0).wait()

    signals_ref[...] = nn(normed_ref[...], weights[0]).astype(bf16)
    spot(1)

    lows = [[], [], []]
    for inner in range(GROUP):
        for which in range(3):
            first = pl.multiple_of((which * heads + group * GROUP + inner) * size, 128)
            taps = all_taps[:, pl.ds(first, size)]
            taps_ref[inner, which] = taps
            wide[...] = signals_ref[:, pl.ds((inner * 3 + which) * size, size)].astype(f32)
            pre = conv_pre(wide, taps, rows)
            act = pre * sigmoid(pre)
            if which < 2:
                act = act * lax.rsqrt(jnp.sum(act * act, axis=1, keepdims=True) + epsilon)
            lows[which].append(act.astype(bf16))
        if inner == 0:
            spot(2)
    spot(3)
    logits = logit_ref[...].astype(f32)
    rates = [sigmoid(head_column(logits, group * GROUP + inner)) for inner in range(GROUP)]
    scaling = size ** (-0.5)
    eye = jnp.where(row == col, 1.0, 0.0)
    lower = row >= col

    work = [(inner, chunk) for inner in range(GROUP) for chunk in range(chunks)]

    def cut(values, item):
        inner, chunk = item
        return values[inner][chunk * CHUNK : (chunk + 1) * CHUNK]

    queries, keys, values = lows
    stricts = [(cut(rates, i) * nt(cut(keys, i), cut(keys, i))).astype(bf16) for i in work]
    results = [eye - (strict * level_masks[0]).astype(f32) for strict in stricts]
    scores = [jnp.where(lower, nt(cut(queries, i), cut(keys, i)), 0.0).astype(bf16) for i in work]
    for level in range(1, levels):
        mask = level_masks[level]
        lowered = [result.astype(bf16) for result in results]
        inners = [nn(low, strict * mask).astype(bf16) for low, strict in zip(lowered, stricts)]
        results = [
            result - nn(inner, low) for result, inner, low in zip(results, inners, lowered)
        ]
        if level in (2, 4, 6):
            spot(3 + level // 2)
    inverses = [result.astype(bf16) for result in results]
    for (inner, chunk), inverse in zip(work, inverses):
        part = slice(chunk * CHUNK, (chunk + 1) * CHUNK)
        inverse_ref[part, inner * CHUNK : (inner + 1) * CHUNK] = inverse
    spot(7)

    srow = lax.broadcasted_iota(jnp.int32, (size, size), 0)
    scol = lax.broadcasted_iota(jnp.int32, (size, size), 1)
    memories = [
        jnp.concatenate(
            [jnp.zeros((size, size), f32), jnp.where(srow == scol, 1.0, 0.0)], axis=1
        )
    ] * GROUP
    for chunk in range(chunks):
        part = slice(chunk * CHUNK, (chunk + 1) * CHUNK)
        for inner in range(GROUP):
            item = (inner, chunk)
            key_part, query_part, rate_part = cut(keys, item), cut(queries, item), cut(rates, item)
            low_memory = memories[inner].astype(bf16)
            starts_ref[inner, chunk] = low_memory
            seen = nn(key_part, low_memory)
            aim = jnp.concatenate(
                [cut(values, item).astype(f32), jnp.zeros((CHUNK, size), f32)], axis=1
            )
            aim = (rate_part * (aim - seen)).astype(bf16)
            fresh = nn(inverses[work.index(item)], aim).astype(bf16)
            fresh_ref[part, inner * 2 * size : (inner + 1) * 2 * size] = fresh
            both = scaling * (
                nn(query_part, low_memory) + nn(scores[work.index(item)], fresh)
            )
            out_ref[part, inner * size : (inner + 1) * size] = both[:, :size]
            carry_ref[part, inner * size : (inner + 1) * size] = both[:, size:].astype(bf16)
            memories[inner] = memories[inner] + tn(key_part, fresh)

    def send_final(step, hop):
        position = lax.rem(place.position + hop, 4)
        block = pl.ds(step * GROUP, GROUP)
        return remote(
            final.at[block],
            finals_ref.at[place.position, block],
            final_sem.at[0, step, hop],
            final_sem.at[1, step, hop],
            {"seq": position, "fsdp": place.index},
        )

    def keep_final(step):
        block = pl.ds(step * GROUP, GROUP)
        return pltpu.make_async_copy(
            final.at[block], finals_ref.at[place.position, block], final_sem.at[0, step, 0]
        )

    def take_final(step, hop):
        position = lax.rem(place.position + 4 - hop, 4)
        block = pl.ds(step * GROUP, GROUP)
        return remote(
            final.at[block],
            finals_ref.at[position, block],
            final_sem.at[0, step, hop],
            final_sem.at[1, step, hop],
            {"seq": position, "fsdp": place.index},
        )

    for step in range(groups):

        @pl.when(group == step)
        def _():
            for inner in range(GROUP):
                final[step * GROUP + inner] = memories[inner].astype(bf16)
            for hop in range(1, 4):
                send_final(step, hop).start()
            keep_final(step).start()

    spot(8)

    @pl.when(group == groups - 1)
    def _():
        run(remaining)
        for k in range(len(pieces)):
            gather.sent(k)
        for step in range(groups):
            for hop in range(1, 4):
                send_final(step, hop).wait_send()
                take_final(step, hop).wait_recv()
            keep_final(step).wait()

        @pl.when(place.position < 3)
        def _():
            halo(False).wait_send()


def plan_pieces(depths, widths, span):
    def portions(a, wanted):
        while depths[a] % (16 * wanted) != 0:
            wanted //= 2
        return wanted

    pieces = [(0, 0, widths[0], 1), (1, 0, widths[1], portions(1, 2))]
    for step in range(widths[2] // span):
        pieces.append((2, step * span, span, portions(2, 4)))
    pieces.append((3, 0, widths[3], portions(3, 4)))
    for a in (4, 5, 6):
        half = widths[a] // 2
        for part in range(2):
            wanted = 2 if (a, part) in ((5, 0), (6, 1)) else 4
            pieces.append((a, part * half, half, portions(a, wanted)))
    return pieces


def forward(tokens, shards, heads, tap_width):
    count = lax.axis_size("fsdp")
    rows, width = tokens.shape
    size = width // heads
    span = GROUP * size
    groups = heads // GROUP
    chunks = rows // CHUNK
    wide_rows = rows + HALO
    depths = [shard.shape[0] for shard in shards]
    widths = [shard.shape[1] for shard in shards]
    pieces = plan_pieces(depths, widths, 3 * span)
    anywhere = pl.BlockSpec(memory_space=pl.ANY)
    shape = jax.ShapeDtypeStruct
    return pl.pallas_call(
        functools.partial(forward_kernel, count, pieces, 2, heads, tap_width),
        grid=(groups,),
        in_specs=[anywhere] * (1 + ARRAYS),
        out_specs=[anywhere] * (ARRAYS + 1)
        + [
            pl.BlockSpec((wide_rows, width), lambda g: (0, 0)),
            pl.BlockSpec((wide_rows, 3 * span), lambda g: (0, g)),
            pl.BlockSpec((rows, widths[1]), lambda g: (0, 0)),
            pl.BlockSpec((GROUP, 3, TAPS, size), lambda g: (g, 0, 0, 0)),
            pl.BlockSpec((rows, span), lambda g: (0, g)),
            pl.BlockSpec((rows, span), lambda g: (0, g)),
            pl.BlockSpec((rows, 2 * span), lambda g: (0, g)),
            pl.BlockSpec((rows, GROUP * CHUNK), lambda g: (0, g)),
            pl.BlockSpec((GROUP, chunks, size, 2 * size), lambda g: (g, 0, 0, 0)),
        ],
        out_shape=[shape((count * d, w), bf16) for d, w in zip(depths, widths)]
        + [
            shape((4, heads, size, 2 * size), bf16),
            shape((wide_rows, width), bf16),
            shape((wide_rows, 3 * width), bf16),
            shape((rows, widths[1]), bf16),
            shape((heads, 3, TAPS, size), f32),
            shape((rows, width), f32),
            shape((rows, width), bf16),
            shape((rows, 2 * width), bf16),
            shape((rows, heads * CHUNK), bf16),
            shape((heads, chunks, size, 2 * size), bf16),
        ],
        scratch_shapes=[
            pltpu.VMEM((wide_rows, width), bf16),
            pltpu.VMEM((1, width, 3 * span), bf16),
            pltpu.VMEM((width, widths[1]), bf16),
            pltpu.VMEM((count * PACK[0], PACK[1]), bf16),
            pltpu.VMEM((TAPS, 3 * width), f32),
            pltpu.VMEM((wide_rows, size), f32),
            pltpu.VMEM((CHUNK.bit_length() - 1, CHUNK, CHUNK), bf16),
            pltpu.VMEM((heads, size, 2 * size), bf16),
            pltpu.SemaphoreType.DMA((2,)),
            pltpu.SemaphoreType.DMA((2,)),
            pltpu.SemaphoreType.DMA((2,)),
            pltpu.SemaphoreType.DMA((2, groups, 4)),
        ]
        + Gather.scratch(pieces, count),
        compiler_params=pltpu.CompilerParams(
            collective_id=0, has_side_effects=True, vmem_limit_bytes=60 * MIB
        ),
    )(tokens, *shards)


def mix_kernel(position_ref, out_ref, carry_ref, finals_ref, gain_ref, mixed_ref, state_ref):
    position = position_ref[0]
    size = out_ref.shape[1]
    state = jnp.zeros((size, size), f32)
    for index in range(finals_ref.shape[0] - 1):
        pair = finals_ref[index, 0].astype(f32)
        later = pair[:, :size] + jnp.dot(pair[:, size:], state, precision=highest)
        state = jnp.where(index < position, later, state)
    state_ref[0] = state
    output = out_ref[...] + nn(carry_ref[...], state.astype(bf16))
    gain = gain_ref[...].astype(f32)
    mixed_ref[...] = rms_scale(output, gain).astype(bf16)


def mix(position, outputs, carries, finals, gain):
    rows, width = outputs.shape
    groups, heads, size, _ = finals.shape
    plain = pl.BlockSpec((rows, size), lambda h: (0, h))
    return pl.pallas_call(
        mix_kernel,
        grid=(heads,),
        in_specs=[
            pl.BlockSpec(memory_space=pltpu.SMEM),
            plain,
            plain,
            pl.BlockSpec((groups, 1, size, 2 * size), lambda h: (0, h, 0, 0)),
            pl.BlockSpec((1, size), lambda h: (0, 0)),
        ],
        out_specs=[plain, pl.BlockSpec((1, size, size), lambda h: (h, 0, 0))],
        out_shape=[
            jax.ShapeDtypeStruct((rows, width), bf16),
            jax.ShapeDtypeStruct((heads, size, size), f32),
        ],
        compiler_params=pltpu.CompilerParams(vmem_limit_bytes=32 * MIB),
    )(position, outputs, carries, finals, gain)


def unmix_kernel(
    out_ref, carry_ref, state_ref, gain_ref, grad_ref, grad_out_ref, grad_state_ref, grad_gain_ref
):
    output = out_ref[...] + nn(carry_ref[...], state_ref[0].astype(bf16))
    gain = gain_ref[...].astype(f32)
    grad = grad_ref[...].astype(f32)
    scaling = lax.rsqrt(jnp.mean(output * output, axis=1, keepdims=True) + epsilon)
    unit_rows = output * scaling

    @pl.when(pl.program_id(0) == 0)
    def _():
        grad_gain_ref[...] = jnp.zeros_like(grad_gain_ref)

    grad_gain_ref[...] += jnp.sum(grad * unit_rows, axis=0, keepdims=True)
    scaled = grad * gain
    grad_out = scaling * (scaled - unit_rows * jnp.mean(scaled * unit_rows, axis=1, keepdims=True))
    low_grad = grad_out.astype(bf16)
    grad_state_ref[0] = tn(carry_ref[...], low_grad)
    grad_out_ref[...] = (grad_out * output.shape[1] ** (-0.5)).astype(bf16)


def unmix(outputs, carries, states, gain, grad_heads):
    rows, width = outputs.shape
    heads, size, _ = states.shape
    plain = pl.BlockSpec((rows, size), lambda h: (0, h))
    state = pl.BlockSpec((1, size, size), lambda h: (h, 0, 0))
    vector = pl.BlockSpec((1, size), lambda h: (0, 0))
    return pl.pallas_call(
        unmix_kernel,
        grid=(heads,),
        in_specs=[plain, plain, state, vector, plain],
        out_specs=[plain, state, vector],
        out_shape=[
            jax.ShapeDtypeStruct((rows, width), bf16),
            jax.ShapeDtypeStruct((heads, size, size), f32),
            jax.ShapeDtypeStruct((1, size), f32),
        ],
        compiler_params=pltpu.CompilerParams(vmem_limit_bytes=32 * MIB),
    )(outputs, carries, states, gain, grad_heads)


def backward_kernel(
    signals_ref,
    logit_ref,
    taps_ref,
    grad_ref,
    fresh_ref,
    inverse_ref,
    starts_ref,
    state_ref,
    grad_state_ref,
    grad_signals_ref,
    tails_ref,
    firsts_ref,
    grad_taps_ref,
    grad_logit_ref,
    wides,
    pres,
    grads,
    padded,
):
    group = pl.program_id(0)
    rows, span = grad_ref.shape
    size = span // BACK
    chunks = rows // CHUNK
    row, col = grid_indices()
    lower, upper = row >= col, row <= col

    def tap_row(which):
        return jnp.concatenate([taps_ref[inner, which] for inner in range(BACK)], axis=1)

    def split(values):
        return [values[:, inner * size : (inner + 1) * size] for inner in range(BACK)]

    lows, scales = [], []
    for which in range(3):
        wides[which] = signals_ref[:, pl.ds(which * span, span)].astype(f32)
        pre = conv_pre(wides.at[which], tap_row(which), rows)
        pres[which] = pre
        act = split(pre * sigmoid(pre))
        if which < 2:
            scale = [
                lax.rsqrt(jnp.sum(part * part, axis=1, keepdims=True) + epsilon) for part in act
            ]
            act = [part * one for part, one in zip(act, scale)]
            scales.append(scale)
        lows.append([part.astype(bf16) for part in act])
    queries, keys, values = lows
    logits = logit_ref[...].astype(f32)
    rates = [sigmoid(head_column(logits, group * BACK + inner)) for inner in range(BACK)]

    states = [state_ref[inner].astype(bf16) for inner in range(BACK)]
    fresh_all = []
    for inner in range(BACK):
        first = fresh_ref[:, pl.ds(inner * 2 * size, size)].astype(f32)
        second = fresh_ref[:, pl.ds((inner * 2 + 1) * size, size)]
        fresh_all.append((first + nn(second, states[inner])).astype(bf16))

    grad_memories = [grad_state_ref[inner] for inner in range(BACK)]
    grad_rates = [[None] * chunks for _ in range(BACK)]
    for chunk in reversed(range(chunks)):
        part = slice(chunk * CHUNK, (chunk + 1) * CHUNK)
        for inner in range(BACK):
            key, query, value = keys[inner][part], queries[inner][part], values[inner][part]
            rate = rates[inner][part]
            columns = slice(inner * size, (inner + 1) * size)
            grad_out = grad_ref[part, columns]
            fresh = fresh_all[inner][part]
            start = starts_ref[inner, chunk]
            memory = (start[:, :size].astype(f32) + nn(start[:, size:], states[inner])).astype(
                bf16
            )
            low_grad = grad_memories[inner].astype(bf16)
            key_f = key.astype(f32)
            rated = (rate * key_f).astype(bf16)

            scores_t = jnp.where(upper, nt(key, query), 0.0).astype(bf16)
            grad_fresh = (nn(scores_t, grad_out) + nn(key, low_grad)).astype(bf16)
            aim = tn(inverse_ref[part, inner * CHUNK : (inner + 1) * CHUNK], grad_fresh)
            low_aim = aim.astype(bf16)
            grad_memories[inner] = (
                grad_memories[inner] + tn(query, grad_out) - tn(rated, low_aim)
            )

            grad_scores = jnp.where(lower, nt(grad_out, fresh), 0.0).astype(bf16)
            grad_scores_t = jnp.where(upper, nt(fresh, grad_out), 0.0).astype(bf16)
            grad_strict = jnp.where(row > col, nt(low_aim, fresh), 0.0).astype(bf16)
            grad_strict_t = jnp.where(row < col, nt(fresh, low_aim), 0.0).astype(bf16)

            grad_query = nt(grad_out, memory) + nn(grad_scores, key)
            within = -(nn(grad_strict, key) + nt(low_aim, memory))
            grad_rates[inner][chunk] = jnp.sum(
                key_f * within + value.astype(f32) * aim, axis=1, keepdims=True
            )
            grad_key = (
                rate * within
                - nn(grad_strict_t, rated)
                + nn(grad_scores_t, query)
                + nt(fresh, low_grad)
            )
            grads[0, part, columns] = grad_query
            grads[1, part, columns] = grad_key
            grads[2, part, columns] = rate * aim

    @pl.when(group == 0)
    def _():
        grad_logit_ref[...] = jnp.zeros_like(grad_logit_ref)
        padded[...] = jnp.zeros_like(padded)

    lane = lax.broadcasted_iota(jnp.int32, grad_logit_ref.shape, 1)
    for inner in range(BACK):
        grad_rate = jnp.concatenate(grad_rates[inner], axis=0)
        grad_logit = grad_rate * rates[inner] * (1.0 - rates[inner])
        grad_logit_ref[...] = jnp.where(
            lane == group * BACK + inner, grad_logit, grad_logit_ref[...]
        )

    for which in range(3):
        taps = tap_row(which)
        pre = pres[which]
        sig = sigmoid(pre)
        grad_act = grads[which]
        if which < 2:
            unit_rows = split(pre * sig)
            parts = []
            for one, unit, scale in zip(split(grad_act), unit_rows, scales[which]):
                unit = unit * scale
                parts.append(scale * (one - unit * jnp.sum(one * unit, axis=1, keepdims=True)))
            grad_act = jnp.concatenate(parts, axis=1)
        grad_pre = grad_act * sig * (1.0 + pre * (1.0 - sig))
        padded[pl.ds(HALO, rows), :] = grad_pre
        for offset in range(TAPS):
            shifted = wides[which, pl.ds(HALO - TAPS + 1 + offset, rows), :]
            total = jnp.sum(grad_pre * shifted, axis=0, keepdims=True)
            for inner, one in enumerate(split(total)):
                grad_taps_ref[inner, which, pl.ds(offset, 1), :] = one

        def back(start, number):
            total = None
            for offset in range(TAPS):
                term = (
                    taps[offset : offset + 1, :]
                    * padded[pl.ds(start + TAPS - 1 - offset, number), :]
                )
                total = term if total is None else total + term
            return total

        columns = pl.ds(which * span, span)
        grad_signal = back(HALO, rows)
        grad_signals_ref[:, columns] = grad_signal.astype(bf16)
        tails_ref[:, columns] = grad_signal[rows - HALO :]
        firsts_ref[:, columns] = back(0, HALO)


def delta_backward(
    signals, logits, taps, grad_out, fresh, inverses, starts, state, grad_state
):
    wide_rows = signals.shape[0]
    rows, width = grad_out.shape
    heads, _, _, size = taps.shape
    span = BACK * size
    chunks = rows // CHUNK
    whole = pl.BlockSpec(logits.shape, lambda g: (0, 0))
    tap = pl.BlockSpec((BACK, 3, TAPS, size), lambda g: (g, 0, 0, 0))
    state_spec = pl.BlockSpec((BACK, size, size), lambda g: (g, 0, 0))
    edge = pl.BlockSpec((HALO, 3 * span), lambda g: (0, g))
    return pl.pallas_call(
        backward_kernel,
        grid=(heads // BACK,),
        in_specs=[
            pl.BlockSpec((wide_rows, 3 * span), lambda g: (0, g)),
            whole,
            tap,
            pl.BlockSpec((rows, span), lambda g: (0, g)),
            pl.BlockSpec((rows, 2 * span), lambda g: (0, g)),
            pl.BlockSpec((rows, BACK * CHUNK), lambda g: (0, g)),
            pl.BlockSpec((BACK, chunks, size, 2 * size), lambda g: (g, 0, 0, 0)),
            state_spec,
            state_spec,
        ],
        out_specs=[pl.BlockSpec((rows, 3 * span), lambda g: (0, g)), edge, edge, tap, whole],
        out_shape=[
            jax.ShapeDtypeStruct((rows, 3 * width), bf16),
            jax.ShapeDtypeStruct((HALO, 3 * width), f32),
            jax.ShapeDtypeStruct((HALO, 3 * width), f32),
            jax.ShapeDtypeStruct(taps.shape, f32),
            jax.ShapeDtypeStruct(logits.shape, f32),
        ],
        scratch_shapes=[
            pltpu.VMEM((3, wide_rows, span), f32),
            pltpu.VMEM((3, rows, span), f32),
            pltpu.VMEM((3, rows, span), f32),
            pltpu.VMEM((rows + 2 * HALO, span), f32),
        ],
        compiler_params=pltpu.CompilerParams(vmem_limit_bytes=60 * MIB),
    )(signals, logits, taps, grad_out, fresh, inverses, starts, state, grad_state)


def batched(left_side, right_side, transpose_left=False):
    return lax.dot_general(
        left_side,
        right_side,
        (((1 if transpose_left else 2,), (1,)), ((0,), (0,))),
        precision=highest,
        preferred_element_type=f32,
    )


def local(
    inputs,
    g_attn,
    w_query,
    w_key,
    w_value,
    w_beta,
    conv_taps,
    o_gain,
    w_out,
    g_mlp,
    w_gate,
    w_up,
    w_down,
    cotangent,
):
    count = lax.axis_size("fsdp")
    position = lax.axis_index("seq")
    groups = lax.axis_size("seq")
    tokens_low = inputs[0]
    rows, width = tokens_low.shape
    heads = w_beta.shape[1]
    size = width // heads
    depth = w_query.shape[0]
    small = (g_attn.shape, g_mlp.shape, o_gain.shape, conv_taps.shape)
    packed = pack_small((g_attn[None], g_mlp[None], o_gain[None]), conv_taps[None])
    mixed = jnp.stack([w.reshape(depth, -1, size) for w in (w_query, w_key, w_value)], axis=2)
    shards = (
        packed,
        jnp.pad(w_beta, ((0, 0), (0, 128 - heads))),
        mixed.reshape(depth, 3 * width),
        w_out,
        w_gate,
        w_up,
        jnp.transpose(w_down),
    )
    results = forward(tokens_low, shards, heads, conv_taps.shape[1])
    packed, w_beta, w_mixed, w_out, w_gate, w_up, w_down_t = results[:ARRAYS]
    finals, wide_normed, signals, logits, taps = results[ARRAYS : ARRAYS + 5]
    outputs, carries, fresh, inverses, starts = results[ARRAYS + 5 :]
    g_attn, g_mlp, o_gain, _ = unpack_small(packed, small)
    g_attn, g_mlp, o_gain = g_attn.reshape(-1), g_mlp.reshape(-1), o_gain.reshape(-1)
    gain_attn = g_attn.astype(f32)
    tokens = tokens_low.astype(f32)
    normed = wide_normed[HALO:]

    gain_out = o_gain.reshape(1, size)
    head_rows, state_in = mix(position.reshape(1), outputs, carries, finals, gain_out)
    attended = tokens + nn(head_rows, w_out)
    gain_mlp = g_mlp.astype(f32)
    normed_ff = rms_scale(attended, gain_mlp).astype(bf16)
    gated = nn(normed_ff, w_gate)
    upward = nn(normed_ff, w_up)
    sigmoid_gate = jax.nn.sigmoid(gated)
    activated = gated * sigmoid_gate
    hidden = (activated * upward).astype(bf16)
    layer_out = (attended + nt(hidden, w_down_t)).astype(bf16)

    grad_out = cotangent[0]
    grad_down_t = tn(grad_out, hidden).astype(bf16)
    grad_hidden = nn(grad_out, w_down_t)
    grad_gate = (grad_hidden * upward * sigmoid_gate * (1.0 + gated * (1.0 - sigmoid_gate))).astype(
        bf16
    )
    grad_upward = (grad_hidden * activated).astype(bf16)
    grad_gate_matrix = tn(normed_ff, grad_gate).astype(bf16)
    grad_up_matrix = tn(normed_ff, grad_upward).astype(bf16)
    grad_normed_ff = nt(grad_gate, w_gate) + nt(grad_upward, w_up)
    grad_from_ff, grad_gain_mlp = norm_backward(attended, gain_mlp, grad_normed_ff)
    grad_attended = grad_out.astype(f32) + grad_from_ff

    grad_mixed = grad_attended.astype(bf16)
    grad_out_matrix = tn(head_rows, grad_mixed).astype(bf16)
    grad_heads = nt(grad_mixed, w_out).astype(bf16)
    grad_delta, grad_starts, grad_gain_out = unmix(
        outputs, carries, state_in, gain_out, grad_heads
    )
    grads_all = lax.all_gather(grad_starts, "seq", axis=0)
    grad_state = jnp.zeros((heads, size, size), f32)
    grad_states = [grad_state]
    for index in reversed(range(1, groups)):
        grad_state = grads_all[index] + batched(
            finals[index, :, :, size:].astype(f32), grad_state, transpose_left=True
        )
        grad_states.append(grad_state)
    grad_states.reverse()
    grad_final = lax.dynamic_index_in_dim(jnp.stack(grad_states), position, 0, keepdims=False)

    grad_signals, tails, firsts, grad_taps, grad_logits = delta_backward(
        signals,
        logits,
        taps,
        grad_delta,
        fresh,
        inverses,
        starts,
        state_in,
        grad_final,
    )
    backward_pairs = [(index + 1, index) for index in range(groups - 1)]
    received = lax.ppermute(firsts, "seq", backward_pairs)
    fixed = (tails + received).astype(bf16)
    grad_signals = lax.dynamic_update_slice(grad_signals, fixed, (rows - HALO, 0))
    grad_logits = grad_logits.astype(bf16)

    grad_mixed_matrix = tn(normed, grad_signals).astype(bf16)
    grad_beta_matrix = jnp.pad(tn(normed, grad_logits).astype(bf16), ((0, 0), (0, 128)))
    grad_normed = nt(grad_signals, w_mixed) + nt(grad_logits, w_beta)
    grad_from_attn, grad_gain_attn = norm_backward(tokens, gain_attn, grad_normed)
    grad_inputs = (grad_attended + grad_from_attn)[None]
    grad_taps = jnp.transpose(grad_taps, (2, 1, 0, 3)).reshape(TAPS, count, -1)
    packed = pack_small(
        [g.reshape(count, -1) for g in (grad_gain_attn, grad_gain_mlp, grad_gain_out)],
        jnp.transpose(grad_taps, (1, 0, 2)),
    )
    grad_gate_matrix, grad_up_matrix, grad_down_t, grad_out_matrix = reduce_all(
        (grad_gate_matrix, grad_up_matrix, grad_down_t, grad_out_matrix), 2
    )
    packed, grad_beta_matrix, grad_mixed_matrix = reduce_all(
        (packed, grad_beta_matrix, grad_mixed_matrix), 3
    )
    parts = [part[0].astype(f32) for part in unpack_small(packed, small)]
    grad_gain_attn, grad_gain_mlp, grad_gain_out, grad_taps = parts
    grad_mixed_matrix = grad_mixed_matrix.astype(f32).reshape(depth, heads, 3, size)
    grad_query_matrix, grad_key_matrix, grad_value_matrix = (
        grad_mixed_matrix[:, :, which].reshape(depth, width) for which in range(3)
    )
    return (
        layer_out[None],
        grad_inputs,
        grad_gain_attn,
        grad_query_matrix,
        grad_key_matrix,
        grad_value_matrix,
        grad_beta_matrix[:, :heads].astype(f32),
        grad_taps,
        grad_gain_out,
        grad_out_matrix.astype(f32),
        grad_gain_mlp,
        grad_gate_matrix.astype(f32),
        grad_up_matrix.astype(f32),
        jnp.transpose(grad_down_t).astype(f32),
    )


def solution(mesh):
    vector = P("fsdp")
    rows = P("fsdp", None)
    columns = P(None, "fsdp")
    tokens = P("fsdp", "seq", None)
    return jax.shard_map(
        local,
        mesh=mesh,
        in_specs=(
            tokens,
            vector,
            rows,
            rows,
            rows,
            rows,
            columns,
            vector,
            rows,
            vector,
            rows,
            rows,
            columns,
            tokens,
        ),
        out_specs=(
            tokens,
            tokens,
            vector,
            rows,
            rows,
            rows,
            rows,
            columns,
            vector,
            rows,
            vector,
            rows,
            rows,
            columns,
        ),
        check_vma=False,
    )
```

```python
import functools

import jax
import jax.numpy as jnp
from jax import lax
from jax.experimental import pallas as pl
from jax.experimental.pallas import tpu as pltpu
from jax.sharding import PartitionSpec as P

CHUNK = 256
HALO = 16
TAPS = 4
MIB = 1024 * 1024

highest = lax.Precision.HIGHEST
epsilon = 1e-06
f32 = jnp.float32
bf16 = jnp.bfloat16


def nn(left_side, right_side):
    return lax.dot_general(
        left_side, right_side, (((1,), (0,)), ((), ())), preferred_element_type=f32
    )


def nt(left_side, right_side):
    return lax.dot_general(
        left_side, right_side, (((1,), (1,)), ((), ())), preferred_element_type=f32
    )


def tn(left_side, right_side):
    return lax.dot_general(
        left_side, right_side, (((0,), (0,)), ((), ())), preferred_element_type=f32
    )


def rms_scale(values, gain_vec):
    return (
        values * lax.rsqrt(jnp.mean(values * values, axis=-1, keepdims=True) + epsilon) * gain_vec
    )


def norm_backward(values, gain_vec, grad_out):
    scaling = lax.rsqrt(jnp.mean(values * values, axis=-1, keepdims=True) + epsilon)
    unit_rows = values * scaling
    gain_grad = jnp.sum(grad_out * unit_rows, axis=0)
    scaled_grad = grad_out * gain_vec
    input_grad = scaling * (
        scaled_grad - unit_rows * jnp.mean(scaled_grad * unit_rows, axis=-1, keepdims=True)
    )
    return (input_grad, gain_grad)


MESH = pl.DeviceIdType.MESH


class Place:
    def __init__(self, count):
        self.count = count
        self.sides = 2 if count % 2 == 0 else 1
        self.length = count // self.sides
        self.position = lax.axis_index("seq")
        self.index = lax.axis_index("fsdp")
        self.core = lax.rem(self.position, 2)
        self.chip = lax.div(self.position, 2)
        self.side = lax.rem(self.index, self.sides)
        self.spot = lax.div(self.index, self.sides)

    def sibling(self):
        return {"seq": self.position + 1 - 2 * self.core, "fsdp": self.index}

    def across(self):
        return {"seq": lax.rem(self.position + 2, 4), "fsdp": self.index}

    def partner(self):
        return {"seq": self.position, "fsdp": self.spot * 2 + 1 - self.side}

    def ahead(self, step):
        spot = lax.rem(self.spot + step, self.length)
        return {"seq": self.position, "fsdp": spot * self.sides + self.side}

    def shard(self, spot, side):
        return spot * self.sides + side

    def behind(self, step):
        return lax.rem(self.spot + self.length - step, self.length)

    def greet_all(self):
        self.greet(False, True)

    def greet(self, across, sequence=False):
        barrier = pltpu.get_barrier_semaphore()
        total = self.length - 1

        def signal(device):
            pl.semaphore_signal(barrier, inc=1, device_id=device, device_id_type=MESH)

        def one(step, carry):
            signal(self.ahead(step))
            return carry

        lax.fori_loop(1, self.length, one, 0)
        if sequence:
            for hop in range(1, 4):
                signal({"seq": lax.rem(self.position + hop, 4), "fsdp": self.index})
            total += 3
        else:
            signal(self.sibling())
            total += 1
        if self.sides == 2:
            signal(self.partner())
            total += 1
        if across:
            signal(self.across())
            total += 1
        pl.semaphore_wait(barrier, total)


def remote(source, target, send, recv, device):
    return pltpu.make_async_remote_copy(
        src_ref=source,
        dst_ref=target,
        send_sem=send,
        recv_sem=recv,
        device_id=device,
        device_id_type=MESH,
    )


def steps(first, last, body):
    def one(step, carry):
        body(step)
        return carry

    lax.fori_loop(first, last, one, 0)


class Reduce:
    BUFFERS = 6

    def __init__(self, count, pieces, sources, targets, buffers, staging, sems):
        self.place = Place(count)
        self.pieces, self.sources, self.targets, self.staging = pieces, sources, targets, staging
        self.acc, self.x_in, self.y_in, self.z_in, self.parts_in, self.result = buffers
        (
            self.core_sem,
            self.load_sem,
            self.x_sem,
            self.y_sem,
            self.z_sem,
            self.share_sem,
            self.final_sem,
            self.store_sem,
        ) = sems

    @staticmethod
    def buffers(count, pieces):
        length = count // 2 if count % 2 == 0 else count
        acc, x_in, y_in, z_in, parts_in, result = [], [], [], [], [], []
        for depth, width, parts in pieces:
            rows = depth // parts
            acc.append(pltpu.VMEM((count, depth // min(parts, 2), width), bf16))
            x_in.append(pltpu.VMEM((count, rows, width) if parts == 4 else (1, 16, 128), bf16))
            y_in.append(pltpu.VMEM((length, rows, width), bf16))
            z_in.append(pltpu.VMEM((length, rows, width), bf16))
            parts_in.append(
                pltpu.VMEM((4 // parts, rows, width) if parts < 4 else (1, 16, 128), bf16)
            )
            result.append(pltpu.VMEM((rows, width), bf16))
        return acc + x_in + y_in + z_in + parts_in + result

    @staticmethod
    def semaphores(count, number):
        length = count // 2 if count % 2 == 0 else count
        return [
            pltpu.SemaphoreType.DMA((number, 2)),
            pltpu.SemaphoreType.DMA((number,)),
            pltpu.SemaphoreType.DMA((number, 2)),
            pltpu.SemaphoreType.DMA((number, 2, length)),
            pltpu.SemaphoreType.DMA((number, 2, length)),
            pltpu.SemaphoreType.DMA((number, 2, 4)),
            pltpu.SemaphoreType.DMA((number, 2, 4)),
            pltpu.SemaphoreType.DMA((number,)),
        ]

    def half(self, p, core):
        depth, _, parts = self.pieces[p]
        rows = depth // min(parts, 2)
        return pl.ds(pl.multiple_of(core * rows, 16) if parts > 1 else 0, rows)

    def quarter(self, p, chip):
        depth, _, parts = self.pieces[p]
        rows = depth // parts
        return pl.ds(pl.multiple_of(chip * rows, 16) if parts == 4 else 0, rows)

    def device(self, hop):
        return {"seq": lax.rem(self.place.position + hop, 4), "fsdp": self.place.index}

    def to_sibling(self, p):
        return remote(
            self.sources[p].at[:, self.half(p, 1 - self.place.core), :],
            self.acc[p],
            self.core_sem.at[p, 0],
            self.core_sem.at[p, 1],
            self.place.sibling(),
        )

    def stage(self, p):
        depth, width, parts = self.pieces[p]
        return self.staging.at[p % 2, :, pl.ds(0, depth // min(parts, 2)), pl.ds(0, width)]

    def load(self, p):
        target = self.stage(p) if self.pieces[p][2] > 1 else self.acc[p]
        return pltpu.make_async_copy(
            self.sources[p].at[:, self.half(p, self.place.core), :], target, self.load_sem.at[p]
        )

    def to_x(self, p):
        return remote(
            self.acc[p].at[:, self.quarter(p, 1 - self.place.chip), :],
            self.x_in[p],
            self.x_sem.at[p, 0],
            self.x_sem.at[p, 1],
            self.place.across(),
        )

    def to_y(self, p, spot):
        place = self.place
        return remote(
            self.acc[p].at[place.shard(spot, 1 - place.side), self.quarter(p, place.chip), :],
            self.y_in[p].at[spot],
            self.y_sem.at[p, 0, spot],
            self.y_sem.at[p, 1, spot],
            place.partner(),
        )

    def to_z(self, p, step):
        place = self.place
        spot = lax.rem(place.spot + step, place.length)
        return remote(
            self.acc[p].at[place.shard(spot, place.side), self.quarter(p, place.chip), :],
            self.z_in[p].at[step],
            self.z_sem.at[p, 0, step],
            self.z_sem.at[p, 1, step],
            place.ahead(step),
        )

    def sharers(self, p):
        return {1: (1, 2, 3), 2: (2,), 4: ()}[self.pieces[p][2]]

    def receivers(self, p):
        return {1: (), 2: (0,), 4: (1, 2, 3)}[self.pieces[p][2]]

    def sharer(self, p, position):
        return position if self.pieces[p][2] == 1 else lax.div(position, 2)

    def to_share(self, p, hop, arriving=False):
        position = self.place.position
        source = lax.rem(position + 4 - hop, 4) if arriving else position
        buffer = self.parts_in[p].at[self.sharer(p, source)]
        return remote(
            self.parts_in[p].at[self.sharer(p, position)] if not arriving else buffer,
            buffer,
            self.share_sem.at[p, 0, hop],
            self.share_sem.at[p, 1, hop],
            self.device(hop),
        )

    def target(self, p, position):
        depth, _, parts = self.pieces[p]
        rows = depth // parts
        core, chip = lax.rem(position, 2), lax.div(position, 2)
        first = {1: 0, 2: core * rows, 4: (core * 2 + chip) * rows}[parts]
        return self.targets[p].at[pl.ds(pl.multiple_of(first, 16) if parts > 1 else 0, rows), :]

    def to_result(self, p, hop, arriving=False):
        place = self.place
        if hop == 0:
            other = place.position + 1 - 2 * place.core
            device = place.sibling()
        else:
            other = lax.rem(place.position + 4 - hop, 4)
            device = self.device(hop)
        return remote(
            self.result[p],
            self.target(p, other if arriving else place.position),
            self.final_sem.at[p, 0, hop],
            self.final_sem.at[p, 1, hop],
            device,
        )

    def store(self, p):
        return pltpu.make_async_copy(
            self.result[p], self.target(p, self.place.position), self.store_sem.at[p]
        )

    def start(self, p, loaded):
        if self.pieces[p][2] > 1:
            self.to_sibling(p).start()
        if loaded:
            self.load(p).start()

    def send_sides(self, p, add):
        place = self.place

        def one(step):
            spot = lax.rem(place.spot + step, place.length)
            if add is not None:
                add(place.shard(spot, 1 - place.side))
            self.to_y(p, spot).start()

        if place.sides == 2:
            steps(1, place.length + 1, one)

    def on_core(self, p, loaded):
        parts = self.pieces[p][2]
        place = self.place
        acc = self.acc[p]
        if loaded:
            self.load(p).wait()
        if parts == 1:
            if not loaded:
                acc[...] = self.sources[p][...]
            self.send_sides(p, None)
            return
        copy = self.to_sibling(p)
        copy.wait_recv()
        half = self.half(p, place.core)
        width = self.pieces[p][1]
        rows = self.pieces[p][0] // 2

        def add(shard):
            if loaded:
                own = self.staging[p % 2, shard, pl.ds(0, rows), pl.ds(0, width)]
            else:
                own = self.sources[p][shard, half, :]
            acc[shard] = (acc[shard].astype(f32) + own.astype(f32)).astype(bf16)

        if parts == 4:
            steps(0, place.count, add)
            self.to_x(p).start()
        else:
            self.send_sides(p, add)
            if place.sides == 2:
                steps(0, place.length, lambda spot: add(place.shard(spot, place.side)))
            else:
                steps(0, place.count, add)
        copy.wait_send()

    def on_x(self, p):
        acc = self.acc[p]
        rows = self.quarter(p, self.place.chip)
        self.to_x(p).wait_recv()

        def add(shard):
            acc[shard, rows, :] = (
                acc[shard, rows, :].astype(f32) + self.x_in[p][shard].astype(f32)
            ).astype(bf16)

        self.send_sides(p, add)

    def on_y(self, p):
        place = self.place
        acc = self.acc[p]
        rows = self.quarter(p, place.chip)
        parts = self.pieces[p][2]

        def one(step):
            spot = lax.rem(place.spot + step, place.length)
            shard = place.shard(spot, place.side)
            total = acc[shard, rows, :].astype(f32)
            if parts == 4:
                total = total + self.x_in[p][shard].astype(f32)
            if place.sides == 2:
                self.to_y(p, spot).wait_recv()
                total = total + self.y_in[p][spot].astype(f32)
            acc[shard, rows, :] = total.astype(bf16)

        def send(step):
            one(step)
            self.to_z(p, step).start()

        steps(1, place.length, send)
        one(0)

    def on_z(self, p):
        place = self.place
        parts = self.pieces[p][2]
        rows = self.quarter(p, place.chip)
        steps(1, place.length, lambda step: self.to_z(p, step).wait_recv())
        total = self.acc[p][place.index, rows, :].astype(f32)
        if place.length <= 8:
            for step in range(1, place.length):
                total = total + self.z_in[p][step].astype(f32)
        else:
            total = lax.fori_loop(
                1,
                place.length,
                lambda step, carry: carry + self.z_in[p][step].astype(f32),
                total,
            )
        if parts == 4:
            self.result[p][...] = total.astype(bf16)
            self.publish(p)
        else:
            self.parts_in[p][self.sharer(p, place.position)] = total.astype(bf16)
            for hop in self.sharers(p):
                self.to_share(p, hop).start()

    def on_share(self, p):
        total = None
        for hop in self.sharers(p):
            self.to_share(p, hop, True).wait_recv()
        for index in range(4 // self.pieces[p][2]):
            term = self.parts_in[p][index].astype(f32)
            total = term if total is None else total + term
        self.result[p][...] = total.astype(bf16)
        self.publish(p)

    def publish(self, p):
        for hop in self.receivers(p):
            self.to_result(p, hop).start()
        self.store(p).start()

    def finish(self, p):
        place = self.place
        if self.pieces[p][2] == 4:
            self.to_x(p).wait_send()
        if place.sides == 2:
            steps(0, place.length, lambda spot: self.to_y(p, spot).wait_send())
        steps(1, place.length, lambda step: self.to_z(p, step).wait_send())
        for hop in self.sharers(p):
            self.to_share(p, hop).wait_send()
        for hop in self.receivers(p):
            self.to_result(p, hop).wait_send()
            self.to_result(p, hop, True).wait_recv()
        self.store(p).wait()

    def events(self, ready, loaded):
        made = []
        core = x = y = z = 0.0
        for p, (depth, width, parts) in enumerate(self.pieces):
            tiles = depth * width / 128.0 / 128.0
            core = max(core, ready[p]) + 0.7 * tiles + 6.0
            at = core
            made.append((at, p, 0))
            if parts == 4:
                x = max(x, at) + 4.0 * tiles
                at = x + 6.0
                made.append((at, p, 1))
            load = {1: 8.0, 2: 4.0, 4: 2.0}[parts] * tiles
            y = max(y, at) + load
            at = y + 6.0
            made.append((at, p, 2))
            z = max(z, at) + load
            at = z + 6.0
            made.append((at, p, 3))
            if parts < 4:
                made.append((at + tiles + 8.0, p, 4))
        made.sort()

        def action(p, kind):
            if kind == 0:
                self.on_core(p, loaded[p])
                if loaded[p] and p + 2 < len(self.pieces) and loaded[p + 2]:
                    self.start(p + 2, True)
            else:
                (self.on_x, self.on_y, self.on_z, self.on_share)[kind - 1](p)

        return [(when, p, kind, functools.partial(action, p, kind)) for when, p, kind in made]


class Gather:
    SEMS = 6

    def __init__(self, count, pieces, shards, outs, sems):
        self.place = Place(count)
        self.pieces, self.shards, self.outs = pieces, shards, outs
        self.line_sem, self.side_sem, self.core_sem, self.across_sem, self.relay_sem, self.own = (
            sems
        )

    @staticmethod
    def scratch(pieces, count):
        length = count // 2 if count % 2 == 0 else count
        number = len(pieces)
        slots = 2 * length if max(piece[3] for piece in pieces) > 1 else 1
        return [
            pltpu.SemaphoreType.DMA((number, 2, length)),
            pltpu.SemaphoreType.DMA((number, 2, length)),
            pltpu.SemaphoreType.DMA((number, 2, slots)),
            pltpu.SemaphoreType.DMA((number, 2, slots)),
            pltpu.SemaphoreType.DMA((number, 2, slots)),
            pltpu.SemaphoreType.DMA((number,)),
        ]

    def portion(self, k, core, chip):
        parts = self.pieces[k][3]
        if parts == 1:
            return 0
        return core if parts == 2 else 2 * chip + core

    def region(self, k, shard, core, chip):
        a, offset, width, parts = self.pieces[k]
        depth = self.shards[a].shape[0]
        rows = depth // parts
        first = shard * depth + self.portion(k, core, chip) * rows
        return self.outs[a].at[pl.ds(pl.multiple_of(first, 16), rows), pl.ds(offset, width)]

    def source(self, k):
        p = self.place
        a, offset, width, parts = self.pieces[k]
        rows = self.shards[a].shape[0] // parts
        first = self.portion(k, p.core, p.chip) * rows
        return self.shards[a].at[pl.ds(pl.multiple_of(first, 16), rows), pl.ds(offset, width)]

    def line(self, k, step, arriving=False):
        p = self.place
        shard = p.shard(p.behind(step), p.side) if arriving else p.index
        target = self.region(k, shard, p.core, p.chip)
        return remote(
            target if arriving else self.source(k),
            target,
            self.line_sem.at[k, 0, step],
            self.line_sem.at[k, 1, step],
            p.ahead(step),
        )

    def side(self, k, step, arriving=False, own=False):
        p = self.place
        shard = p.shard(p.behind(step), 1 - p.side if arriving else p.side)
        target = self.region(k, shard, p.core, p.chip)
        return remote(
            self.source(k) if own else target,
            target,
            self.side_sem.at[k, 0, step],
            self.side_sem.at[k, 1, step],
            p.partner(),
        )

    def cross(self, k, step, other, sems, core, chip, device):
        p = self.place
        shard = p.shard(p.behind(step), 1 - p.side if other else p.side)
        target = self.region(k, shard, core, chip)
        slot = 2 * step + (1 if other else 0)
        return remote(target, target, sems.at[k, 0, slot], sems.at[k, 1, slot], device)

    def core(self, k, step, other, arriving=False):
        p = self.place
        core = 1 - p.core if arriving else p.core
        return self.cross(k, step, other, self.core_sem, core, p.chip, p.sibling())

    def across(self, k, step, other, arriving=False):
        p = self.place
        chip = 1 - p.chip if arriving else p.chip
        return self.cross(k, step, other, self.across_sem, p.core, chip, p.across())

    def relay(self, k, step, other, arriving=False):
        p = self.place
        core = 1 - p.core if arriving else p.core
        return self.cross(k, step, other, self.relay_sem, core, 1 - p.chip, p.sibling())

    def keep(self, k):
        a, offset, width, _ = self.pieces[k]
        depth = self.shards[a].shape[0]
        rows = pl.ds(pl.multiple_of(self.place.index * depth, 16), depth)
        columns = pl.ds(offset, width)
        return pltpu.make_async_copy(
            self.shards[a].at[:, columns], self.outs[a].at[rows, columns], self.own.at[k]
        )

    def hand(self, k, step, other):
        parts = self.pieces[k][3]
        if parts == 4:
            self.across(k, step, other).start()
        if parts > 1:
            self.core(k, step, other).start()

    def start(self, k):
        steps(1, self.place.length, lambda step: self.line(k, step).start())
        if self.place.sides == 2:
            self.side(k, 0, own=True).start()
        self.keep(k).start()

    def forward(self, k):
        def one(step):
            self.line(k, step, True).wait_recv()
            if self.place.sides == 2:
                self.side(k, step).start()
            self.hand(k, step, False)

        steps(1, self.place.length, one)

    def spread(self, k):
        def one(step):
            self.side(k, step, True).wait_recv()
            self.hand(k, step, True)

        if self.place.sides == 2:
            steps(0, self.place.length, one)

    def each(self, body):
        steps(1, self.place.length, lambda step: body(step, False))
        if self.place.sides == 2:
            steps(0, self.place.length, lambda step: body(step, True))

    def exchange(self, k):
        def one(step, other):
            self.across(k, step, other, True).wait_recv()
            self.relay(k, step, other).start()

        if self.pieces[k][3] == 4:
            self.each(one)

    def arrive(self, k):
        parts = self.pieces[k][3]

        def one(step, other):
            self.core(k, step, other, True).wait_recv()
            if parts == 4:
                self.relay(k, step, other, True).wait_recv()

        self.keep(k).wait()
        if parts > 1:
            self.each(one)

    def sent(self, k):
        parts = self.pieces[k][3]

        def one(step, other):
            self.core(k, step, other).wait_send()
            if parts == 4:
                self.across(k, step, other).wait_send()
                self.relay(k, step, other).wait_send()

        steps(1, self.place.length, lambda step: self.line(k, step).wait_send())
        if self.place.sides == 2:
            steps(0, self.place.length, lambda step: self.side(k, step).wait_send())
        if parts > 1:
            self.each(one)

    def events(self, tiles, urgent, ahead=3):
        made = []
        line = side = across = 0.0
        hop = 8.0
        number = len(self.pieces)
        for k in range(number):
            parts = self.pieces[k][3]
            margin = 8.0 if k < urgent else 30.0
            load = tiles[k] * (2 if parts == 4 else 4)
            line = line + load
            side = max(side + load, line + load / 4 + hop)
            last = side
            made.append((line + hop, k, 0))
            made.append((side + hop, k, 1))
            if parts == 4:
                across = max(across + 3.5 * tiles[k], side + tiles[k] / 2 + hop)
                last = across
                made.append((across + hop + margin, k, 2))
            wait = 0.0 if k < urgent else 2 * margin
            made.append((last + 2 * hop + wait + (margin if parts == 4 else 0.0), k, 3))
        made.sort()

        def action(k, kind):
            if kind == 0:
                self.forward(k)
                if k + ahead < number:
                    self.start(k + ahead)
            else:
                (self.spread, self.exchange, self.arrive)[kind - 1](k)

        return [(when, k, kind, functools.partial(action, k, kind)) for when, k, kind in made]


PACK = (16, 512)


def pack_small(gains, taps):
    count = taps.shape[0]

    def fit(values, rows):
        values = values.reshape(count, -1, values.shape[-1]).astype(bf16)
        return jnp.pad(
            values, ((0, 0), (0, rows - values.shape[1]), (0, PACK[1] - values.shape[2]))
        )

    rows = [fit(gains[0], 1), fit(gains[1], 1), fit(gains[2], 2), fit(taps, PACK[0] - 4)]
    return jnp.concatenate(rows, axis=1).reshape(count * PACK[0], PACK[1])


def unpack_small(packed, shapes):
    packed = packed.reshape(-1, PACK[0], PACK[1])
    gains = [packed[:, row, : shape[0]] for row, shape in enumerate(shapes[:3])]
    return gains + [packed[:, 4 : 4 + shapes[3][0], : shapes[3][1]]]


def place_rows(packed, count, width):
    if width % 128 == 0:
        return jnp.concatenate(
            [packed[s * PACK[0] : (s + 1) * PACK[0], :width] for s in range(count)], axis=1
        )
    total = count * width
    row = lax.broadcasted_iota(jnp.int32, (PACK[1], total), 0)
    col = lax.broadcasted_iota(jnp.int32, (PACK[1], total), 1)
    pick = jnp.where(lax.rem(col, width) == row, 1.0, 0.0).astype(bf16)
    wide = nn(packed.astype(bf16), pick)
    row = lax.broadcasted_iota(jnp.int32, wide.shape, 0)
    col = lax.broadcasted_iota(jnp.int32, wide.shape, 1)
    wide = jnp.where(lax.div(row, PACK[0]) == lax.div(col, width), wide, 0.0).astype(bf16)
    row = lax.broadcasted_iota(jnp.int32, (PACK[0], count * PACK[0]), 0)
    col = lax.broadcasted_iota(jnp.int32, (PACK[0], count * PACK[0]), 1)
    fold = jnp.where(lax.rem(col, PACK[0]) == row, 1.0, 0.0).astype(bf16)
    return nn(fold, wide)


GROUP = 2


def grid_indices():
    row = lax.broadcasted_iota(jnp.int32, (CHUNK, CHUNK), 0)
    col = lax.broadcasted_iota(jnp.int32, (CHUNK, CHUNK), 1)
    return row, col


def conv_pre(wide_ref, taps, rows):
    total = None
    for offset in range(TAPS):
        term = taps[offset : offset + 1, :] * wide_ref[pl.ds(HALO - TAPS + 1 + offset, rows), :]
        total = term if total is None else total + term
    return total


def sigmoid(values):
    return 1.0 / (1.0 + jnp.exp(-values))


def head_column(table, head):
    lane = lax.broadcasted_iota(jnp.int32, table.shape, 1)
    return jnp.sum(jnp.where(lane == head, table, 0.0), axis=1, keepdims=True)


ARRAYS = 7


def forward_kernel(count, pieces, mixed, heads, tap_width, *refs):
    tokens_ref = refs[0]
    shards, refs = refs[1 : 1 + ARRAYS], refs[1 + ARRAYS :]
    gathered, refs = refs[:ARRAYS], refs[ARRAYS:]
    (
        finals_ref,
        normed_ref,
        signals_ref,
        logit_ref,
        taps_ref,
        out_ref,
        carry_ref,
        fresh_ref,
        inverse_ref,
        starts_ref,
    ), refs = refs[:10], refs[10:]
    (
        tokens,
        weights,
        rates_weight,
        packed,
        all_taps,
        wide,
        level_masks,
        final,
        halo_sem,
        token_sem,
        load_sem,
        final_sem,
        *sems,
    ) = refs
    group = pl.program_id(0)
    groups = heads // GROUP
    rows = out_ref.shape[0]
    size = out_ref.shape[1] // GROUP
    span = GROUP * size
    chunks = rows // CHUNK
    levels = CHUNK.bit_length() - 1
    row, col = grid_indices()
    gather = Gather(count, pieces, shards, gathered, sems)
    place = gather.place
    tiles = [piece[2] / 128 * shards[piece[0]].shape[0] / 128 for piece in pieces]
    events = gather.events(tiles, 2 + groups)

    def halo(arriving):
        return remote(
            tokens_ref.at[pl.ds(rows - HALO, HALO), :],
            tokens.at[pl.ds(0, HALO), :],
            halo_sem.at[0],
            halo_sem.at[1],
            {"seq": lax.rem(place.position + 1, 4), "fsdp": place.index},
        )

    def load(step, slot):
        return pltpu.make_async_copy(
            gathered[mixed].at[:, pl.ds(pl.multiple_of(step * 3 * span, 128), 3 * span)],
            weights.at[slot],
            load_sem.at[slot],
        )

    per_step = 9
    plan = {}
    mark = 0
    for step in range(groups):
        for spot in range(per_step):
            now = 60.0 + (step * per_step + spot) * 5.0
            upto = mark
            for index in range(mark, len(events)):
                when, k, kind, _ = events[index]
                if spot == 0 and kind == 3 and (k == 2 + step or (step == 0 and k < 2)):
                    upto = index + 1
                elif when <= now and upto == index:
                    upto = index + 1
            plan[step, spot] = (mark, upto)
            mark = upto
    remaining = (mark, len(events))

    def run(bounds):
        for _, _, _, action in events[bounds[0] : bounds[1]]:
            action()

    def spot(number):
        for step in range(groups):
            bounds = plan[step, number]
            if bounds[1] > bounds[0]:

                @pl.when(group == step)
                def _():
                    run(bounds)

    @pl.when(group == 0)
    def _():
        own = pltpu.make_async_copy(tokens_ref, tokens.at[pl.ds(HALO, rows), :], token_sem.at[0])
        own.start()
        place.greet_all()

        @pl.when(place.position < 3)
        def _():
            halo(False).start()

        gather.start(0)
        gather.start(1)
        gather.start(2)

        @pl.when(place.position == 0)
        def _():
            tokens[pl.ds(0, HALO), :] = jnp.zeros((HALO, tokens.shape[1]), bf16)

        for level in range(levels):
            same = (row >> (level + 1)) == (col >> (level + 1))
            below = ((row >> level) & 1 == 1) & ((col >> level) & 1 == 0)
            level_masks[level] = jnp.where(same & below, 1.0, 0.0).astype(bf16)

        limit = max(i for i, event in enumerate(events) if event[1] == 0) + 1
        run((0, limit))
        copy = pltpu.make_async_copy(gathered[0], packed, token_sem.at[1])
        copy.start()
        copy.wait()
        small = packed[...].astype(f32)
        gain = place_rows(small, count, tokens.shape[1] // count)[0:1, :]
        all_taps[...] = place_rows(small, count, tap_width)[4 : 4 + TAPS, :]
        own.wait()

        @pl.when(place.position > 0)
        def _():
            halo(True).wait_recv()

        block = 208 if tokens.shape[0] % 208 == 0 else HALO

        def norm(index):
            part = pl.ds(pl.multiple_of(index * block, HALO), block)
            normed_ref[part, :] = rms_scale(tokens[part, :].astype(f32), gain).astype(bf16)

        steps(0, tokens.shape[0] // block, norm)
        run((limit, plan[0, 0][1]))
        copy = pltpu.make_async_copy(gathered[1], rates_weight, token_sem.at[1])
        copy.start()
        load(0, 0).start()
        copy.wait()
        logit_ref[...] = nn(normed_ref[pl.ds(HALO, rows), :], rates_weight[...]).astype(bf16)
        load(0, 0).wait()

    for step in range(1, groups):
        bounds = plan[step, 0]

        @pl.when(group == step)
        def _():
            run(bounds)
            load(step, 0).start()
            load(step, 0).wait()

    signals_ref[...] = nn(normed_ref[...], weights[0]).astype(bf16)
    spot(1)

    lows = [[], [], []]
    for inner in range(GROUP):
        for which in range(3):
            first = pl.multiple_of((which * heads + group * GROUP + inner) * size, 128)
            taps = all_taps[:, pl.ds(first, size)]
            taps_ref[inner, which] = taps
            wide[...] = signals_ref[:, pl.ds((inner * 3 + which) * size, size)].astype(f32)
            pre = conv_pre(wide, taps, rows)
            act = pre * sigmoid(pre)
            if which < 2:
                act = act * lax.rsqrt(jnp.sum(act * act, axis=1, keepdims=True) + epsilon)
            lows[which].append(act.astype(bf16))
        if inner == 0:
            spot(2)
    spot(3)
    logits = logit_ref[...].astype(f32)
    rates = [sigmoid(head_column(logits, group * GROUP + inner)) for inner in range(GROUP)]
    scaling = size ** (-0.5)
    eye = jnp.where(row == col, 1.0, 0.0)
    lower = row >= col

    work = [(inner, chunk) for inner in range(GROUP) for chunk in range(chunks)]

    def cut(values, item):
        inner, chunk = item
        return values[inner][chunk * CHUNK : (chunk + 1) * CHUNK]

    queries, keys, values = lows
    stricts = [(cut(rates, i) * nt(cut(keys, i), cut(keys, i))).astype(bf16) for i in work]
    results = [eye - (strict * level_masks[0]).astype(f32) for strict in stricts]
    scores = [jnp.where(lower, nt(cut(queries, i), cut(keys, i)), 0.0).astype(bf16) for i in work]
    for level in range(1, levels):
        mask = level_masks[level]
        lowered = [result.astype(bf16) for result in results]
        inners = [nn(low, strict * mask).astype(bf16) for low, strict in zip(lowered, stricts)]
        results = [
            result - nn(inner, low) for result, inner, low in zip(results, inners, lowered)
        ]
        if level in (2, 4, 6):
            spot(3 + level // 2)
    inverses = [result.astype(bf16) for result in results]
    for (inner, chunk), inverse in zip(work, inverses):
        part = slice(chunk * CHUNK, (chunk + 1) * CHUNK)
        inverse_ref[part, inner * CHUNK : (inner + 1) * CHUNK] = inverse
    spot(7)

    srow = lax.broadcasted_iota(jnp.int32, (size, size), 0)
    scol = lax.broadcasted_iota(jnp.int32, (size, size), 1)
    memories = [
        jnp.concatenate(
            [jnp.zeros((size, size), f32), jnp.where(srow == scol, 1.0, 0.0)], axis=1
        )
    ] * GROUP
    for chunk in range(chunks):
        part = slice(chunk * CHUNK, (chunk + 1) * CHUNK)
        for inner in range(GROUP):
            item = (inner, chunk)
            key_part, query_part, rate_part = cut(keys, item), cut(queries, item), cut(rates, item)
            low_memory = memories[inner].astype(bf16)
            starts_ref[inner, chunk] = low_memory
            seen = nn(key_part, low_memory)
            aim = jnp.concatenate(
                [cut(values, item).astype(f32), jnp.zeros((CHUNK, size), f32)], axis=1
            )
            aim = (rate_part * (aim - seen)).astype(bf16)
            fresh = nn(inverses[work.index(item)], aim).astype(bf16)
            fresh_ref[part, inner * 2 * size : (inner + 1) * 2 * size] = fresh
            both = scaling * (
                nn(query_part, low_memory) + nn(scores[work.index(item)], fresh)
            )
            out_ref[part, inner * size : (inner + 1) * size] = both[:, :size]
            carry_ref[part, inner * size : (inner + 1) * size] = both[:, size:].astype(bf16)
            memories[inner] = memories[inner] + tn(key_part, fresh)

    def send_final(step, hop):
        position = lax.rem(place.position + hop, 4)
        block = pl.ds(step * GROUP, GROUP)
        return remote(
            final.at[block],
            finals_ref.at[place.position, block],
            final_sem.at[0, step, hop],
            final_sem.at[1, step, hop],
            {"seq": position, "fsdp": place.index},
        )

    def keep_final(step):
        block = pl.ds(step * GROUP, GROUP)
        return pltpu.make_async_copy(
            final.at[block], finals_ref.at[place.position, block], final_sem.at[0, step, 0]
        )

    def take_final(step, hop):
        position = lax.rem(place.position + 4 - hop, 4)
        block = pl.ds(step * GROUP, GROUP)
        return remote(
            final.at[block],
            finals_ref.at[position, block],
            final_sem.at[0, step, hop],
            final_sem.at[1, step, hop],
            {"seq": position, "fsdp": place.index},
        )

    for step in range(groups):

        @pl.when(group == step)
        def _():
            for inner in range(GROUP):
                final[step * GROUP + inner] = memories[inner].astype(bf16)
            for hop in range(1, 4):
                send_final(step, hop).start()
            keep_final(step).start()

    spot(8)

    @pl.when(group == groups - 1)
    def _():
        run(remaining)
        for k in range(len(pieces)):
            gather.sent(k)
        for step in range(groups):
            for hop in range(1, 4):
                send_final(step, hop).wait_send()
                take_final(step, hop).wait_recv()
            keep_final(step).wait()

        @pl.when(place.position < 3)
        def _():
            halo(False).wait_send()


def plan_pieces(depths, widths, span):
    def portions(a, wanted):
        while depths[a] % (16 * wanted) != 0:
            wanted //= 2
        return wanted

    pieces = [(0, 0, widths[0], 1), (1, 0, widths[1], portions(1, 2))]
    for step in range(widths[2] // span):
        pieces.append((2, step * span, span, portions(2, 4)))
    pieces.append((3, 0, widths[3], portions(3, 4)))
    for a in (4, 5, 6):
        half = widths[a] // 2
        for part in range(2):
            wanted = 2 if (a, part) in ((5, 0), (6, 1)) else 4
            pieces.append((a, part * half, half, portions(a, wanted)))
    return pieces


def forward(tokens, shards, heads, tap_width):
    count = lax.axis_size("fsdp")
    rows, width = tokens.shape
    size = width // heads
    span = GROUP * size
    groups = heads // GROUP
    chunks = rows // CHUNK
    wide_rows = rows + HALO
    depths = [shard.shape[0] for shard in shards]
    widths = [shard.shape[1] for shard in shards]
    pieces = plan_pieces(depths, widths, 3 * span)
    anywhere = pl.BlockSpec(memory_space=pl.ANY)
    shape = jax.ShapeDtypeStruct
    return pl.pallas_call(
        functools.partial(forward_kernel, count, pieces, 2, heads, tap_width),
        grid=(groups,),
        in_specs=[anywhere] * (1 + ARRAYS),
        out_specs=[anywhere] * (ARRAYS + 1)
        + [
            pl.BlockSpec((wide_rows, width), lambda g: (0, 0)),
            pl.BlockSpec((wide_rows, 3 * span), lambda g: (0, g)),
            pl.BlockSpec((rows, widths[1]), lambda g: (0, 0)),
            pl.BlockSpec((GROUP, 3, TAPS, size), lambda g: (g, 0, 0, 0)),
            pl.BlockSpec((rows, span), lambda g: (0, g)),
            pl.BlockSpec((rows, span), lambda g: (0, g)),
            pl.BlockSpec((rows, 2 * span), lambda g: (0, g)),
            pl.BlockSpec((rows, GROUP * CHUNK), lambda g: (0, g)),
            pl.BlockSpec((GROUP, chunks, size, 2 * size), lambda g: (g, 0, 0, 0)),
        ],
        out_shape=[shape((count * d, w), bf16) for d, w in zip(depths, widths)]
        + [
            shape((4, heads, size, 2 * size), bf16),
            shape((wide_rows, width), bf16),
            shape((wide_rows, 3 * width), bf16),
            shape((rows, widths[1]), bf16),
            shape((heads, 3, TAPS, size), f32),
            shape((rows, width), f32),
            shape((rows, width), bf16),
            shape((rows, 2 * width), bf16),
            shape((rows, heads * CHUNK), bf16),
            shape((heads, chunks, size, 2 * size), bf16),
        ],
        scratch_shapes=[
            pltpu.VMEM((wide_rows, width), bf16),
            pltpu.VMEM((1, width, 3 * span), bf16),
            pltpu.VMEM((width, widths[1]), bf16),
            pltpu.VMEM((count * PACK[0], PACK[1]), bf16),
            pltpu.VMEM((TAPS, 3 * width), f32),
            pltpu.VMEM((wide_rows, size), f32),
            pltpu.VMEM((CHUNK.bit_length() - 1, CHUNK, CHUNK), bf16),
            pltpu.VMEM((heads, size, 2 * size), bf16),
            pltpu.SemaphoreType.DMA((2,)),
            pltpu.SemaphoreType.DMA((2,)),
            pltpu.SemaphoreType.DMA((2,)),
            pltpu.SemaphoreType.DMA((2, groups, 4)),
        ]
        + Gather.scratch(pieces, count),
        compiler_params=pltpu.CompilerParams(
            collective_id=0, has_side_effects=True, vmem_limit_bytes=60 * MIB
        ),
    )(tokens, *shards)


def mix_kernel(position_ref, out_ref, carry_ref, finals_ref, gain_ref, mixed_ref, state_ref):
    position = position_ref[0]
    size = out_ref.shape[1]
    state = jnp.zeros((size, size), f32)
    for index in range(finals_ref.shape[0] - 1):
        pair = finals_ref[index, 0].astype(f32)
        later = pair[:, :size] + jnp.dot(pair[:, size:], state, precision=highest)
        state = jnp.where(index < position, later, state)
    state_ref[0] = state
    output = out_ref[...] + nn(carry_ref[...], state.astype(bf16))
    gain = gain_ref[...].astype(f32)
    mixed_ref[...] = rms_scale(output, gain).astype(bf16)


def mix(position, outputs, carries, finals, gain):
    rows, width = outputs.shape
    groups, heads, size, _ = finals.shape
    plain = pl.BlockSpec((rows, size), lambda h: (0, h))
    return pl.pallas_call(
        mix_kernel,
        grid=(heads,),
        in_specs=[
            pl.BlockSpec(memory_space=pltpu.SMEM),
            plain,
            plain,
            pl.BlockSpec((groups, 1, size, 2 * size), lambda h: (0, h, 0, 0)),
            pl.BlockSpec((1, size), lambda h: (0, 0)),
        ],
        out_specs=[plain, pl.BlockSpec((1, size, size), lambda h: (h, 0, 0))],
        out_shape=[
            jax.ShapeDtypeStruct((rows, width), bf16),
            jax.ShapeDtypeStruct((heads, size, size), f32),
        ],
        compiler_params=pltpu.CompilerParams(vmem_limit_bytes=32 * MIB),
    )(position, outputs, carries, finals, gain)


def unmix_kernel(
    heads,
    out_ref,
    carry_ref,
    state_ref,
    gain_ref,
    grad_ref,
    grad_out_ref,
    grad_gain_ref,
    grads_ref,
    grad_states,
    sems,
):
    head = pl.program_id(0)
    position, index = lax.axis_index("seq"), lax.axis_index("fsdp")

    def device(hop):
        return {"seq": lax.rem(position + hop, 4), "fsdp": index}

    def send(one, hop, arriving=False):
        source = lax.rem(position + 4 - hop, 4) if arriving else position
        return remote(
            grad_states.at[one],
            grads_ref.at[source, one],
            sems.at[0, one, hop],
            sems.at[1, one, hop],
            device(hop),
        )

    def keep(one):
        return pltpu.make_async_copy(
            grad_states.at[one], grads_ref.at[position, one], sems.at[0, one, 0]
        )

    @pl.when(head == 0)
    def _():
        barrier = pltpu.get_barrier_semaphore()
        for hop in range(1, 4):
            pl.semaphore_signal(barrier, inc=1, device_id=device(hop), device_id_type=MESH)
        grad_gain_ref[...] = jnp.zeros_like(grad_gain_ref)
        pl.semaphore_wait(barrier, 3)

    output = out_ref[...] + nn(carry_ref[...], state_ref[0].astype(bf16))
    gain = gain_ref[...].astype(f32)
    grad = grad_ref[...].astype(f32)
    scaling = lax.rsqrt(jnp.mean(output * output, axis=1, keepdims=True) + epsilon)
    unit_rows = output * scaling
    grad_gain_ref[...] += jnp.sum(grad * unit_rows, axis=0, keepdims=True)
    scaled = grad * gain
    grad_out = scaling * (scaled - unit_rows * jnp.mean(scaled * unit_rows, axis=1, keepdims=True))
    low_grad = grad_out.astype(bf16)
    grad_states[head] = tn(carry_ref[...], low_grad).astype(bf16)
    for hop in range(1, 4):
        send(head, hop).start()
    keep(head).start()
    grad_out_ref[...] = (grad_out * output.shape[1] ** (-0.5)).astype(bf16)

    @pl.when(head == heads - 1)
    def _():
        def one(step):
            keep(step).wait()
            for hop in range(1, 4):
                send(step, hop).wait_send()
                send(step, hop, True).wait_recv()

        steps(0, heads, one)


def unmix(outputs, carries, states, gain, grad_heads):
    rows, width = outputs.shape
    heads, size, _ = states.shape
    plain = pl.BlockSpec((rows, size), lambda h: (0, h))
    state = pl.BlockSpec((1, size, size), lambda h: (h, 0, 0))
    vector = pl.BlockSpec((1, size), lambda h: (0, 0))
    return pl.pallas_call(
        functools.partial(unmix_kernel, heads),
        grid=(heads,),
        in_specs=[plain, plain, state, vector, plain],
        out_specs=[plain, vector, pl.BlockSpec(memory_space=pl.ANY)],
        out_shape=[
            jax.ShapeDtypeStruct((rows, width), bf16),
            jax.ShapeDtypeStruct((1, size), f32),
            jax.ShapeDtypeStruct((4, heads, size, size), bf16),
        ],
        scratch_shapes=[
            pltpu.VMEM((heads, size, size), bf16),
            pltpu.SemaphoreType.DMA((2, heads, 4)),
        ],
        compiler_params=pltpu.CompilerParams(
            collective_id=1, has_side_effects=True, vmem_limit_bytes=32 * MIB
        ),
    )(outputs, carries, states, gain, grad_heads)


SPOTS = (0.0, 4.0, 8.0, 11.0, 14.0, 17.0, 20.0, 25.0)
STEP = 26.0


def schedule(events, groups, begin, earliest, needed):
    plan, mark = {}, 0
    for step in range(groups):
        for spot, offset in enumerate(SPOTS):
            now = begin + step * STEP + offset
            upto = mark
            if step == groups - 1 and 0 < spot < 6:
                plan[step, spot] = (mark, mark)
                continue
            last = spot == len(SPOTS) - 1
            for index in range(mark, len(events)):
                if last and events[index][1:3] in needed.get(step, ()):
                    upto = index + 1
            while upto < len(events):
                when, p, _, _ = events[upto]
                if when > now or earliest[p] > (step, spot):
                    break
                upto += 1
            plan[step, spot] = (mark, upto)
            mark = upto
    return plan, (mark, len(events))


def backward_kernel(
    count, arrays, shapes, loaded_number, heads, tap_width, gain_width, *refs
):
    (
        signals_ref,
        logit_ref,
        taps_ref,
        grad_ref,
        fresh_ref,
        inverse_ref,
        starts_ref,
        state_ref,
        finals_ref,
        grads_ref,
        weights_ref,
        rates_weight_ref,
        gain_ref,
        grad_mlp_ref,
        grad_gain_ref,
        normed_ref,
        tokens_ref,
    ), refs = refs[:17], refs[17:]
    full, refs = refs[:arrays], refs[arrays:]
    grad_tokens_ref, refs = refs[0], refs[1:]
    outs, refs = refs[: arrays + 3], refs[arrays + 3 :]
    (
        normed_t,
        tokens,
        total,
        grad_signals,
        tails,
        firsts,
        edges,
        wides,
        pres,
        grads,
        padded,
        grad_logits,
        small_rows,
        small_source,
        beta_source,
        mixed_source,
        staging,
        plain_sem,
        edge_sem,
    ), refs = refs[:19], refs[19:]
    number = len(shapes)
    buffers = [refs[i * number : (i + 1) * number] for i in range(Reduce.BUFFERS)]
    sems = refs[Reduce.BUFFERS * number :]

    head = pl.program_id(0)
    rows, size = grad_ref.shape
    width = total.shape[1]
    chunks = rows // CHUNK
    row, col = grid_indices()
    lower, upper = row >= col, row <= col

    sources, targets = [], []
    for a in range(arrays):
        halves = 2 if a < 3 else 1
        half = full[a].shape[2] // halves
        for part in range(halves):
            columns = pl.ds(part * half, half)
            sources.append(full[a].at[:, :, columns])
            targets.append(outs[a].at[:, columns])
    slots = mixed_source.shape[0]
    for one in range(heads):
        sources.append(mixed_source.at[one % slots])
        targets.append(outs[arrays].at[:, pl.ds(one * 3 * size, 3 * size)])
    sources += [beta_source, small_source]
    targets += [outs[arrays + 1], outs[arrays + 2]]
    reduce = Reduce(count, shapes, sources, targets, buffers, staging, sems)
    place = reduce.place
    position = place.position
    loaded = [p < loaded_number for p in range(number)]
    begin = 12.0
    end = (heads, len(SPOTS) - 1)
    ready = [0.0] * loaded_number
    earliest = [(0, 0)] * loaded_number
    for one in range(heads):
        ready.append(begin + (one + 1) * STEP + SPOTS[-1] + 1.0)
        earliest.append((one + 2, 0))
    ready += [begin + heads * STEP + SPOTS[-1] + 4.0, begin + heads * STEP + SPOTS[-1] + 20.0]
    earliest += [(heads + 2, 0)] * 2
    events = reduce.events(ready, loaded)
    needed = {
        one + 1: ((loaded_number + one - slots, 0),) for one in range(slots, heads)
    }
    plan, remaining = schedule(events, heads + 1, begin, earliest, needed)

    def run(bounds):
        for _, _, _, action in events[bounds[0] : bounds[1]]:
            action()

    def spot(which):
        for step in range(heads + 1):
            bounds = plan[step, which]
            if bounds[1] > bounds[0]:

                @pl.when(head == step)
                def _():
                    run(bounds)

    def fetch(source, target, slot):
        return pltpu.make_async_copy(source, target, plain_sem.at[slot])

    def edge(one, slot, arriving=False):
        return remote(
            firsts.at[slot],
            edges.at[one],
            edge_sem.at[0, one],
            edge_sem.at[1, one],
            reduce.device(3),
        )

    @pl.when(head == 0)
    def _():
        fetch(normed_ref, normed_t, 0).start()
        fetch(tokens_ref, tokens, 1).start()
        place.greet_all()
        for p in range(min(2, loaded_number)):
            reduce.start(p, True)
        total[...] = jnp.zeros_like(total)
        padded[...] = jnp.zeros_like(padded)
        grad_logits[...] = jnp.zeros_like(grad_logits)
        small_rows[...] = jnp.zeros_like(small_rows)
        fetch(normed_ref, normed_t, 0).wait()
        fetch(tokens_ref, tokens, 1).wait()

    spot(0)

    @pl.when(head < heads)
    def _():
        slot = lax.rem(head, 2)
        lows, scales = [], []
        for which in range(3):
            wides[which] = signals_ref[:, pl.ds(which * size, size)].astype(f32)
            pre = conv_pre(wides.at[which], taps_ref[0, which], rows)
            pres[which] = pre
            act = pre * sigmoid(pre)
            if which < 2:
                scale = lax.rsqrt(jnp.sum(act * act, axis=1, keepdims=True) + epsilon)
                act = act * scale
                scales.append(scale)
            lows.append(act.astype(bf16))
        queries, keys, values = lows
        rates = sigmoid(head_column(logit_ref[...].astype(f32), head))

        state = state_ref[0].astype(bf16)
        first = fresh_ref[:, pl.ds(0, size)].astype(f32)
        fresh_all = (first + nn(fresh_ref[:, pl.ds(size, size)], state)).astype(bf16)

        grad_memory = jnp.zeros((size, size), f32)
        for index in reversed(range(1, 4)):
            later = grads_ref[index, 0].astype(f32) + lax.dot_general(
                finals_ref[index, 0, :, pl.ds(size, size)].astype(f32),
                grad_memory,
                (((0,), (0,)), ((), ())),
                precision=highest,
                preferred_element_type=f32,
            )
            grad_memory = jnp.where(index > position, later, grad_memory)
        spot(1)

        grad_rates = [None] * chunks
        for chunk in reversed(range(chunks)):
            part = slice(chunk * CHUNK, (chunk + 1) * CHUNK)
            key, query, value, rate = keys[part], queries[part], values[part], rates[part]
            grad_out = grad_ref[part, :]
            fresh = fresh_all[part]
            start = starts_ref[0, chunk]
            memory = (start[:, :size].astype(f32) + nn(start[:, size:], state)).astype(bf16)
            low_grad = grad_memory.astype(bf16)
            key_f = key.astype(f32)
            rated = (rate * key_f).astype(bf16)

            scores_t = jnp.where(upper, nt(key, query), 0.0).astype(bf16)
            grad_fresh = (nn(scores_t, grad_out) + nn(key, low_grad)).astype(bf16)
            aim = tn(inverse_ref[part, :], grad_fresh)
            low_aim = aim.astype(bf16)
            grad_memory = grad_memory + tn(query, grad_out) - tn(rated, low_aim)

            grad_scores = jnp.where(lower, nt(grad_out, fresh), 0.0).astype(bf16)
            grad_scores_t = jnp.where(upper, nt(fresh, grad_out), 0.0).astype(bf16)
            grad_strict = jnp.where(row > col, nt(low_aim, fresh), 0.0).astype(bf16)
            grad_strict_t = jnp.where(row < col, nt(fresh, low_aim), 0.0).astype(bf16)

            grad_query = nt(grad_out, memory) + nn(grad_scores, key)
            within = -(nn(grad_strict, key) + nt(low_aim, memory))
            grad_rates[chunk] = jnp.sum(
                key_f * within + value.astype(f32) * aim, axis=1, keepdims=True
            )
            grad_key = (
                rate * within
                - nn(grad_strict_t, rated)
                + nn(grad_scores_t, query)
                + nt(fresh, low_grad)
            )
            grads[0, part, :] = grad_query
            grads[1, part, :] = grad_key
            grads[2, part, :] = rate * aim
            spot(2 + chunks - 1 - chunk if chunks - 1 - chunk < 4 else 5)

        lane = lax.broadcasted_iota(jnp.int32, grad_logits.shape, 1)
        grad_rate = jnp.concatenate(grad_rates, axis=0)
        grad_logit = grad_rate * rates * (1.0 - rates)
        grad_logits[...] = jnp.where(lane == head, grad_logit, grad_logits[...])

        @pl.when((head >= 2) & (position > 0))
        def _():
            edge(head - 2, slot).wait_send()

        for which in range(3):
            taps = taps_ref[0, which]
            pre = pres[which]
            sig = sigmoid(pre)
            grad_act = grads[which]
            if which < 2:
                unit = pre * sig * scales[which]
                grad_act = scales[which] * (
                    grad_act - unit * jnp.sum(grad_act * unit, axis=1, keepdims=True)
                )
            grad_pre = grad_act * sig * (1.0 + pre * (1.0 - sig))
            padded[pl.ds(HALO, rows), :] = grad_pre
            sums = []
            for offset in range(TAPS):
                shifted = wides[which, pl.ds(HALO - TAPS + 1 + offset, rows), :]
                sums.append(jnp.sum(grad_pre * shifted, axis=0, keepdims=True))
            where = pl.multiple_of((which * heads + head) * size, 128)
            small_rows[4:8, pl.ds(where, size)] = jnp.concatenate(sums, axis=0)

            def back(start, amount):
                result = None
                for offset in range(TAPS):
                    term = (
                        taps[offset : offset + 1, :]
                        * padded[pl.ds(start + TAPS - 1 - offset, amount), :]
                    )
                    result = term if result is None else result + term
                return result

            columns = pl.ds(which * size, size)
            grad_signal = back(HALO, rows)
            grad_signals[slot, :, columns] = grad_signal.astype(bf16)
            tails[slot, :, columns] = grad_signal[rows - HALO :]
            firsts[slot, :, columns] = back(0, HALO)

        @pl.when(position > 0)
        def _():
            edge(head, slot).start()

    spot(6)
    spot(7)

    for one in range(heads):

        @pl.when(head == one + 1)
        def _():
            slot = one % 2

            @pl.when(position < 3)
            def _():
                edge(one, slot).wait_recv()
                tails[slot] = tails[slot] + edges[one]

            grad_signals[slot, pl.ds(rows - HALO, HALO), :] = tails[slot].astype(bf16)
            grad = grad_signals[slot]
            source = mixed_source.at[one % slots]
            depth = width // count
            half = count // 2 if count % 2 == 0 else count
            for part in range(count // half):
                piece = nn(normed_t[pl.ds(part * half * depth, half * depth), :], grad)
                source[pl.ds(part * half, half)] = piece.astype(bf16).reshape(
                    half, depth, 3 * size
                )
            reduce.start(loaded_number + one, False)
            weights = weights_ref[...]
            for part in range(0, rows, CHUNK):
                block = pl.ds(part, CHUNK)
                total[block, :] += nt(grad[part : part + CHUNK], weights)

    @pl.when(head == heads)
    def _():
        depth = width // count
        low_logits = grad_logits[...].astype(bf16)
        beta_source[...] = (
            nn(normed_t[...], low_logits).astype(bf16).reshape(count, depth, low_logits.shape[1])
        )
        reduce.start(number - 2, False)
        gain = gain_ref[...].astype(f32)
        weights = rates_weight_ref[...]
        gain_grad = jnp.zeros((1, width), f32)
        for part in range(0, rows, CHUNK):
            block = pl.ds(part, CHUNK)
            grad = total[block, :] + nt(low_logits[part : part + CHUNK], weights)
            values = tokens[block, :].astype(f32)
            scaling = lax.rsqrt(jnp.mean(values * values, axis=1, keepdims=True) + epsilon)
            unit = values * scaling
            gain_grad = gain_grad + jnp.sum(grad * unit, axis=0, keepdims=True)
            scaled = grad * gain
            total[block, :] = scaling * (
                scaled - unit * jnp.mean(scaled * unit, axis=1, keepdims=True)
            )
        fetch(total, grad_tokens_ref, 0).start()
        small_rows[0:1, pl.ds(0, width)] = gain_grad
        small_rows[1:2, pl.ds(0, width)] = grad_mlp_ref[...]
        small_rows[2:3, pl.ds(0, size)] = grad_gain_ref[...]
        small = small_rows[...]
        gains = gather_rows(small[:, :width], count, gain_width)
        last = gather_rows(small[:, :size], count, size // count)
        taps = gather_rows(small, count, tap_width)
        which = lax.broadcasted_iota(jnp.int32, gains.shape, 1)
        small_source[...] = jnp.where(which == 2, last, jnp.where(which < 2, gains, taps)).astype(
            bf16
        )
        reduce.start(number - 1, False)
        run(remaining)
        for p in range(number):
            reduce.finish(p)
        fetch(total, grad_tokens_ref, 0).wait()
        for one in range(heads - 2, heads):

            @pl.when(position > 0)
            def _():
                edge(one, one % 2).wait_send()


def gather_rows(wide, count, width):
    total = count * width
    rows = wide.shape[0]
    if width % 128 == 0:
        blank = jnp.zeros((rows, PACK[1] - width), f32)
        return jnp.stack(
            [
                jnp.concatenate([wide[:, s * width : (s + 1) * width], blank], axis=1)
                for s in range(count)
            ]
        )
    row = lax.broadcasted_iota(jnp.int32, (count * rows, rows), 0)
    col = lax.broadcasted_iota(jnp.int32, (count * rows, rows), 1)
    spread = jnp.where(lax.rem(row, rows) == col, 1.0, 0.0).astype(bf16)
    tall = nn(spread, wide[:, :total].astype(bf16))
    row = lax.broadcasted_iota(jnp.int32, tall.shape, 0)
    col = lax.broadcasted_iota(jnp.int32, tall.shape, 1)
    tall = jnp.where(lax.div(row, rows) == lax.div(col, width), tall, 0.0).astype(bf16)
    row = lax.broadcasted_iota(jnp.int32, (total, PACK[1]), 0)
    col = lax.broadcasted_iota(jnp.int32, (total, PACK[1]), 1)
    pick = jnp.where(lax.rem(row, width) == col, 1.0, 0.0).astype(bf16)
    return nn(tall, pick).reshape(count, rows, PACK[1])


def backward(
    signals,
    logits,
    taps,
    grad_out,
    fresh,
    inverses,
    starts,
    state,
    finals,
    grad_starts,
    w_mixed,
    w_rates,
    gain,
    grad_mlp,
    grad_gain,
    normed_t,
    tokens,
    full,
    tap_width,
    gain_width,
):
    count = lax.axis_size("fsdp")
    wide_rows = signals.shape[0]
    rows, width = grad_out.shape
    heads, _, _, size = taps.shape
    chunks = rows // CHUNK
    depth = width // count
    views = [array.reshape(count, -1, array.shape[1]) for array in full]

    def portions(depth, wanted):
        while depth % (16 * wanted) != 0:
            wanted //= 2
        return wanted

    shapes = []
    for a, view in enumerate(views):
        halves = 2 if a < 3 else 1
        for part in range(halves):
            shapes.append((depth, view.shape[2] // halves, 4 if part == 0 else 2))
    loaded = len(shapes)
    for head in range(heads):
        shapes.append((depth, 3 * size, portions(depth, 4 if head % 2 == 0 else 2)))
    shapes.append((depth, logits.shape[1], portions(depth, 2)))
    shapes.append(PACK + (1,))
    staged = max([d // 2 for d, _, _ in shapes[:loaded]] + [16])
    widest = max([w for _, w, _ in shapes[:loaded]] + [128])

    def now(h):
        return jnp.minimum(h, heads - 1)

    def before(h):
        return jnp.maximum(h - 1, 0)

    whole = pl.BlockSpec(logits.shape, lambda h: (0, 0))
    vector = pl.BlockSpec((1, width), lambda h: (0, 0))
    anywhere = pl.BlockSpec(memory_space=pl.ANY)
    shape = jax.ShapeDtypeStruct
    return pl.pallas_call(
        functools.partial(
            backward_kernel, count, len(views), shapes, loaded, heads, tap_width, gain_width
        ),
        grid=(heads + 1,),
        in_specs=[
            pl.BlockSpec((wide_rows, 3 * size), lambda h: (0, now(h))),
            whole,
            pl.BlockSpec((1, 3, TAPS, size), lambda h: (now(h), 0, 0, 0)),
            pl.BlockSpec((rows, size), lambda h: (0, now(h))),
            pl.BlockSpec((rows, 2 * size), lambda h: (0, now(h))),
            pl.BlockSpec((rows, CHUNK), lambda h: (0, now(h))),
            pl.BlockSpec((1, chunks, size, 2 * size), lambda h: (now(h), 0, 0, 0)),
            pl.BlockSpec((1, size, size), lambda h: (now(h), 0, 0)),
            pl.BlockSpec((4, 1, size, 2 * size), lambda h: (0, now(h), 0, 0)),
            pl.BlockSpec((4, 1, size, size), lambda h: (0, now(h), 0, 0)),
            pl.BlockSpec((width, 3 * size), lambda h: (0, before(h))),
            pl.BlockSpec(w_rates.shape, lambda h: (0, 0)),
            vector,
            vector,
            pl.BlockSpec((1, size), lambda h: (0, 0)),
        ]
        + [anywhere] * (2 + len(views)),
        out_specs=[anywhere] * (4 + len(views)),
        out_shape=[shape((rows, width), f32)]
        + [shape(view.shape[1:], bf16) for view in views]
        + [
            shape((depth, 3 * width), bf16),
            shape((depth, logits.shape[1]), bf16),
            shape(PACK, bf16),
        ],
        scratch_shapes=[
            pltpu.VMEM((width, rows), bf16),
            pltpu.VMEM((rows, width), bf16),
            pltpu.VMEM((rows, width), f32),
            pltpu.VMEM((2, rows, 3 * size), bf16),
            pltpu.VMEM((2, HALO, 3 * size), f32),
            pltpu.VMEM((2, HALO, 3 * size), f32),
            pltpu.VMEM((heads, HALO, 3 * size), f32),
            pltpu.VMEM((3, wide_rows, size), f32),
            pltpu.VMEM((3, rows, size), f32),
            pltpu.VMEM((3, rows, size), f32),
            pltpu.VMEM((rows + 2 * HALO, size), f32),
            pltpu.VMEM(logits.shape, f32),
            pltpu.VMEM((PACK[0], 3 * width), f32),
            pltpu.VMEM((count,) + PACK, bf16),
            pltpu.VMEM((count, depth, logits.shape[1]), bf16),
            pltpu.VMEM((3, count, depth, 3 * size), bf16),
            pltpu.VMEM((2, count, staged, widest), bf16),
            pltpu.SemaphoreType.DMA((2,)),
            pltpu.SemaphoreType.DMA((2, heads)),
        ]
        + Reduce.buffers(count, shapes)
        + Reduce.semaphores(count, len(shapes)),
        compiler_params=pltpu.CompilerParams(
            collective_id=2, has_side_effects=True, vmem_limit_bytes=63 * MIB
        ),
    )(
        signals,
        logits,
        taps,
        grad_out,
        fresh,
        inverses,
        starts,
        state,
        finals,
        grad_starts,
        w_mixed,
        w_rates,
        gain,
        grad_mlp,
        grad_gain,
        normed_t,
        tokens,
        *views,
    )


def local(
    inputs,
    g_attn,
    w_query,
    w_key,
    w_value,
    w_beta,
    conv_taps,
    o_gain,
    w_out,
    g_mlp,
    w_gate,
    w_up,
    w_down,
    cotangent,
):
    count = lax.axis_size("fsdp")
    position = lax.axis_index("seq")
    groups = lax.axis_size("seq")
    tokens_low = inputs[0]
    rows, width = tokens_low.shape
    heads = w_beta.shape[1]
    size = width // heads
    depth = w_query.shape[0]
    small = (g_attn.shape, g_mlp.shape, o_gain.shape, conv_taps.shape)
    packed = pack_small((g_attn[None], g_mlp[None], o_gain[None]), conv_taps[None])
    mixed = jnp.stack([w.reshape(depth, -1, size) for w in (w_query, w_key, w_value)], axis=2)
    shards = (
        packed,
        jnp.pad(w_beta, ((0, 0), (0, 128 - heads))),
        mixed.reshape(depth, 3 * width),
        w_out,
        w_gate,
        w_up,
        jnp.transpose(w_down),
    )
    results = forward(tokens_low, shards, heads, conv_taps.shape[1])
    packed, w_beta, w_mixed, w_out, w_gate, w_up, w_down_t = results[:ARRAYS]
    finals, wide_normed, signals, logits, taps = results[ARRAYS : ARRAYS + 5]
    outputs, carries, fresh, inverses, starts = results[ARRAYS + 5 :]
    g_attn, g_mlp, o_gain, _ = unpack_small(packed, small)
    g_attn, g_mlp, o_gain = g_attn.reshape(-1), g_mlp.reshape(-1), o_gain.reshape(-1)
    gain_attn = g_attn.astype(f32)
    tokens = tokens_low.astype(f32)
    normed = wide_normed[HALO:]

    gain_out = o_gain.reshape(1, size)
    head_rows, state_in = mix(position.reshape(1), outputs, carries, finals, gain_out)
    attended = tokens + nn(head_rows, w_out)
    gain_mlp = g_mlp.astype(f32)
    normed_ff = rms_scale(attended, gain_mlp).astype(bf16)
    gated = nn(normed_ff, w_gate)
    upward = nn(normed_ff, w_up)
    sigmoid_gate = jax.nn.sigmoid(gated)
    activated = gated * sigmoid_gate
    hidden = (activated * upward).astype(bf16)
    layer_out = (attended + nt(hidden, w_down_t)).astype(bf16)

    grad_out = cotangent[0]
    grad_down_t = tn(grad_out, hidden).astype(bf16)
    grad_hidden = nn(grad_out, w_down_t)
    grad_gate = (grad_hidden * upward * sigmoid_gate * (1.0 + gated * (1.0 - sigmoid_gate))).astype(
        bf16
    )
    grad_upward = (grad_hidden * activated).astype(bf16)
    grad_gate_matrix = tn(normed_ff, grad_gate).astype(bf16)
    grad_up_matrix = tn(normed_ff, grad_upward).astype(bf16)
    grad_normed_ff = nt(grad_gate, w_gate) + nt(grad_upward, w_up)
    grad_from_ff, grad_gain_mlp = norm_backward(attended, gain_mlp, grad_normed_ff)
    grad_attended = grad_out.astype(f32) + grad_from_ff

    grad_mixed = grad_attended.astype(bf16)
    grad_out_matrix = tn(head_rows, grad_mixed).astype(bf16)
    grad_heads = nt(grad_mixed, w_out).astype(bf16)
    grad_delta, grad_gain_out, grad_starts = unmix(
        outputs, carries, state_in, gain_out, grad_heads
    )
    full = (grad_gate_matrix, grad_up_matrix, grad_down_t, grad_out_matrix)
    beside = depth % 64 == 0
    results = backward(
        signals,
        logits,
        taps,
        grad_delta,
        fresh,
        inverses,
        starts,
        state_in,
        finals,
        grad_starts,
        w_mixed,
        w_beta,
        g_attn.reshape(1, -1),
        grad_gain_mlp.reshape(1, -1),
        grad_gain_out,
        jnp.transpose(normed),
        tokens_low,
        full if beside else (),
        small[3][1],
        small[0][0],
    )
    grad_from_attn, full_sums = results[0], results[1:-3]
    grad_mixed_matrix, grad_beta_matrix, packed = results[-3:]
    if not beside:
        full_sums = [
            lax.psum(lax.psum_scatter(g, "fsdp", scatter_dimension=0, tiled=True), "seq")
            for g in full
        ]
    grad_gate_matrix, grad_up_matrix, grad_down_t, grad_out_matrix = full_sums
    grad_inputs = (grad_attended + grad_from_attn)[None]
    parts = [part[0].astype(f32) for part in unpack_small(packed, small)]
    grad_gain_attn, grad_gain_mlp, grad_gain_out, grad_taps = parts
    grad_mixed_matrix = grad_mixed_matrix.astype(f32).reshape(depth, heads, 3, size)
    grad_query_matrix, grad_key_matrix, grad_value_matrix = (
        grad_mixed_matrix[:, :, which].reshape(depth, width) for which in range(3)
    )
    return (
        layer_out[None],
        grad_inputs,
        grad_gain_attn,
        grad_query_matrix,
        grad_key_matrix,
        grad_value_matrix,
        grad_beta_matrix[:, :heads].astype(f32),
        grad_taps,
        grad_gain_out,
        grad_out_matrix.astype(f32),
        grad_gain_mlp,
        grad_gate_matrix.astype(f32),
        grad_up_matrix.astype(f32),
        jnp.transpose(grad_down_t).astype(f32),
    )


def solution(mesh):
    vector = P("fsdp")
    rows = P("fsdp", None)
    columns = P(None, "fsdp")
    tokens = P("fsdp", "seq", None)
    return jax.shard_map(
        local,
        mesh=mesh,
        in_specs=(
            tokens,
            vector,
            rows,
            rows,
            rows,
            rows,
            columns,
            vector,
            rows,
            vector,
            rows,
            rows,
            columns,
            tokens,
        ),
        out_specs=(
            tokens,
            tokens,
            vector,
            rows,
            rows,
            rows,
            rows,
            columns,
            vector,
            rows,
            vector,
            rows,
            rows,
            columns,
        ),
        check_vma=False,
    )
```

```python
import functools

import jax
import jax.numpy as jnp
from jax import lax
from jax.experimental import pallas as pl
from jax.experimental.pallas import tpu as pltpu
from jax.sharding import PartitionSpec as P

CHUNK = 256
HALO = 16
TAPS = 4
MIB = 1024 * 1024

highest = lax.Precision.HIGHEST
epsilon = 1e-06
f32 = jnp.float32
bf16 = jnp.bfloat16


def nn(left_side, right_side):
    return lax.dot_general(
        left_side, right_side, (((1,), (0,)), ((), ())), preferred_element_type=f32
    )


def nt(left_side, right_side):
    return lax.dot_general(
        left_side, right_side, (((1,), (1,)), ((), ())), preferred_element_type=f32
    )


def tn(left_side, right_side):
    return lax.dot_general(
        left_side, right_side, (((0,), (0,)), ((), ())), preferred_element_type=f32
    )


def rms_scale(values, gain_vec):
    return (
        values * lax.rsqrt(jnp.mean(values * values, axis=-1, keepdims=True) + epsilon) * gain_vec
    )


def norm_backward(values, gain_vec, grad_out):
    scaling = lax.rsqrt(jnp.mean(values * values, axis=-1, keepdims=True) + epsilon)
    unit_rows = values * scaling
    gain_grad = jnp.sum(grad_out * unit_rows, axis=0)
    scaled_grad = grad_out * gain_vec
    input_grad = scaling * (
        scaled_grad - unit_rows * jnp.mean(scaled_grad * unit_rows, axis=-1, keepdims=True)
    )
    return (input_grad, gain_grad)


MESH = pl.DeviceIdType.MESH


class Place:
    def __init__(self, count):
        self.count = count
        self.sides = 2 if count % 2 == 0 else 1
        self.length = count // self.sides
        self.position = lax.axis_index("seq")
        self.index = lax.axis_index("fsdp")
        self.core = lax.rem(self.position, 2)
        self.chip = lax.div(self.position, 2)
        self.side = lax.rem(self.index, self.sides)
        self.spot = lax.div(self.index, self.sides)

    def sibling(self):
        return {"seq": self.position + 1 - 2 * self.core, "fsdp": self.index}

    def across(self):
        return {"seq": lax.rem(self.position + 2, 4), "fsdp": self.index}

    def partner(self):
        return {"seq": self.position, "fsdp": self.spot * 2 + 1 - self.side}

    def ahead(self, step):
        spot = lax.rem(self.spot + step, self.length)
        return {"seq": self.position, "fsdp": spot * self.sides + self.side}

    def shard(self, spot, side):
        return spot * self.sides + side

    def behind(self, step):
        return lax.rem(self.spot + self.length - step, self.length)

    def greet_all(self):
        self.greet(False, True)

    def greet(self, across, sequence=False):
        barrier = pltpu.get_barrier_semaphore()
        total = self.length - 1

        def signal(device):
            pl.semaphore_signal(barrier, inc=1, device_id=device, device_id_type=MESH)

        def one(step, carry):
            signal(self.ahead(step))
            return carry

        lax.fori_loop(1, self.length, one, 0)
        if sequence:
            for hop in range(1, 4):
                signal({"seq": lax.rem(self.position + hop, 4), "fsdp": self.index})
            total += 3
        else:
            signal(self.sibling())
            total += 1
        if self.sides == 2:
            signal(self.partner())
            total += 1
        if across:
            signal(self.across())
            total += 1
        pl.semaphore_wait(barrier, total)


def remote(source, target, send, recv, device):
    return pltpu.make_async_remote_copy(
        src_ref=source,
        dst_ref=target,
        send_sem=send,
        recv_sem=recv,
        device_id=device,
        device_id_type=MESH,
    )


def steps(first, last, body):
    def one(step, carry):
        body(step)
        return carry

    lax.fori_loop(first, last, one, 0)


class Reduce:
    BUFFERS = 6

    def __init__(self, count, pieces, sources, targets, buffers, staging, sems):
        self.place = Place(count)
        self.pieces, self.sources, self.targets, self.staging = pieces, sources, targets, staging
        self.acc, self.x_in, self.y_in, self.z_in, self.parts_in, self.result = buffers
        (
            self.core_sem,
            self.load_sem,
            self.x_sem,
            self.y_sem,
            self.z_sem,
            self.share_sem,
            self.final_sem,
            self.store_sem,
        ) = sems

    @staticmethod
    def buffers(count, pieces):
        length = count // 2
        acc, x_in, y_in, z_in, parts_in, result = [], [], [], [], [], []
        for depth, width, parts in pieces:
            rows = depth // parts
            acc.append(pltpu.VMEM((length, 2, depth // min(parts, 2), width), bf16))
            x_in.append(
                pltpu.VMEM((length, 2, rows, width) if parts == 4 else (1, 1, 16, 128), bf16)
            )
            y_in.append(pltpu.VMEM((length, rows, width), bf16))
            z_in.append(pltpu.VMEM((length, rows, width), bf16))
            parts_in.append(
                pltpu.VMEM((4 // parts, rows, width) if parts < 4 else (1, 16, 128), bf16)
            )
            result.append(pltpu.VMEM((rows, width), bf16))
        return acc + x_in + y_in + z_in + parts_in + result

    @staticmethod
    def semaphores(count, number):
        pair = pltpu.SemaphoreType.DMA((number, 2))
        one = pltpu.SemaphoreType.DMA((number,))
        hops = pltpu.SemaphoreType.DMA((number, 2, 4))
        return [pair, one, pair, pair, pair, hops, hops, one]

    def half(self, p, core):
        depth, _, parts = self.pieces[p]
        rows = depth // min(parts, 2)
        return pl.ds(pl.multiple_of(core * rows, 16) if parts > 1 else 0, rows)

    def quarter(self, p, chip):
        depth, _, parts = self.pieces[p]
        rows = depth // parts
        return pl.ds(pl.multiple_of(chip * rows, 16) if parts == 4 else 0, rows)

    def device(self, hop):
        return {"seq": lax.rem(self.place.position + hop, 4), "fsdp": self.place.index}

    def to_sibling(self, p):
        return remote(
            self.sources[p].at[:, :, self.half(p, 1 - self.place.core), :],
            self.acc[p],
            self.core_sem.at[p, 0],
            self.core_sem.at[p, 1],
            self.place.sibling(),
        )

    def stage(self, p):
        depth, width, parts = self.pieces[p]
        return self.staging.at[p % 2, :, :, pl.ds(0, depth // 2), pl.ds(0, width)]

    def load(self, p):
        return pltpu.make_async_copy(
            self.sources[p].at[:, :, self.half(p, self.place.core), :],
            self.stage(p),
            self.load_sem.at[p],
        )

    def to_x(self, p):
        return remote(
            self.acc[p].at[:, :, self.quarter(p, 1 - self.place.chip), :],
            self.x_in[p],
            self.x_sem.at[p, 0],
            self.x_sem.at[p, 1],
            self.place.across(),
        )

    def to_y(self, p):
        place = self.place
        return remote(
            self.acc[p].at[:, 1 - place.side, self.quarter(p, place.chip), :],
            self.y_in[p],
            self.y_sem.at[p, 0],
            self.y_sem.at[p, 1],
            place.partner(),
        )

    def to_z(self, p, step):
        place = self.place
        spot = lax.rem(place.spot + step, place.length)
        return remote(
            self.acc[p].at[spot, place.side, self.quarter(p, place.chip), :],
            self.z_in[p].at[step],
            self.z_sem.at[p, 0],
            self.z_sem.at[p, 1],
            place.ahead(step),
        )

    def all_z(self, p):
        both = self.z_in[p].at[pl.ds(1, self.place.length - 1)]
        return remote(
            both, both, self.z_sem.at[p, 0], self.z_sem.at[p, 1], self.place.ahead(1)
        )

    def sharers(self, p):
        return {1: (1, 2, 3), 2: (2,), 4: ()}[self.pieces[p][2]]

    def receivers(self, p):
        return {1: (), 2: (0,), 4: (1, 2, 3)}[self.pieces[p][2]]

    def sharer(self, p, position):
        return position if self.pieces[p][2] == 1 else lax.div(position, 2)

    def to_share(self, p, hop, arriving=False):
        position = self.place.position
        source = lax.rem(position + 4 - hop, 4) if arriving else position
        buffer = self.parts_in[p].at[self.sharer(p, source)]
        return remote(
            buffer,
            buffer,
            self.share_sem.at[p, 0, hop],
            self.share_sem.at[p, 1, hop],
            self.device(hop),
        )

    def target(self, p, position):
        depth, _, parts = self.pieces[p]
        rows = depth // parts
        core, chip = lax.rem(position, 2), lax.div(position, 2)
        first = {1: 0, 2: core * rows, 4: (core * 2 + chip) * rows}[parts]
        return self.targets[p].at[pl.ds(pl.multiple_of(first, 16) if parts > 1 else 0, rows), :]

    def to_result(self, p, hop, arriving=False):
        place = self.place
        if hop == 0:
            other = place.position + 1 - 2 * place.core
            device = place.sibling()
        else:
            other = lax.rem(place.position + 4 - hop, 4)
            device = self.device(hop)
        return remote(
            self.result[p],
            self.target(p, other if arriving else place.position),
            self.final_sem.at[p, 0, hop],
            self.final_sem.at[p, 1, hop],
            device,
        )

    def store(self, p):
        return pltpu.make_async_copy(
            self.result[p], self.target(p, self.place.position), self.store_sem.at[p]
        )

    def start(self, p, loaded):
        if self.pieces[p][2] > 1:
            self.to_sibling(p).start()
        if loaded:
            self.load(p).start()

    def on_core(self, p, loaded):
        parts = self.pieces[p][2]
        acc = self.acc[p]
        half = self.half(p, self.place.core)
        rows, width = acc.shape[2], acc.shape[3]
        if loaded:
            self.load(p).wait()
        if parts == 1:
            acc[...] = self.sources[p][...]
        else:
            self.to_sibling(p).wait_recv()

            def add(spot):
                if loaded:
                    own = self.staging[p % 2, spot, :, pl.ds(0, rows), pl.ds(0, width)]
                else:
                    own = self.sources[p][spot, :, half, :]
                acc[spot] = acc[spot] + own

            steps(0, self.place.length, add)
        (self.to_x if parts == 4 else self.to_y)(p).start()
        if parts > 1:
            self.to_sibling(p).wait_send()

    def on_x(self, p):
        acc, side = self.acc[p], 1 - self.place.side
        rows = self.quarter(p, self.place.chip)
        self.to_x(p).wait_recv()

        def add(spot):
            acc[spot, side, rows, :] = acc[spot, side, rows, :] + self.x_in[p][spot, side]

        steps(0, self.place.length, add)
        self.to_y(p).start()

    def on_y(self, p):
        place = self.place
        acc = self.acc[p]
        rows = self.quarter(p, place.chip)
        self.to_y(p).wait_recv()

        def one(step):
            spot = lax.rem(place.spot + step, place.length)
            total = acc[spot, place.side, rows, :].astype(f32) + self.y_in[p][spot].astype(f32)
            if self.pieces[p][2] == 4:
                total = total + self.x_in[p][spot, place.side].astype(f32)
            acc[spot, place.side, rows, :] = total.astype(bf16)

        def send(step):
            one(step)
            self.to_z(p, step).start()

        steps(1, place.length, send)
        one(0)

    def on_z(self, p):
        place = self.place
        rows = self.quarter(p, place.chip)
        self.all_z(p).wait_recv()
        total = self.acc[p][place.spot, place.side, rows, :].astype(f32)
        if place.length <= 8:
            for step in range(1, place.length):
                total = total + self.z_in[p][step].astype(f32)
        else:
            total = lax.fori_loop(
                1,
                place.length,
                lambda step, carry: carry + self.z_in[p][step].astype(f32),
                total,
            )
        if self.pieces[p][2] == 4:
            self.result[p][...] = total.astype(bf16)
            self.publish(p)
        else:
            self.parts_in[p][self.sharer(p, place.position)] = total.astype(bf16)
            for hop in self.sharers(p):
                self.to_share(p, hop).start()

    def on_share(self, p):
        total = None
        for hop in self.sharers(p):
            self.to_share(p, hop, True).wait_recv()
        for index in range(4 // self.pieces[p][2]):
            term = self.parts_in[p][index].astype(f32)
            total = term if total is None else total + term
        self.result[p][...] = total.astype(bf16)
        self.publish(p)

    def publish(self, p):
        for hop in self.receivers(p):
            self.to_result(p, hop).start()
        self.store(p).start()

    def finish(self, p):
        if self.pieces[p][2] == 4:
            self.to_x(p).wait_send()
        self.to_y(p).wait_send()
        self.all_z(p).wait_send()
        for hop in self.sharers(p):
            self.to_share(p, hop).wait_send()
        for hop in self.receivers(p):
            self.to_result(p, hop).wait_send()
            self.to_result(p, hop, True).wait_recv()
        self.store(p).wait()

    def plan(self, begin, stride, last, loaded, idle=()):
        due = []
        for p, (_, _, parts) in enumerate(self.pieces):
            for index, kind in enumerate((0, 1, 2, 3) if parts == 4 else (0, 2, 3, 4)):
                half = begin[p] + stride * index
                while half in idle:
                    half += 1
                due.append((half, -index, p, kind))
        due.sort()

        def action(p, kind):
            if kind == 0:
                self.on_core(p, loaded[p])
                if loaded[p] and p + 2 < len(self.pieces) and loaded[p + 2]:
                    self.start(p + 2, True)
            else:
                (self.on_x, self.on_y, self.on_z, self.on_share)[kind - 1](p)

        def at(test):
            return [functools.partial(action, p, kind) for half, _, p, kind in due if test(half)]

        return (
            {half: at(lambda when: when == half) for half in range(last + 1)},
            at(lambda when: when > last),
        )


class Gather:
    SEMS = 6

    def __init__(self, count, pieces, shards, outs, sems):
        self.place = Place(count)
        self.pieces, self.shards, self.outs = pieces, shards, outs
        self.line_sem, self.side_sem, self.core_sem, self.across_sem, self.relay_sem, self.own = (
            sems
        )

    @staticmethod
    def scratch(pieces, count):
        length = count // 2 if count % 2 == 0 else count
        number = len(pieces)
        slots = 2 * length if max(piece[3] for piece in pieces) > 1 else 1
        return [
            pltpu.SemaphoreType.DMA((number, 2, length)),
            pltpu.SemaphoreType.DMA((number, 2, length)),
            pltpu.SemaphoreType.DMA((number, 2, slots)),
            pltpu.SemaphoreType.DMA((number, 2, slots)),
            pltpu.SemaphoreType.DMA((number, 2, slots)),
            pltpu.SemaphoreType.DMA((number,)),
        ]

    def portion(self, k, core, chip):
        parts = self.pieces[k][3]
        if parts == 1:
            return 0
        return core if parts == 2 else 2 * chip + core

    def region(self, k, shard, core, chip):
        a, offset, width, parts = self.pieces[k]
        depth = self.shards[a].shape[0]
        rows = depth // parts
        first = shard * depth + self.portion(k, core, chip) * rows
        return self.outs[a].at[pl.ds(pl.multiple_of(first, 16), rows), pl.ds(offset, width)]

    def source(self, k):
        p = self.place
        a, offset, width, parts = self.pieces[k]
        rows = self.shards[a].shape[0] // parts
        first = self.portion(k, p.core, p.chip) * rows
        return self.shards[a].at[pl.ds(pl.multiple_of(first, 16), rows), pl.ds(offset, width)]

    def line(self, k, step, arriving=False):
        p = self.place
        shard = p.shard(p.behind(step), p.side) if arriving else p.index
        target = self.region(k, shard, p.core, p.chip)
        return remote(
            target if arriving else self.source(k),
            target,
            self.line_sem.at[k, 0, step],
            self.line_sem.at[k, 1, step],
            p.ahead(step),
        )

    def side(self, k, step, arriving=False, own=False):
        p = self.place
        shard = p.shard(p.behind(step), 1 - p.side if arriving else p.side)
        target = self.region(k, shard, p.core, p.chip)
        return remote(
            self.source(k) if own else target,
            target,
            self.side_sem.at[k, 0, step],
            self.side_sem.at[k, 1, step],
            p.partner(),
        )

    def cross(self, k, step, other, sems, core, chip, device):
        p = self.place
        shard = p.shard(p.behind(step), 1 - p.side if other else p.side)
        target = self.region(k, shard, core, chip)
        slot = 2 * step + (1 if other else 0)
        return remote(target, target, sems.at[k, 0, slot], sems.at[k, 1, slot], device)

    def core(self, k, step, other, arriving=False):
        p = self.place
        core = 1 - p.core if arriving else p.core
        return self.cross(k, step, other, self.core_sem, core, p.chip, p.sibling())

    def across(self, k, step, other, arriving=False):
        p = self.place
        chip = 1 - p.chip if arriving else p.chip
        return self.cross(k, step, other, self.across_sem, p.core, chip, p.across())

    def relay(self, k, step, other, arriving=False):
        p = self.place
        core = 1 - p.core if arriving else p.core
        return self.cross(k, step, other, self.relay_sem, core, 1 - p.chip, p.sibling())

    def keep(self, k):
        a, offset, width, _ = self.pieces[k]
        depth = self.shards[a].shape[0]
        rows = pl.ds(pl.multiple_of(self.place.index * depth, 16), depth)
        columns = pl.ds(offset, width)
        return pltpu.make_async_copy(
            self.shards[a].at[:, columns], self.outs[a].at[rows, columns], self.own.at[k]
        )

    def hand(self, k, step, other):
        parts = self.pieces[k][3]
        if parts == 4:
            self.across(k, step, other).start()
        if parts > 1:
            self.core(k, step, other).start()

    def start(self, k):
        steps(1, self.place.length, lambda step: self.line(k, step).start())
        if self.place.sides == 2:
            self.side(k, 0, own=True).start()
        self.keep(k).start()

    def forward(self, k):
        def one(step):
            self.line(k, step, True).wait_recv()
            if self.place.sides == 2:
                self.side(k, step).start()
            self.hand(k, step, False)

        steps(1, self.place.length, one)

    def spread(self, k):
        def one(step):
            self.side(k, step, True).wait_recv()
            self.hand(k, step, True)

        if self.place.sides == 2:
            steps(0, self.place.length, one)

    def each(self, body):
        steps(1, self.place.length, lambda step: body(step, False))
        if self.place.sides == 2:
            steps(0, self.place.length, lambda step: body(step, True))

    def exchange(self, k):
        def one(step, other):
            self.across(k, step, other, True).wait_recv()
            self.relay(k, step, other).start()

        if self.pieces[k][3] == 4:
            self.each(one)

    def arrive(self, k):
        parts = self.pieces[k][3]

        def one(step, other):
            self.core(k, step, other, True).wait_recv()
            if parts == 4:
                self.relay(k, step, other, True).wait_recv()

        self.keep(k).wait()
        if parts > 1:
            self.each(one)

    def sent(self, k):
        parts = self.pieces[k][3]

        def one(step, other):
            self.core(k, step, other).wait_send()
            if parts == 4:
                self.across(k, step, other).wait_send()
                self.relay(k, step, other).wait_send()

        steps(1, self.place.length, lambda step: self.line(k, step).wait_send())
        if self.place.sides == 2:
            steps(0, self.place.length, lambda step: self.side(k, step).wait_send())
        if parts > 1:
            self.each(one)

    def events(self, tiles, urgent, ahead=3):
        made = []
        line = side = across = 0.0
        hop = 8.0
        number = len(self.pieces)
        for k in range(number):
            parts = self.pieces[k][3]
            margin = 8.0 if k < urgent else 30.0
            load = tiles[k] * (2 if parts == 4 else 4)
            line = line + load
            side = max(side + load, line + load / 4 + hop)
            last = side
            made.append((line + hop, k, 0))
            made.append((side + hop, k, 1))
            if parts == 4:
                across = max(across + 3.5 * tiles[k], side + tiles[k] / 2 + hop)
                last = across
                made.append((across + hop + margin, k, 2))
            wait = 0.0 if k < urgent else 2 * margin
            made.append((last + 2 * hop + wait + (margin if parts == 4 else 0.0), k, 3))
        made.sort()

        def action(k, kind):
            if kind == 0:
                self.forward(k)
                if k + ahead < number:
                    self.start(k + ahead)
            else:
                (self.spread, self.exchange, self.arrive)[kind - 1](k)

        return [(when, k, kind, functools.partial(action, k, kind)) for when, k, kind in made]


PACK = (16, 512)


def pack_small(gains, taps):
    count = taps.shape[0]

    def fit(values, rows):
        values = values.reshape(count, -1, values.shape[-1]).astype(bf16)
        return jnp.pad(
            values, ((0, 0), (0, rows - values.shape[1]), (0, PACK[1] - values.shape[2]))
        )

    rows = [fit(gains[0], 1), fit(gains[1], 1), fit(gains[2], 2), fit(taps, PACK[0] - 4)]
    return jnp.concatenate(rows, axis=1).reshape(count * PACK[0], PACK[1])


def unpack_small(packed, shapes):
    packed = packed.reshape(-1, PACK[0], PACK[1])
    gains = [packed[:, row, : shape[0]] for row, shape in enumerate(shapes[:3])]
    return gains + [packed[:, 4 : 4 + shapes[3][0], : shapes[3][1]]]


def place_rows(packed, count, width):
    if width % 128 == 0:
        return jnp.concatenate(
            [packed[s * PACK[0] : (s + 1) * PACK[0], :width] for s in range(count)], axis=1
        )
    total = count * width
    row = lax.broadcasted_iota(jnp.int32, (PACK[1], total), 0)
    col = lax.broadcasted_iota(jnp.int32, (PACK[1], total), 1)
    pick = jnp.where(lax.rem(col, width) == row, 1.0, 0.0).astype(bf16)
    wide = nn(packed.astype(bf16), pick)
    row = lax.broadcasted_iota(jnp.int32, wide.shape, 0)
    col = lax.broadcasted_iota(jnp.int32, wide.shape, 1)
    wide = jnp.where(lax.div(row, PACK[0]) == lax.div(col, width), wide, 0.0).astype(bf16)
    row = lax.broadcasted_iota(jnp.int32, (PACK[0], count * PACK[0]), 0)
    col = lax.broadcasted_iota(jnp.int32, (PACK[0], count * PACK[0]), 1)
    fold = jnp.where(lax.rem(col, PACK[0]) == row, 1.0, 0.0).astype(bf16)
    return nn(fold, wide)


GROUP = 2


def grid_indices():
    row = lax.broadcasted_iota(jnp.int32, (CHUNK, CHUNK), 0)
    col = lax.broadcasted_iota(jnp.int32, (CHUNK, CHUNK), 1)
    return row, col


def conv_pre(wide_ref, taps, rows):
    total = None
    for offset in range(TAPS):
        term = taps[offset : offset + 1, :] * wide_ref[pl.ds(HALO - TAPS + 1 + offset, rows), :]
        total = term if total is None else total + term
    return total


def sigmoid(values):
    return 1.0 / (1.0 + jnp.exp(-values))


def head_column(table, head):
    lane = lax.broadcasted_iota(jnp.int32, table.shape, 1)
    return jnp.sum(jnp.where(lane == head, table, 0.0), axis=1, keepdims=True)


ARRAYS = 7


def forward_kernel(count, pieces, mixed, heads, tap_width, *refs):
    tokens_ref = refs[0]
    shards, refs = refs[1 : 1 + ARRAYS], refs[1 + ARRAYS :]
    gathered, refs = refs[:ARRAYS], refs[ARRAYS:]
    (
        finals_ref,
        normed_ref,
        normed_t_ref,
        signals_ref,
        logit_ref,
        taps_ref,
        out_ref,
        carry_ref,
        fresh_ref,
        inverse_ref,
        starts_ref,
    ), refs = refs[:11], refs[11:]
    (
        tokens,
        weights,
        rates_weight,
        packed,
        all_taps,
        wide,
        level_masks,
        final,
        halo_sem,
        token_sem,
        load_sem,
        final_sem,
        *sems,
    ) = refs
    group = pl.program_id(0)
    groups = heads // GROUP
    rows = out_ref.shape[0]
    size = out_ref.shape[1] // GROUP
    span = GROUP * size
    chunks = rows // CHUNK
    levels = CHUNK.bit_length() - 1
    row, col = grid_indices()
    gather = Gather(count, pieces, shards, gathered, sems)
    place = gather.place
    tiles = [piece[2] / 128 * shards[piece[0]].shape[0] / 128 for piece in pieces]
    events = gather.events(tiles, 2 + groups)

    def halo(arriving):
        return remote(
            tokens_ref.at[pl.ds(rows - HALO, HALO), :],
            tokens.at[pl.ds(0, HALO), :],
            halo_sem.at[0],
            halo_sem.at[1],
            {"seq": lax.rem(place.position + 1, 4), "fsdp": place.index},
        )

    def load(step, slot):
        return pltpu.make_async_copy(
            gathered[mixed].at[:, pl.ds(pl.multiple_of(step * 3 * span, 128), 3 * span)],
            weights.at[slot],
            load_sem.at[slot],
        )

    per_step = 9
    plan = {}
    mark = 0
    for step in range(groups):
        for spot in range(per_step):
            now = 60.0 + (step * per_step + spot) * 5.0
            upto = mark
            for index in range(mark, len(events)):
                when, k, kind, _ = events[index]
                if spot == 0 and kind == 3 and (k == 2 + step or (step == 0 and k < 2)):
                    upto = index + 1
                elif when <= now and upto == index:
                    upto = index + 1
            plan[step, spot] = (mark, upto)
            mark = upto
    remaining = (mark, len(events))

    def run(bounds):
        for _, _, _, action in events[bounds[0] : bounds[1]]:
            action()

    def spot(number):
        for step in range(groups):
            bounds = plan[step, number]
            if bounds[1] > bounds[0]:

                @pl.when(group == step)
                def _():
                    run(bounds)

    @pl.when(group == 0)
    def _():
        own = pltpu.make_async_copy(tokens_ref, tokens.at[pl.ds(HALO, rows), :], token_sem.at[0])
        own.start()
        place.greet_all()

        @pl.when(place.position < 3)
        def _():
            halo(False).start()

        gather.start(0)
        gather.start(1)
        gather.start(2)

        @pl.when(place.position == 0)
        def _():
            tokens[pl.ds(0, HALO), :] = jnp.zeros((HALO, tokens.shape[1]), bf16)

        for level in range(levels):
            same = (row >> (level + 1)) == (col >> (level + 1))
            below = ((row >> level) & 1 == 1) & ((col >> level) & 1 == 0)
            level_masks[level] = jnp.where(same & below, 1.0, 0.0).astype(bf16)

        limit = max(i for i, event in enumerate(events) if event[1] == 0) + 1
        run((0, limit))
        copy = pltpu.make_async_copy(gathered[0], packed, token_sem.at[1])
        copy.start()
        copy.wait()
        small = packed[...].astype(f32)
        gain = place_rows(small, count, tokens.shape[1] // count)[0:1, :]
        all_taps[...] = place_rows(small, count, tap_width)[4 : 4 + TAPS, :]
        own.wait()

        @pl.when(place.position > 0)
        def _():
            halo(True).wait_recv()

        block = 208 if tokens.shape[0] % 208 == 0 else HALO

        def norm(index):
            part = pl.ds(pl.multiple_of(index * block, HALO), block)
            normed_ref[part, :] = rms_scale(tokens[part, :].astype(f32), gain).astype(bf16)

        steps(0, tokens.shape[0] // block, norm)
        for first in range(0, rows, CHUNK):
            part = normed_ref[pl.ds(HALO + first, CHUNK), :]
            normed_t_ref[:, first : first + CHUNK] = part.T
        run((limit, plan[0, 0][1]))
        copy = pltpu.make_async_copy(gathered[1], rates_weight, token_sem.at[1])
        copy.start()
        load(0, 0).start()
        copy.wait()
        logit_ref[...] = nn(normed_ref[pl.ds(HALO, rows), :], rates_weight[...]).astype(bf16)
        load(0, 0).wait()

    for step in range(1, groups):
        bounds = plan[step, 0]

        @pl.when(group == step)
        def _():
            run(bounds)
            load(step, 0).start()
            load(step, 0).wait()

    signals_ref[...] = nn(normed_ref[...], weights[0]).astype(bf16)
    spot(1)

    lows = [[], [], []]
    for inner in range(GROUP):
        for which in range(3):
            first = pl.multiple_of((which * heads + group * GROUP + inner) * size, 128)
            taps = all_taps[:, pl.ds(first, size)]
            taps_ref[inner, which] = taps
            wide[...] = signals_ref[:, pl.ds((inner * 3 + which) * size, size)].astype(f32)
            pre = conv_pre(wide, taps, rows)
            act = pre * sigmoid(pre)
            if which < 2:
                act = act * lax.rsqrt(jnp.sum(act * act, axis=1, keepdims=True) + epsilon)
            lows[which].append(act.astype(bf16))
        if inner == 0:
            spot(2)
    spot(3)
    logits = logit_ref[...].astype(f32)
    rates = [sigmoid(head_column(logits, group * GROUP + inner)) for inner in range(GROUP)]
    scaling = size ** (-0.5)
    eye = jnp.where(row == col, 1.0, 0.0)
    lower = row >= col

    work = [(inner, chunk) for inner in range(GROUP) for chunk in range(chunks)]

    def cut(values, item):
        inner, chunk = item
        return values[inner][chunk * CHUNK : (chunk + 1) * CHUNK]

    queries, keys, values = lows
    stricts = [(cut(rates, i) * nt(cut(keys, i), cut(keys, i))).astype(bf16) for i in work]
    results = [eye - (strict * level_masks[0]).astype(f32) for strict in stricts]
    scores = [jnp.where(lower, nt(cut(queries, i), cut(keys, i)), 0.0).astype(bf16) for i in work]
    for level in range(1, levels):
        mask = level_masks[level]
        lowered = [result.astype(bf16) for result in results]
        inners = [nn(low, strict * mask).astype(bf16) for low, strict in zip(lowered, stricts)]
        results = [
            result - nn(inner, low) for result, inner, low in zip(results, inners, lowered)
        ]
        if level in (2, 4, 6):
            spot(3 + level // 2)
    inverses = [result.astype(bf16) for result in results]
    for (inner, chunk), inverse in zip(work, inverses):
        part = slice(chunk * CHUNK, (chunk + 1) * CHUNK)
        inverse_ref[part, inner * CHUNK : (inner + 1) * CHUNK] = inverse
    spot(7)

    srow = lax.broadcasted_iota(jnp.int32, (size, size), 0)
    scol = lax.broadcasted_iota(jnp.int32, (size, size), 1)
    memories = [
        jnp.concatenate(
            [jnp.zeros((size, size), f32), jnp.where(srow == scol, 1.0, 0.0)], axis=1
        )
    ] * GROUP
    for chunk in range(chunks):
        part = slice(chunk * CHUNK, (chunk + 1) * CHUNK)
        for inner in range(GROUP):
            item = (inner, chunk)
            key_part, query_part, rate_part = cut(keys, item), cut(queries, item), cut(rates, item)
            low_memory = memories[inner].astype(bf16)
            starts_ref[inner, chunk] = low_memory
            seen = nn(key_part, low_memory)
            aim = jnp.concatenate(
                [cut(values, item).astype(f32), jnp.zeros((CHUNK, size), f32)], axis=1
            )
            aim = (rate_part * (aim - seen)).astype(bf16)
            fresh = nn(inverses[work.index(item)], aim).astype(bf16)
            fresh_ref[part, inner * 2 * size : (inner + 1) * 2 * size] = fresh
            both = scaling * (
                nn(query_part, low_memory) + nn(scores[work.index(item)], fresh)
            )
            out_ref[part, inner * size : (inner + 1) * size] = both[:, :size]
            carry_ref[part, inner * size : (inner + 1) * size] = both[:, size:].astype(bf16)
            memories[inner] = memories[inner] + tn(key_part, fresh)

    def send_final(step, hop):
        position = lax.rem(place.position + hop, 4)
        block = pl.ds(step * GROUP, GROUP)
        return remote(
            final.at[block],
            finals_ref.at[place.position, block],
            final_sem.at[0, step, hop],
            final_sem.at[1, step, hop],
            {"seq": position, "fsdp": place.index},
        )

    def keep_final(step):
        block = pl.ds(step * GROUP, GROUP)
        return pltpu.make_async_copy(
            final.at[block], finals_ref.at[place.position, block], final_sem.at[0, step, 0]
        )

    def take_final(step, hop):
        position = lax.rem(place.position + 4 - hop, 4)
        block = pl.ds(step * GROUP, GROUP)
        return remote(
            final.at[block],
            finals_ref.at[position, block],
            final_sem.at[0, step, hop],
            final_sem.at[1, step, hop],
            {"seq": position, "fsdp": place.index},
        )

    for step in range(groups):

        @pl.when(group == step)
        def _():
            for inner in range(GROUP):
                final[step * GROUP + inner] = memories[inner].astype(bf16)
            for hop in range(1, 4):
                send_final(step, hop).start()
            keep_final(step).start()

    spot(8)

    @pl.when(group == groups - 1)
    def _():
        run(remaining)
        for k in range(len(pieces)):
            gather.sent(k)
        for step in range(groups):
            for hop in range(1, 4):
                send_final(step, hop).wait_send()
                take_final(step, hop).wait_recv()
            keep_final(step).wait()

        @pl.when(place.position < 3)
        def _():
            halo(False).wait_send()


def plan_pieces(depths, widths, span):
    def portions(a, wanted):
        while depths[a] % (16 * wanted) != 0:
            wanted //= 2
        return wanted

    pieces = [(0, 0, widths[0], 1), (1, 0, widths[1], portions(1, 2))]
    for step in range(widths[2] // span):
        pieces.append((2, step * span, span, portions(2, 4)))
    pieces.append((3, 0, widths[3], portions(3, 4)))
    for a in (4, 5, 6):
        half = widths[a] // 2
        for part in range(2):
            wanted = 2 if (a, part) in ((5, 0), (6, 1)) else 4
            pieces.append((a, part * half, half, portions(a, wanted)))
    return pieces


def forward(tokens, shards, heads, tap_width):
    count = lax.axis_size("fsdp")
    rows, width = tokens.shape
    size = width // heads
    span = GROUP * size
    groups = heads // GROUP
    chunks = rows // CHUNK
    wide_rows = rows + HALO
    depths = [shard.shape[0] for shard in shards]
    widths = [shard.shape[1] for shard in shards]
    pieces = plan_pieces(depths, widths, 3 * span)
    anywhere = pl.BlockSpec(memory_space=pl.ANY)
    shape = jax.ShapeDtypeStruct
    return pl.pallas_call(
        functools.partial(forward_kernel, count, pieces, 2, heads, tap_width),
        grid=(groups,),
        in_specs=[anywhere] * (1 + ARRAYS),
        out_specs=[anywhere] * (ARRAYS + 1)
        + [
            pl.BlockSpec((wide_rows, width), lambda g: (0, 0)),
            pl.BlockSpec((width, rows), lambda g: (0, 0)),
            pl.BlockSpec((wide_rows, 3 * span), lambda g: (0, g)),
            pl.BlockSpec((rows, widths[1]), lambda g: (0, 0)),
            pl.BlockSpec((GROUP, 3, TAPS, size), lambda g: (g, 0, 0, 0)),
            pl.BlockSpec((rows, span), lambda g: (0, g)),
            pl.BlockSpec((rows, span), lambda g: (0, g)),
            pl.BlockSpec((rows, 2 * span), lambda g: (0, g)),
            pl.BlockSpec((rows, GROUP * CHUNK), lambda g: (0, g)),
            pl.BlockSpec((GROUP, chunks, size, 2 * size), lambda g: (g, 0, 0, 0)),
        ],
        out_shape=[shape((count * d, w), bf16) for d, w in zip(depths, widths)]
        + [
            shape((4, heads, size, 2 * size), bf16),
            shape((wide_rows, width), bf16),
            shape((width, rows), bf16),
            shape((wide_rows, 3 * width), bf16),
            shape((rows, widths[1]), bf16),
            shape((heads, 3, TAPS, size), f32),
            shape((rows, width), f32),
            shape((rows, width), bf16),
            shape((rows, 2 * width), bf16),
            shape((rows, heads * CHUNK), bf16),
            shape((heads, chunks, size, 2 * size), bf16),
        ],
        scratch_shapes=[
            pltpu.VMEM((wide_rows, width), bf16),
            pltpu.VMEM((1, width, 3 * span), bf16),
            pltpu.VMEM((width, widths[1]), bf16),
            pltpu.VMEM((count * PACK[0], PACK[1]), bf16),
            pltpu.VMEM((TAPS, 3 * width), f32),
            pltpu.VMEM((wide_rows, size), f32),
            pltpu.VMEM((CHUNK.bit_length() - 1, CHUNK, CHUNK), bf16),
            pltpu.VMEM((heads, size, 2 * size), bf16),
            pltpu.SemaphoreType.DMA((2,)),
            pltpu.SemaphoreType.DMA((2,)),
            pltpu.SemaphoreType.DMA((2,)),
            pltpu.SemaphoreType.DMA((2, groups, 4)),
        ]
        + Gather.scratch(pieces, count),
        compiler_params=pltpu.CompilerParams(
            collective_id=0, has_side_effects=True, vmem_limit_bytes=60 * MIB
        ),
    )(tokens, *shards)


def mix_kernel(position_ref, out_ref, carry_ref, finals_ref, gain_ref, mixed_ref, state_ref):
    position = position_ref[0]
    size = out_ref.shape[1]
    state = jnp.zeros((size, size), f32)
    for index in range(finals_ref.shape[0] - 1):
        pair = finals_ref[index, 0].astype(f32)
        later = pair[:, :size] + jnp.dot(pair[:, size:], state, precision=highest)
        state = jnp.where(index < position, later, state)
    state_ref[0] = state
    output = out_ref[...] + nn(carry_ref[...], state.astype(bf16))
    gain = gain_ref[...].astype(f32)
    mixed_ref[...] = rms_scale(output, gain).astype(bf16)


def mix(position, outputs, carries, finals, gain):
    rows, width = outputs.shape
    groups, heads, size, _ = finals.shape
    plain = pl.BlockSpec((rows, size), lambda h: (0, h))
    return pl.pallas_call(
        mix_kernel,
        grid=(heads,),
        in_specs=[
            pl.BlockSpec(memory_space=pltpu.SMEM),
            plain,
            plain,
            pl.BlockSpec((groups, 1, size, 2 * size), lambda h: (0, h, 0, 0)),
            pl.BlockSpec((1, size), lambda h: (0, 0)),
        ],
        out_specs=[plain, pl.BlockSpec((1, size, size), lambda h: (h, 0, 0))],
        out_shape=[
            jax.ShapeDtypeStruct((rows, width), bf16),
            jax.ShapeDtypeStruct((heads, size, size), f32),
        ],
        compiler_params=pltpu.CompilerParams(vmem_limit_bytes=32 * MIB),
    )(position, outputs, carries, finals, gain)


def unmix_kernel(
    heads,
    out_ref,
    carry_ref,
    state_ref,
    gain_ref,
    grad_ref,
    grad_out_ref,
    grad_gain_ref,
    grads_ref,
    grad_states,
    sems,
):
    head = pl.program_id(0)
    position, index = lax.axis_index("seq"), lax.axis_index("fsdp")

    def device(hop):
        return {"seq": lax.rem(position + hop, 4), "fsdp": index}

    def send(one, hop, arriving=False):
        source = lax.rem(position + 4 - hop, 4) if arriving else position
        return remote(
            grad_states.at[one],
            grads_ref.at[source, one],
            sems.at[0, one, hop],
            sems.at[1, one, hop],
            device(hop),
        )

    def keep(one):
        return pltpu.make_async_copy(
            grad_states.at[one], grads_ref.at[position, one], sems.at[0, one, 0]
        )

    @pl.when(head == 0)
    def _():
        barrier = pltpu.get_barrier_semaphore()
        for hop in range(1, 4):
            pl.semaphore_signal(barrier, inc=1, device_id=device(hop), device_id_type=MESH)
        grad_gain_ref[...] = jnp.zeros_like(grad_gain_ref)
        pl.semaphore_wait(barrier, 3)

    output = out_ref[...] + nn(carry_ref[...], state_ref[0].astype(bf16))
    gain = gain_ref[...].astype(f32)
    grad = grad_ref[...].astype(f32)
    scaling = lax.rsqrt(jnp.mean(output * output, axis=1, keepdims=True) + epsilon)
    unit_rows = output * scaling
    grad_gain_ref[...] += jnp.sum(grad * unit_rows, axis=0, keepdims=True)
    scaled = grad * gain
    grad_out = scaling * (scaled - unit_rows * jnp.mean(scaled * unit_rows, axis=1, keepdims=True))
    low_grad = grad_out.astype(bf16)
    grad_states[head] = tn(carry_ref[...], low_grad).astype(bf16)
    for hop in range(1, 4):
        send(head, hop).start()
    keep(head).start()
    grad_out_ref[...] = (grad_out * output.shape[1] ** (-0.5)).astype(bf16)

    @pl.when(head == heads - 1)
    def _():
        def one(step):
            keep(step).wait()
            for hop in range(1, 4):
                send(step, hop).wait_send()
                send(step, hop, True).wait_recv()

        steps(0, heads, one)


def unmix(outputs, carries, states, gain, grad_heads):
    rows, width = outputs.shape
    heads, size, _ = states.shape
    plain = pl.BlockSpec((rows, size), lambda h: (0, h))
    state = pl.BlockSpec((1, size, size), lambda h: (h, 0, 0))
    vector = pl.BlockSpec((1, size), lambda h: (0, 0))
    return pl.pallas_call(
        functools.partial(unmix_kernel, heads),
        grid=(heads,),
        in_specs=[plain, plain, state, vector, plain],
        out_specs=[plain, vector, pl.BlockSpec(memory_space=pl.ANY)],
        out_shape=[
            jax.ShapeDtypeStruct((rows, width), bf16),
            jax.ShapeDtypeStruct((1, size), f32),
            jax.ShapeDtypeStruct((4, heads, size, size), bf16),
        ],
        scratch_shapes=[
            pltpu.VMEM((heads, size, size), bf16),
            pltpu.SemaphoreType.DMA((2, heads, 4)),
        ],
        compiler_params=pltpu.CompilerParams(
            collective_id=1, has_side_effects=True, vmem_limit_bytes=32 * MIB
        ),
    )(outputs, carries, states, gain, grad_heads)


TILE = 256
SLOTS = 3
DENSE_STRIDE = 4


def dense_kernel(count, shapes, *refs):
    (
        mixed_ref,
        w_out_ref,
        gain_ref,
        cotangent_ref,
        gate_ref,
        up_ref,
        down_ref,
        tokens_ref,
        layer_out_ref,
        grad_gain_ref,
        grad_out_ref,
        grad_attended_ref,
        grad_heads_ref,
        rest_ref,
        sums_ref,
        attended,
        normed,
        normed_t,
        cotangent_t,
        result,
        grad_normed,
        source,
        plain_sem,
        rest_sem,
    ), refs = refs[:24], refs[24:]
    tile = pl.program_id(0)
    rows, width = attended.shape
    depth = width // count
    number = len(shapes)
    tiles = number + rest_ref.shape[3] // (3 * TILE)
    blocks = [slice(first, first + CHUNK) for first in range(0, rows, CHUNK)]
    columns = [slice(first, first + CHUNK) for first in range(0, width, CHUNK)]
    gain = gain_ref[...].astype(f32)

    due, later, reduce = {}, [], None
    if number > 0:
        buffers = [refs[i * number : (i + 1) * number] for i in range(Reduce.BUFFERS)]
        sems = refs[Reduce.BUFFERS * number :]
        sources = [source.at[p % SLOTS] for p in range(number)]
        targets = [sums_ref.at[:, pl.ds(p * 3 * TILE, 3 * TILE)] for p in range(number)]
        reduce = Reduce(count, shapes, sources, targets, buffers, None, sems)
        begin = [2 * p + 3 for p in range(number)]
        due, later = reduce.plan(begin, DENSE_STRIDE, 2 * tiles - 1, [False] * number)

    def spot(which):
        for step in range(tiles):
            actions = due.get(2 * step + which, ())
            if actions:

                @pl.when(tile == step)
                def _():
                    for action in actions:
                        action()

    def rest(step):
        slot = lax.rem(step, SLOTS)
        first = pl.multiple_of((step - number) * 3 * TILE, 128)
        return pltpu.make_async_copy(
            source.at[slot], rest_ref.at[:, :, :, pl.ds(first, 3 * TILE)], rest_sem.at[slot]
        )

    def fetch(start, target, slot):
        return pltpu.make_async_copy(start, target, plain_sem.at[slot])

    @pl.when(tile == 0)
    def _():
        load = fetch(tokens_ref, normed, 0)
        load.start()
        if reduce is not None:
            reduce.place.greet_all()
        load.wait()
        for block in blocks:
            values = normed[block, :].astype(f32) + nn(mixed_ref[block, :], w_out_ref[...])
            attended[block, :] = values
            result[block, :] = values
            low = rms_scale(values, gain).astype(bf16)
            normed[block, :] = low
            normed_t[:, block] = low.T
            cotangent_t[:, block] = cotangent_ref[block, :].T
        grad_normed[...] = jnp.zeros_like(grad_normed)

    @pl.when(tile >= number + SLOTS)
    def _():
        rest(tile - SLOTS).wait()

    spot(0)
    gate = nn(normed[...], gate_ref[...])
    up = nn(normed[...], up_ref[...])
    grad_hidden = nn(cotangent_ref[...], down_ref[...])
    sig = sigmoid(gate)
    activated = gate * sig
    hidden = (activated * up).astype(bf16)
    grad_gate = (grad_hidden * up * sig * (1.0 + gate * (1.0 - sig))).astype(bf16)
    grad_up = (grad_hidden * activated).astype(bf16)
    slot = lax.rem(tile, SLOTS)
    for which, (left, right) in enumerate(
        ((normed_t, grad_gate), (normed_t, grad_up), (cotangent_t, hidden))
    ):
        piece = nn(left[...], right).astype(bf16).reshape(count // 2, 2, depth, TILE)
        source[slot, :, :, :, pl.ds(which * TILE, TILE)] = piece

    spot(1)
    for column in columns:
        result[:, column] += nt(hidden, down_ref[column, :])
        grad_normed[:, column] += nt(grad_gate, gate_ref[column, :]) + nt(
            grad_up, up_ref[column, :]
        )

    for p in range(number):

        @pl.when(tile == p)
        def _():
            reduce.start(p, False)

    @pl.when(tile >= number)
    def _():
        rest(tile).start()

    @pl.when(tile == tiles - 1)
    def _():
        gain_grad = jnp.zeros((1, width), f32)
        for block in blocks:
            layer_out_ref[block, :] = result[block, :].astype(bf16)
            values = attended[block, :]
            grad = grad_normed[block, :]
            scaling = lax.rsqrt(jnp.mean(values * values, axis=1, keepdims=True) + epsilon)
            unit = values * scaling
            gain_grad = gain_grad + jnp.sum(grad * unit, axis=0, keepdims=True)
            scaled = grad * gain
            grad = cotangent_ref[block, :].astype(f32) + scaling * (
                scaled - unit * jnp.mean(scaled * unit, axis=1, keepdims=True)
            )
            attended[block, :] = grad
            low = grad.astype(bf16)
            normed[block, :] = low
            normed_t[:, block] = mixed_ref[block, :].T
        fetch(attended, grad_attended_ref, 0).start()
        grad_gain_ref[...] = gain_grad
        for block in blocks:
            cotangent_t[block, :] = nt(normed[block, :], w_out_ref[...]).astype(bf16)
        fetch(cotangent_t, grad_heads_ref, 1).start()
        for action in later[: len(later) // 2]:
            action()
        for column in columns:
            grad_out_ref[column, :] = nn(normed_t[column, :], normed[...]).astype(bf16)
        for action in later[len(later) // 2 :]:
            action()
        for p in range(number):
            reduce.finish(p)
        for step in range(max(number, tiles - SLOTS), tiles):
            rest(step).wait()
        fetch(attended, grad_attended_ref, 0).wait()
        fetch(cotangent_t, grad_heads_ref, 1).wait()


def dense(mixed, tokens, w_out, gain, cotangent, w_gate, w_up, w_down_t, number):
    count = lax.axis_size("fsdp")
    rows, width = tokens.shape
    hidden = w_gate.shape[1]
    tiles = hidden // TILE
    depth = width // count
    shapes = [(depth, 3 * TILE, 2 if p % 2 == 0 else 4) for p in range(number)]
    whole = pl.BlockSpec((rows, width), lambda j: (0, 0))
    square = pl.BlockSpec((width, width), lambda j: (0, 0))
    vector = pl.BlockSpec((1, width), lambda j: (0, 0))
    slab = pl.BlockSpec((width, TILE), lambda j: (0, j))
    anywhere = pl.BlockSpec(memory_space=pl.ANY)
    shape = jax.ShapeDtypeStruct
    more = dict(collective_id=3, has_side_effects=True) if number > 0 else {}
    extra = []
    if number > 0:
        extra = Reduce.buffers(count, shapes) + Reduce.semaphores(count, number)
    return pl.pallas_call(
        functools.partial(dense_kernel, count, shapes),
        grid=(tiles,),
        in_specs=[whole, square, vector, whole, slab, slab, slab, anywhere],
        out_specs=[whole, vector, square] + [anywhere] * 4,
        out_shape=[
            shape((rows, width), bf16),
            shape((1, width), f32),
            shape((width, width), bf16),
            shape((rows, width), f32),
            shape((rows, width), bf16),
            shape((count // 2, 2, depth, (tiles - number) * 3 * TILE), bf16),
            shape((depth, max(number, 1) * 3 * TILE), bf16),
        ],
        scratch_shapes=[
            pltpu.VMEM((rows, width), f32),
            pltpu.VMEM((rows, width), bf16),
            pltpu.VMEM((width, rows), bf16),
            pltpu.VMEM((width, rows), bf16),
            pltpu.VMEM((rows, width), f32),
            pltpu.VMEM((rows, width), f32),
            pltpu.VMEM((SLOTS, count // 2, 2, depth, 3 * TILE), bf16),
            pltpu.SemaphoreType.DMA((2,)),
            pltpu.SemaphoreType.DMA((SLOTS,)),
        ]
        + extra,
        compiler_params=pltpu.CompilerParams(vmem_limit_bytes=63 * MIB, **more),
    )(mixed, w_out, gain, cotangent, w_gate, w_up, w_down_t, tokens)


STRIDE = 4


def backward_kernel(
    count, arrays, shapes, loaded_number, heads, tap_width, gain_width, *refs
):
    (
        signals_ref,
        logit_ref,
        taps_ref,
        grad_ref,
        fresh_ref,
        inverse_ref,
        starts_ref,
        state_ref,
        finals_ref,
        grads_ref,
        weights_ref,
        rates_weight_ref,
        gain_ref,
        grad_mlp_ref,
        grad_gain_ref,
        normed_ref,
        tokens_ref,
    ), refs = refs[:17], refs[17:]
    full, refs = refs[:arrays], refs[arrays:]
    grad_tokens_ref, refs = refs[0], refs[1:]
    outs, refs = refs[: arrays + 3], refs[arrays + 3 :]
    (
        normed_t,
        tokens,
        total,
        grad_signals,
        tails,
        firsts,
        edges,
        wides,
        pres,
        grads,
        padded,
        grad_logits,
        small_rows,
        small_source,
        beta_source,
        mixed_source,
        staging,
        plain_sem,
        edge_sem,
    ), refs = refs[:19], refs[19:]
    number = len(shapes)
    buffers = [refs[i * number : (i + 1) * number] for i in range(Reduce.BUFFERS)]
    sems = refs[Reduce.BUFFERS * number :]

    head = pl.program_id(0)
    rows, size = grad_ref.shape
    width = total.shape[1]
    chunks = rows // CHUNK
    row, col = grid_indices()
    lower, upper = row >= col, row <= col

    sources, targets = [], []
    for a in range(arrays):
        halves = max(full[a].shape[3] // (3 * TILE), 1)
        half = full[a].shape[3] // halves
        for part in range(halves):
            columns = pl.ds(part * half, half)
            sources.append(full[a].at[:, :, :, columns])
            targets.append(outs[a].at[:, columns])
    slots = mixed_source.shape[0]
    for one in range(heads):
        sources.append(mixed_source.at[one % slots])
        targets.append(outs[arrays].at[:, pl.ds(one * 3 * size, 3 * size)])
    sources += [beta_source, small_source]
    targets += [outs[arrays + 1], outs[arrays + 2]]
    reduce = Reduce(count, shapes, sources, targets, buffers, staging, sems)
    place = reduce.place
    position = place.position
    loaded = [p < loaded_number for p in range(number)]
    begin = [1 + 2 * (p // 2) for p in range(loaded_number)]
    begin += [2 * one + 5 for one in range(heads)] + [2 * heads + 5, 2 * heads + 6]
    due, later = reduce.plan(begin, STRIDE, 2 * heads, loaded)

    def spot(which):
        for step in range(heads + 1):
            actions = due.get(2 * step + which, ())
            if actions:

                @pl.when(head == step)
                def _():
                    for action in actions:
                        action()

    def fetch(source, target, slot):
        return pltpu.make_async_copy(source, target, plain_sem.at[slot])

    def edge(one, slot, arriving=False):
        return remote(
            firsts.at[slot],
            edges.at[one],
            edge_sem.at[0, one],
            edge_sem.at[1, one],
            reduce.device(3),
        )

    @pl.when(head == 0)
    def _():
        fetch(normed_ref, normed_t, 0).start()
        fetch(tokens_ref, tokens, 1).start()
        place.greet_all()
        for p in range(min(2, loaded_number)):
            reduce.start(p, True)
        total[...] = jnp.zeros_like(total)
        padded[...] = jnp.zeros_like(padded)
        grad_logits[...] = jnp.zeros_like(grad_logits)
        small_rows[...] = jnp.zeros_like(small_rows)
        fetch(normed_ref, normed_t, 0).wait()
        fetch(tokens_ref, tokens, 1).wait()

    spot(0)

    @pl.when(head < heads)
    def _():
        slot = lax.rem(head, 2)
        lows, scales = [], []
        for which in range(3):
            wides[which] = signals_ref[:, pl.ds(which * size, size)].astype(f32)
            pre = conv_pre(wides.at[which], taps_ref[0, which], rows)
            pres[which] = pre
            act = pre * sigmoid(pre)
            if which < 2:
                scale = lax.rsqrt(jnp.sum(act * act, axis=1, keepdims=True) + epsilon)
                act = act * scale
                scales.append(scale)
            lows.append(act.astype(bf16))
        queries, keys, values = lows
        rates = sigmoid(head_column(logit_ref[...].astype(f32), head))

        state = state_ref[0].astype(bf16)
        first = fresh_ref[:, pl.ds(0, size)].astype(f32)
        fresh_all = (first + nn(fresh_ref[:, pl.ds(size, size)], state)).astype(bf16)

        grad_memory = jnp.zeros((size, size), f32)
        for index in reversed(range(1, 4)):
            later = grads_ref[index, 0].astype(f32) + lax.dot_general(
                finals_ref[index, 0, :, pl.ds(size, size)].astype(f32),
                grad_memory,
                (((0,), (0,)), ((), ())),
                precision=highest,
                preferred_element_type=f32,
            )
            grad_memory = jnp.where(index > position, later, grad_memory)
        grad_rates = [None] * chunks
        for chunk in reversed(range(chunks)):
            part = slice(chunk * CHUNK, (chunk + 1) * CHUNK)
            key, query, value, rate = keys[part], queries[part], values[part], rates[part]
            grad_out = grad_ref[part, :]
            fresh = fresh_all[part]
            start = starts_ref[0, chunk]
            memory = (start[:, :size].astype(f32) + nn(start[:, size:], state)).astype(bf16)
            low_grad = grad_memory.astype(bf16)
            key_f = key.astype(f32)
            rated = (rate * key_f).astype(bf16)

            scores_t = jnp.where(upper, nt(key, query), 0.0).astype(bf16)
            grad_fresh = (nn(scores_t, grad_out) + nn(key, low_grad)).astype(bf16)
            aim = tn(inverse_ref[part, :], grad_fresh)
            low_aim = aim.astype(bf16)
            grad_memory = grad_memory + tn(query, grad_out) - tn(rated, low_aim)

            grad_scores = jnp.where(lower, nt(grad_out, fresh), 0.0).astype(bf16)
            grad_scores_t = jnp.where(upper, nt(fresh, grad_out), 0.0).astype(bf16)
            grad_strict = jnp.where(row > col, nt(low_aim, fresh), 0.0).astype(bf16)
            grad_strict_t = jnp.where(row < col, nt(fresh, low_aim), 0.0).astype(bf16)

            grad_query = nt(grad_out, memory) + nn(grad_scores, key)
            within = -(nn(grad_strict, key) + nt(low_aim, memory))
            grad_rates[chunk] = jnp.sum(
                key_f * within + value.astype(f32) * aim, axis=1, keepdims=True
            )
            grad_key = (
                rate * within
                - nn(grad_strict_t, rated)
                + nn(grad_scores_t, query)
                + nt(fresh, low_grad)
            )
            grads[0, part, :] = grad_query
            grads[1, part, :] = grad_key
            grads[2, part, :] = rate * aim
            if chunk == chunks // 2:
                spot(1)

        lane = lax.broadcasted_iota(jnp.int32, grad_logits.shape, 1)
        grad_rate = jnp.concatenate(grad_rates, axis=0)
        grad_logit = grad_rate * rates * (1.0 - rates)
        grad_logits[...] = jnp.where(lane == head, grad_logit, grad_logits[...])

        @pl.when((head >= 2) & (position > 0))
        def _():
            edge(head - 2, slot).wait_send()

        for which in range(3):
            taps = taps_ref[0, which]
            pre = pres[which]
            sig = sigmoid(pre)
            grad_act = grads[which]
            if which < 2:
                unit = pre * sig * scales[which]
                grad_act = scales[which] * (
                    grad_act - unit * jnp.sum(grad_act * unit, axis=1, keepdims=True)
                )
            grad_pre = grad_act * sig * (1.0 + pre * (1.0 - sig))
            padded[pl.ds(HALO, rows), :] = grad_pre
            sums = []
            for offset in range(TAPS):
                shifted = wides[which, pl.ds(HALO - TAPS + 1 + offset, rows), :]
                sums.append(jnp.sum(grad_pre * shifted, axis=0, keepdims=True))
            where = pl.multiple_of((which * heads + head) * size, 128)
            small_rows[4:8, pl.ds(where, size)] = jnp.concatenate(sums, axis=0)

            def back(start, amount):
                result = None
                for offset in range(TAPS):
                    term = (
                        taps[offset : offset + 1, :]
                        * padded[pl.ds(start + TAPS - 1 - offset, amount), :]
                    )
                    result = term if result is None else result + term
                return result

            columns = pl.ds(which * size, size)
            grad_signal = back(HALO, rows)
            grad_signals[slot, :, columns] = grad_signal.astype(bf16)
            tails[slot, :, columns] = grad_signal[rows - HALO :]
            firsts[slot, :, columns] = back(0, HALO)

        @pl.when(position > 0)
        def _():
            edge(head, slot).start()

    for one in range(heads):

        @pl.when(head == one + 1)
        def _():
            slot = one % 2

            @pl.when(position < 3)
            def _():
                edge(one, slot).wait_recv()
                tails[slot] = tails[slot] + edges[one]

            grad_signals[slot, pl.ds(rows - HALO, HALO), :] = tails[slot].astype(bf16)
            grad = grad_signals[slot]
            source = mixed_source.at[one % slots]
            depth = width // count
            half = count // 4
            for part in range(2):
                piece = nn(normed_t[pl.ds(part * 2 * half * depth, 2 * half * depth), :], grad)
                source[pl.ds(part * half, half)] = piece.astype(bf16).reshape(
                    half, 2, depth, 3 * size
                )
            reduce.start(loaded_number + one, False)
            weights = weights_ref[...]
            for part in range(0, rows, CHUNK):
                block = pl.ds(part, CHUNK)
                total[block, :] += nt(grad[part : part + CHUNK], weights)

    @pl.when(head == heads)
    def _():
        depth = width // count
        low_logits = grad_logits[...].astype(bf16)
        beta_source[...] = (
            nn(normed_t[...], low_logits).astype(bf16).reshape(beta_source.shape)
        )
        reduce.start(number - 2, False)
        gain = gain_ref[...].astype(f32)
        weights = rates_weight_ref[...]
        gain_grad = jnp.zeros((1, width), f32)
        for part in range(0, rows, CHUNK):
            block = pl.ds(part, CHUNK)
            grad = total[block, :] + nt(low_logits[part : part + CHUNK], weights)
            values = tokens[block, :].astype(f32)
            scaling = lax.rsqrt(jnp.mean(values * values, axis=1, keepdims=True) + epsilon)
            unit = values * scaling
            gain_grad = gain_grad + jnp.sum(grad * unit, axis=0, keepdims=True)
            scaled = grad * gain
            total[block, :] = scaling * (
                scaled - unit * jnp.mean(scaled * unit, axis=1, keepdims=True)
            )
        fetch(total, grad_tokens_ref, 0).start()
        small_rows[0:1, pl.ds(0, width)] = gain_grad
        small_rows[1:2, pl.ds(0, width)] = grad_mlp_ref[...]
        small_rows[2:3, pl.ds(0, size)] = grad_gain_ref[...]
        small = small_rows[...]
        gains = gather_rows(small[:, :width], count, gain_width)
        last = gather_rows(small[:, :size], count, size // count)
        taps = gather_rows(small, count, tap_width)
        which = lax.broadcasted_iota(jnp.int32, gains.shape, 1)
        small = jnp.where(which == 2, last, jnp.where(which < 2, gains, taps))
        small_source[...] = small.astype(bf16).reshape(small_source.shape)
        reduce.start(number - 1, False)
        for action in later:
            action()
        for p in range(number):
            reduce.finish(p)
        fetch(total, grad_tokens_ref, 0).wait()
        for one in range(heads - 2, heads):

            @pl.when(position > 0)
            def _():
                edge(one, one % 2).wait_send()


def gather_rows(wide, count, width):
    total = count * width
    rows = wide.shape[0]
    if width % 128 == 0:
        blank = jnp.zeros((rows, PACK[1] - width), f32)
        return jnp.stack(
            [
                jnp.concatenate([wide[:, s * width : (s + 1) * width], blank], axis=1)
                for s in range(count)
            ]
        )
    row = lax.broadcasted_iota(jnp.int32, (count * rows, rows), 0)
    col = lax.broadcasted_iota(jnp.int32, (count * rows, rows), 1)
    spread = jnp.where(lax.rem(row, rows) == col, 1.0, 0.0).astype(bf16)
    tall = nn(spread, wide[:, :total].astype(bf16))
    row = lax.broadcasted_iota(jnp.int32, tall.shape, 0)
    col = lax.broadcasted_iota(jnp.int32, tall.shape, 1)
    tall = jnp.where(lax.div(row, rows) == lax.div(col, width), tall, 0.0).astype(bf16)
    row = lax.broadcasted_iota(jnp.int32, (total, PACK[1]), 0)
    col = lax.broadcasted_iota(jnp.int32, (total, PACK[1]), 1)
    pick = jnp.where(lax.rem(row, width) == col, 1.0, 0.0).astype(bf16)
    return nn(tall, pick).reshape(count, rows, PACK[1])


def backward(
    signals,
    logits,
    taps,
    grad_out,
    fresh,
    inverses,
    starts,
    state,
    finals,
    grad_starts,
    w_mixed,
    w_rates,
    gain,
    grad_mlp,
    grad_gain,
    normed_t,
    tokens,
    full,
    tap_width,
    gain_width,
):
    count = lax.axis_size("fsdp")
    wide_rows = signals.shape[0]
    rows, width = grad_out.shape
    heads, _, _, size = taps.shape
    chunks = rows // CHUNK
    depth = width // count
    views = full

    def portions(depth, wanted):
        while depth % (16 * wanted) != 0:
            wanted //= 2
        return wanted

    shapes = []
    for a, view in enumerate(views):
        halves = max(view.shape[3] // (3 * TILE), 1)
        for part in range(halves):
            shapes.append((depth, view.shape[3] // halves, 4 if (a + part) % 2 else 2))
    loaded = len(shapes)
    for head in range(heads):
        shapes.append((depth, 3 * size, portions(depth, 4 if head % 2 == 0 else 2)))
    shapes.append((depth, logits.shape[1], portions(depth, 2)))
    shapes.append(PACK + (1,))
    staged = max([d // 2 for d, _, _ in shapes[:loaded]] + [16])
    widest = max([w for _, w, _ in shapes[:loaded]] + [128])

    def now(h):
        return jnp.minimum(h, heads - 1)

    def before(h):
        return jnp.maximum(h - 1, 0)

    whole = pl.BlockSpec(logits.shape, lambda h: (0, 0))
    vector = pl.BlockSpec((1, width), lambda h: (0, 0))
    anywhere = pl.BlockSpec(memory_space=pl.ANY)
    shape = jax.ShapeDtypeStruct
    return pl.pallas_call(
        functools.partial(
            backward_kernel, count, len(views), shapes, loaded, heads, tap_width, gain_width
        ),
        grid=(heads + 1,),
        in_specs=[
            pl.BlockSpec((wide_rows, 3 * size), lambda h: (0, now(h))),
            whole,
            pl.BlockSpec((1, 3, TAPS, size), lambda h: (now(h), 0, 0, 0)),
            pl.BlockSpec((rows, size), lambda h: (0, now(h))),
            pl.BlockSpec((rows, 2 * size), lambda h: (0, now(h))),
            pl.BlockSpec((rows, CHUNK), lambda h: (0, now(h))),
            pl.BlockSpec((1, chunks, size, 2 * size), lambda h: (now(h), 0, 0, 0)),
            pl.BlockSpec((1, size, size), lambda h: (now(h), 0, 0)),
            pl.BlockSpec((4, 1, size, 2 * size), lambda h: (0, now(h), 0, 0)),
            pl.BlockSpec((4, 1, size, size), lambda h: (0, now(h), 0, 0)),
            pl.BlockSpec((width, 3 * size), lambda h: (0, before(h))),
            pl.BlockSpec(w_rates.shape, lambda h: (0, 0)),
            vector,
            vector,
            pl.BlockSpec((1, size), lambda h: (0, 0)),
        ]
        + [anywhere] * (2 + len(views)),
        out_specs=[anywhere] * (4 + len(views)),
        out_shape=[shape((rows, width), f32)]
        + [shape(view.shape[2:], bf16) for view in views]
        + [
            shape((depth, 3 * width), bf16),
            shape((depth, logits.shape[1]), bf16),
            shape(PACK, bf16),
        ],
        scratch_shapes=[
            pltpu.VMEM((width, rows), bf16),
            pltpu.VMEM((rows, width), bf16),
            pltpu.VMEM((rows, width), f32),
            pltpu.VMEM((2, rows, 3 * size), bf16),
            pltpu.VMEM((2, HALO, 3 * size), f32),
            pltpu.VMEM((2, HALO, 3 * size), f32),
            pltpu.VMEM((heads, HALO, 3 * size), f32),
            pltpu.VMEM((3, wide_rows, size), f32),
            pltpu.VMEM((3, rows, size), f32),
            pltpu.VMEM((3, rows, size), f32),
            pltpu.VMEM((rows + 2 * HALO, size), f32),
            pltpu.VMEM(logits.shape, f32),
            pltpu.VMEM((PACK[0], 3 * width), f32),
            pltpu.VMEM((count // 2, 2) + PACK, bf16),
            pltpu.VMEM((count // 2, 2, depth, logits.shape[1]), bf16),
            pltpu.VMEM((SLOTS, count // 2, 2, depth, 3 * size), bf16),
            pltpu.VMEM((2, count // 2, 2, staged, widest), bf16),
            pltpu.SemaphoreType.DMA((2,)),
            pltpu.SemaphoreType.DMA((2, heads)),
        ]
        + Reduce.buffers(count, shapes)
        + Reduce.semaphores(count, len(shapes)),
        compiler_params=pltpu.CompilerParams(
            collective_id=2, has_side_effects=True, vmem_limit_bytes=63 * MIB
        ),
    )(
        signals,
        logits,
        taps,
        grad_out,
        fresh,
        inverses,
        starts,
        state,
        finals,
        grad_starts,
        w_mixed,
        w_rates,
        gain,
        grad_mlp,
        grad_gain,
        normed_t,
        tokens,
        *views,
    )


def local(
    inputs,
    g_attn,
    w_query,
    w_key,
    w_value,
    w_beta,
    conv_taps,
    o_gain,
    w_out,
    g_mlp,
    w_gate,
    w_up,
    w_down,
    cotangent,
):
    count = lax.axis_size("fsdp")
    position = lax.axis_index("seq")
    groups = lax.axis_size("seq")
    tokens_low = inputs[0]
    rows, width = tokens_low.shape
    heads = w_beta.shape[1]
    size = width // heads
    depth = w_query.shape[0]
    small = (g_attn.shape, g_mlp.shape, o_gain.shape, conv_taps.shape)
    packed = pack_small((g_attn[None], g_mlp[None], o_gain[None]), conv_taps[None])
    mixed = jnp.concatenate(
        [
            w[:, head * size : (head + 1) * size]
            for head in range(heads)
            for w in (w_query, w_key, w_value)
        ],
        axis=1,
    )
    shards = (
        packed,
        jnp.pad(w_beta, ((0, 0), (0, 128 - heads))),
        mixed,
        w_out,
        w_gate,
        w_up,
        jnp.transpose(w_down),
    )
    results = forward(tokens_low, shards, heads, conv_taps.shape[1])
    packed, w_beta, w_mixed, w_out, w_gate, w_up, w_down_t = results[:ARRAYS]
    finals, _, normed_t, signals, logits, taps = results[ARRAYS : ARRAYS + 6]
    outputs, carries, fresh, inverses, starts = results[ARRAYS + 6 :]
    g_attn, g_mlp, o_gain, _ = unpack_small(packed, small)
    g_attn, g_mlp, o_gain = g_attn.reshape(-1), g_mlp.reshape(-1), o_gain.reshape(-1)

    gain_out = o_gain.reshape(1, size)
    head_rows, state_in = mix(position.reshape(1), outputs, carries, finals, gain_out)
    tiles = w_gate.shape[1] // TILE
    beside = depth % 64 == 0
    number = tiles - 2 if beside else 0
    layer_out, grad_gain_mlp, grad_out_matrix, grad_attended, grad_heads, rest, sums = dense(
        head_rows,
        tokens_low,
        w_out,
        g_mlp.reshape(1, -1),
        cotangent[0],
        w_gate,
        w_up,
        w_down_t,
        number,
    )
    grad_delta, grad_gain_out, grad_starts = unmix(
        outputs, carries, state_in, gain_out, grad_heads
    )
    full = (rest, grad_out_matrix.reshape(count // 2, 2, depth, width))
    results = backward(
        signals,
        logits,
        taps,
        grad_delta,
        fresh,
        inverses,
        starts,
        state_in,
        finals,
        grad_starts,
        w_mixed,
        w_beta,
        g_attn.reshape(1, -1),
        grad_gain_mlp,
        grad_gain_out,
        normed_t,
        tokens_low,
        full if beside else (),
        small[3][1],
        small[0][0],
    )
    grad_from_attn, full_sums = results[0], results[1:-3]
    grad_mixed_matrix, grad_beta_matrix, packed = results[-3:]
    if beside:
        sums = [sums, full_sums[0]]
        grad_out_matrix = full_sums[1]
    else:
        sums, grad_out_matrix = (
            lax.psum(
                lax.psum_scatter(g.reshape((count,) + g.shape[2:]), "fsdp", scatter_dimension=0),
                "seq",
            )
            for g in full
        )
        sums = [sums]

    def columns(arrays, which, wide):
        return jnp.concatenate(
            [
                array[:, first + which * wide : first + (which + 1) * wide].astype(f32)
                for array in arrays
                for first in range(0, array.shape[1], 3 * wide)
            ],
            axis=1,
        )

    grad_gate_matrix, grad_up_matrix, grad_down_t = (
        columns(sums, which, TILE) for which in range(3)
    )
    grad_inputs = (grad_attended + grad_from_attn)[None]
    parts = [part[0].astype(f32) for part in unpack_small(packed, small)]
    grad_gain_attn, grad_gain_mlp, grad_gain_out, grad_taps = parts
    grad_query_matrix, grad_key_matrix, grad_value_matrix = (
        columns([grad_mixed_matrix], which, size) for which in range(3)
    )
    return (
        layer_out[None],
        grad_inputs,
        grad_gain_attn,
        grad_query_matrix,
        grad_key_matrix,
        grad_value_matrix,
        grad_beta_matrix[:, :heads].astype(f32),
        grad_taps,
        grad_gain_out,
        grad_out_matrix.astype(f32),
        grad_gain_mlp,
        grad_gate_matrix,
        grad_up_matrix,
        jnp.transpose(grad_down_t),
    )


def solution(mesh):
    vector = P("fsdp")
    rows = P("fsdp", None)
    columns = P(None, "fsdp")
    tokens = P("fsdp", "seq", None)
    return jax.shard_map(
        local,
        mesh=mesh,
        in_specs=(
            tokens,
            vector,
            rows,
            rows,
            rows,
            rows,
            columns,
            vector,
            rows,
            vector,
            rows,
            rows,
            columns,
            tokens,
        ),
        out_specs=(
            tokens,
            tokens,
            vector,
            rows,
            rows,
            rows,
            rows,
            columns,
            vector,
            rows,
            vector,
            rows,
            rows,
            columns,
        ),
        check_vma=False,
    )
```

```python
import functools

import jax
import jax.numpy as jnp
from jax import lax
from jax.experimental import pallas as pl
from jax.experimental.pallas import tpu as pltpu
from jax.sharding import PartitionSpec as P

CHUNK = 256
HALO = 16
TAPS = 4
MIB = 1024 * 1024

highest = lax.Precision.HIGHEST
epsilon = 1e-06
f32 = jnp.float32
bf16 = jnp.bfloat16


def nn(left_side, right_side):
    return lax.dot_general(
        left_side, right_side, (((1,), (0,)), ((), ())), preferred_element_type=f32
    )


def nt(left_side, right_side):
    return lax.dot_general(
        left_side, right_side, (((1,), (1,)), ((), ())), preferred_element_type=f32
    )


def tn(left_side, right_side):
    return lax.dot_general(
        left_side, right_side, (((0,), (0,)), ((), ())), preferred_element_type=f32
    )


def rms_scale(values, gain_vec):
    return (
        values * lax.rsqrt(jnp.mean(values * values, axis=-1, keepdims=True) + epsilon) * gain_vec
    )


def norm_backward(values, gain_vec, grad_out):
    scaling = lax.rsqrt(jnp.mean(values * values, axis=-1, keepdims=True) + epsilon)
    unit_rows = values * scaling
    gain_grad = jnp.sum(grad_out * unit_rows, axis=0)
    scaled_grad = grad_out * gain_vec
    input_grad = scaling * (
        scaled_grad - unit_rows * jnp.mean(scaled_grad * unit_rows, axis=-1, keepdims=True)
    )
    return (input_grad, gain_grad)


MESH = pl.DeviceIdType.MESH


class Place:
    def __init__(self, count):
        self.count = count
        self.sides = 2 if count % 2 == 0 else 1
        self.length = count // self.sides
        self.position = lax.axis_index("seq")
        self.index = lax.axis_index("fsdp")
        self.core = lax.rem(self.position, 2)
        self.chip = lax.div(self.position, 2)
        self.side = lax.rem(self.index, self.sides)
        self.spot = lax.div(self.index, self.sides)

    def sibling(self):
        return {"seq": self.position + 1 - 2 * self.core, "fsdp": self.index}

    def across(self):
        return {"seq": lax.rem(self.position + 2, 4), "fsdp": self.index}

    def partner(self):
        return {"seq": self.position, "fsdp": self.spot * 2 + 1 - self.side}

    def ahead(self, step):
        spot = lax.rem(self.spot + step, self.length)
        return {"seq": self.position, "fsdp": spot * self.sides + self.side}

    def shard(self, spot, side):
        return spot * self.sides + side

    def behind(self, step):
        return lax.rem(self.spot + self.length - step, self.length)

    def greet_all(self):
        self.greet(False, True)

    def greet(self, across, sequence=False):
        barrier = pltpu.get_barrier_semaphore()
        total = self.length - 1

        def signal(device):
            pl.semaphore_signal(barrier, inc=1, device_id=device, device_id_type=MESH)

        def one(step, carry):
            signal(self.ahead(step))
            return carry

        lax.fori_loop(1, self.length, one, 0)
        if sequence:
            for hop in range(1, 4):
                signal({"seq": lax.rem(self.position + hop, 4), "fsdp": self.index})
            total += 3
        else:
            signal(self.sibling())
            total += 1
        if self.sides == 2:
            signal(self.partner())
            total += 1
        if across:
            signal(self.across())
            total += 1
        pl.semaphore_wait(barrier, total)


def remote(source, target, send, recv, device):
    return pltpu.make_async_remote_copy(
        src_ref=source,
        dst_ref=target,
        send_sem=send,
        recv_sem=recv,
        device_id=device,
        device_id_type=MESH,
    )


def steps(first, last, body):
    def one(step, carry):
        body(step)
        return carry

    lax.fori_loop(first, last, one, 0)


class Reduce:
    BUFFERS = 6

    def __init__(self, count, pieces, sources, targets, buffers, staging, sems):
        self.place = Place(count)
        self.pieces, self.sources, self.targets, self.staging = pieces, sources, targets, staging
        self.acc, self.x_in, self.y_in, self.z_in, self.parts_in, self.result = buffers
        (
            self.core_sem,
            self.load_sem,
            self.x_sem,
            self.y_sem,
            self.z_sem,
            self.share_sem,
            self.final_sem,
            self.store_sem,
        ) = sems

    @staticmethod
    def buffers(count, pieces):
        length = count // 2
        acc, x_in, y_in, z_in, parts_in, result = [], [], [], [], [], []
        for depth, width, parts in pieces:
            rows = depth // parts
            acc.append(pltpu.VMEM((length, 2, depth // min(parts, 2), width), bf16))
            x_in.append(
                pltpu.VMEM((length, 2, rows, width) if parts == 4 else (1, 1, 16, 128), bf16)
            )
            y_in.append(pltpu.VMEM((length, rows, width), bf16))
            z_in.append(pltpu.VMEM((length, rows, width), bf16))
            parts_in.append(
                pltpu.VMEM((4 // parts, rows, width) if parts < 4 else (1, 16, 128), bf16)
            )
            result.append(pltpu.VMEM((rows, width), bf16))
        return acc + x_in + y_in + z_in + parts_in + result

    @staticmethod
    def semaphores(count, number):
        pair = pltpu.SemaphoreType.DMA((number, 2))
        one = pltpu.SemaphoreType.DMA((number,))
        hops = pltpu.SemaphoreType.DMA((number, 2, 4))
        return [pair, one, pair, pair, pair, hops, hops, one]

    def half(self, p, core):
        depth, _, parts = self.pieces[p]
        rows = depth // min(parts, 2)
        return pl.ds(pl.multiple_of(core * rows, 16) if parts > 1 else 0, rows)

    def quarter(self, p, chip):
        depth, _, parts = self.pieces[p]
        rows = depth // parts
        return pl.ds(pl.multiple_of(chip * rows, 16) if parts == 4 else 0, rows)

    def device(self, hop):
        return {"seq": lax.rem(self.place.position + hop, 4), "fsdp": self.place.index}

    def to_sibling(self, p):
        return remote(
            self.sources[p].at[:, :, self.half(p, 1 - self.place.core), :],
            self.acc[p],
            self.core_sem.at[p, 0],
            self.core_sem.at[p, 1],
            self.place.sibling(),
        )

    def stage(self, p):
        depth, width, parts = self.pieces[p]
        return self.staging.at[p % 2, :, :, pl.ds(0, depth // 2), pl.ds(0, width)]

    def load(self, p):
        return pltpu.make_async_copy(
            self.sources[p].at[:, :, self.half(p, self.place.core), :],
            self.stage(p),
            self.load_sem.at[p],
        )

    def to_x(self, p):
        return remote(
            self.acc[p].at[:, :, self.quarter(p, 1 - self.place.chip), :],
            self.x_in[p],
            self.x_sem.at[p, 0],
            self.x_sem.at[p, 1],
            self.place.across(),
        )

    def to_y(self, p):
        place = self.place
        return remote(
            self.acc[p].at[:, 1 - place.side, self.quarter(p, place.chip), :],
            self.y_in[p],
            self.y_sem.at[p, 0],
            self.y_sem.at[p, 1],
            place.partner(),
        )

    def to_z(self, p, step):
        place = self.place
        spot = lax.rem(place.spot + step, place.length)
        return remote(
            self.acc[p].at[spot, place.side, self.quarter(p, place.chip), :],
            self.z_in[p].at[step],
            self.z_sem.at[p, 0],
            self.z_sem.at[p, 1],
            place.ahead(step),
        )

    def all_z(self, p):
        both = self.z_in[p].at[pl.ds(1, self.place.length - 1)]
        return remote(
            both, both, self.z_sem.at[p, 0], self.z_sem.at[p, 1], self.place.ahead(1)
        )

    def sharers(self, p):
        return {1: (1, 2, 3), 2: (2,), 4: ()}[self.pieces[p][2]]

    def receivers(self, p):
        return {1: (), 2: (0,), 4: (1, 2, 3)}[self.pieces[p][2]]

    def sharer(self, p, position):
        return position if self.pieces[p][2] == 1 else lax.div(position, 2)

    def to_share(self, p, hop, arriving=False):
        position = self.place.position
        source = lax.rem(position + 4 - hop, 4) if arriving else position
        buffer = self.parts_in[p].at[self.sharer(p, source)]
        return remote(
            buffer,
            buffer,
            self.share_sem.at[p, 0, hop],
            self.share_sem.at[p, 1, hop],
            self.device(hop),
        )

    def target(self, p, position):
        depth, _, parts = self.pieces[p]
        rows = depth // parts
        core, chip = lax.rem(position, 2), lax.div(position, 2)
        first = {1: 0, 2: core * rows, 4: (core * 2 + chip) * rows}[parts]
        return self.targets[p].at[pl.ds(pl.multiple_of(first, 16) if parts > 1 else 0, rows), :]

    def to_result(self, p, hop, arriving=False):
        place = self.place
        if hop == 0:
            other = place.position + 1 - 2 * place.core
            device = place.sibling()
        else:
            other = lax.rem(place.position + 4 - hop, 4)
            device = self.device(hop)
        return remote(
            self.result[p],
            self.target(p, other if arriving else place.position),
            self.final_sem.at[p, 0, hop],
            self.final_sem.at[p, 1, hop],
            device,
        )

    def store(self, p):
        return pltpu.make_async_copy(
            self.result[p], self.target(p, self.place.position), self.store_sem.at[p]
        )

    def start(self, p, loaded):
        if self.pieces[p][2] > 1:
            self.to_sibling(p).start()
        if loaded:
            self.load(p).start()

    def on_core(self, p, loaded):
        parts = self.pieces[p][2]
        acc = self.acc[p]
        half = self.half(p, self.place.core)
        rows, width = acc.shape[2], acc.shape[3]
        if loaded:
            self.load(p).wait()
        if parts == 1:
            acc[...] = self.sources[p][...]
        else:
            self.to_sibling(p).wait_recv()

            def add(spot):
                if loaded:
                    own = self.staging[p % 2, spot, :, pl.ds(0, rows), pl.ds(0, width)]
                else:
                    own = self.sources[p][spot, :, half, :]
                acc[spot] = acc[spot] + own

            steps(0, self.place.length, add)
        (self.to_x if parts == 4 else self.to_y)(p).start()
        if parts > 1:
            self.to_sibling(p).wait_send()

    def on_x(self, p):
        acc, side = self.acc[p], 1 - self.place.side
        rows = self.quarter(p, self.place.chip)
        self.to_x(p).wait_recv()

        def add(spot):
            acc[spot, side, rows, :] = acc[spot, side, rows, :] + self.x_in[p][spot, side]

        steps(0, self.place.length, add)
        self.to_y(p).start()

    def on_y(self, p):
        place = self.place
        acc = self.acc[p]
        rows = self.quarter(p, place.chip)
        self.to_y(p).wait_recv()

        def one(step):
            spot = lax.rem(place.spot + step, place.length)
            total = acc[spot, place.side, rows, :].astype(f32) + self.y_in[p][spot].astype(f32)
            if self.pieces[p][2] == 4:
                total = total + self.x_in[p][spot, place.side].astype(f32)
            acc[spot, place.side, rows, :] = total.astype(bf16)

        def send(step):
            one(step)
            self.to_z(p, step).start()

        steps(1, place.length, send)
        one(0)

    def on_z(self, p):
        place = self.place
        rows = self.quarter(p, place.chip)
        self.all_z(p).wait_recv()
        total = self.acc[p][place.spot, place.side, rows, :].astype(f32)
        if place.length <= 8:
            for step in range(1, place.length):
                total = total + self.z_in[p][step].astype(f32)
        else:
            total = lax.fori_loop(
                1,
                place.length,
                lambda step, carry: carry + self.z_in[p][step].astype(f32),
                total,
            )
        if self.pieces[p][2] == 4:
            self.result[p][...] = total.astype(bf16)
            self.publish(p)
        else:
            self.parts_in[p][self.sharer(p, place.position)] = total.astype(bf16)
            for hop in self.sharers(p):
                self.to_share(p, hop).start()

    def on_share(self, p):
        total = None
        for hop in self.sharers(p):
            self.to_share(p, hop, True).wait_recv()
        for index in range(4 // self.pieces[p][2]):
            term = self.parts_in[p][index].astype(f32)
            total = term if total is None else total + term
        self.result[p][...] = total.astype(bf16)
        self.publish(p)

    def publish(self, p):
        for hop in self.receivers(p):
            self.to_result(p, hop).start()
        self.store(p).start()

    def finish(self, p):
        if self.pieces[p][2] == 4:
            self.to_x(p).wait_send()
        self.to_y(p).wait_send()
        self.all_z(p).wait_send()
        for hop in self.sharers(p):
            self.to_share(p, hop).wait_send()
        for hop in self.receivers(p):
            self.to_result(p, hop).wait_send()
            self.to_result(p, hop, True).wait_recv()
        self.store(p).wait()

    def plan(self, begin, stride, last, loaded, idle=()):
        due = []
        for p, (_, _, parts) in enumerate(self.pieces):
            for index, kind in enumerate((0, 1, 2, 3) if parts == 4 else (0, 2, 3, 4)):
                half = begin[p] + stride[p] * index
                while half in idle:
                    half += 1
                due.append((half, -index, p, kind))
        due.sort()

        def action(p, kind):
            if kind == 0:
                self.on_core(p, loaded[p])
                if loaded[p] and p + 2 < len(self.pieces) and loaded[p + 2]:
                    self.start(p + 2, True)
            else:
                (self.on_x, self.on_y, self.on_z, self.on_share)[kind - 1](p)

        def at(test):
            return [functools.partial(action, p, kind) for half, _, p, kind in due if test(half)]

        return (
            {half: at(lambda when: when == half) for half in range(last + 1)},
            at(lambda when: when > last),
        )


class Gather:
    SEMS = 6

    def __init__(self, count, pieces, shards, outs, sems):
        self.place = Place(count)
        self.pieces, self.shards, self.outs = pieces, shards, outs
        self.line_sem, self.side_sem, self.core_sem, self.across_sem, self.relay_sem, self.own = (
            sems
        )

    @staticmethod
    def scratch(pieces, count):
        length = count // 2 if count % 2 == 0 else count
        number = len(pieces)
        slots = 2 * length if max(piece[3] for piece in pieces) > 1 else 1
        return [
            pltpu.SemaphoreType.DMA((number, 2, length)),
            pltpu.SemaphoreType.DMA((number, 2, length)),
            pltpu.SemaphoreType.DMA((number, 2, slots)),
            pltpu.SemaphoreType.DMA((number, 2, slots)),
            pltpu.SemaphoreType.DMA((number, 2, slots)),
            pltpu.SemaphoreType.DMA((number,)),
        ]

    def portion(self, k, core, chip):
        parts = self.pieces[k][3]
        if parts == 1:
            return 0
        return core if parts == 2 else 2 * chip + core

    def region(self, k, shard, core, chip):
        a, offset, width, parts = self.pieces[k]
        depth = self.shards[a].shape[0]
        rows = depth // parts
        first = shard * depth + self.portion(k, core, chip) * rows
        return self.outs[a].at[pl.ds(pl.multiple_of(first, 16), rows), pl.ds(offset, width)]

    def source(self, k):
        p = self.place
        a, offset, width, parts = self.pieces[k]
        rows = self.shards[a].shape[0] // parts
        first = self.portion(k, p.core, p.chip) * rows
        return self.shards[a].at[pl.ds(pl.multiple_of(first, 16), rows), pl.ds(offset, width)]

    def line(self, k, step, arriving=False):
        p = self.place
        shard = p.shard(p.behind(step), p.side) if arriving else p.index
        target = self.region(k, shard, p.core, p.chip)
        return remote(
            target if arriving else self.source(k),
            target,
            self.line_sem.at[k, 0, step],
            self.line_sem.at[k, 1, step],
            p.ahead(step),
        )

    def side(self, k, step, arriving=False, own=False):
        p = self.place
        shard = p.shard(p.behind(step), 1 - p.side if arriving else p.side)
        target = self.region(k, shard, p.core, p.chip)
        return remote(
            self.source(k) if own else target,
            target,
            self.side_sem.at[k, 0, step],
            self.side_sem.at[k, 1, step],
            p.partner(),
        )

    def cross(self, k, step, other, sems, core, chip, device):
        p = self.place
        shard = p.shard(p.behind(step), 1 - p.side if other else p.side)
        target = self.region(k, shard, core, chip)
        slot = 2 * step + (1 if other else 0)
        return remote(target, target, sems.at[k, 0, slot], sems.at[k, 1, slot], device)

    def core(self, k, step, other, arriving=False):
        p = self.place
        core = 1 - p.core if arriving else p.core
        return self.cross(k, step, other, self.core_sem, core, p.chip, p.sibling())

    def across(self, k, step, other, arriving=False):
        p = self.place
        chip = 1 - p.chip if arriving else p.chip
        return self.cross(k, step, other, self.across_sem, p.core, chip, p.across())

    def relay(self, k, step, other, arriving=False):
        p = self.place
        core = 1 - p.core if arriving else p.core
        return self.cross(k, step, other, self.relay_sem, core, 1 - p.chip, p.sibling())

    def keep(self, k):
        a, offset, width, _ = self.pieces[k]
        depth = self.shards[a].shape[0]
        rows = pl.ds(pl.multiple_of(self.place.index * depth, 16), depth)
        columns = pl.ds(offset, width)
        return pltpu.make_async_copy(
            self.shards[a].at[:, columns], self.outs[a].at[rows, columns], self.own.at[k]
        )

    def hand(self, k, step, other):
        parts = self.pieces[k][3]
        if parts == 4:
            self.across(k, step, other).start()
        if parts > 1:
            self.core(k, step, other).start()

    def start(self, k):
        steps(1, self.place.length, lambda step: self.line(k, step).start())
        if self.place.sides == 2:
            self.side(k, 0, own=True).start()
        self.keep(k).start()

    def forward(self, k):
        def one(step):
            self.line(k, step, True).wait_recv()
            if self.place.sides == 2:
                self.side(k, step).start()
            self.hand(k, step, False)

        steps(1, self.place.length, one)

    def spread(self, k):
        def one(step):
            self.side(k, step, True).wait_recv()
            self.hand(k, step, True)

        if self.place.sides == 2:
            steps(0, self.place.length, one)

    def each(self, body):
        steps(1, self.place.length, lambda step: body(step, False))
        if self.place.sides == 2:
            steps(0, self.place.length, lambda step: body(step, True))

    def exchange(self, k):
        def one(step, other):
            self.across(k, step, other, True).wait_recv()
            self.relay(k, step, other).start()

        if self.pieces[k][3] == 4:
            self.each(one)

    def arrive(self, k):
        parts = self.pieces[k][3]

        def one(step, other):
            self.core(k, step, other, True).wait_recv()
            if parts == 4:
                self.relay(k, step, other, True).wait_recv()

        self.keep(k).wait()
        if parts > 1:
            self.each(one)

    def sent(self, k):
        parts = self.pieces[k][3]

        def one(step, other):
            self.core(k, step, other).wait_send()
            if parts == 4:
                self.across(k, step, other).wait_send()
                self.relay(k, step, other).wait_send()

        steps(1, self.place.length, lambda step: self.line(k, step).wait_send())
        if self.place.sides == 2:
            steps(0, self.place.length, lambda step: self.side(k, step).wait_send())
        if parts > 1:
            self.each(one)

    def events(self, tiles, urgent, ahead=3):
        made = []
        line = side = across = 0.0
        hop = 8.0
        number = len(self.pieces)
        for k in range(number):
            parts = self.pieces[k][3]
            margin = 8.0 if k < urgent else 30.0
            load = tiles[k] * (2 if parts == 4 else 4)
            line = line + load
            side = max(side + load, line + load / 4 + hop)
            last = side
            made.append((line + hop, k, 0))
            made.append((side + hop, k, 1))
            if parts == 4:
                across = max(across + 3.5 * tiles[k], side + tiles[k] / 2 + hop)
                last = across
                made.append((across + hop + margin, k, 2))
            wait = 0.0 if k < urgent else 2 * margin
            made.append((last + 2 * hop + wait + (margin if parts == 4 else 0.0), k, 3))
        made.sort()

        def action(k, kind):
            if kind == 0:
                self.forward(k)
                if k + ahead < number:
                    self.start(k + ahead)
            else:
                (self.spread, self.exchange, self.arrive)[kind - 1](k)

        return [(when, k, kind, functools.partial(action, k, kind)) for when, k, kind in made]


PACK = (16, 512)


def pack_small(gains, taps):
    count = taps.shape[0]

    def fit(values, rows):
        values = values.reshape(count, -1, values.shape[-1]).astype(bf16)
        return jnp.pad(
            values, ((0, 0), (0, rows - values.shape[1]), (0, PACK[1] - values.shape[2]))
        )

    rows = [fit(gains[0], 1), fit(gains[1], 1), fit(gains[2], 2), fit(taps, PACK[0] - 4)]
    return jnp.concatenate(rows, axis=1).reshape(count * PACK[0], PACK[1])


def unpack_small(packed, shapes):
    packed = packed.reshape(-1, PACK[0], PACK[1])
    gains = [packed[:, row, : shape[0]] for row, shape in enumerate(shapes[:3])]
    return gains + [packed[:, 4 : 4 + shapes[3][0], : shapes[3][1]]]


def place_rows(packed, count, width):
    if width % 128 == 0:
        return jnp.concatenate(
            [packed[s * PACK[0] : (s + 1) * PACK[0], :width] for s in range(count)], axis=1
        )
    total = count * width
    row = lax.broadcasted_iota(jnp.int32, (PACK[1], total), 0)
    col = lax.broadcasted_iota(jnp.int32, (PACK[1], total), 1)
    pick = jnp.where(lax.rem(col, width) == row, 1.0, 0.0).astype(bf16)
    wide = nn(packed.astype(bf16), pick)
    row = lax.broadcasted_iota(jnp.int32, wide.shape, 0)
    col = lax.broadcasted_iota(jnp.int32, wide.shape, 1)
    wide = jnp.where(lax.div(row, PACK[0]) == lax.div(col, width), wide, 0.0).astype(bf16)
    row = lax.broadcasted_iota(jnp.int32, (PACK[0], count * PACK[0]), 0)
    col = lax.broadcasted_iota(jnp.int32, (PACK[0], count * PACK[0]), 1)
    fold = jnp.where(lax.rem(col, PACK[0]) == row, 1.0, 0.0).astype(bf16)
    return nn(fold, wide)


GROUP = 2


def grid_indices():
    row = lax.broadcasted_iota(jnp.int32, (CHUNK, CHUNK), 0)
    col = lax.broadcasted_iota(jnp.int32, (CHUNK, CHUNK), 1)
    return row, col


def conv_pre(wide_ref, taps, rows):
    total = None
    for offset in range(TAPS):
        term = taps[offset : offset + 1, :] * wide_ref[pl.ds(HALO - TAPS + 1 + offset, rows), :]
        total = term if total is None else total + term
    return total


def sigmoid(values):
    return 1.0 / (1.0 + jnp.exp(-values))


def head_column(table, head):
    lane = lax.broadcasted_iota(jnp.int32, table.shape, 1)
    return jnp.sum(jnp.where(lane == head, table, 0.0), axis=1, keepdims=True)


ARRAYS = 7


def forward_kernel(count, pieces, mixed, heads, tap_width, *refs):
    tokens_ref = refs[0]
    shards, refs = refs[1 : 1 + ARRAYS], refs[1 + ARRAYS :]
    gathered, refs = refs[:ARRAYS], refs[ARRAYS:]
    (
        finals_ref,
        normed_ref,
        normed_t_ref,
        signals_ref,
        logit_ref,
        taps_ref,
        out_ref,
        carry_ref,
        fresh_ref,
        inverse_ref,
        starts_ref,
    ), refs = refs[:11], refs[11:]
    (
        tokens,
        weights,
        rates_weight,
        packed,
        all_taps,
        wide,
        level_masks,
        final,
        halo_sem,
        token_sem,
        load_sem,
        final_sem,
        *sems,
    ) = refs
    group = pl.program_id(0)
    groups = heads // GROUP
    rows = out_ref.shape[0]
    size = out_ref.shape[1] // GROUP
    span = GROUP * size
    chunks = rows // CHUNK
    levels = CHUNK.bit_length() - 1
    row, col = grid_indices()
    gather = Gather(count, pieces, shards, gathered, sems)
    place = gather.place
    tiles = [piece[2] / 128 * shards[piece[0]].shape[0] / 128 for piece in pieces]
    events = gather.events(tiles, 2 + groups)

    def halo(arriving):
        return remote(
            tokens_ref.at[pl.ds(rows - HALO, HALO), :],
            tokens.at[pl.ds(0, HALO), :],
            halo_sem.at[0],
            halo_sem.at[1],
            {"seq": lax.rem(place.position + 1, 4), "fsdp": place.index},
        )

    def load(step, slot):
        return pltpu.make_async_copy(
            gathered[mixed].at[:, pl.ds(pl.multiple_of(step * 3 * span, 128), 3 * span)],
            weights.at[slot],
            load_sem.at[slot],
        )

    per_step = 9
    plan = {}
    mark = 0
    for step in range(groups):
        for spot in range(per_step):
            now = 60.0 + (step * per_step + spot) * 5.0
            upto = mark
            for index in range(mark, len(events)):
                when, k, kind, _ = events[index]
                if spot == 0 and kind == 3 and (k == 2 + step or (step == 0 and k < 2)):
                    upto = index + 1
                elif when <= now and upto == index:
                    upto = index + 1
            plan[step, spot] = (mark, upto)
            mark = upto
    remaining = (mark, len(events))

    def run(bounds):
        for _, _, _, action in events[bounds[0] : bounds[1]]:
            action()

    def spot(number):
        for step in range(groups):
            bounds = plan[step, number]
            if bounds[1] > bounds[0]:

                @pl.when(group == step)
                def _():
                    run(bounds)

    @pl.when(group == 0)
    def _():
        own = pltpu.make_async_copy(tokens_ref, tokens.at[pl.ds(HALO, rows), :], token_sem.at[0])
        own.start()
        place.greet_all()

        @pl.when(place.position < 3)
        def _():
            halo(False).start()

        gather.start(0)
        gather.start(1)
        gather.start(2)

        @pl.when(place.position == 0)
        def _():
            tokens[pl.ds(0, HALO), :] = jnp.zeros((HALO, tokens.shape[1]), bf16)

        for level in range(levels):
            same = (row >> (level + 1)) == (col >> (level + 1))
            below = ((row >> level) & 1 == 1) & ((col >> level) & 1 == 0)
            level_masks[level] = jnp.where(same & below, 1.0, 0.0).astype(bf16)

        limit = max(i for i, event in enumerate(events) if event[1] == 0) + 1
        run((0, limit))
        copy = pltpu.make_async_copy(gathered[0], packed, token_sem.at[1])
        copy.start()
        copy.wait()
        small = packed[...].astype(f32)
        gain = place_rows(small, count, tokens.shape[1] // count)[0:1, :]
        all_taps[...] = place_rows(small, count, tap_width)[4 : 4 + TAPS, :]
        own.wait()

        @pl.when(place.position > 0)
        def _():
            halo(True).wait_recv()

        block = 208 if tokens.shape[0] % 208 == 0 else HALO

        def norm(index):
            part = pl.ds(pl.multiple_of(index * block, HALO), block)
            normed_ref[part, :] = rms_scale(tokens[part, :].astype(f32), gain).astype(bf16)

        steps(0, tokens.shape[0] // block, norm)
        for first in range(0, rows, CHUNK):
            part = normed_ref[pl.ds(HALO + first, CHUNK), :]
            normed_t_ref[:, first : first + CHUNK] = part.T
        run((limit, plan[0, 0][1]))
        copy = pltpu.make_async_copy(gathered[1], rates_weight, token_sem.at[1])
        copy.start()
        load(0, 0).start()
        copy.wait()
        logit_ref[...] = nn(normed_ref[pl.ds(HALO, rows), :], rates_weight[...]).astype(bf16)
        load(0, 0).wait()

    for step in range(1, groups):
        bounds = plan[step, 0]

        @pl.when(group == step)
        def _():
            run(bounds)
            load(step, 0).start()
            load(step, 0).wait()

    signals_ref[...] = nn(normed_ref[...], weights[0]).astype(bf16)
    spot(1)

    lows = [[], [], []]
    for inner in range(GROUP):
        for which in range(3):
            first = pl.multiple_of((which * heads + group * GROUP + inner) * size, 128)
            taps = all_taps[:, pl.ds(first, size)]
            taps_ref[inner, which] = taps
            wide[...] = signals_ref[:, pl.ds((inner * 3 + which) * size, size)].astype(f32)
            pre = conv_pre(wide, taps, rows)
            act = pre * sigmoid(pre)
            if which < 2:
                act = act * lax.rsqrt(jnp.sum(act * act, axis=1, keepdims=True) + epsilon)
            lows[which].append(act.astype(bf16))
        if inner == 0:
            spot(2)
    spot(3)
    logits = logit_ref[...].astype(f32)
    rates = [sigmoid(head_column(logits, group * GROUP + inner)) for inner in range(GROUP)]
    scaling = size ** (-0.5)
    eye = jnp.where(row == col, 1.0, 0.0)
    lower = row >= col

    work = [(inner, chunk) for inner in range(GROUP) for chunk in range(chunks)]

    def cut(values, item):
        inner, chunk = item
        return values[inner][chunk * CHUNK : (chunk + 1) * CHUNK]

    queries, keys, values = lows
    stricts = [(cut(rates, i) * nt(cut(keys, i), cut(keys, i))).astype(bf16) for i in work]
    results = [eye - (strict * level_masks[0]).astype(f32) for strict in stricts]
    scores = [jnp.where(lower, nt(cut(queries, i), cut(keys, i)), 0.0).astype(bf16) for i in work]
    for level in range(1, levels):
        mask = level_masks[level]
        lowered = [result.astype(bf16) for result in results]
        inners = [nn(low, strict * mask).astype(bf16) for low, strict in zip(lowered, stricts)]
        results = [
            result - nn(inner, low) for result, inner, low in zip(results, inners, lowered)
        ]
        if level in (2, 4, 6):
            spot(3 + level // 2)
    inverses = [result.astype(bf16) for result in results]
    for (inner, chunk), inverse in zip(work, inverses):
        part = slice(chunk * CHUNK, (chunk + 1) * CHUNK)
        inverse_ref[part, inner * CHUNK : (inner + 1) * CHUNK] = inverse
    spot(7)

    srow = lax.broadcasted_iota(jnp.int32, (size, size), 0)
    scol = lax.broadcasted_iota(jnp.int32, (size, size), 1)
    memories = [
        jnp.concatenate(
            [jnp.zeros((size, size), f32), jnp.where(srow == scol, 1.0, 0.0)], axis=1
        )
    ] * GROUP
    for chunk in range(chunks):
        part = slice(chunk * CHUNK, (chunk + 1) * CHUNK)
        for inner in range(GROUP):
            item = (inner, chunk)
            key_part, query_part, rate_part = cut(keys, item), cut(queries, item), cut(rates, item)
            low_memory = memories[inner].astype(bf16)
            starts_ref[inner, chunk] = low_memory
            seen = nn(key_part, low_memory)
            aim = jnp.concatenate(
                [cut(values, item).astype(f32), jnp.zeros((CHUNK, size), f32)], axis=1
            )
            aim = (rate_part * (aim - seen)).astype(bf16)
            fresh = nn(inverses[work.index(item)], aim).astype(bf16)
            fresh_ref[part, inner * 2 * size : (inner + 1) * 2 * size] = fresh
            both = scaling * (
                nn(query_part, low_memory) + nn(scores[work.index(item)], fresh)
            )
            out_ref[part, inner * size : (inner + 1) * size] = both[:, :size]
            carry_ref[part, inner * size : (inner + 1) * size] = both[:, size:].astype(bf16)
            memories[inner] = memories[inner] + tn(key_part, fresh)

    def send_final(step, hop):
        position = lax.rem(place.position + hop, 4)
        block = pl.ds(step * GROUP, GROUP)
        return remote(
            final.at[block],
            finals_ref.at[place.position, block],
            final_sem.at[0, step, hop],
            final_sem.at[1, step, hop],
            {"seq": position, "fsdp": place.index},
        )

    def keep_final(step):
        block = pl.ds(step * GROUP, GROUP)
        return pltpu.make_async_copy(
            final.at[block], finals_ref.at[place.position, block], final_sem.at[0, step, 0]
        )

    def take_final(step, hop):
        position = lax.rem(place.position + 4 - hop, 4)
        block = pl.ds(step * GROUP, GROUP)
        return remote(
            final.at[block],
            finals_ref.at[position, block],
            final_sem.at[0, step, hop],
            final_sem.at[1, step, hop],
            {"seq": position, "fsdp": place.index},
        )

    for step in range(groups):

        @pl.when(group == step)
        def _():
            for inner in range(GROUP):
                final[step * GROUP + inner] = memories[inner].astype(bf16)
            for hop in range(1, 4):
                send_final(step, hop).start()
            keep_final(step).start()

    spot(8)

    @pl.when(group == groups - 1)
    def _():
        run(remaining)
        for k in range(len(pieces)):
            gather.sent(k)
        for step in range(groups):
            for hop in range(1, 4):
                send_final(step, hop).wait_send()
                take_final(step, hop).wait_recv()
            keep_final(step).wait()

        @pl.when(place.position < 3)
        def _():
            halo(False).wait_send()


def plan_pieces(depths, widths, span):
    def portions(a, wanted):
        while depths[a] % (16 * wanted) != 0:
            wanted //= 2
        return wanted

    pieces = [(0, 0, widths[0], 1), (1, 0, widths[1], portions(1, 2))]
    for step in range(widths[2] // span):
        pieces.append((2, step * span, span, portions(2, 4)))
    pieces.append((3, 0, widths[3], portions(3, 4)))
    for a in (4, 5, 6):
        half = widths[a] // 2
        for part in range(2):
            wanted = 2 if (a, part) in ((5, 0), (6, 1)) else 4
            pieces.append((a, part * half, half, portions(a, wanted)))
    return pieces


def forward(tokens, shards, heads, tap_width):
    count = lax.axis_size("fsdp")
    rows, width = tokens.shape
    size = width // heads
    span = GROUP * size
    groups = heads // GROUP
    chunks = rows // CHUNK
    wide_rows = rows + HALO
    depths = [shard.shape[0] for shard in shards]
    widths = [shard.shape[1] for shard in shards]
    pieces = plan_pieces(depths, widths, 3 * span)
    anywhere = pl.BlockSpec(memory_space=pl.ANY)
    shape = jax.ShapeDtypeStruct
    return pl.pallas_call(
        functools.partial(forward_kernel, count, pieces, 2, heads, tap_width),
        grid=(groups,),
        in_specs=[anywhere] * (1 + ARRAYS),
        out_specs=[anywhere] * (ARRAYS + 1)
        + [
            pl.BlockSpec((wide_rows, width), lambda g: (0, 0)),
            pl.BlockSpec((width, rows), lambda g: (0, 0)),
            pl.BlockSpec((wide_rows, 3 * span), lambda g: (0, g)),
            pl.BlockSpec((rows, widths[1]), lambda g: (0, 0)),
            pl.BlockSpec((GROUP, 3, TAPS, size), lambda g: (g, 0, 0, 0)),
            pl.BlockSpec((rows, span), lambda g: (0, g)),
            pl.BlockSpec((rows, span), lambda g: (0, g)),
            pl.BlockSpec((rows, 2 * span), lambda g: (0, g)),
            pl.BlockSpec((rows, GROUP * CHUNK), lambda g: (0, g)),
            pl.BlockSpec((GROUP, chunks, size, 2 * size), lambda g: (g, 0, 0, 0)),
        ],
        out_shape=[shape((count * d, w), bf16) for d, w in zip(depths, widths)]
        + [
            shape((4, heads, size, 2 * size), bf16),
            shape((wide_rows, width), bf16),
            shape((width, rows), bf16),
            shape((wide_rows, 3 * width), bf16),
            shape((rows, widths[1]), bf16),
            shape((heads, 3, TAPS, size), f32),
            shape((rows, width), f32),
            shape((rows, width), bf16),
            shape((rows, 2 * width), bf16),
            shape((rows, heads * CHUNK), bf16),
            shape((heads, chunks, size, 2 * size), bf16),
        ],
        scratch_shapes=[
            pltpu.VMEM((wide_rows, width), bf16),
            pltpu.VMEM((1, width, 3 * span), bf16),
            pltpu.VMEM((width, widths[1]), bf16),
            pltpu.VMEM((count * PACK[0], PACK[1]), bf16),
            pltpu.VMEM((TAPS, 3 * width), f32),
            pltpu.VMEM((wide_rows, size), f32),
            pltpu.VMEM((CHUNK.bit_length() - 1, CHUNK, CHUNK), bf16),
            pltpu.VMEM((heads, size, 2 * size), bf16),
            pltpu.SemaphoreType.DMA((2,)),
            pltpu.SemaphoreType.DMA((2,)),
            pltpu.SemaphoreType.DMA((2,)),
            pltpu.SemaphoreType.DMA((2, groups, 4)),
        ]
        + Gather.scratch(pieces, count),
        compiler_params=pltpu.CompilerParams(
            collective_id=0, has_side_effects=True, vmem_limit_bytes=60 * MIB
        ),
    )(tokens, *shards)


def mix_kernel(position_ref, out_ref, carry_ref, finals_ref, gain_ref, mixed_ref, state_ref):
    position = position_ref[0]
    size = out_ref.shape[1]
    state = jnp.zeros((size, size), f32)
    for index in range(finals_ref.shape[0] - 1):
        pair = finals_ref[index, 0].astype(f32)
        later = pair[:, :size] + jnp.dot(pair[:, size:], state, precision=highest)
        state = jnp.where(index < position, later, state)
    state_ref[0] = state
    output = out_ref[...] + nn(carry_ref[...], state.astype(bf16))
    gain = gain_ref[...].astype(f32)
    mixed_ref[...] = rms_scale(output, gain).astype(bf16)


def mix(position, outputs, carries, finals, gain):
    rows, width = outputs.shape
    groups, heads, size, _ = finals.shape
    plain = pl.BlockSpec((rows, size), lambda h: (0, h))
    return pl.pallas_call(
        mix_kernel,
        grid=(heads,),
        in_specs=[
            pl.BlockSpec(memory_space=pltpu.SMEM),
            plain,
            plain,
            pl.BlockSpec((groups, 1, size, 2 * size), lambda h: (0, h, 0, 0)),
            pl.BlockSpec((1, size), lambda h: (0, 0)),
        ],
        out_specs=[plain, pl.BlockSpec((1, size, size), lambda h: (h, 0, 0))],
        out_shape=[
            jax.ShapeDtypeStruct((rows, width), bf16),
            jax.ShapeDtypeStruct((heads, size, size), f32),
        ],
        compiler_params=pltpu.CompilerParams(vmem_limit_bytes=32 * MIB),
    )(position, outputs, carries, finals, gain)


def unmix_kernel(
    heads,
    out_ref,
    carry_ref,
    state_ref,
    gain_ref,
    grad_ref,
    grad_out_ref,
    grad_gain_ref,
    grads_ref,
    grad_states,
    sems,
):
    head = pl.program_id(0)
    position, index = lax.axis_index("seq"), lax.axis_index("fsdp")

    def device(hop):
        return {"seq": lax.rem(position + hop, 4), "fsdp": index}

    def send(one, hop, arriving=False):
        source = lax.rem(position + 4 - hop, 4) if arriving else position
        return remote(
            grad_states.at[one],
            grads_ref.at[source, one],
            sems.at[0, one, hop],
            sems.at[1, one, hop],
            device(hop),
        )

    def keep(one):
        return pltpu.make_async_copy(
            grad_states.at[one], grads_ref.at[position, one], sems.at[0, one, 0]
        )

    @pl.when(head == 0)
    def _():
        barrier = pltpu.get_barrier_semaphore()
        for hop in range(1, 4):
            pl.semaphore_signal(barrier, inc=1, device_id=device(hop), device_id_type=MESH)
        grad_gain_ref[...] = jnp.zeros_like(grad_gain_ref)
        pl.semaphore_wait(barrier, 3)

    output = out_ref[...] + nn(carry_ref[...], state_ref[0].astype(bf16))
    gain = gain_ref[...].astype(f32)
    grad = grad_ref[...].astype(f32)
    scaling = lax.rsqrt(jnp.mean(output * output, axis=1, keepdims=True) + epsilon)
    unit_rows = output * scaling
    grad_gain_ref[...] += jnp.sum(grad * unit_rows, axis=0, keepdims=True)
    scaled = grad * gain
    grad_out = scaling * (scaled - unit_rows * jnp.mean(scaled * unit_rows, axis=1, keepdims=True))
    low_grad = grad_out.astype(bf16)
    grad_states[head] = tn(carry_ref[...], low_grad).astype(bf16)
    for hop in range(1, 4):
        send(head, hop).start()
    keep(head).start()
    grad_out_ref[...] = (grad_out * output.shape[1] ** (-0.5)).astype(bf16)

    @pl.when(head == heads - 1)
    def _():
        def one(step):
            keep(step).wait()
            for hop in range(1, 4):
                send(step, hop).wait_send()
                send(step, hop, True).wait_recv()

        steps(0, heads, one)


def unmix(outputs, carries, states, gain, grad_heads):
    rows, width = outputs.shape
    heads, size, _ = states.shape
    plain = pl.BlockSpec((rows, size), lambda h: (0, h))
    state = pl.BlockSpec((1, size, size), lambda h: (h, 0, 0))
    vector = pl.BlockSpec((1, size), lambda h: (0, 0))
    return pl.pallas_call(
        functools.partial(unmix_kernel, heads),
        grid=(heads,),
        in_specs=[plain, plain, state, vector, plain],
        out_specs=[plain, vector, pl.BlockSpec(memory_space=pl.ANY)],
        out_shape=[
            jax.ShapeDtypeStruct((rows, width), bf16),
            jax.ShapeDtypeStruct((1, size), f32),
            jax.ShapeDtypeStruct((4, heads, size, size), bf16),
        ],
        scratch_shapes=[
            pltpu.VMEM((heads, size, size), bf16),
            pltpu.SemaphoreType.DMA((2, heads, 4)),
        ],
        compiler_params=pltpu.CompilerParams(
            collective_id=1, has_side_effects=True, vmem_limit_bytes=32 * MIB
        ),
    )(outputs, carries, states, gain, grad_heads)


TILE = 256
SLOTS = 3
DENSE_STRIDE = 4


def dense_kernel(count, shapes, *refs):
    (
        mixed_ref,
        w_out_ref,
        gain_ref,
        cotangent_ref,
        gate_ref,
        up_ref,
        down_ref,
        tokens_ref,
        layer_out_ref,
        grad_gain_ref,
        grad_out_ref,
        grad_attended_ref,
        grad_heads_ref,
        rest_ref,
        sums_ref,
        attended,
        normed,
        normed_t,
        cotangent_t,
        result,
        grad_normed,
        source,
        plain_sem,
        rest_sem,
    ), refs = refs[:24], refs[24:]
    tile = pl.program_id(0)
    rows, width = attended.shape
    depth = width // count
    number = len(shapes)
    tiles = number + rest_ref.shape[3] // (3 * TILE)
    blocks = [slice(first, first + CHUNK) for first in range(0, rows, CHUNK)]
    columns = [slice(first, first + CHUNK) for first in range(0, width, CHUNK)]
    gain = gain_ref[...].astype(f32)

    due, later, reduce = {}, [], None
    if number > 0:
        buffers = [refs[i * number : (i + 1) * number] for i in range(Reduce.BUFFERS)]
        sems = refs[Reduce.BUFFERS * number :]
        sources = [source.at[p % SLOTS] for p in range(number)]
        targets = [sums_ref.at[:, pl.ds(p * 3 * TILE, 3 * TILE)] for p in range(number)]
        reduce = Reduce(count, shapes, sources, targets, buffers, None, sems)
        begin = [2 * p + 3 for p in range(number)]
        due, later = reduce.plan(
            begin, [DENSE_STRIDE] * number, 2 * tiles - 1, [False] * number
        )

    def spot(which):
        for step in range(tiles):
            actions = due.get(2 * step + which, ())
            if actions:

                @pl.when(tile == step)
                def _():
                    for action in actions:
                        action()

    def rest(step):
        slot = lax.rem(step, SLOTS)
        first = pl.multiple_of((step - number) * 3 * TILE, 128)
        return pltpu.make_async_copy(
            source.at[slot], rest_ref.at[:, :, :, pl.ds(first, 3 * TILE)], rest_sem.at[slot]
        )

    def fetch(start, target, slot):
        return pltpu.make_async_copy(start, target, plain_sem.at[slot])

    @pl.when(tile == 0)
    def _():
        load = fetch(tokens_ref, normed, 0)
        load.start()
        if reduce is not None:
            reduce.place.greet_all()
        load.wait()
        for block in blocks:
            values = normed[block, :].astype(f32) + nn(mixed_ref[block, :], w_out_ref[...])
            attended[block, :] = values
            result[block, :] = values
            low = rms_scale(values, gain).astype(bf16)
            normed[block, :] = low
            normed_t[:, block] = low.T
            cotangent_t[:, block] = cotangent_ref[block, :].T
        grad_normed[...] = jnp.zeros_like(grad_normed)

    @pl.when(tile >= number + SLOTS)
    def _():
        rest(tile - SLOTS).wait()

    spot(0)
    gate = nn(normed[...], gate_ref[...])
    up = nn(normed[...], up_ref[...])
    grad_hidden = nn(cotangent_ref[...], down_ref[...])
    sig = sigmoid(gate)
    activated = gate * sig
    hidden = (activated * up).astype(bf16)
    grad_gate = (grad_hidden * up * sig * (1.0 + gate * (1.0 - sig))).astype(bf16)
    grad_up = (grad_hidden * activated).astype(bf16)
    slot = lax.rem(tile, SLOTS)
    for which, (left, right) in enumerate(
        ((normed_t, grad_gate), (normed_t, grad_up), (cotangent_t, hidden))
    ):
        piece = nn(left[...], right).astype(bf16).reshape(count // 2, 2, depth, TILE)
        source[slot, :, :, :, pl.ds(which * TILE, TILE)] = piece

    spot(1)
    for column in columns:
        result[:, column] += nt(hidden, down_ref[column, :])
        grad_normed[:, column] += nt(grad_gate, gate_ref[column, :]) + nt(
            grad_up, up_ref[column, :]
        )

    for p in range(number):

        @pl.when(tile == p)
        def _():
            reduce.start(p, False)

    @pl.when(tile >= number)
    def _():
        rest(tile).start()

    @pl.when(tile == tiles - 1)
    def _():
        gain_grad = jnp.zeros((1, width), f32)
        for block in blocks:
            layer_out_ref[block, :] = result[block, :].astype(bf16)
            values = attended[block, :]
            grad = grad_normed[block, :]
            scaling = lax.rsqrt(jnp.mean(values * values, axis=1, keepdims=True) + epsilon)
            unit = values * scaling
            gain_grad = gain_grad + jnp.sum(grad * unit, axis=0, keepdims=True)
            scaled = grad * gain
            grad = cotangent_ref[block, :].astype(f32) + scaling * (
                scaled - unit * jnp.mean(scaled * unit, axis=1, keepdims=True)
            )
            attended[block, :] = grad
            low = grad.astype(bf16)
            normed[block, :] = low
            normed_t[:, block] = mixed_ref[block, :].T
        fetch(attended, grad_attended_ref, 0).start()
        grad_gain_ref[...] = gain_grad
        for block in blocks:
            cotangent_t[block, :] = nt(normed[block, :], w_out_ref[...]).astype(bf16)
        fetch(cotangent_t, grad_heads_ref, 1).start()
        for action in later[: len(later) // 2]:
            action()
        for column in columns:
            grad_out_ref[column, :] = nn(normed_t[column, :], normed[...]).astype(bf16)
        for action in later[len(later) // 2 :]:
            action()
        for p in range(number):
            reduce.finish(p)
        for step in range(max(number, tiles - SLOTS), tiles):
            rest(step).wait()
        fetch(attended, grad_attended_ref, 0).wait()
        fetch(cotangent_t, grad_heads_ref, 1).wait()


def dense(mixed, tokens, w_out, gain, cotangent, w_gate, w_up, w_down_t, number):
    count = lax.axis_size("fsdp")
    rows, width = tokens.shape
    hidden = w_gate.shape[1]
    tiles = hidden // TILE
    depth = width // count
    shapes = [(depth, 3 * TILE, 2 if p % 2 == 0 else 4) for p in range(number)]
    whole = pl.BlockSpec((rows, width), lambda j: (0, 0))
    square = pl.BlockSpec((width, width), lambda j: (0, 0))
    vector = pl.BlockSpec((1, width), lambda j: (0, 0))
    slab = pl.BlockSpec((width, TILE), lambda j: (0, j))
    anywhere = pl.BlockSpec(memory_space=pl.ANY)
    shape = jax.ShapeDtypeStruct
    more = dict(collective_id=3, has_side_effects=True) if number > 0 else {}
    extra = []
    if number > 0:
        extra = Reduce.buffers(count, shapes) + Reduce.semaphores(count, number)
    return pl.pallas_call(
        functools.partial(dense_kernel, count, shapes),
        grid=(tiles,),
        in_specs=[whole, square, vector, whole, slab, slab, slab, anywhere],
        out_specs=[whole, vector, square] + [anywhere] * 4,
        out_shape=[
            shape((rows, width), bf16),
            shape((1, width), f32),
            shape((width, width), bf16),
            shape((rows, width), f32),
            shape((rows, width), bf16),
            shape((count // 2, 2, depth, (tiles - number) * 3 * TILE), bf16),
            shape((depth, max(number, 1) * 3 * TILE), bf16),
        ],
        scratch_shapes=[
            pltpu.VMEM((rows, width), f32),
            pltpu.VMEM((rows, width), bf16),
            pltpu.VMEM((width, rows), bf16),
            pltpu.VMEM((width, rows), bf16),
            pltpu.VMEM((rows, width), f32),
            pltpu.VMEM((rows, width), f32),
            pltpu.VMEM((SLOTS, count // 2, 2, depth, 3 * TILE), bf16),
            pltpu.SemaphoreType.DMA((2,)),
            pltpu.SemaphoreType.DMA((SLOTS,)),
        ]
        + extra,
        compiler_params=pltpu.CompilerParams(vmem_limit_bytes=63 * MIB, **more),
    )(mixed, w_out, gain, cotangent, w_gate, w_up, w_down_t, tokens)


STRIDE = 4


def backward_kernel(
    count, arrays, shapes, loaded_number, heads, tap_width, gain_width, *refs
):
    (
        signals_ref,
        logit_ref,
        taps_ref,
        grad_ref,
        fresh_ref,
        inverse_ref,
        starts_ref,
        state_ref,
        finals_ref,
        grads_ref,
        weights_ref,
        rates_weight_ref,
        gain_ref,
        grad_mlp_ref,
        grad_gain_ref,
        normed_ref,
        tokens_ref,
    ), refs = refs[:17], refs[17:]
    full, refs = refs[:arrays], refs[arrays:]
    grad_tokens_ref, refs = refs[0], refs[1:]
    outs, refs = refs[: arrays + 3], refs[arrays + 3 :]
    (
        normed_t,
        tokens,
        total,
        grad_signals,
        tails,
        firsts,
        edges,
        wides,
        pres,
        grads,
        padded,
        grad_logits,
        small_rows,
        small_source,
        beta_source,
        mixed_source,
        staging,
        plain_sem,
        edge_sem,
    ), refs = refs[:19], refs[19:]
    number = len(shapes)
    buffers = [refs[i * number : (i + 1) * number] for i in range(Reduce.BUFFERS)]
    sems = refs[Reduce.BUFFERS * number :]

    head = pl.program_id(0)
    rows, size = grad_ref.shape
    width = total.shape[1]
    chunks = rows // CHUNK
    row, col = grid_indices()
    lower, upper = row >= col, row <= col

    sources, targets = [], []
    for a in range(arrays):
        halves = max(full[a].shape[3] // (3 * TILE), 1)
        half = full[a].shape[3] // halves
        for part in range(halves):
            columns = pl.ds(part * half, half)
            sources.append(full[a].at[:, :, :, columns])
            targets.append(outs[a].at[:, columns])
    slots = mixed_source.shape[0]
    for one in range(heads):
        sources.append(mixed_source.at[one % slots])
        targets.append(outs[arrays].at[:, pl.ds(one * 3 * size, 3 * size)])
    sources += [beta_source, small_source]
    targets += [outs[arrays + 1], outs[arrays + 2]]
    reduce = Reduce(count, shapes, sources, targets, buffers, staging, sems)
    place = reduce.place
    position = place.position
    loaded = [p < loaded_number for p in range(number)]
    begin = [1 + 3 * (p // 2) for p in range(loaded_number)]
    begin += [2 * one + 5 for one in range(heads)] + [2 * heads + 5, 2 * heads + 6]
    stride = [STRIDE] * loaded_number + [STRIDE - 1] * (number - loaded_number)
    due, later = reduce.plan(begin, stride, 2 * heads, loaded)

    def spot(which):
        for step in range(heads + 1):
            actions = due.get(2 * step + which, ())
            if actions:

                @pl.when(head == step)
                def _():
                    for action in actions:
                        action()

    def fetch(source, target, slot):
        return pltpu.make_async_copy(source, target, plain_sem.at[slot])

    def edge(one, slot, arriving=False):
        return remote(
            firsts.at[slot],
            edges.at[one],
            edge_sem.at[0, one],
            edge_sem.at[1, one],
            reduce.device(3),
        )

    @pl.when(head == 0)
    def _():
        fetch(normed_ref, normed_t, 0).start()
        fetch(tokens_ref, tokens, 1).start()
        place.greet_all()
        for p in range(min(2, loaded_number)):
            reduce.start(p, True)
        total[...] = jnp.zeros_like(total)
        padded[...] = jnp.zeros_like(padded)
        grad_logits[...] = jnp.zeros_like(grad_logits)
        small_rows[...] = jnp.zeros_like(small_rows)
        fetch(normed_ref, normed_t, 0).wait()
        fetch(tokens_ref, tokens, 1).wait()

    spot(0)

    @pl.when(head < heads)
    def _():
        slot = lax.rem(head, 2)
        lows, scales = [], []
        for which in range(3):
            wides[which] = signals_ref[:, pl.ds(which * size, size)].astype(f32)
            pre = conv_pre(wides.at[which], taps_ref[0, which], rows)
            pres[which] = pre
            act = pre * sigmoid(pre)
            if which < 2:
                scale = lax.rsqrt(jnp.sum(act * act, axis=1, keepdims=True) + epsilon)
                act = act * scale
                scales.append(scale)
            lows.append(act.astype(bf16))
        queries, keys, values = lows
        rates = sigmoid(head_column(logit_ref[...].astype(f32), head))

        state = state_ref[0].astype(bf16)
        first = fresh_ref[:, pl.ds(0, size)].astype(f32)
        fresh_all = (first + nn(fresh_ref[:, pl.ds(size, size)], state)).astype(bf16)

        grad_memory = jnp.zeros((size, size), f32)
        for index in reversed(range(1, 4)):
            later = grads_ref[index, 0].astype(f32) + lax.dot_general(
                finals_ref[index, 0, :, pl.ds(size, size)].astype(f32),
                grad_memory,
                (((0,), (0,)), ((), ())),
                precision=highest,
                preferred_element_type=f32,
            )
            grad_memory = jnp.where(index > position, later, grad_memory)
        grad_rates = [None] * chunks
        for chunk in reversed(range(chunks)):
            part = slice(chunk * CHUNK, (chunk + 1) * CHUNK)
            key, query, value, rate = keys[part], queries[part], values[part], rates[part]
            grad_out = grad_ref[part, :]
            fresh = fresh_all[part]
            start = starts_ref[0, chunk]
            memory = (start[:, :size].astype(f32) + nn(start[:, size:], state)).astype(bf16)
            low_grad = grad_memory.astype(bf16)
            key_f = key.astype(f32)
            rated = (rate * key_f).astype(bf16)

            scores_t = jnp.where(upper, nt(key, query), 0.0).astype(bf16)
            grad_fresh = (nn(scores_t, grad_out) + nn(key, low_grad)).astype(bf16)
            aim = tn(inverse_ref[part, :], grad_fresh)
            low_aim = aim.astype(bf16)
            grad_memory = grad_memory + tn(query, grad_out) - tn(rated, low_aim)

            grad_scores = jnp.where(lower, nt(grad_out, fresh), 0.0).astype(bf16)
            grad_scores_t = jnp.where(upper, nt(fresh, grad_out), 0.0).astype(bf16)
            grad_strict = jnp.where(row > col, nt(low_aim, fresh), 0.0).astype(bf16)
            grad_strict_t = jnp.where(row < col, nt(fresh, low_aim), 0.0).astype(bf16)

            grad_query = nt(grad_out, memory) + nn(grad_scores, key)
            within = -(nn(grad_strict, key) + nt(low_aim, memory))
            grad_rates[chunk] = jnp.sum(
                key_f * within + value.astype(f32) * aim, axis=1, keepdims=True
            )
            grad_key = (
                rate * within
                - nn(grad_strict_t, rated)
                + nn(grad_scores_t, query)
                + nt(fresh, low_grad)
            )
            grads[0, part, :] = grad_query
            grads[1, part, :] = grad_key
            grads[2, part, :] = rate * aim
            if chunk == chunks // 2:
                spot(1)

        lane = lax.broadcasted_iota(jnp.int32, grad_logits.shape, 1)
        grad_rate = jnp.concatenate(grad_rates, axis=0)
        grad_logit = grad_rate * rates * (1.0 - rates)
        grad_logits[...] = jnp.where(lane == head, grad_logit, grad_logits[...])

        @pl.when((head >= 2) & (position > 0))
        def _():
            edge(head - 2, slot).wait_send()

        for which in range(3):
            taps = taps_ref[0, which]
            pre = pres[which]
            sig = sigmoid(pre)
            grad_act = grads[which]
            if which < 2:
                unit = pre * sig * scales[which]
                grad_act = scales[which] * (
                    grad_act - unit * jnp.sum(grad_act * unit, axis=1, keepdims=True)
                )
            grad_pre = grad_act * sig * (1.0 + pre * (1.0 - sig))
            padded[pl.ds(HALO, rows), :] = grad_pre
            sums = []
            for offset in range(TAPS):
                shifted = wides[which, pl.ds(HALO - TAPS + 1 + offset, rows), :]
                sums.append(jnp.sum(grad_pre * shifted, axis=0, keepdims=True))
            where = pl.multiple_of((which * heads + head) * size, 128)
            small_rows[4:8, pl.ds(where, size)] = jnp.concatenate(sums, axis=0)

            def back(start, amount):
                result = None
                for offset in range(TAPS):
                    term = (
                        taps[offset : offset + 1, :]
                        * padded[pl.ds(start + TAPS - 1 - offset, amount), :]
                    )
                    result = term if result is None else result + term
                return result

            columns = pl.ds(which * size, size)
            grad_signal = back(HALO, rows)
            grad_signals[slot, :, columns] = grad_signal.astype(bf16)
            tails[slot, :, columns] = grad_signal[rows - HALO :]
            firsts[slot, :, columns] = back(0, HALO)

        @pl.when(position > 0)
        def _():
            edge(head, slot).start()

    for one in range(heads):

        @pl.when(head == one + 1)
        def _():
            slot = one % 2

            @pl.when(position < 3)
            def _():
                edge(one, slot).wait_recv()
                tails[slot] = tails[slot] + edges[one]

            grad_signals[slot, pl.ds(rows - HALO, HALO), :] = tails[slot].astype(bf16)
            grad = grad_signals[slot]
            source = mixed_source.at[one % slots]
            depth = width // count
            half = count // 4
            for part in range(2):
                piece = nn(normed_t[pl.ds(part * 2 * half * depth, 2 * half * depth), :], grad)
                source[pl.ds(part * half, half)] = piece.astype(bf16).reshape(
                    half, 2, depth, 3 * size
                )
            reduce.start(loaded_number + one, False)
            weights = weights_ref[...]
            for part in range(0, rows, CHUNK):
                block = pl.ds(part, CHUNK)
                total[block, :] += nt(grad[part : part + CHUNK], weights)

    @pl.when(head == heads)
    def _():
        depth = width // count
        low_logits = grad_logits[...].astype(bf16)
        beta_source[...] = (
            nn(normed_t[...], low_logits).astype(bf16).reshape(beta_source.shape)
        )
        reduce.start(number - 2, False)
        gain = gain_ref[...].astype(f32)
        weights = rates_weight_ref[...]
        gain_grad = jnp.zeros((1, width), f32)
        for part in range(0, rows, CHUNK):
            block = pl.ds(part, CHUNK)
            grad = total[block, :] + nt(low_logits[part : part + CHUNK], weights)
            values = tokens[block, :].astype(f32)
            scaling = lax.rsqrt(jnp.mean(values * values, axis=1, keepdims=True) + epsilon)
            unit = values * scaling
            gain_grad = gain_grad + jnp.sum(grad * unit, axis=0, keepdims=True)
            scaled = grad * gain
            total[block, :] = scaling * (
                scaled - unit * jnp.mean(scaled * unit, axis=1, keepdims=True)
            )
        fetch(total, grad_tokens_ref, 0).start()
        small_rows[0:1, pl.ds(0, width)] = gain_grad
        small_rows[1:2, pl.ds(0, width)] = grad_mlp_ref[...]
        small_rows[2:3, pl.ds(0, size)] = grad_gain_ref[...]
        small = small_rows[...]
        gains = gather_rows(small[:, :width], count, gain_width)
        last = gather_rows(small[:, :size], count, size // count)
        taps = gather_rows(small, count, tap_width)
        which = lax.broadcasted_iota(jnp.int32, gains.shape, 1)
        small = jnp.where(which == 2, last, jnp.where(which < 2, gains, taps))
        small_source[...] = small.astype(bf16).reshape(small_source.shape)
        reduce.start(number - 1, False)
        for action in later:
            action()
        for p in range(number):
            reduce.finish(p)
        fetch(total, grad_tokens_ref, 0).wait()
        for one in range(heads - 2, heads):

            @pl.when(position > 0)
            def _():
                edge(one, one % 2).wait_send()


def gather_rows(wide, count, width):
    total = count * width
    rows = wide.shape[0]
    if width % 128 == 0:
        blank = jnp.zeros((rows, PACK[1] - width), f32)
        return jnp.stack(
            [
                jnp.concatenate([wide[:, s * width : (s + 1) * width], blank], axis=1)
                for s in range(count)
            ]
        )
    row = lax.broadcasted_iota(jnp.int32, (count * rows, rows), 0)
    col = lax.broadcasted_iota(jnp.int32, (count * rows, rows), 1)
    spread = jnp.where(lax.rem(row, rows) == col, 1.0, 0.0).astype(bf16)
    tall = nn(spread, wide[:, :total].astype(bf16))
    row = lax.broadcasted_iota(jnp.int32, tall.shape, 0)
    col = lax.broadcasted_iota(jnp.int32, tall.shape, 1)
    tall = jnp.where(lax.div(row, rows) == lax.div(col, width), tall, 0.0).astype(bf16)
    row = lax.broadcasted_iota(jnp.int32, (total, PACK[1]), 0)
    col = lax.broadcasted_iota(jnp.int32, (total, PACK[1]), 1)
    pick = jnp.where(lax.rem(row, width) == col, 1.0, 0.0).astype(bf16)
    return nn(tall, pick).reshape(count, rows, PACK[1])


def backward(
    signals,
    logits,
    taps,
    grad_out,
    fresh,
    inverses,
    starts,
    state,
    finals,
    grad_starts,
    w_mixed,
    w_rates,
    gain,
    grad_mlp,
    grad_gain,
    normed_t,
    tokens,
    full,
    tap_width,
    gain_width,
):
    count = lax.axis_size("fsdp")
    wide_rows = signals.shape[0]
    rows, width = grad_out.shape
    heads, _, _, size = taps.shape
    chunks = rows // CHUNK
    depth = width // count
    views = full

    def portions(depth, wanted):
        while depth % (16 * wanted) != 0:
            wanted //= 2
        return wanted

    shapes = []
    for a, view in enumerate(views):
        halves = max(view.shape[3] // (3 * TILE), 1)
        for part in range(halves):
            shapes.append((depth, view.shape[3] // halves, 4 if (a + part) % 2 else 2))
    loaded = len(shapes)
    for head in range(heads):
        shapes.append((depth, 3 * size, portions(depth, 4 if head % 2 == 0 else 2)))
    shapes.append((depth, logits.shape[1], portions(depth, 2)))
    shapes.append(PACK + (1,))
    staged = max([d // 2 for d, _, _ in shapes[:loaded]] + [16])
    widest = max([w for _, w, _ in shapes[:loaded]] + [128])

    def now(h):
        return jnp.minimum(h, heads - 1)

    def before(h):
        return jnp.maximum(h - 1, 0)

    whole = pl.BlockSpec(logits.shape, lambda h: (0, 0))
    vector = pl.BlockSpec((1, width), lambda h: (0, 0))
    anywhere = pl.BlockSpec(memory_space=pl.ANY)
    shape = jax.ShapeDtypeStruct
    return pl.pallas_call(
        functools.partial(
            backward_kernel, count, len(views), shapes, loaded, heads, tap_width, gain_width
        ),
        grid=(heads + 1,),
        in_specs=[
            pl.BlockSpec((wide_rows, 3 * size), lambda h: (0, now(h))),
            whole,
            pl.BlockSpec((1, 3, TAPS, size), lambda h: (now(h), 0, 0, 0)),
            pl.BlockSpec((rows, size), lambda h: (0, now(h))),
            pl.BlockSpec((rows, 2 * size), lambda h: (0, now(h))),
            pl.BlockSpec((rows, CHUNK), lambda h: (0, now(h))),
            pl.BlockSpec((1, chunks, size, 2 * size), lambda h: (now(h), 0, 0, 0)),
            pl.BlockSpec((1, size, size), lambda h: (now(h), 0, 0)),
            pl.BlockSpec((4, 1, size, 2 * size), lambda h: (0, now(h), 0, 0)),
            pl.BlockSpec((4, 1, size, size), lambda h: (0, now(h), 0, 0)),
            pl.BlockSpec((width, 3 * size), lambda h: (0, before(h))),
            pl.BlockSpec(w_rates.shape, lambda h: (0, 0)),
            vector,
            vector,
            pl.BlockSpec((1, size), lambda h: (0, 0)),
        ]
        + [anywhere] * (2 + len(views)),
        out_specs=[anywhere] * (4 + len(views)),
        out_shape=[shape((rows, width), f32)]
        + [shape(view.shape[2:], bf16) for view in views]
        + [
            shape((depth, 3 * width), bf16),
            shape((depth, logits.shape[1]), bf16),
            shape(PACK, bf16),
        ],
        scratch_shapes=[
            pltpu.VMEM((width, rows), bf16),
            pltpu.VMEM((rows, width), bf16),
            pltpu.VMEM((rows, width), f32),
            pltpu.VMEM((2, rows, 3 * size), bf16),
            pltpu.VMEM((2, HALO, 3 * size), f32),
            pltpu.VMEM((2, HALO, 3 * size), f32),
            pltpu.VMEM((heads, HALO, 3 * size), f32),
            pltpu.VMEM((3, wide_rows, size), f32),
            pltpu.VMEM((3, rows, size), f32),
            pltpu.VMEM((3, rows, size), f32),
            pltpu.VMEM((rows + 2 * HALO, size), f32),
            pltpu.VMEM(logits.shape, f32),
            pltpu.VMEM((PACK[0], 3 * width), f32),
            pltpu.VMEM((count // 2, 2) + PACK, bf16),
            pltpu.VMEM((count // 2, 2, depth, logits.shape[1]), bf16),
            pltpu.VMEM((SLOTS, count // 2, 2, depth, 3 * size), bf16),
            pltpu.VMEM((2, count // 2, 2, staged, widest), bf16),
            pltpu.SemaphoreType.DMA((2,)),
            pltpu.SemaphoreType.DMA((2, heads)),
        ]
        + Reduce.buffers(count, shapes)
        + Reduce.semaphores(count, len(shapes)),
        compiler_params=pltpu.CompilerParams(
            collective_id=2, has_side_effects=True, vmem_limit_bytes=63 * MIB
        ),
    )(
        signals,
        logits,
        taps,
        grad_out,
        fresh,
        inverses,
        starts,
        state,
        finals,
        grad_starts,
        w_mixed,
        w_rates,
        gain,
        grad_mlp,
        grad_gain,
        normed_t,
        tokens,
        *views,
    )


def arrange_kernel(q_ref, k_ref, v_ref, down_ref, mixed_ref, down_t_ref):
    size = q_ref.shape[1]
    for which, ref in enumerate((q_ref, k_ref, v_ref)):
        mixed_ref[:, which * size : (which + 1) * size] = ref[...]
    down_t_ref[...] = down_ref[...].T


def arrange(w_query, w_key, w_value, w_down, heads):
    depth, width = w_query.shape
    size = width // heads
    tiles = w_down.shape[0] // TILE
    column = pl.BlockSpec((depth, size), lambda j: (0, jnp.minimum(j, heads - 1)))
    return pl.pallas_call(
        arrange_kernel,
        grid=(tiles,),
        in_specs=[column, column, column, pl.BlockSpec((TILE, depth), lambda j: (j, 0))],
        out_specs=[
            pl.BlockSpec((depth, 3 * size), lambda j: (0, jnp.minimum(j, heads - 1))),
            pl.BlockSpec((depth, TILE), lambda j: (0, j)),
        ],
        out_shape=[
            jax.ShapeDtypeStruct((depth, 3 * width), bf16),
            jax.ShapeDtypeStruct((depth, w_down.shape[0]), bf16),
        ],
        compiler_params=pltpu.CompilerParams(vmem_limit_bytes=16 * MIB),
    )(w_query, w_key, w_value, w_down)


def deliver_kernel(
    number,
    sums_ref,
    rest_ref,
    mixed_ref,
    out_ref,
    attended_ref,
    tokens_ref,
    gate_out,
    up_out,
    down_out,
    query_out,
    key_out,
    value_out,
    out_out,
    tokens_out,
):
    tile = pl.program_id(0)
    packed = jnp.where(tile < number, sums_ref[...], rest_ref[...]).astype(f32)
    gate_out[...] = packed[:, :TILE]
    up_out[...] = packed[:, TILE : 2 * TILE]
    down_out[...] = packed[:, 2 * TILE :].T
    size = query_out.shape[1]
    for which, ref in enumerate((query_out, key_out, value_out)):
        ref[...] = mixed_ref[:, which * size : (which + 1) * size].astype(f32)
    out_out[...] = out_ref[...].astype(f32)
    tokens_out[...] = attended_ref[...] + tokens_ref[...]


def deliver(number, sums, rest, mixed, out, grad_attended, grad_tokens, heads):
    depth, width = out.shape
    size = width // heads
    rows = grad_tokens.shape[0] // heads
    tiles = number + rest.shape[1] // (3 * TILE)

    def head(j):
        return jnp.minimum(j, heads - 1)

    column = pl.BlockSpec((depth, size), lambda j: (0, head(j)))
    block = pl.BlockSpec((rows, width), lambda j: (head(j), 0))
    tile = pl.BlockSpec((depth, TILE), lambda j: (0, j))
    shape = jax.ShapeDtypeStruct
    return pl.pallas_call(
        functools.partial(deliver_kernel, number),
        grid=(tiles,),
        in_specs=[
            pl.BlockSpec((depth, 3 * TILE), lambda j: (0, jnp.minimum(j, number - 1))),
            pl.BlockSpec((depth, 3 * TILE), lambda j: (0, jnp.maximum(j - number, 0))),
            pl.BlockSpec((depth, 3 * size), lambda j: (0, head(j))),
            column,
            block,
            block,
        ],
        out_specs=[
            tile,
            tile,
            pl.BlockSpec((TILE, depth), lambda j: (j, 0)),
            column,
            column,
            column,
            column,
            block,
        ],
        out_shape=[
            shape((depth, tiles * TILE), f32),
            shape((depth, tiles * TILE), f32),
            shape((tiles * TILE, depth), f32),
            shape((depth, width), f32),
            shape((depth, width), f32),
            shape((depth, width), f32),
            shape((depth, width), f32),
            shape(grad_tokens.shape, f32),
        ],
        compiler_params=pltpu.CompilerParams(vmem_limit_bytes=24 * MIB),
    )(sums, rest, mixed, out, grad_attended, grad_tokens)


def local(
    inputs,
    g_attn,
    w_query,
    w_key,
    w_value,
    w_beta,
    conv_taps,
    o_gain,
    w_out,
    g_mlp,
    w_gate,
    w_up,
    w_down,
    cotangent,
):
    count = lax.axis_size("fsdp")
    position = lax.axis_index("seq")
    groups = lax.axis_size("seq")
    tokens_low = inputs[0]
    rows, width = tokens_low.shape
    heads = w_beta.shape[1]
    size = width // heads
    depth = w_query.shape[0]
    small = (g_attn.shape, g_mlp.shape, o_gain.shape, conv_taps.shape)
    packed = pack_small((g_attn[None], g_mlp[None], o_gain[None]), conv_taps[None])
    if depth % 128 == 0:
        mixed, down_t = arrange(w_query, w_key, w_value, w_down, heads)
    else:
        mixed = jnp.stack([w.reshape(depth, -1, size) for w in (w_query, w_key, w_value)], axis=2)
        mixed, down_t = mixed.reshape(depth, 3 * width), jnp.transpose(w_down)
    shards = (
        packed,
        jnp.pad(w_beta, ((0, 0), (0, 128 - heads))),
        mixed,
        w_out,
        w_gate,
        w_up,
        down_t,
    )
    results = forward(tokens_low, shards, heads, conv_taps.shape[1])
    packed, w_beta, w_mixed, w_out, w_gate, w_up, w_down_t = results[:ARRAYS]
    finals, _, normed_t, signals, logits, taps = results[ARRAYS : ARRAYS + 6]
    outputs, carries, fresh, inverses, starts = results[ARRAYS + 6 :]
    g_attn, g_mlp, o_gain, _ = unpack_small(packed, small)
    g_attn, g_mlp, o_gain = g_attn.reshape(-1), g_mlp.reshape(-1), o_gain.reshape(-1)

    gain_out = o_gain.reshape(1, size)
    head_rows, state_in = mix(position.reshape(1), outputs, carries, finals, gain_out)
    tiles = w_gate.shape[1] // TILE
    beside = depth % 64 == 0
    number = tiles - 4 if beside else 0
    layer_out, grad_gain_mlp, grad_out_matrix, grad_attended, grad_heads, rest, sums = dense(
        head_rows,
        tokens_low,
        w_out,
        g_mlp.reshape(1, -1),
        cotangent[0],
        w_gate,
        w_up,
        w_down_t,
        number,
    )
    grad_delta, grad_gain_out, grad_starts = unmix(
        outputs, carries, state_in, gain_out, grad_heads
    )
    full = (rest, grad_out_matrix.reshape(count // 2, 2, depth, width))
    results = backward(
        signals,
        logits,
        taps,
        grad_delta,
        fresh,
        inverses,
        starts,
        state_in,
        finals,
        grad_starts,
        w_mixed,
        w_beta,
        g_attn.reshape(1, -1),
        grad_gain_mlp,
        grad_gain_out,
        normed_t,
        tokens_low,
        full if beside else (),
        small[3][1],
        small[0][0],
    )
    grad_from_attn, full_sums = results[0], results[1:-3]
    grad_mixed_matrix, grad_beta_matrix, packed = results[-3:]
    if beside and depth % 128 == 0:
        (
            grad_gate_matrix,
            grad_up_matrix,
            grad_down_matrix,
            grad_query_matrix,
            grad_key_matrix,
            grad_value_matrix,
            grad_out_matrix,
            grad_inputs,
        ) = deliver(
            number,
            sums,
            full_sums[0],
            grad_mixed_matrix,
            full_sums[1],
            grad_attended,
            grad_from_attn,
            heads,
        )
    else:
        if beside:
            sums, grad_out_matrix = jnp.concatenate([sums, full_sums[0]], axis=1), full_sums[1]
        else:
            sums, grad_out_matrix = (
                lax.psum(
                    lax.psum_scatter(
                        g.reshape((count,) + g.shape[2:]), "fsdp", scatter_dimension=0
                    ),
                    "seq",
                )
                for g in full
            )
        sums = sums.astype(f32).reshape(depth, tiles, 3, TILE)
        grad_gate_matrix, grad_up_matrix, grad_down_t = (
            sums[:, :, which].reshape(depth, tiles * TILE) for which in range(3)
        )
        grad_down_matrix = jnp.transpose(grad_down_t)
        grad_mixed_matrix = grad_mixed_matrix.astype(f32).reshape(depth, heads, 3, size)
        grad_query_matrix, grad_key_matrix, grad_value_matrix = (
            grad_mixed_matrix[:, :, which].reshape(depth, width) for which in range(3)
        )
        grad_out_matrix = grad_out_matrix.astype(f32)
        grad_inputs = grad_attended + grad_from_attn
    parts = [part[0].astype(f32) for part in unpack_small(packed, small)]
    grad_gain_attn, grad_gain_mlp, grad_gain_out, grad_taps = parts
    return (
        layer_out[None],
        grad_inputs[None],
        grad_gain_attn,
        grad_query_matrix,
        grad_key_matrix,
        grad_value_matrix,
        grad_beta_matrix[:, :heads].astype(f32),
        grad_taps,
        grad_gain_out,
        grad_out_matrix,
        grad_gain_mlp,
        grad_gate_matrix,
        grad_up_matrix,
        grad_down_matrix,
    )


def solution(mesh):
    vector = P("fsdp")
    rows = P("fsdp", None)
    columns = P(None, "fsdp")
    tokens = P("fsdp", "seq", None)
    return jax.shard_map(
        local,
        mesh=mesh,
        in_specs=(
            tokens,
            vector,
            rows,
            rows,
            rows,
            rows,
            columns,
            vector,
            rows,
            vector,
            rows,
            rows,
            columns,
            tokens,
        ),
        out_specs=(
            tokens,
            tokens,
            vector,
            rows,
            rows,
            rows,
            rows,
            columns,
            vector,
            rows,
            vector,
            rows,
            rows,
            columns,
        ),
        check_vma=False,
    )
```

```python
import functools

import jax
import jax.numpy as jnp
from jax import lax
from jax.experimental import pallas as pl
from jax.experimental.pallas import tpu as pltpu
from jax.sharding import PartitionSpec as P

CHUNK = 256
HALO = 16
TAPS = 4
MIB = 1024 * 1024

highest = lax.Precision.HIGHEST
epsilon = 1e-06
f32 = jnp.float32
bf16 = jnp.bfloat16


def nn(left_side, right_side):
    return lax.dot_general(
        left_side, right_side, (((1,), (0,)), ((), ())), preferred_element_type=f32
    )


def nt(left_side, right_side):
    return lax.dot_general(
        left_side, right_side, (((1,), (1,)), ((), ())), preferred_element_type=f32
    )


def tn(left_side, right_side):
    return lax.dot_general(
        left_side, right_side, (((0,), (0,)), ((), ())), preferred_element_type=f32
    )


def rms_scale(values, gain_vec):
    return (
        values * lax.rsqrt(jnp.mean(values * values, axis=-1, keepdims=True) + epsilon) * gain_vec
    )


def norm_backward(values, gain_vec, grad_out):
    scaling = lax.rsqrt(jnp.mean(values * values, axis=-1, keepdims=True) + epsilon)
    unit_rows = values * scaling
    gain_grad = jnp.sum(grad_out * unit_rows, axis=0)
    scaled_grad = grad_out * gain_vec
    input_grad = scaling * (
        scaled_grad - unit_rows * jnp.mean(scaled_grad * unit_rows, axis=-1, keepdims=True)
    )
    return (input_grad, gain_grad)


MESH = pl.DeviceIdType.MESH


class Place:
    def __init__(self, count):
        self.count = count
        self.sides = 2 if count % 2 == 0 else 1
        self.length = count // self.sides
        self.position = lax.axis_index("seq")
        self.index = lax.axis_index("fsdp")
        self.core = lax.rem(self.position, 2)
        self.chip = lax.div(self.position, 2)
        self.side = lax.rem(self.index, self.sides)
        self.spot = lax.div(self.index, self.sides)

    def sibling(self):
        return {"seq": self.position + 1 - 2 * self.core, "fsdp": self.index}

    def across(self):
        return {"seq": lax.rem(self.position + 2, 4), "fsdp": self.index}

    def partner(self):
        return {"seq": self.position, "fsdp": self.spot * 2 + 1 - self.side}

    def ahead(self, step):
        spot = lax.rem(self.spot + step, self.length)
        return {"seq": self.position, "fsdp": spot * self.sides + self.side}

    def shard(self, spot, side):
        return spot * self.sides + side

    def behind(self, step):
        return lax.rem(self.spot + self.length - step, self.length)

    def greet_all(self):
        self.greet(False, True)

    def greet(self, across, sequence=False):
        barrier = pltpu.get_barrier_semaphore()
        total = self.length - 1

        def signal(device):
            pl.semaphore_signal(barrier, inc=1, device_id=device, device_id_type=MESH)

        def one(step, carry):
            signal(self.ahead(step))
            return carry

        lax.fori_loop(1, self.length, one, 0)
        if sequence:
            for hop in range(1, 4):
                signal({"seq": lax.rem(self.position + hop, 4), "fsdp": self.index})
            total += 3
        else:
            signal(self.sibling())
            total += 1
        if self.sides == 2:
            signal(self.partner())
            total += 1
        if across:
            signal(self.across())
            total += 1
        pl.semaphore_wait(barrier, total)


def remote(source, target, send, recv, device):
    return pltpu.make_async_remote_copy(
        src_ref=source,
        dst_ref=target,
        send_sem=send,
        recv_sem=recv,
        device_id=device,
        device_id_type=MESH,
    )


def steps(first, last, body):
    def one(step, carry):
        body(step)
        return carry

    lax.fori_loop(first, last, one, 0)


class Reduce:
    BUFFERS = 6

    def __init__(self, count, pieces, sources, targets, buffers, staging, sems):
        self.place = Place(count)
        self.pieces, self.sources, self.targets, self.staging = pieces, sources, targets, staging
        self.acc, self.x_in, self.y_in, self.z_in, self.parts_in, self.result = buffers
        (
            self.core_sem,
            self.load_sem,
            self.x_sem,
            self.y_sem,
            self.z_sem,
            self.share_sem,
            self.final_sem,
            self.store_sem,
        ) = sems

    @staticmethod
    def buffers(count, pieces):
        length = count // 2
        acc, x_in, y_in, z_in, parts_in, result = [], [], [], [], [], []
        for depth, width, parts in pieces:
            rows = depth // parts
            acc.append(pltpu.VMEM((length, 2, depth // min(parts, 2), width), bf16))
            x_in.append(
                pltpu.VMEM((length, 2, rows, width) if parts == 4 else (1, 1, 16, 128), bf16)
            )
            y_in.append(pltpu.VMEM((length, rows, width), bf16))
            z_in.append(pltpu.VMEM((length, rows, width), bf16))
            parts_in.append(
                pltpu.VMEM((4 // parts, rows, width) if parts < 4 else (1, 16, 128), bf16)
            )
            result.append(pltpu.VMEM((rows, width), bf16))
        return acc + x_in + y_in + z_in + parts_in + result

    @staticmethod
    def semaphores(count, number):
        pair = pltpu.SemaphoreType.DMA((number, 2))
        one = pltpu.SemaphoreType.DMA((number,))
        hops = pltpu.SemaphoreType.DMA((number, 2, 4))
        return [pair, one, pair, pair, pair, hops, hops, one]

    def half(self, p, core):
        depth, _, parts = self.pieces[p]
        rows = depth // min(parts, 2)
        return pl.ds(pl.multiple_of(core * rows, 16) if parts > 1 else 0, rows)

    def quarter(self, p, chip):
        depth, _, parts = self.pieces[p]
        rows = depth // parts
        return pl.ds(pl.multiple_of(chip * rows, 16) if parts == 4 else 0, rows)

    def device(self, hop):
        return {"seq": lax.rem(self.place.position + hop, 4), "fsdp": self.place.index}

    def to_sibling(self, p):
        return remote(
            self.sources[p].at[:, :, self.half(p, 1 - self.place.core), :],
            self.acc[p],
            self.core_sem.at[p, 0],
            self.core_sem.at[p, 1],
            self.place.sibling(),
        )

    def stage(self, p):
        depth, width, parts = self.pieces[p]
        return self.staging.at[p % 2, :, :, pl.ds(0, depth // 2), pl.ds(0, width)]

    def load(self, p):
        return pltpu.make_async_copy(
            self.sources[p].at[:, :, self.half(p, self.place.core), :],
            self.stage(p),
            self.load_sem.at[p],
        )

    def to_x(self, p):
        return remote(
            self.acc[p].at[:, :, self.quarter(p, 1 - self.place.chip), :],
            self.x_in[p],
            self.x_sem.at[p, 0],
            self.x_sem.at[p, 1],
            self.place.across(),
        )

    def to_y(self, p):
        place = self.place
        return remote(
            self.acc[p].at[:, 1 - place.side, self.quarter(p, place.chip), :],
            self.y_in[p],
            self.y_sem.at[p, 0],
            self.y_sem.at[p, 1],
            place.partner(),
        )

    def to_z(self, p, step):
        place = self.place
        spot = lax.rem(place.spot + step, place.length)
        return remote(
            self.acc[p].at[spot, place.side, self.quarter(p, place.chip), :],
            self.z_in[p].at[step],
            self.z_sem.at[p, 0],
            self.z_sem.at[p, 1],
            place.ahead(step),
        )

    def all_z(self, p):
        both = self.z_in[p].at[pl.ds(1, self.place.length - 1)]
        return remote(
            both, both, self.z_sem.at[p, 0], self.z_sem.at[p, 1], self.place.ahead(1)
        )

    def sharers(self, p):
        return {1: (1, 2, 3), 2: (2,), 4: ()}[self.pieces[p][2]]

    def receivers(self, p):
        return {1: (), 2: (0,), 4: (1, 2, 3)}[self.pieces[p][2]]

    def sharer(self, p, position):
        return position if self.pieces[p][2] == 1 else lax.div(position, 2)

    def to_share(self, p, hop, arriving=False):
        position = self.place.position
        source = lax.rem(position + 4 - hop, 4) if arriving else position
        buffer = self.parts_in[p].at[self.sharer(p, source)]
        return remote(
            buffer,
            buffer,
            self.share_sem.at[p, 0, hop],
            self.share_sem.at[p, 1, hop],
            self.device(hop),
        )

    def target(self, p, position):
        depth, _, parts = self.pieces[p]
        rows = depth // parts
        core, chip = lax.rem(position, 2), lax.div(position, 2)
        first = {1: 0, 2: core * rows, 4: (core * 2 + chip) * rows}[parts]
        return self.targets[p].at[pl.ds(pl.multiple_of(first, 16) if parts > 1 else 0, rows), :]

    def to_result(self, p, hop, arriving=False):
        place = self.place
        if hop == 0:
            other = place.position + 1 - 2 * place.core
            device = place.sibling()
        else:
            other = lax.rem(place.position + 4 - hop, 4)
            device = self.device(hop)
        return remote(
            self.result[p],
            self.target(p, other if arriving else place.position),
            self.final_sem.at[p, 0, hop],
            self.final_sem.at[p, 1, hop],
            device,
        )

    def store(self, p):
        return pltpu.make_async_copy(
            self.result[p], self.target(p, self.place.position), self.store_sem.at[p]
        )

    def start(self, p, loaded):
        if self.pieces[p][2] > 1:
            self.to_sibling(p).start()
        if loaded:
            self.load(p).start()

    def on_core(self, p, loaded):
        parts = self.pieces[p][2]
        acc = self.acc[p]
        half = self.half(p, self.place.core)
        rows, width = acc.shape[2], acc.shape[3]
        if loaded:
            self.load(p).wait()
        if parts == 1:
            acc[...] = self.sources[p][...]
        else:
            self.to_sibling(p).wait_recv()

            def add(spot):
                if loaded:
                    own = self.staging[p % 2, spot, :, pl.ds(0, rows), pl.ds(0, width)]
                else:
                    own = self.sources[p][spot, :, half, :]
                acc[spot] = acc[spot] + own

            steps(0, self.place.length, add)
        (self.to_x if parts == 4 else self.to_y)(p).start()
        if parts > 1:
            self.to_sibling(p).wait_send()

    def on_x(self, p):
        acc, side = self.acc[p], 1 - self.place.side
        rows = self.quarter(p, self.place.chip)
        self.to_x(p).wait_recv()

        def add(spot):
            acc[spot, side, rows, :] = acc[spot, side, rows, :] + self.x_in[p][spot, side]

        steps(0, self.place.length, add)
        self.to_y(p).start()

    def on_y(self, p):
        place = self.place
        acc = self.acc[p]
        rows = self.quarter(p, place.chip)
        self.to_y(p).wait_recv()

        def one(step):
            spot = lax.rem(place.spot + step, place.length)
            total = acc[spot, place.side, rows, :].astype(f32) + self.y_in[p][spot].astype(f32)
            if self.pieces[p][2] == 4:
                total = total + self.x_in[p][spot, place.side].astype(f32)
            acc[spot, place.side, rows, :] = total.astype(bf16)

        def send(step):
            one(step)
            self.to_z(p, step).start()

        steps(1, place.length, send)
        one(0)

    def on_z(self, p):
        place = self.place
        rows = self.quarter(p, place.chip)
        self.all_z(p).wait_recv()
        total = self.acc[p][place.spot, place.side, rows, :].astype(f32)
        if place.length <= 8:
            for step in range(1, place.length):
                total = total + self.z_in[p][step].astype(f32)
        else:
            total = lax.fori_loop(
                1,
                place.length,
                lambda step, carry: carry + self.z_in[p][step].astype(f32),
                total,
            )
        if self.pieces[p][2] == 4:
            self.result[p][...] = total.astype(bf16)
            self.publish(p)
        else:
            self.parts_in[p][self.sharer(p, place.position)] = total.astype(bf16)
            for hop in self.sharers(p):
                self.to_share(p, hop).start()

    def on_share(self, p):
        total = None
        for hop in self.sharers(p):
            self.to_share(p, hop, True).wait_recv()
        for index in range(4 // self.pieces[p][2]):
            term = self.parts_in[p][index].astype(f32)
            total = term if total is None else total + term
        self.result[p][...] = total.astype(bf16)
        self.publish(p)

    def publish(self, p):
        for hop in self.receivers(p):
            self.to_result(p, hop).start()
        self.store(p).start()

    def finish(self, p):
        if self.pieces[p][2] == 4:
            self.to_x(p).wait_send()
        self.to_y(p).wait_send()
        self.all_z(p).wait_send()
        for hop in self.sharers(p):
            self.to_share(p, hop).wait_send()
        for hop in self.receivers(p):
            self.to_result(p, hop).wait_send()
            self.to_result(p, hop, True).wait_recv()
        self.store(p).wait()

    def plan(self, begin, stride, last, loaded, idle=()):
        due = []
        for p, (_, _, parts) in enumerate(self.pieces):
            for index, kind in enumerate((0, 1, 2, 3) if parts == 4 else (0, 2, 3, 4)):
                half = begin[p] + stride[p] * index
                while half in idle:
                    half += 1
                due.append((half, -index, p, kind))
        due.sort()

        def action(p, kind):
            if kind == 0:
                self.on_core(p, loaded[p])
                if loaded[p] and p + 2 < len(self.pieces) and loaded[p + 2]:
                    self.start(p + 2, True)
            else:
                (self.on_x, self.on_y, self.on_z, self.on_share)[kind - 1](p)

        def at(test):
            return [functools.partial(action, p, kind) for half, _, p, kind in due if test(half)]

        return (
            {half: at(lambda when: when == half) for half in range(last + 1)},
            at(lambda when: when > last),
        )


class Gather:
    SEMS = 6

    def __init__(self, count, pieces, shards, outs, sems):
        self.place = Place(count)
        self.pieces, self.shards, self.outs = pieces, shards, outs
        self.line_sem, self.side_sem, self.core_sem, self.across_sem, self.relay_sem, self.own = (
            sems
        )

    @staticmethod
    def scratch(pieces, count):
        length = count // 2 if count % 2 == 0 else count
        number = len(pieces)
        slots = 2 * length if max(piece[3] for piece in pieces) > 1 else 1
        return [
            pltpu.SemaphoreType.DMA((number, 2, length)),
            pltpu.SemaphoreType.DMA((number, 2, length)),
            pltpu.SemaphoreType.DMA((number, 2, slots)),
            pltpu.SemaphoreType.DMA((number, 2, slots)),
            pltpu.SemaphoreType.DMA((number, 2, slots)),
            pltpu.SemaphoreType.DMA((number,)),
        ]

    def portion(self, k, core, chip):
        parts = self.pieces[k][3]
        if parts == 1:
            return 0
        return core if parts == 2 else 2 * chip + core

    def region(self, k, shard, core, chip):
        a, offset, width, parts = self.pieces[k]
        depth = self.shards[a].shape[0]
        rows = depth // parts
        first = shard * depth + self.portion(k, core, chip) * rows
        return self.outs[a].at[pl.ds(pl.multiple_of(first, 16), rows), pl.ds(offset, width)]

    def source(self, k):
        p = self.place
        a, offset, width, parts = self.pieces[k]
        rows = self.shards[a].shape[0] // parts
        first = self.portion(k, p.core, p.chip) * rows
        return self.shards[a].at[pl.ds(pl.multiple_of(first, 16), rows), pl.ds(offset, width)]

    def line(self, k, step, arriving=False):
        p = self.place
        shard = p.shard(p.behind(step), p.side) if arriving else p.index
        target = self.region(k, shard, p.core, p.chip)
        return remote(
            target if arriving else self.source(k),
            target,
            self.line_sem.at[k, 0, step],
            self.line_sem.at[k, 1, step],
            p.ahead(step),
        )

    def side(self, k, step, arriving=False, own=False):
        p = self.place
        shard = p.shard(p.behind(step), 1 - p.side if arriving else p.side)
        target = self.region(k, shard, p.core, p.chip)
        return remote(
            self.source(k) if own else target,
            target,
            self.side_sem.at[k, 0, step],
            self.side_sem.at[k, 1, step],
            p.partner(),
        )

    def cross(self, k, step, other, sems, core, chip, device):
        p = self.place
        shard = p.shard(p.behind(step), 1 - p.side if other else p.side)
        target = self.region(k, shard, core, chip)
        slot = 2 * step + (1 if other else 0)
        return remote(target, target, sems.at[k, 0, slot], sems.at[k, 1, slot], device)

    def core(self, k, step, other, arriving=False):
        p = self.place
        core = 1 - p.core if arriving else p.core
        return self.cross(k, step, other, self.core_sem, core, p.chip, p.sibling())

    def across(self, k, step, other, arriving=False):
        p = self.place
        chip = 1 - p.chip if arriving else p.chip
        return self.cross(k, step, other, self.across_sem, p.core, chip, p.across())

    def relay(self, k, step, other, arriving=False):
        p = self.place
        core = 1 - p.core if arriving else p.core
        return self.cross(k, step, other, self.relay_sem, core, 1 - p.chip, p.sibling())

    def keep(self, k):
        a, offset, width, _ = self.pieces[k]
        depth = self.shards[a].shape[0]
        rows = pl.ds(pl.multiple_of(self.place.index * depth, 16), depth)
        columns = pl.ds(offset, width)
        return pltpu.make_async_copy(
            self.shards[a].at[:, columns], self.outs[a].at[rows, columns], self.own.at[k]
        )

    def hand(self, k, step, other):
        parts = self.pieces[k][3]
        if parts == 4:
            self.across(k, step, other).start()
        if parts > 1:
            self.core(k, step, other).start()

    def start(self, k):
        steps(1, self.place.length, lambda step: self.line(k, step).start())
        if self.place.sides == 2:
            self.side(k, 0, own=True).start()
        self.keep(k).start()

    def forward(self, k):
        def one(step):
            self.line(k, step, True).wait_recv()
            if self.place.sides == 2:
                self.side(k, step).start()
            self.hand(k, step, False)

        steps(1, self.place.length, one)

    def spread(self, k):
        def one(step):
            self.side(k, step, True).wait_recv()
            self.hand(k, step, True)

        if self.place.sides == 2:
            steps(0, self.place.length, one)

    def each(self, body):
        steps(1, self.place.length, lambda step: body(step, False))
        if self.place.sides == 2:
            steps(0, self.place.length, lambda step: body(step, True))

    def exchange(self, k):
        def one(step, other):
            self.across(k, step, other, True).wait_recv()
            self.relay(k, step, other).start()

        if self.pieces[k][3] == 4:
            self.each(one)

    def arrive(self, k):
        parts = self.pieces[k][3]

        def one(step, other):
            self.core(k, step, other, True).wait_recv()
            if parts == 4:
                self.relay(k, step, other, True).wait_recv()

        self.keep(k).wait()
        if parts > 1:
            self.each(one)

    def sent(self, k):
        parts = self.pieces[k][3]

        def one(step, other):
            self.core(k, step, other).wait_send()
            if parts == 4:
                self.across(k, step, other).wait_send()
                self.relay(k, step, other).wait_send()

        steps(1, self.place.length, lambda step: self.line(k, step).wait_send())
        if self.place.sides == 2:
            steps(0, self.place.length, lambda step: self.side(k, step).wait_send())
        if parts > 1:
            self.each(one)

    def events(self, tiles, urgent, ahead=4):
        made = []
        line = side = across = 0.0
        hop = 8.0
        number = len(self.pieces)
        for k in range(number):
            parts = self.pieces[k][3]
            margin = 8.0 if k < urgent else 30.0
            load = tiles[k] * (2 if parts == 4 else 4)
            line = line + load
            side = max(side + load, line + load / 4 + hop)
            last = side
            made.append((line + hop, k, 0))
            made.append((side + hop, k, 1))
            if parts == 4:
                across = max(across + 3.5 * tiles[k], side + tiles[k] / 2 + hop)
                last = across
                made.append((across + hop + margin, k, 2))
            wait = 0.0 if k < urgent else 2 * margin
            made.append((last + 2 * hop + wait + (margin if parts == 4 else 0.0), k, 3))
        made.sort()

        def action(k, kind):
            if kind == 0:
                self.forward(k)
                if k + ahead < number:
                    self.start(k + ahead)
            else:
                (self.spread, self.exchange, self.arrive)[kind - 1](k)

        return [(when, k, kind, functools.partial(action, k, kind)) for when, k, kind in made]


PACK = (16, 512)


def pack_small(gains, taps):
    count = taps.shape[0]

    def fit(values, rows):
        values = values.reshape(count, -1, values.shape[-1]).astype(bf16)
        return jnp.pad(
            values, ((0, 0), (0, rows - values.shape[1]), (0, PACK[1] - values.shape[2]))
        )

    rows = [fit(gains[0], 1), fit(gains[1], 1), fit(gains[2], 2), fit(taps, PACK[0] - 4)]
    return jnp.concatenate(rows, axis=1).reshape(count * PACK[0], PACK[1])


def unpack_small(packed, shapes):
    packed = packed.reshape(-1, PACK[0], PACK[1])
    gains = [packed[:, row, : shape[0]] for row, shape in enumerate(shapes[:3])]
    return gains + [packed[:, 4 : 4 + shapes[3][0], : shapes[3][1]]]


def place_rows(packed, count, width):
    if width % 128 == 0:
        return jnp.concatenate(
            [packed[s * PACK[0] : (s + 1) * PACK[0], :width] for s in range(count)], axis=1
        )
    total = count * width
    row = lax.broadcasted_iota(jnp.int32, (PACK[1], total), 0)
    col = lax.broadcasted_iota(jnp.int32, (PACK[1], total), 1)
    pick = jnp.where(lax.rem(col, width) == row, 1.0, 0.0).astype(bf16)
    wide = nn(packed.astype(bf16), pick)
    row = lax.broadcasted_iota(jnp.int32, wide.shape, 0)
    col = lax.broadcasted_iota(jnp.int32, wide.shape, 1)
    wide = jnp.where(lax.div(row, PACK[0]) == lax.div(col, width), wide, 0.0).astype(bf16)
    row = lax.broadcasted_iota(jnp.int32, (PACK[0], count * PACK[0]), 0)
    col = lax.broadcasted_iota(jnp.int32, (PACK[0], count * PACK[0]), 1)
    fold = jnp.where(lax.rem(col, PACK[0]) == row, 1.0, 0.0).astype(bf16)
    return nn(fold, wide)


GROUP = 2


def grid_indices():
    row = lax.broadcasted_iota(jnp.int32, (CHUNK, CHUNK), 0)
    col = lax.broadcasted_iota(jnp.int32, (CHUNK, CHUNK), 1)
    return row, col


def conv_pre(wide_ref, taps, rows):
    total = None
    for offset in range(TAPS):
        term = taps[offset : offset + 1, :] * wide_ref[pl.ds(HALO - TAPS + 1 + offset, rows), :]
        total = term if total is None else total + term
    return total


def sigmoid(values):
    return 1.0 / (1.0 + jnp.exp(-values))


def head_column(table, head):
    lane = lax.broadcasted_iota(jnp.int32, table.shape, 1)
    return jnp.sum(jnp.where(lane == head, table, 0.0), axis=1, keepdims=True)


ARRAYS = 7


def forward_kernel(count, pieces, mixed, heads, tap_width, *refs):
    tokens_ref = refs[0]
    shards, refs = refs[1 : 1 + ARRAYS], refs[1 + ARRAYS :]
    gathered, refs = refs[:ARRAYS], refs[ARRAYS:]
    (
        finals_ref,
        normed_ref,
        normed_t_ref,
        signals_ref,
        logit_ref,
        taps_ref,
        out_ref,
        carry_ref,
        fresh_ref,
        inverse_ref,
        starts_ref,
    ), refs = refs[:11], refs[11:]
    (
        tokens,
        weights,
        rates_weight,
        packed,
        all_taps,
        wide,
        level_masks,
        final,
        halo_sem,
        token_sem,
        load_sem,
        final_sem,
        *sems,
    ) = refs
    group = pl.program_id(0)
    groups = heads // GROUP
    rows = out_ref.shape[0]
    size = out_ref.shape[1] // GROUP
    span = GROUP * size
    chunks = rows // CHUNK
    levels = CHUNK.bit_length() - 1
    row, col = grid_indices()
    gather = Gather(count, pieces, shards, gathered, sems)
    place = gather.place
    tiles = [piece[2] / 128 * shards[piece[0]].shape[0] / 128 for piece in pieces]
    events = gather.events(tiles, 2 + groups)

    def halo(arriving):
        return remote(
            tokens_ref.at[pl.ds(rows - HALO, HALO), :],
            tokens.at[pl.ds(0, HALO), :],
            halo_sem.at[0],
            halo_sem.at[1],
            {"seq": lax.rem(place.position + 1, 4), "fsdp": place.index},
        )

    def load(step, slot):
        return pltpu.make_async_copy(
            gathered[mixed].at[:, pl.ds(pl.multiple_of(step * 3 * span, 128), 3 * span)],
            weights.at[slot],
            load_sem.at[slot],
        )

    per_step = 12
    plan = {}
    mark = 0
    for step in range(groups):
        for spot in range(per_step):
            now = 50.0 + (step * per_step + spot) * 5.5
            upto = mark
            for index in range(mark, len(events)):
                when, k, kind, _ = events[index]
                if spot == 0 and kind == 3 and (k == 2 + step or (step == 0 and k < 2)):
                    upto = index + 1
                elif when <= now and upto == index:
                    upto = index + 1
            plan[step, spot] = (mark, upto)
            mark = upto
    remaining = (mark, len(events))

    def run(bounds):
        for _, _, _, action in events[bounds[0] : bounds[1]]:
            action()

    def spot(number):
        for step in range(groups):
            bounds = plan[step, number]
            if bounds[1] > bounds[0]:

                @pl.when(group == step)
                def _():
                    run(bounds)

    @pl.when(group == 0)
    def _():
        own = pltpu.make_async_copy(tokens_ref, tokens.at[pl.ds(HALO, rows), :], token_sem.at[0])
        own.start()
        place.greet_all()

        @pl.when(place.position < 3)
        def _():
            halo(False).start()

        gather.start(0)
        gather.start(1)
        gather.start(2)
        gather.start(3)

        @pl.when(place.position == 0)
        def _():
            tokens[pl.ds(0, HALO), :] = jnp.zeros((HALO, tokens.shape[1]), bf16)

        for level in range(levels):
            same = (row >> (level + 1)) == (col >> (level + 1))
            below = ((row >> level) & 1 == 1) & ((col >> level) & 1 == 0)
            level_masks[level] = jnp.where(same & below, 1.0, 0.0).astype(bf16)

        limit = max(i for i, event in enumerate(events) if event[1] == 0) + 1
        run((0, limit))
        copy = pltpu.make_async_copy(gathered[0], packed, token_sem.at[1])
        copy.start()
        copy.wait()
        small = packed[...].astype(f32)
        gain = place_rows(small, count, tokens.shape[1] // count)[0:1, :]
        all_taps[...] = place_rows(small, count, tap_width)[4 : 4 + TAPS, :]
        own.wait()

        @pl.when(place.position > 0)
        def _():
            halo(True).wait_recv()

        block = 208 if tokens.shape[0] % 208 == 0 else HALO

        def norm(index):
            part = pl.ds(pl.multiple_of(index * block, HALO), block)
            normed_ref[part, :] = rms_scale(tokens[part, :].astype(f32), gain).astype(bf16)

        steps(0, tokens.shape[0] // block, norm)
        for first in range(0, rows, CHUNK):
            part = normed_ref[pl.ds(HALO + first, CHUNK), :]
            normed_t_ref[:, first : first + CHUNK] = part.T
        run((limit, plan[0, 0][1]))
        copy = pltpu.make_async_copy(gathered[1], rates_weight, token_sem.at[1])
        copy.start()
        load(0, 0).start()
        copy.wait()
        logit_ref[...] = nn(normed_ref[pl.ds(HALO, rows), :], rates_weight[...]).astype(bf16)
        load(0, 0).wait()

    for step in range(1, groups):
        bounds = plan[step, 0]

        @pl.when(group == step)
        def _():
            run(bounds)
            load(step, 0).start()
            load(step, 0).wait()

    signals_ref[...] = nn(normed_ref[...], weights[0]).astype(bf16)
    spot(1)

    lows = [[], [], []]
    for inner in range(GROUP):
        for which in range(3):
            first = pl.multiple_of((which * heads + group * GROUP + inner) * size, 128)
            taps = all_taps[:, pl.ds(first, size)]
            taps_ref[inner, which] = taps
            wide[...] = signals_ref[:, pl.ds((inner * 3 + which) * size, size)].astype(f32)
            pre = conv_pre(wide, taps, rows)
            act = pre * sigmoid(pre)
            if which < 2:
                act = act * lax.rsqrt(jnp.sum(act * act, axis=1, keepdims=True) + epsilon)
            lows[which].append(act.astype(bf16))
        if inner == 0:
            spot(2)
    spot(3)
    logits = logit_ref[...].astype(f32)
    rates = [sigmoid(head_column(logits, group * GROUP + inner)) for inner in range(GROUP)]
    scaling = size ** (-0.5)
    eye = jnp.where(row == col, 1.0, 0.0)
    lower = row >= col

    work = [(inner, chunk) for inner in range(GROUP) for chunk in range(chunks)]

    def cut(values, item):
        inner, chunk = item
        return values[inner][chunk * CHUNK : (chunk + 1) * CHUNK]

    queries, keys, values = lows
    stricts = [(cut(rates, i) * nt(cut(keys, i), cut(keys, i))).astype(bf16) for i in work]
    results = [eye - (strict * level_masks[0]).astype(f32) for strict in stricts]
    scores = [jnp.where(lower, nt(cut(queries, i), cut(keys, i)), 0.0).astype(bf16) for i in work]
    for level in range(1, levels):
        mask = level_masks[level]
        lowered = [result.astype(bf16) for result in results]
        inners = [nn(low, strict * mask).astype(bf16) for low, strict in zip(lowered, stricts)]
        results = [
            result - nn(inner, low) for result, inner, low in zip(results, inners, lowered)
        ]
        if level in (2, 4, 6):
            spot(3 + level // 2)
    inverses = [result.astype(bf16) for result in results]
    for (inner, chunk), inverse in zip(work, inverses):
        part = slice(chunk * CHUNK, (chunk + 1) * CHUNK)
        inverse_ref[part, inner * CHUNK : (inner + 1) * CHUNK] = inverse
    spot(7)

    srow = lax.broadcasted_iota(jnp.int32, (size, size), 0)
    scol = lax.broadcasted_iota(jnp.int32, (size, size), 1)
    memories = [
        jnp.concatenate(
            [jnp.zeros((size, size), f32), jnp.where(srow == scol, 1.0, 0.0)], axis=1
        )
    ] * GROUP
    for chunk in range(chunks):
        part = slice(chunk * CHUNK, (chunk + 1) * CHUNK)
        for inner in range(GROUP):
            item = (inner, chunk)
            key_part, query_part, rate_part = cut(keys, item), cut(queries, item), cut(rates, item)
            low_memory = memories[inner].astype(bf16)
            starts_ref[inner, chunk] = low_memory
            seen = nn(key_part, low_memory)
            aim = jnp.concatenate(
                [cut(values, item).astype(f32), jnp.zeros((CHUNK, size), f32)], axis=1
            )
            aim = (rate_part * (aim - seen)).astype(bf16)
            fresh = nn(inverses[work.index(item)], aim).astype(bf16)
            fresh_ref[part, inner * 2 * size : (inner + 1) * 2 * size] = fresh
            both = scaling * (
                nn(query_part, low_memory) + nn(scores[work.index(item)], fresh)
            )
            out_ref[part, inner * size : (inner + 1) * size] = both[:, :size]
            carry_ref[part, inner * size : (inner + 1) * size] = both[:, size:].astype(bf16)
            memories[inner] = memories[inner] + tn(key_part, fresh)
        if chunk < 3:
            spot(8 + chunk)

    def send_final(step, hop):
        position = lax.rem(place.position + hop, 4)
        block = pl.ds(step * GROUP, GROUP)
        return remote(
            final.at[block],
            finals_ref.at[place.position, block],
            final_sem.at[0, step, hop],
            final_sem.at[1, step, hop],
            {"seq": position, "fsdp": place.index},
        )

    def keep_final(step):
        block = pl.ds(step * GROUP, GROUP)
        return pltpu.make_async_copy(
            final.at[block], finals_ref.at[place.position, block], final_sem.at[0, step, 0]
        )

    def take_final(step, hop):
        position = lax.rem(place.position + 4 - hop, 4)
        block = pl.ds(step * GROUP, GROUP)
        return remote(
            final.at[block],
            finals_ref.at[position, block],
            final_sem.at[0, step, hop],
            final_sem.at[1, step, hop],
            {"seq": position, "fsdp": place.index},
        )

    for step in range(groups):

        @pl.when(group == step)
        def _():
            for inner in range(GROUP):
                final[step * GROUP + inner] = memories[inner].astype(bf16)
            for hop in range(1, 4):
                send_final(step, hop).start()
            keep_final(step).start()

    spot(11)

    @pl.when(group == groups - 1)
    def _():
        run(remaining)
        for k in range(len(pieces)):
            gather.sent(k)
        for step in range(groups):
            for hop in range(1, 4):
                send_final(step, hop).wait_send()
                take_final(step, hop).wait_recv()
            keep_final(step).wait()

        @pl.when(place.position < 3)
        def _():
            halo(False).wait_send()


def plan_pieces(depths, widths, span):
    def portions(a, wanted):
        while depths[a] % (16 * wanted) != 0:
            wanted //= 2
        return wanted

    pieces = [(0, 0, widths[0], 1), (1, 0, widths[1], portions(1, 2))]
    for step in range(widths[2] // span):
        pieces.append((2, step * span, span, portions(2, 4)))
    pieces.append((3, 0, widths[3], portions(3, 4)))
    for a in (4, 5, 6):
        half = widths[a] // 2
        for part in range(2):
            wanted = 2 if (a, part) in ((5, 0), (6, 1)) else 4
            pieces.append((a, part * half, half, portions(a, wanted)))
    return pieces


def forward(tokens, shards, heads, tap_width):
    count = lax.axis_size("fsdp")
    rows, width = tokens.shape
    size = width // heads
    span = GROUP * size
    groups = heads // GROUP
    chunks = rows // CHUNK
    wide_rows = rows + HALO
    depths = [shard.shape[0] for shard in shards]
    widths = [shard.shape[1] for shard in shards]
    pieces = plan_pieces(depths, widths, 3 * span)
    anywhere = pl.BlockSpec(memory_space=pl.ANY)
    shape = jax.ShapeDtypeStruct
    return pl.pallas_call(
        functools.partial(forward_kernel, count, pieces, 2, heads, tap_width),
        grid=(groups,),
        in_specs=[anywhere] * (1 + ARRAYS),
        out_specs=[anywhere] * (ARRAYS + 1)
        + [
            pl.BlockSpec((wide_rows, width), lambda g: (0, 0)),
            pl.BlockSpec((width, rows), lambda g: (0, 0)),
            pl.BlockSpec((wide_rows, 3 * span), lambda g: (0, g)),
            pl.BlockSpec((rows, widths[1]), lambda g: (0, 0)),
            pl.BlockSpec((GROUP, 3, TAPS, size), lambda g: (g, 0, 0, 0)),
            pl.BlockSpec((rows, span), lambda g: (0, g)),
            pl.BlockSpec((rows, span), lambda g: (0, g)),
            pl.BlockSpec((rows, 2 * span), lambda g: (0, g)),
            pl.BlockSpec((rows, GROUP * CHUNK), lambda g: (0, g)),
            pl.BlockSpec((GROUP, chunks, size, 2 * size), lambda g: (g, 0, 0, 0)),
        ],
        out_shape=[shape((count * d, w), bf16) for d, w in zip(depths, widths)]
        + [
            shape((4, heads, size, 2 * size), bf16),
            shape((wide_rows, width), bf16),
            shape((width, rows), bf16),
            shape((wide_rows, 3 * width), bf16),
            shape((rows, widths[1]), bf16),
            shape((heads, 3, TAPS, size), f32),
            shape((rows, width), f32),
            shape((rows, width), bf16),
            shape((rows, 2 * width), bf16),
            shape((rows, heads * CHUNK), bf16),
            shape((heads, chunks, size, 2 * size), bf16),
        ],
        scratch_shapes=[
            pltpu.VMEM((wide_rows, width), bf16),
            pltpu.VMEM((1, width, 3 * span), bf16),
            pltpu.VMEM((width, widths[1]), bf16),
            pltpu.VMEM((count * PACK[0], PACK[1]), bf16),
            pltpu.VMEM((TAPS, 3 * width), f32),
            pltpu.VMEM((wide_rows, size), f32),
            pltpu.VMEM((CHUNK.bit_length() - 1, CHUNK, CHUNK), bf16),
            pltpu.VMEM((heads, size, 2 * size), bf16),
            pltpu.SemaphoreType.DMA((2,)),
            pltpu.SemaphoreType.DMA((2,)),
            pltpu.SemaphoreType.DMA((2,)),
            pltpu.SemaphoreType.DMA((2, groups, 4)),
        ]
        + Gather.scratch(pieces, count),
        compiler_params=pltpu.CompilerParams(
            collective_id=0, has_side_effects=True, vmem_limit_bytes=60 * MIB
        ),
    )(tokens, *shards)


def mix_kernel(position_ref, out_ref, carry_ref, finals_ref, gain_ref, mixed_ref, state_ref):
    position = position_ref[0]
    size = out_ref.shape[1]
    state = jnp.zeros((size, size), f32)
    for index in range(finals_ref.shape[0] - 1):
        pair = finals_ref[index, 0]
        later = pair[:, :size].astype(f32) + nn(pair[:, size:], state.astype(bf16))
        state = jnp.where(index < position, later, state)
    state_ref[0] = state
    output = out_ref[...] + nn(carry_ref[...], state.astype(bf16))
    gain = gain_ref[...].astype(f32)
    mixed_ref[...] = rms_scale(output, gain).astype(bf16)


def mix(position, outputs, carries, finals, gain):
    rows, width = outputs.shape
    groups, heads, size, _ = finals.shape
    plain = pl.BlockSpec((rows, size), lambda h: (0, h))
    return pl.pallas_call(
        mix_kernel,
        grid=(heads,),
        in_specs=[
            pl.BlockSpec(memory_space=pltpu.SMEM),
            plain,
            plain,
            pl.BlockSpec((groups, 1, size, 2 * size), lambda h: (0, h, 0, 0)),
            pl.BlockSpec((1, size), lambda h: (0, 0)),
        ],
        out_specs=[plain, pl.BlockSpec((1, size, size), lambda h: (h, 0, 0))],
        out_shape=[
            jax.ShapeDtypeStruct((rows, width), bf16),
            jax.ShapeDtypeStruct((heads, size, size), f32),
        ],
        compiler_params=pltpu.CompilerParams(vmem_limit_bytes=32 * MIB),
    )(position, outputs, carries, finals, gain)


def unmix_kernel(
    heads,
    out_ref,
    carry_ref,
    state_ref,
    gain_ref,
    grad_ref,
    grad_out_ref,
    grad_gain_ref,
    grads_ref,
    grad_states,
    sems,
):
    head = pl.program_id(0)
    position, index = lax.axis_index("seq"), lax.axis_index("fsdp")

    def device(hop):
        return {"seq": lax.rem(position + hop, 4), "fsdp": index}

    def send(one, hop, arriving=False):
        source = lax.rem(position + 4 - hop, 4) if arriving else position
        return remote(
            grad_states.at[one],
            grads_ref.at[source, one],
            sems.at[0, one, hop],
            sems.at[1, one, hop],
            device(hop),
        )

    def keep(one):
        return pltpu.make_async_copy(
            grad_states.at[one], grads_ref.at[position, one], sems.at[0, one, 0]
        )

    @pl.when(head == 0)
    def _():
        barrier = pltpu.get_barrier_semaphore()
        for hop in range(1, 4):
            pl.semaphore_signal(barrier, inc=1, device_id=device(hop), device_id_type=MESH)
        grad_gain_ref[...] = jnp.zeros_like(grad_gain_ref)

    output = out_ref[...] + nn(carry_ref[...], state_ref[0].astype(bf16))
    gain = gain_ref[...].astype(f32)
    grad = grad_ref[...].astype(f32)
    scaling = lax.rsqrt(jnp.mean(output * output, axis=1, keepdims=True) + epsilon)
    unit_rows = output * scaling
    grad_gain_ref[...] += jnp.sum(grad * unit_rows, axis=0, keepdims=True)
    scaled = grad * gain
    grad_out = scaling * (scaled - unit_rows * jnp.mean(scaled * unit_rows, axis=1, keepdims=True))
    low_grad = grad_out.astype(bf16)
    grad_states[head] = tn(carry_ref[...], low_grad).astype(bf16)

    @pl.when(head == 0)
    def _():
        pl.semaphore_wait(pltpu.get_barrier_semaphore(), 3)

    for hop in range(1, 4):
        send(head, hop).start()
    keep(head).start()
    grad_out_ref[...] = (grad_out * output.shape[1] ** (-0.5)).astype(bf16)

    @pl.when(head == heads - 1)
    def _():
        def one(step):
            keep(step).wait()
            for hop in range(1, 4):
                send(step, hop).wait_send()
                send(step, hop, True).wait_recv()

        steps(0, heads, one)


def unmix(outputs, carries, states, gain, grad_heads):
    rows, width = outputs.shape
    heads, size, _ = states.shape
    plain = pl.BlockSpec((rows, size), lambda h: (0, h))
    state = pl.BlockSpec((1, size, size), lambda h: (h, 0, 0))
    vector = pl.BlockSpec((1, size), lambda h: (0, 0))
    return pl.pallas_call(
        functools.partial(unmix_kernel, heads),
        grid=(heads,),
        in_specs=[plain, plain, state, vector, plain],
        out_specs=[plain, vector, pl.BlockSpec(memory_space=pl.ANY)],
        out_shape=[
            jax.ShapeDtypeStruct((rows, width), bf16),
            jax.ShapeDtypeStruct((1, size), f32),
            jax.ShapeDtypeStruct((4, heads, size, size), bf16),
        ],
        scratch_shapes=[
            pltpu.VMEM((heads, size, size), bf16),
            pltpu.SemaphoreType.DMA((2, heads, 4)),
        ],
        compiler_params=pltpu.CompilerParams(
            collective_id=1, has_side_effects=True, vmem_limit_bytes=32 * MIB
        ),
    )(outputs, carries, states, gain, grad_heads)


TILE = 256
SLOTS = 3
DENSE_STRIDE = 4


def dense_kernel(count, shapes, *refs):
    (
        mixed_ref,
        w_out_ref,
        gain_ref,
        cotangent_ref,
        gate_ref,
        up_ref,
        down_ref,
        tokens_ref,
        layer_out_ref,
        grad_gain_ref,
        grad_out_ref,
        grad_attended_ref,
        grad_heads_ref,
        rest_ref,
        sums_ref,
        attended,
        normed,
        normed_t,
        cotangent_t,
        result,
        grad_normed,
        source,
        plain_sem,
        rest_sem,
    ), refs = refs[:24], refs[24:]
    tile = pl.program_id(0)
    rows, width = attended.shape
    depth = width // count
    number = len(shapes)
    tiles = number + rest_ref.shape[3] // (3 * TILE)
    blocks = [slice(first, first + CHUNK) for first in range(0, rows, CHUNK)]
    columns = [slice(first, first + CHUNK) for first in range(0, width, CHUNK)]
    gain = gain_ref[...].astype(f32)

    due, later, reduce = {}, [], None
    if number > 0:
        buffers = [refs[i * number : (i + 1) * number] for i in range(Reduce.BUFFERS)]
        sems = refs[Reduce.BUFFERS * number :]
        sources = [source.at[p % SLOTS] for p in range(number)]
        targets = [sums_ref.at[:, pl.ds(p * 3 * TILE, 3 * TILE)] for p in range(number)]
        reduce = Reduce(count, shapes, sources, targets, buffers, None, sems)
        begin = [2 * p + 3 for p in range(number)]
        due, later = reduce.plan(
            begin, [DENSE_STRIDE] * number, 2 * tiles - 1, [False] * number
        )

    def spot(which):
        for step in range(tiles):
            actions = due.get(2 * step + which, ())
            if actions:

                @pl.when(tile == step)
                def _():
                    for action in actions:
                        action()

    def rest(step):
        slot = lax.rem(step, SLOTS)
        first = pl.multiple_of((step - number) * 3 * TILE, 128)
        return pltpu.make_async_copy(
            source.at[slot], rest_ref.at[:, :, :, pl.ds(first, 3 * TILE)], rest_sem.at[slot]
        )

    def fetch(start, target, slot):
        return pltpu.make_async_copy(start, target, plain_sem.at[slot])

    @pl.when(tile == 0)
    def _():
        load = fetch(tokens_ref, normed, 0)
        load.start()
        if reduce is not None:
            reduce.place.greet_all()
        load.wait()
        for block in blocks:
            values = normed[block, :].astype(f32) + nn(mixed_ref[block, :], w_out_ref[...])
            attended[block, :] = values
            result[block, :] = values
            low = rms_scale(values, gain).astype(bf16)
            normed[block, :] = low
            normed_t[:, block] = low.T
            cotangent_t[:, block] = cotangent_ref[block, :].T
        grad_normed[...] = jnp.zeros_like(grad_normed)

    @pl.when(tile >= number + SLOTS)
    def _():
        rest(tile - SLOTS).wait()

    spot(0)
    gate = nn(normed[...], gate_ref[...])
    up = nn(normed[...], up_ref[...])
    grad_hidden = nn(cotangent_ref[...], down_ref[...])
    sig = sigmoid(gate)
    activated = gate * sig
    hidden = (activated * up).astype(bf16)
    grad_gate = (grad_hidden * up * sig * (1.0 + gate * (1.0 - sig))).astype(bf16)
    grad_up = (grad_hidden * activated).astype(bf16)
    slot = lax.rem(tile, SLOTS)
    for which, (left, right) in enumerate(
        ((normed_t, grad_gate), (normed_t, grad_up), (cotangent_t, hidden))
    ):
        piece = nn(left[...], right).astype(bf16).reshape(count // 2, 2, depth, TILE)
        source[slot, :, :, :, pl.ds(which * TILE, TILE)] = piece

    spot(1)
    for column in columns:
        result[:, column] += nt(hidden, down_ref[column, :])
        grad_normed[:, column] += nt(grad_gate, gate_ref[column, :]) + nt(
            grad_up, up_ref[column, :]
        )

    for p in range(number):

        @pl.when(tile == p)
        def _():
            reduce.start(p, False)

    @pl.when(tile >= number)
    def _():
        rest(tile).start()

    @pl.when(tile == tiles - 1)
    def _():
        gain_grad = jnp.zeros((1, width), f32)
        for block in blocks:
            layer_out_ref[block, :] = result[block, :].astype(bf16)
            values = attended[block, :]
            grad = grad_normed[block, :]
            scaling = lax.rsqrt(jnp.mean(values * values, axis=1, keepdims=True) + epsilon)
            unit = values * scaling
            gain_grad = gain_grad + jnp.sum(grad * unit, axis=0, keepdims=True)
            scaled = grad * gain
            grad = cotangent_ref[block, :].astype(f32) + scaling * (
                scaled - unit * jnp.mean(scaled * unit, axis=1, keepdims=True)
            )
            attended[block, :] = grad
            low = grad.astype(bf16)
            normed[block, :] = low
            normed_t[:, block] = mixed_ref[block, :].T
        fetch(attended, grad_attended_ref, 0).start()
        grad_gain_ref[...] = gain_grad
        for block in blocks:
            cotangent_t[block, :] = nt(normed[block, :], w_out_ref[...]).astype(bf16)
        fetch(cotangent_t, grad_heads_ref, 1).start()
        for action in later[: len(later) // 2]:
            action()
        for column in columns:
            grad_out_ref[column, :] = nn(normed_t[column, :], normed[...]).astype(bf16)
        for action in later[len(later) // 2 :]:
            action()
        for p in range(number):
            reduce.finish(p)
        for step in range(max(number, tiles - SLOTS), tiles):
            rest(step).wait()
        fetch(attended, grad_attended_ref, 0).wait()
        fetch(cotangent_t, grad_heads_ref, 1).wait()


def dense(mixed, tokens, w_out, gain, cotangent, w_gate, w_up, w_down_t, number):
    count = lax.axis_size("fsdp")
    rows, width = tokens.shape
    hidden = w_gate.shape[1]
    tiles = hidden // TILE
    depth = width // count
    shapes = [(depth, 3 * TILE, 2 if p % 2 == 0 else 4) for p in range(number)]
    whole = pl.BlockSpec((rows, width), lambda j: (0, 0))
    square = pl.BlockSpec((width, width), lambda j: (0, 0))
    vector = pl.BlockSpec((1, width), lambda j: (0, 0))
    slab = pl.BlockSpec((width, TILE), lambda j: (0, j))
    anywhere = pl.BlockSpec(memory_space=pl.ANY)
    shape = jax.ShapeDtypeStruct
    more = dict(collective_id=3, has_side_effects=True) if number > 0 else {}
    extra = []
    if number > 0:
        extra = Reduce.buffers(count, shapes) + Reduce.semaphores(count, number)
    return pl.pallas_call(
        functools.partial(dense_kernel, count, shapes),
        grid=(tiles,),
        in_specs=[whole, square, vector, whole, slab, slab, slab, anywhere],
        out_specs=[whole, vector, square] + [anywhere] * 4,
        out_shape=[
            shape((rows, width), bf16),
            shape((1, width), f32),
            shape((width, width), bf16),
            shape((rows, width), f32),
            shape((rows, width), bf16),
            shape((count // 2, 2, depth, (tiles - number) * 3 * TILE), bf16),
            shape((depth, max(number, 1) * 3 * TILE), bf16),
        ],
        scratch_shapes=[
            pltpu.VMEM((rows, width), f32),
            pltpu.VMEM((rows, width), bf16),
            pltpu.VMEM((width, rows), bf16),
            pltpu.VMEM((width, rows), bf16),
            pltpu.VMEM((rows, width), f32),
            pltpu.VMEM((rows, width), f32),
            pltpu.VMEM((SLOTS, count // 2, 2, depth, 3 * TILE), bf16),
            pltpu.SemaphoreType.DMA((2,)),
            pltpu.SemaphoreType.DMA((SLOTS,)),
        ]
        + extra,
        compiler_params=pltpu.CompilerParams(vmem_limit_bytes=63 * MIB, **more),
    )(mixed, w_out, gain, cotangent, w_gate, w_up, w_down_t, tokens)


STRIDE = 4


def backward_kernel(
    count, arrays, shapes, loaded_number, heads, tap_width, gain_width, *refs
):
    (
        signals_ref,
        logit_ref,
        taps_ref,
        grad_ref,
        fresh_ref,
        inverse_ref,
        starts_ref,
        state_ref,
        finals_ref,
        grads_ref,
        weights_ref,
        rates_weight_ref,
        gain_ref,
        grad_mlp_ref,
        grad_gain_ref,
        normed_ref,
        tokens_ref,
    ), refs = refs[:17], refs[17:]
    full, refs = refs[:arrays], refs[arrays:]
    grad_tokens_ref, refs = refs[0], refs[1:]
    outs, refs = refs[: arrays + 3], refs[arrays + 3 :]
    (
        normed_t,
        tokens,
        total,
        grad_signals,
        tails,
        firsts,
        edges,
        wides,
        pres,
        grads,
        padded,
        grad_logits,
        small_rows,
        small_source,
        beta_source,
        mixed_source,
        staging,
        plain_sem,
        edge_sem,
    ), refs = refs[:19], refs[19:]
    number = len(shapes)
    buffers = [refs[i * number : (i + 1) * number] for i in range(Reduce.BUFFERS)]
    sems = refs[Reduce.BUFFERS * number :]

    head = pl.program_id(0)
    rows, size = grad_ref.shape
    width = total.shape[1]
    chunks = rows // CHUNK
    row, col = grid_indices()
    lower, upper = row >= col, row <= col

    sources, targets = [], []
    for a in range(arrays):
        halves = max(full[a].shape[3] // (3 * TILE), 1)
        half = full[a].shape[3] // halves
        for part in range(halves):
            columns = pl.ds(part * half, half)
            sources.append(full[a].at[:, :, :, columns])
            targets.append(outs[a].at[:, columns])
    slots = mixed_source.shape[0]
    for one in range(heads):
        sources.append(mixed_source.at[one % slots])
        targets.append(outs[arrays].at[:, pl.ds(one * 3 * size, 3 * size)])
    sources += [beta_source, small_source]
    targets += [outs[arrays + 1], outs[arrays + 2]]
    reduce = Reduce(count, shapes, sources, targets, buffers, staging, sems)
    place = reduce.place
    position = place.position
    loaded = [p < loaded_number for p in range(number)]
    begin = [1 + 3 * (p // 2) for p in range(loaded_number)]
    begin += [2 * one + 5 for one in range(heads)] + [2 * heads + 5, 2 * heads + 6]
    stride = [STRIDE] * loaded_number + [STRIDE - 1] * (number - loaded_number)
    due, later = reduce.plan(begin, stride, 2 * heads, loaded)

    def spot(which):
        for step in range(heads + 1):
            actions = due.get(2 * step + which, ())
            if actions:

                @pl.when(head == step)
                def _():
                    for action in actions:
                        action()

    def fetch(source, target, slot):
        return pltpu.make_async_copy(source, target, plain_sem.at[slot])

    def edge(one, slot, arriving=False):
        return remote(
            firsts.at[slot],
            edges.at[one],
            edge_sem.at[0, one],
            edge_sem.at[1, one],
            reduce.device(3),
        )

    @pl.when(head == 0)
    def _():
        fetch(normed_ref, normed_t, 0).start()
        fetch(tokens_ref, tokens, 1).start()
        place.greet_all()
        for p in range(min(2, loaded_number)):
            reduce.start(p, True)
        total[...] = jnp.zeros_like(total)
        padded[...] = jnp.zeros_like(padded)
        grad_logits[...] = jnp.zeros_like(grad_logits)
        small_rows[...] = jnp.zeros_like(small_rows)
        fetch(normed_ref, normed_t, 0).wait()
        fetch(tokens_ref, tokens, 1).wait()

    spot(0)

    @pl.when(head < heads)
    def _():
        slot = lax.rem(head, 2)
        lows, scales = [], []
        for which in range(3):
            wides[which] = signals_ref[:, pl.ds(which * size, size)].astype(f32)
            pre = conv_pre(wides.at[which], taps_ref[0, which], rows)
            pres[which] = pre
            act = pre * sigmoid(pre)
            if which < 2:
                scale = lax.rsqrt(jnp.sum(act * act, axis=1, keepdims=True) + epsilon)
                act = act * scale
                scales.append(scale)
            lows.append(act.astype(bf16))
        queries, keys, values = lows
        rates = sigmoid(head_column(logit_ref[...].astype(f32), head))

        state = state_ref[0].astype(bf16)
        first = fresh_ref[:, pl.ds(0, size)].astype(f32)
        fresh_all = (first + nn(fresh_ref[:, pl.ds(size, size)], state)).astype(bf16)

        grad_memory = jnp.zeros((size, size), f32)
        for index in reversed(range(1, 4)):
            later = grads_ref[index, 0].astype(f32) + tn(
                finals_ref[index, 0, :, pl.ds(size, size)], grad_memory.astype(bf16)
            )
            grad_memory = jnp.where(index > position, later, grad_memory)
        grad_rates = [None] * chunks
        for chunk in reversed(range(chunks)):
            part = slice(chunk * CHUNK, (chunk + 1) * CHUNK)
            key, query, value, rate = keys[part], queries[part], values[part], rates[part]
            grad_out = grad_ref[part, :]
            fresh = fresh_all[part]
            start = starts_ref[0, chunk]
            memory = (start[:, :size].astype(f32) + nn(start[:, size:], state)).astype(bf16)
            low_grad = grad_memory.astype(bf16)
            key_f = key.astype(f32)
            rated = (rate * key_f).astype(bf16)

            scores_t = jnp.where(upper, nt(key, query), 0.0).astype(bf16)
            grad_fresh = (nn(scores_t, grad_out) + nn(key, low_grad)).astype(bf16)
            aim = tn(inverse_ref[part, :], grad_fresh)
            low_aim = aim.astype(bf16)
            grad_memory = grad_memory + tn(query, grad_out) - tn(rated, low_aim)

            grad_scores = jnp.where(lower, nt(grad_out, fresh), 0.0).astype(bf16)
            grad_scores_t = jnp.where(upper, nt(fresh, grad_out), 0.0).astype(bf16)
            grad_strict = jnp.where(row > col, nt(low_aim, fresh), 0.0).astype(bf16)
            grad_strict_t = jnp.where(row < col, nt(fresh, low_aim), 0.0).astype(bf16)

            grad_query = nt(grad_out, memory) + nn(grad_scores, key)
            within = -(nn(grad_strict, key) + nt(low_aim, memory))
            grad_rates[chunk] = jnp.sum(
                key_f * within + value.astype(f32) * aim, axis=1, keepdims=True
            )
            grad_key = (
                rate * within
                - nn(grad_strict_t, rated)
                + nn(grad_scores_t, query)
                + nt(fresh, low_grad)
            )
            grads[0, part, :] = grad_query
            grads[1, part, :] = grad_key
            grads[2, part, :] = rate * aim
            if chunk == chunks // 2:
                spot(1)

        lane = lax.broadcasted_iota(jnp.int32, grad_logits.shape, 1)
        grad_rate = jnp.concatenate(grad_rates, axis=0)
        grad_logit = grad_rate * rates * (1.0 - rates)
        grad_logits[...] = jnp.where(lane == head, grad_logit, grad_logits[...])

        @pl.when((head >= 2) & (position > 0))
        def _():
            edge(head - 2, slot).wait_send()

        for which in range(3):
            taps = taps_ref[0, which]
            pre = pres[which]
            sig = sigmoid(pre)
            grad_act = grads[which]
            if which < 2:
                unit = pre * sig * scales[which]
                grad_act = scales[which] * (
                    grad_act - unit * jnp.sum(grad_act * unit, axis=1, keepdims=True)
                )
            grad_pre = grad_act * sig * (1.0 + pre * (1.0 - sig))
            padded[pl.ds(HALO, rows), :] = grad_pre
            sums = []
            for offset in range(TAPS):
                shifted = wides[which, pl.ds(HALO - TAPS + 1 + offset, rows), :]
                sums.append(jnp.sum(grad_pre * shifted, axis=0, keepdims=True))
            where = pl.multiple_of((which * heads + head) * size, 128)
            small_rows[4:8, pl.ds(where, size)] = jnp.concatenate(sums, axis=0)

            def back(start, amount):
                result = None
                for offset in range(TAPS):
                    term = (
                        taps[offset : offset + 1, :]
                        * padded[pl.ds(start + TAPS - 1 - offset, amount), :]
                    )
                    result = term if result is None else result + term
                return result

            columns = pl.ds(which * size, size)
            grad_signal = back(HALO, rows)
            grad_signals[slot, :, columns] = grad_signal.astype(bf16)
            tails[slot, :, columns] = grad_signal[rows - HALO :]
            firsts[slot, :, columns] = back(0, HALO)

        @pl.when(position > 0)
        def _():
            edge(head, slot).start()

    for one in range(heads):

        @pl.when(head == one + 1)
        def _():
            slot = one % 2

            @pl.when(position < 3)
            def _():
                edge(one, slot).wait_recv()
                tails[slot] = tails[slot] + edges[one]

            grad_signals[slot, pl.ds(rows - HALO, HALO), :] = tails[slot].astype(bf16)
            grad = grad_signals[slot]
            source = mixed_source.at[one % slots]
            depth = width // count
            half = count // 4
            for part in range(2):
                piece = nn(normed_t[pl.ds(part * 2 * half * depth, 2 * half * depth), :], grad)
                source[pl.ds(part * half, half)] = piece.astype(bf16).reshape(
                    half, 2, depth, 3 * size
                )
            reduce.start(loaded_number + one, False)
            weights = weights_ref[...]
            for part in range(0, rows, CHUNK):
                block = pl.ds(part, CHUNK)
                total[block, :] += nt(grad[part : part + CHUNK], weights)

    @pl.when(head == heads)
    def _():
        depth = width // count
        low_logits = grad_logits[...].astype(bf16)
        beta_source[...] = (
            nn(normed_t[...], low_logits).astype(bf16).reshape(beta_source.shape)
        )
        reduce.start(number - 2, False)
        gain = gain_ref[...].astype(f32)
        weights = rates_weight_ref[...]
        gain_grad = jnp.zeros((1, width), f32)
        for part in range(0, rows, CHUNK):
            block = pl.ds(part, CHUNK)
            grad = total[block, :] + nt(low_logits[part : part + CHUNK], weights)
            values = tokens[block, :].astype(f32)
            scaling = lax.rsqrt(jnp.mean(values * values, axis=1, keepdims=True) + epsilon)
            unit = values * scaling
            gain_grad = gain_grad + jnp.sum(grad * unit, axis=0, keepdims=True)
            scaled = grad * gain
            total[block, :] = scaling * (
                scaled - unit * jnp.mean(scaled * unit, axis=1, keepdims=True)
            )
        fetch(total, grad_tokens_ref, 0).start()
        small_rows[0:1, pl.ds(0, width)] = gain_grad
        small_rows[1:2, pl.ds(0, width)] = grad_mlp_ref[...]
        small_rows[2:3, pl.ds(0, size)] = grad_gain_ref[...]
        small = small_rows[...]
        gains = gather_rows(small[:, :width], count, gain_width)
        last = gather_rows(small[:, :size], count, size // count)
        taps = gather_rows(small, count, tap_width)
        which = lax.broadcasted_iota(jnp.int32, gains.shape, 1)
        small = jnp.where(which == 2, last, jnp.where(which < 2, gains, taps))
        small_source[...] = small.astype(bf16).reshape(small_source.shape)
        reduce.start(number - 1, False)
        for action in later:
            action()
        for p in range(number):
            reduce.finish(p)
        fetch(total, grad_tokens_ref, 0).wait()
        for one in range(heads - 2, heads):

            @pl.when(position > 0)
            def _():
                edge(one, one % 2).wait_send()


def gather_rows(wide, count, width):
    total = count * width
    rows = wide.shape[0]
    if width % 128 == 0:
        blank = jnp.zeros((rows, PACK[1] - width), f32)
        return jnp.stack(
            [
                jnp.concatenate([wide[:, s * width : (s + 1) * width], blank], axis=1)
                for s in range(count)
            ]
        )
    row = lax.broadcasted_iota(jnp.int32, (count * rows, rows), 0)
    col = lax.broadcasted_iota(jnp.int32, (count * rows, rows), 1)
    spread = jnp.where(lax.rem(row, rows) == col, 1.0, 0.0).astype(bf16)
    tall = nn(spread, wide[:, :total].astype(bf16))
    row = lax.broadcasted_iota(jnp.int32, tall.shape, 0)
    col = lax.broadcasted_iota(jnp.int32, tall.shape, 1)
    tall = jnp.where(lax.div(row, rows) == lax.div(col, width), tall, 0.0).astype(bf16)
    row = lax.broadcasted_iota(jnp.int32, (total, PACK[1]), 0)
    col = lax.broadcasted_iota(jnp.int32, (total, PACK[1]), 1)
    pick = jnp.where(lax.rem(row, width) == col, 1.0, 0.0).astype(bf16)
    return nn(tall, pick).reshape(count, rows, PACK[1])


def backward(
    signals,
    logits,
    taps,
    grad_out,
    fresh,
    inverses,
    starts,
    state,
    finals,
    grad_starts,
    w_mixed,
    w_rates,
    gain,
    grad_mlp,
    grad_gain,
    normed_t,
    tokens,
    full,
    tap_width,
    gain_width,
):
    count = lax.axis_size("fsdp")
    wide_rows = signals.shape[0]
    rows, width = grad_out.shape
    heads, _, _, size = taps.shape
    chunks = rows // CHUNK
    depth = width // count
    views = full

    def portions(depth, wanted):
        while depth % (16 * wanted) != 0:
            wanted //= 2
        return wanted

    shapes = []
    for a, view in enumerate(views):
        halves = max(view.shape[3] // (3 * TILE), 1)
        for part in range(halves):
            shapes.append((depth, view.shape[3] // halves, 4 if (a + part) % 2 else 2))
    loaded = len(shapes)
    for head in range(heads):
        shapes.append((depth, 3 * size, portions(depth, 4 if head % 2 == 0 else 2)))
    shapes.append((depth, logits.shape[1], portions(depth, 2)))
    shapes.append(PACK + (1,))
    staged = max([d // 2 for d, _, _ in shapes[:loaded]] + [16])
    widest = max([w for _, w, _ in shapes[:loaded]] + [128])

    def now(h):
        return jnp.minimum(h, heads - 1)

    def before(h):
        return jnp.maximum(h - 1, 0)

    whole = pl.BlockSpec(logits.shape, lambda h: (0, 0))
    vector = pl.BlockSpec((1, width), lambda h: (0, 0))
    anywhere = pl.BlockSpec(memory_space=pl.ANY)
    shape = jax.ShapeDtypeStruct
    return pl.pallas_call(
        functools.partial(
            backward_kernel, count, len(views), shapes, loaded, heads, tap_width, gain_width
        ),
        grid=(heads + 1,),
        in_specs=[
            pl.BlockSpec((wide_rows, 3 * size), lambda h: (0, now(h))),
            whole,
            pl.BlockSpec((1, 3, TAPS, size), lambda h: (now(h), 0, 0, 0)),
            pl.BlockSpec((rows, size), lambda h: (0, now(h))),
            pl.BlockSpec((rows, 2 * size), lambda h: (0, now(h))),
            pl.BlockSpec((rows, CHUNK), lambda h: (0, now(h))),
            pl.BlockSpec((1, chunks, size, 2 * size), lambda h: (now(h), 0, 0, 0)),
            pl.BlockSpec((1, size, size), lambda h: (now(h), 0, 0)),
            pl.BlockSpec((4, 1, size, 2 * size), lambda h: (0, now(h), 0, 0)),
            pl.BlockSpec((4, 1, size, size), lambda h: (0, now(h), 0, 0)),
            pl.BlockSpec((width, 3 * size), lambda h: (0, before(h))),
            pl.BlockSpec(w_rates.shape, lambda h: (0, 0)),
            vector,
            vector,
            pl.BlockSpec((1, size), lambda h: (0, 0)),
        ]
        + [anywhere] * (2 + len(views)),
        out_specs=[anywhere] * (4 + len(views)),
        out_shape=[shape((rows, width), f32)]
        + [shape(view.shape[2:], bf16) for view in views]
        + [
            shape((depth, 3 * width), bf16),
            shape((depth, logits.shape[1]), bf16),
            shape(PACK, bf16),
        ],
        scratch_shapes=[
            pltpu.VMEM((width, rows), bf16),
            pltpu.VMEM((rows, width), bf16),
            pltpu.VMEM((rows, width), f32),
            pltpu.VMEM((2, rows, 3 * size), bf16),
            pltpu.VMEM((2, HALO, 3 * size), f32),
            pltpu.VMEM((2, HALO, 3 * size), f32),
            pltpu.VMEM((heads, HALO, 3 * size), f32),
            pltpu.VMEM((3, wide_rows, size), f32),
            pltpu.VMEM((3, rows, size), f32),
            pltpu.VMEM((3, rows, size), f32),
            pltpu.VMEM((rows + 2 * HALO, size), f32),
            pltpu.VMEM(logits.shape, f32),
            pltpu.VMEM((PACK[0], 3 * width), f32),
            pltpu.VMEM((count // 2, 2) + PACK, bf16),
            pltpu.VMEM((count // 2, 2, depth, logits.shape[1]), bf16),
            pltpu.VMEM((SLOTS, count // 2, 2, depth, 3 * size), bf16),
            pltpu.VMEM((2, count // 2, 2, staged, widest), bf16),
            pltpu.SemaphoreType.DMA((2,)),
            pltpu.SemaphoreType.DMA((2, heads)),
        ]
        + Reduce.buffers(count, shapes)
        + Reduce.semaphores(count, len(shapes)),
        compiler_params=pltpu.CompilerParams(
            collective_id=2, has_side_effects=True, vmem_limit_bytes=63 * MIB
        ),
    )(
        signals,
        logits,
        taps,
        grad_out,
        fresh,
        inverses,
        starts,
        state,
        finals,
        grad_starts,
        w_mixed,
        w_rates,
        gain,
        grad_mlp,
        grad_gain,
        normed_t,
        tokens,
        *views,
    )


def arrange_kernel(q_ref, k_ref, v_ref, down_ref, mixed_ref, down_t_ref):
    size = q_ref.shape[1]
    for which, ref in enumerate((q_ref, k_ref, v_ref)):
        mixed_ref[:, which * size : (which + 1) * size] = ref[...]
    down_t_ref[...] = down_ref[...].T


def arrange(w_query, w_key, w_value, w_down, heads):
    depth, width = w_query.shape
    size = width // heads
    tiles = w_down.shape[0] // TILE
    column = pl.BlockSpec((depth, size), lambda j: (0, jnp.minimum(j, heads - 1)))
    return pl.pallas_call(
        arrange_kernel,
        grid=(tiles,),
        in_specs=[column, column, column, pl.BlockSpec((TILE, depth), lambda j: (j, 0))],
        out_specs=[
            pl.BlockSpec((depth, 3 * size), lambda j: (0, jnp.minimum(j, heads - 1))),
            pl.BlockSpec((depth, TILE), lambda j: (0, j)),
        ],
        out_shape=[
            jax.ShapeDtypeStruct((depth, 3 * width), bf16),
            jax.ShapeDtypeStruct((depth, w_down.shape[0]), bf16),
        ],
        compiler_params=pltpu.CompilerParams(vmem_limit_bytes=16 * MIB),
    )(w_query, w_key, w_value, w_down)


def deliver_kernel(
    number,
    sums_ref,
    rest_ref,
    mixed_ref,
    out_ref,
    attended_ref,
    tokens_ref,
    gate_out,
    up_out,
    down_out,
    query_out,
    key_out,
    value_out,
    out_out,
    tokens_out,
):
    tile = pl.program_id(0)
    packed = jnp.where(tile < number, sums_ref[...], rest_ref[...]).astype(f32)
    gate_out[...] = packed[:, :TILE]
    up_out[...] = packed[:, TILE : 2 * TILE]
    down_out[...] = packed[:, 2 * TILE :].T
    size = query_out.shape[1]
    for which, ref in enumerate((query_out, key_out, value_out)):
        ref[...] = mixed_ref[:, which * size : (which + 1) * size].astype(f32)
    out_out[...] = out_ref[...].astype(f32)
    tokens_out[...] = attended_ref[...] + tokens_ref[...]


def deliver(number, sums, rest, mixed, out, grad_attended, grad_tokens, heads):
    depth, width = out.shape
    size = width // heads
    rows = grad_tokens.shape[0] // heads
    tiles = number + rest.shape[1] // (3 * TILE)

    def head(j):
        return jnp.minimum(j, heads - 1)

    column = pl.BlockSpec((depth, size), lambda j: (0, head(j)))
    block = pl.BlockSpec((rows, width), lambda j: (head(j), 0))
    tile = pl.BlockSpec((depth, TILE), lambda j: (0, j))
    shape = jax.ShapeDtypeStruct
    return pl.pallas_call(
        functools.partial(deliver_kernel, number),
        grid=(tiles,),
        in_specs=[
            pl.BlockSpec((depth, 3 * TILE), lambda j: (0, jnp.minimum(j, number - 1))),
            pl.BlockSpec((depth, 3 * TILE), lambda j: (0, jnp.maximum(j - number, 0))),
            pl.BlockSpec((depth, 3 * size), lambda j: (0, head(j))),
            column,
            block,
            block,
        ],
        out_specs=[
            tile,
            tile,
            pl.BlockSpec((TILE, depth), lambda j: (j, 0)),
            column,
            column,
            column,
            column,
            block,
        ],
        out_shape=[
            shape((depth, tiles * TILE), f32),
            shape((depth, tiles * TILE), f32),
            shape((tiles * TILE, depth), f32),
            shape((depth, width), f32),
            shape((depth, width), f32),
            shape((depth, width), f32),
            shape((depth, width), f32),
            shape(grad_tokens.shape, f32),
        ],
        compiler_params=pltpu.CompilerParams(vmem_limit_bytes=24 * MIB),
    )(sums, rest, mixed, out, grad_attended, grad_tokens)


def local(
    inputs,
    g_attn,
    w_query,
    w_key,
    w_value,
    w_beta,
    conv_taps,
    o_gain,
    w_out,
    g_mlp,
    w_gate,
    w_up,
    w_down,
    cotangent,
):
    count = lax.axis_size("fsdp")
    position = lax.axis_index("seq")
    groups = lax.axis_size("seq")
    tokens_low = inputs[0]
    rows, width = tokens_low.shape
    heads = w_beta.shape[1]
    size = width // heads
    depth = w_query.shape[0]
    small = (g_attn.shape, g_mlp.shape, o_gain.shape, conv_taps.shape)
    packed = pack_small((g_attn[None], g_mlp[None], o_gain[None]), conv_taps[None])
    if depth % 128 == 0:
        mixed, down_t = arrange(w_query, w_key, w_value, w_down, heads)
    else:
        mixed = jnp.stack([w.reshape(depth, -1, size) for w in (w_query, w_key, w_value)], axis=2)
        mixed, down_t = mixed.reshape(depth, 3 * width), jnp.transpose(w_down)
    shards = (
        packed,
        jnp.pad(w_beta, ((0, 0), (0, 128 - heads))),
        mixed,
        w_out,
        w_gate,
        w_up,
        down_t,
    )
    results = forward(tokens_low, shards, heads, conv_taps.shape[1])
    packed, w_beta, w_mixed, w_out, w_gate, w_up, w_down_t = results[:ARRAYS]
    finals, _, normed_t, signals, logits, taps = results[ARRAYS : ARRAYS + 6]
    outputs, carries, fresh, inverses, starts = results[ARRAYS + 6 :]
    g_attn, g_mlp, o_gain, _ = unpack_small(packed, small)
    g_attn, g_mlp, o_gain = g_attn.reshape(-1), g_mlp.reshape(-1), o_gain.reshape(-1)

    gain_out = o_gain.reshape(1, size)
    head_rows, state_in = mix(position.reshape(1), outputs, carries, finals, gain_out)
    tiles = w_gate.shape[1] // TILE
    beside = depth % 64 == 0
    number = tiles - 4 if beside else 0
    layer_out, grad_gain_mlp, grad_out_matrix, grad_attended, grad_heads, rest, sums = dense(
        head_rows,
        tokens_low,
        w_out,
        g_mlp.reshape(1, -1),
        cotangent[0],
        w_gate,
        w_up,
        w_down_t,
        number,
    )
    grad_delta, grad_gain_out, grad_starts = unmix(
        outputs, carries, state_in, gain_out, grad_heads
    )
    full = (rest, grad_out_matrix.reshape(count // 2, 2, depth, width))
    results = backward(
        signals,
        logits,
        taps,
        grad_delta,
        fresh,
        inverses,
        starts,
        state_in,
        finals,
        grad_starts,
        w_mixed,
        w_beta,
        g_attn.reshape(1, -1),
        grad_gain_mlp,
        grad_gain_out,
        normed_t,
        tokens_low,
        full if beside else (),
        small[3][1],
        small[0][0],
    )
    grad_from_attn, full_sums = results[0], results[1:-3]
    grad_mixed_matrix, grad_beta_matrix, packed = results[-3:]
    if beside and depth % 128 == 0:
        (
            grad_gate_matrix,
            grad_up_matrix,
            grad_down_matrix,
            grad_query_matrix,
            grad_key_matrix,
            grad_value_matrix,
            grad_out_matrix,
            grad_inputs,
        ) = deliver(
            number,
            sums,
            full_sums[0],
            grad_mixed_matrix,
            full_sums[1],
            grad_attended,
            grad_from_attn,
            heads,
        )
    else:
        if beside:
            sums, grad_out_matrix = jnp.concatenate([sums, full_sums[0]], axis=1), full_sums[1]
        else:
            sums, grad_out_matrix = (
                lax.psum(
                    lax.psum_scatter(
                        g.reshape((count,) + g.shape[2:]), "fsdp", scatter_dimension=0
                    ),
                    "seq",
                )
                for g in full
            )
        sums = sums.astype(f32).reshape(depth, tiles, 3, TILE)
        grad_gate_matrix, grad_up_matrix, grad_down_t = (
            sums[:, :, which].reshape(depth, tiles * TILE) for which in range(3)
        )
        grad_down_matrix = jnp.transpose(grad_down_t)
        grad_mixed_matrix = grad_mixed_matrix.astype(f32).reshape(depth, heads, 3, size)
        grad_query_matrix, grad_key_matrix, grad_value_matrix = (
            grad_mixed_matrix[:, :, which].reshape(depth, width) for which in range(3)
        )
        grad_out_matrix = grad_out_matrix.astype(f32)
        grad_inputs = grad_attended + grad_from_attn
    parts = [part[0].astype(f32) for part in unpack_small(packed, small)]
    grad_gain_attn, grad_gain_mlp, grad_gain_out, grad_taps = parts
    return (
        layer_out[None],
        grad_inputs[None],
        grad_gain_attn,
        grad_query_matrix,
        grad_key_matrix,
        grad_value_matrix,
        grad_beta_matrix[:, :heads].astype(f32),
        grad_taps,
        grad_gain_out,
        grad_out_matrix,
        grad_gain_mlp,
        grad_gate_matrix,
        grad_up_matrix,
        grad_down_matrix,
    )


def solution(mesh):
    vector = P("fsdp")
    rows = P("fsdp", None)
    columns = P(None, "fsdp")
    tokens = P("fsdp", "seq", None)
    return jax.shard_map(
        local,
        mesh=mesh,
        in_specs=(
            tokens,
            vector,
            rows,
            rows,
            rows,
            rows,
            columns,
            vector,
            rows,
            vector,
            rows,
            rows,
            columns,
            tokens,
        ),
        out_specs=(
            tokens,
            tokens,
            vector,
            rows,
            rows,
            rows,
            rows,
            columns,
            vector,
            rows,
            vector,
            rows,
            rows,
            columns,
        ),
        check_vma=False,
    )
```

```python
import functools

import jax
import jax.numpy as jnp
from jax import lax
from jax.experimental import pallas as pl
from jax.experimental.pallas import tpu as pltpu
from jax.sharding import PartitionSpec as P

CHUNK = 256
HALO = 16
TAPS = 4
MIB = 1024 * 1024

highest = lax.Precision.HIGHEST
epsilon = 1e-06
f32 = jnp.float32
bf16 = jnp.bfloat16


def nn(left_side, right_side):
    return lax.dot_general(
        left_side, right_side, (((1,), (0,)), ((), ())), preferred_element_type=f32
    )


def nt(left_side, right_side):
    return lax.dot_general(
        left_side, right_side, (((1,), (1,)), ((), ())), preferred_element_type=f32
    )


def tn(left_side, right_side):
    return lax.dot_general(
        left_side, right_side, (((0,), (0,)), ((), ())), preferred_element_type=f32
    )


def rms_scale(values, gain_vec):
    return (
        values * lax.rsqrt(jnp.mean(values * values, axis=-1, keepdims=True) + epsilon) * gain_vec
    )


def norm_backward(values, gain_vec, grad_out):
    scaling = lax.rsqrt(jnp.mean(values * values, axis=-1, keepdims=True) + epsilon)
    unit_rows = values * scaling
    gain_grad = jnp.sum(grad_out * unit_rows, axis=0)
    scaled_grad = grad_out * gain_vec
    input_grad = scaling * (
        scaled_grad - unit_rows * jnp.mean(scaled_grad * unit_rows, axis=-1, keepdims=True)
    )
    return (input_grad, gain_grad)


MESH = pl.DeviceIdType.MESH


class Place:
    def __init__(self, count):
        self.count = count
        self.sides = 2 if count % 2 == 0 else 1
        self.length = count // self.sides
        self.position = lax.axis_index("seq")
        self.index = lax.axis_index("fsdp")
        self.core = lax.rem(self.position, 2)
        self.chip = lax.div(self.position, 2)
        self.side = lax.rem(self.index, self.sides)
        self.spot = lax.div(self.index, self.sides)

    def sibling(self):
        return {"seq": self.position + 1 - 2 * self.core, "fsdp": self.index}

    def across(self):
        return {"seq": lax.rem(self.position + 2, 4), "fsdp": self.index}

    def partner(self):
        return {"seq": self.position, "fsdp": self.spot * 2 + 1 - self.side}

    def ahead(self, step):
        spot = lax.rem(self.spot + step, self.length)
        return {"seq": self.position, "fsdp": spot * self.sides + self.side}

    def shard(self, spot, side):
        return spot * self.sides + side

    def behind(self, step):
        return lax.rem(self.spot + self.length - step, self.length)

    def greet_all(self):
        self.greet(False, True)

    def greet(self, across, sequence=False):
        barrier = pltpu.get_barrier_semaphore()
        total = self.length - 1

        def signal(device):
            pl.semaphore_signal(barrier, inc=1, device_id=device, device_id_type=MESH)

        def one(step, carry):
            signal(self.ahead(step))
            return carry

        lax.fori_loop(1, self.length, one, 0)
        if sequence:
            for hop in range(1, 4):
                signal({"seq": lax.rem(self.position + hop, 4), "fsdp": self.index})
            total += 3
        else:
            signal(self.sibling())
            total += 1
        if self.sides == 2:
            signal(self.partner())
            total += 1
        if across:
            signal(self.across())
            total += 1
        pl.semaphore_wait(barrier, total)


def remote(source, target, send, recv, device):
    return pltpu.make_async_remote_copy(
        src_ref=source,
        dst_ref=target,
        send_sem=send,
        recv_sem=recv,
        device_id=device,
        device_id_type=MESH,
    )


def steps(first, last, body):
    def one(step, carry):
        body(step)
        return carry

    lax.fori_loop(first, last, one, 0)


class Reduce:
    BUFFERS = 6

    def __init__(self, count, pieces, sources, targets, buffers, staging, sems):
        self.place = Place(count)
        self.pieces, self.sources, self.targets, self.staging = pieces, sources, targets, staging
        self.acc, self.x_in, self.y_in, self.z_in, self.parts_in, self.result = buffers
        (
            self.core_sem,
            self.load_sem,
            self.x_sem,
            self.y_sem,
            self.z_sem,
            self.share_sem,
            self.final_sem,
            self.store_sem,
        ) = sems

    @staticmethod
    def buffers(count, pieces):
        length = count // 2
        acc, x_in, y_in, z_in, parts_in, result = [], [], [], [], [], []
        for depth, width, parts in pieces:
            rows = depth // parts
            acc.append(pltpu.VMEM((length, 2, depth // min(parts, 2), width), bf16))
            x_in.append(
                pltpu.VMEM((length, 2, rows, width) if parts == 4 else (1, 1, 16, 128), bf16)
            )
            y_in.append(pltpu.VMEM((length, rows, width), bf16))
            z_in.append(pltpu.VMEM((length, rows, width), bf16))
            parts_in.append(
                pltpu.VMEM((4 // parts, rows, width) if parts < 4 else (1, 16, 128), bf16)
            )
            result.append(pltpu.VMEM((rows, width), bf16))
        return acc + x_in + y_in + z_in + parts_in + result

    @staticmethod
    def semaphores(count, number):
        pair = pltpu.SemaphoreType.DMA((number, 2))
        one = pltpu.SemaphoreType.DMA((number,))
        hops = pltpu.SemaphoreType.DMA((number, 2, 4))
        return [pair, one, pair, pair, pair, hops, hops, one]

    def half(self, p, core):
        depth, _, parts = self.pieces[p]
        rows = depth // min(parts, 2)
        return pl.ds(pl.multiple_of(core * rows, 16) if parts > 1 else 0, rows)

    def quarter(self, p, chip):
        depth, _, parts = self.pieces[p]
        rows = depth // parts
        return pl.ds(pl.multiple_of(chip * rows, 16) if parts == 4 else 0, rows)

    def device(self, hop):
        return {"seq": lax.rem(self.place.position + hop, 4), "fsdp": self.place.index}

    def to_sibling(self, p):
        return remote(
            self.sources[p].at[:, :, self.half(p, 1 - self.place.core), :],
            self.acc[p],
            self.core_sem.at[p, 0],
            self.core_sem.at[p, 1],
            self.place.sibling(),
        )

    def stage(self, p):
        depth, width, parts = self.pieces[p]
        return self.staging.at[p % 2, :, :, pl.ds(0, depth // 2), pl.ds(0, width)]

    def load(self, p):
        return pltpu.make_async_copy(
            self.sources[p].at[:, :, self.half(p, self.place.core), :],
            self.stage(p),
            self.load_sem.at[p],
        )

    def to_x(self, p):
        return remote(
            self.acc[p].at[:, :, self.quarter(p, 1 - self.place.chip), :],
            self.x_in[p],
            self.x_sem.at[p, 0],
            self.x_sem.at[p, 1],
            self.place.across(),
        )

    def to_y(self, p):
        place = self.place
        return remote(
            self.acc[p].at[:, 1 - place.side, self.quarter(p, place.chip), :],
            self.y_in[p],
            self.y_sem.at[p, 0],
            self.y_sem.at[p, 1],
            place.partner(),
        )

    def to_z(self, p, step):
        place = self.place
        spot = lax.rem(place.spot + step, place.length)
        return remote(
            self.acc[p].at[spot, place.side, self.quarter(p, place.chip), :],
            self.z_in[p].at[step],
            self.z_sem.at[p, 0],
            self.z_sem.at[p, 1],
            place.ahead(step),
        )

    def all_z(self, p):
        both = self.z_in[p].at[pl.ds(1, self.place.length - 1)]
        return remote(
            both, both, self.z_sem.at[p, 0], self.z_sem.at[p, 1], self.place.ahead(1)
        )

    def sharers(self, p):
        return {1: (1, 2, 3), 2: (2,), 4: ()}[self.pieces[p][2]]

    def receivers(self, p):
        return {1: (), 2: (0,), 4: (1, 2, 3)}[self.pieces[p][2]]

    def sharer(self, p, position):
        return position if self.pieces[p][2] == 1 else lax.div(position, 2)

    def to_share(self, p, hop, arriving=False):
        position = self.place.position
        source = lax.rem(position + 4 - hop, 4) if arriving else position
        buffer = self.parts_in[p].at[self.sharer(p, source)]
        return remote(
            buffer,
            buffer,
            self.share_sem.at[p, 0, hop],
            self.share_sem.at[p, 1, hop],
            self.device(hop),
        )

    def target(self, p, position):
        depth, _, parts = self.pieces[p]
        rows = depth // parts
        core, chip = lax.rem(position, 2), lax.div(position, 2)
        first = {1: 0, 2: core * rows, 4: (core * 2 + chip) * rows}[parts]
        return self.targets[p].at[pl.ds(pl.multiple_of(first, 16) if parts > 1 else 0, rows), :]

    def to_result(self, p, hop, arriving=False):
        place = self.place
        if hop == 0:
            other = place.position + 1 - 2 * place.core
            device = place.sibling()
        else:
            other = lax.rem(place.position + 4 - hop, 4)
            device = self.device(hop)
        return remote(
            self.result[p],
            self.target(p, other if arriving else place.position),
            self.final_sem.at[p, 0, hop],
            self.final_sem.at[p, 1, hop],
            device,
        )

    def store(self, p):
        return pltpu.make_async_copy(
            self.result[p], self.target(p, self.place.position), self.store_sem.at[p]
        )

    def start(self, p, loaded):
        if self.pieces[p][2] > 1:
            self.to_sibling(p).start()
        if loaded:
            self.load(p).start()

    def on_core(self, p, loaded):
        parts = self.pieces[p][2]
        acc = self.acc[p]
        half = self.half(p, self.place.core)
        rows, width = acc.shape[2], acc.shape[3]
        if loaded:
            self.load(p).wait()
        if parts == 1:
            acc[...] = self.sources[p][...]
        else:
            self.to_sibling(p).wait_recv()

            def add(spot):
                if loaded:
                    own = self.staging[p % 2, spot, :, pl.ds(0, rows), pl.ds(0, width)]
                else:
                    own = self.sources[p][spot, :, half, :]
                acc[spot] = acc[spot] + own

            steps(0, self.place.length, add)
        (self.to_x if parts == 4 else self.to_y)(p).start()
        if parts > 1:
            self.to_sibling(p).wait_send()

    def on_x(self, p):
        acc, side = self.acc[p], 1 - self.place.side
        rows = self.quarter(p, self.place.chip)
        self.to_x(p).wait_recv()

        def add(spot):
            acc[spot, side, rows, :] = acc[spot, side, rows, :] + self.x_in[p][spot, side]

        steps(0, self.place.length, add)
        self.to_y(p).start()

    def on_y(self, p):
        place = self.place
        acc = self.acc[p]
        rows = self.quarter(p, place.chip)
        self.to_y(p).wait_recv()

        def one(step):
            spot = lax.rem(place.spot + step, place.length)
            total = acc[spot, place.side, rows, :].astype(f32) + self.y_in[p][spot].astype(f32)
            if self.pieces[p][2] == 4:
                total = total + self.x_in[p][spot, place.side].astype(f32)
            acc[spot, place.side, rows, :] = total.astype(bf16)

        def send(step):
            one(step)
            self.to_z(p, step).start()

        steps(1, place.length, send)
        one(0)

    def on_z(self, p):
        place = self.place
        rows = self.quarter(p, place.chip)
        self.all_z(p).wait_recv()
        total = self.acc[p][place.spot, place.side, rows, :].astype(f32)
        if place.length <= 8:
            for step in range(1, place.length):
                total = total + self.z_in[p][step].astype(f32)
        else:
            total = lax.fori_loop(
                1,
                place.length,
                lambda step, carry: carry + self.z_in[p][step].astype(f32),
                total,
            )
        if self.pieces[p][2] == 4:
            self.result[p][...] = total.astype(bf16)
            self.publish(p)
        else:
            self.parts_in[p][self.sharer(p, place.position)] = total.astype(bf16)
            for hop in self.sharers(p):
                self.to_share(p, hop).start()

    def on_share(self, p):
        total = None
        for hop in self.sharers(p):
            self.to_share(p, hop, True).wait_recv()
        for index in range(4 // self.pieces[p][2]):
            term = self.parts_in[p][index].astype(f32)
            total = term if total is None else total + term
        self.result[p][...] = total.astype(bf16)
        self.publish(p)

    def publish(self, p):
        for hop in self.receivers(p):
            self.to_result(p, hop).start()
        self.store(p).start()

    def finish(self, p):
        if self.pieces[p][2] == 4:
            self.to_x(p).wait_send()
        self.to_y(p).wait_send()
        self.all_z(p).wait_send()
        for hop in self.sharers(p):
            self.to_share(p, hop).wait_send()
        for hop in self.receivers(p):
            self.to_result(p, hop).wait_send()
            self.to_result(p, hop, True).wait_recv()
        self.store(p).wait()

    def plan(self, begin, stride, last, loaded, idle=()):
        due = []
        for p, (_, _, parts) in enumerate(self.pieces):
            for index, kind in enumerate((0, 1, 2, 3) if parts == 4 else (0, 2, 3, 4)):
                half = begin[p] + stride[p] * index
                while half in idle:
                    half += 1
                due.append((half, -index, p, kind))
        due.sort()

        def action(p, kind):
            if kind == 0:
                self.on_core(p, loaded[p])
                if loaded[p] and p + 2 < len(self.pieces) and loaded[p + 2]:
                    self.start(p + 2, True)
            else:
                (self.on_x, self.on_y, self.on_z, self.on_share)[kind - 1](p)

        def at(test):
            return [functools.partial(action, p, kind) for half, _, p, kind in due if test(half)]

        return (
            {half: at(lambda when: when == half) for half in range(last + 1)},
            at(lambda when: when > last),
        )


class Gather:
    SEMS = 6

    def __init__(self, count, pieces, shards, outs, sems):
        self.place = Place(count)
        self.pieces, self.shards, self.outs = pieces, shards, outs
        self.line_sem, self.side_sem, self.core_sem, self.across_sem, self.relay_sem, self.own = (
            sems
        )

    @staticmethod
    def scratch(pieces, count):
        length = count // 2 if count % 2 == 0 else count
        number = len(pieces)
        slots = 2 * length if max(piece[3] for piece in pieces) > 1 else 1
        return [
            pltpu.SemaphoreType.DMA((number, 2, length)),
            pltpu.SemaphoreType.DMA((number, 2, length)),
            pltpu.SemaphoreType.DMA((number, 2, slots)),
            pltpu.SemaphoreType.DMA((number, 2, slots)),
            pltpu.SemaphoreType.DMA((number, 2, slots)),
            pltpu.SemaphoreType.DMA((number,)),
        ]

    def portion(self, k, core, chip):
        parts = self.pieces[k][3]
        if parts == 1:
            return 0
        return core if parts == 2 else 2 * chip + core

    def region(self, k, shard, core, chip):
        a, offset, width, parts = self.pieces[k]
        depth = self.shards[a].shape[0]
        rows = depth // parts
        first = shard * depth + self.portion(k, core, chip) * rows
        return self.outs[a].at[pl.ds(pl.multiple_of(first, 16), rows), pl.ds(offset, width)]

    def source(self, k):
        p = self.place
        a, offset, width, parts = self.pieces[k]
        rows = self.shards[a].shape[0] // parts
        first = self.portion(k, p.core, p.chip) * rows
        return self.shards[a].at[pl.ds(pl.multiple_of(first, 16), rows), pl.ds(offset, width)]

    def line(self, k, step, arriving=False):
        p = self.place
        shard = p.shard(p.behind(step), p.side) if arriving else p.index
        target = self.region(k, shard, p.core, p.chip)
        return remote(
            target if arriving else self.source(k),
            target,
            self.line_sem.at[k, 0, step],
            self.line_sem.at[k, 1, step],
            p.ahead(step),
        )

    def side(self, k, step, arriving=False, own=False):
        p = self.place
        shard = p.shard(p.behind(step), 1 - p.side if arriving else p.side)
        target = self.region(k, shard, p.core, p.chip)
        return remote(
            self.source(k) if own else target,
            target,
            self.side_sem.at[k, 0, step],
            self.side_sem.at[k, 1, step],
            p.partner(),
        )

    def cross(self, k, step, other, sems, core, chip, device):
        p = self.place
        shard = p.shard(p.behind(step), 1 - p.side if other else p.side)
        target = self.region(k, shard, core, chip)
        slot = 2 * step + (1 if other else 0)
        return remote(target, target, sems.at[k, 0, slot], sems.at[k, 1, slot], device)

    def core(self, k, step, other, arriving=False):
        p = self.place
        core = 1 - p.core if arriving else p.core
        return self.cross(k, step, other, self.core_sem, core, p.chip, p.sibling())

    def across(self, k, step, other, arriving=False):
        p = self.place
        chip = 1 - p.chip if arriving else p.chip
        return self.cross(k, step, other, self.across_sem, p.core, chip, p.across())

    def relay(self, k, step, other, arriving=False):
        p = self.place
        core = 1 - p.core if arriving else p.core
        return self.cross(k, step, other, self.relay_sem, core, 1 - p.chip, p.sibling())

    def keep(self, k):
        a, offset, width, _ = self.pieces[k]
        depth = self.shards[a].shape[0]
        rows = pl.ds(pl.multiple_of(self.place.index * depth, 16), depth)
        columns = pl.ds(offset, width)
        return pltpu.make_async_copy(
            self.shards[a].at[:, columns], self.outs[a].at[rows, columns], self.own.at[k]
        )

    def hand(self, k, step, other):
        parts = self.pieces[k][3]
        if parts == 4:
            self.across(k, step, other).start()
        if parts > 1:
            self.core(k, step, other).start()

    def start(self, k):
        steps(1, self.place.length, lambda step: self.line(k, step).start())
        if self.place.sides == 2:
            self.side(k, 0, own=True).start()
        self.keep(k).start()

    def forward(self, k):
        def one(step):
            self.line(k, step, True).wait_recv()
            if self.place.sides == 2:
                self.side(k, step).start()
            self.hand(k, step, False)

        steps(1, self.place.length, one)

    def spread(self, k):
        def one(step):
            self.side(k, step, True).wait_recv()
            self.hand(k, step, True)

        if self.place.sides == 2:
            steps(0, self.place.length, one)

    def each(self, body):
        steps(1, self.place.length, lambda step: body(step, False))
        if self.place.sides == 2:
            steps(0, self.place.length, lambda step: body(step, True))

    def exchange(self, k):
        def one(step, other):
            self.across(k, step, other, True).wait_recv()
            self.relay(k, step, other).start()

        if self.pieces[k][3] == 4:
            self.each(one)

    def arrive(self, k):
        parts = self.pieces[k][3]

        def one(step, other):
            self.core(k, step, other, True).wait_recv()
            if parts == 4:
                self.relay(k, step, other, True).wait_recv()

        self.keep(k).wait()
        if parts > 1:
            self.each(one)

    def sent(self, k):
        parts = self.pieces[k][3]

        def one(step, other):
            self.core(k, step, other).wait_send()
            if parts == 4:
                self.across(k, step, other).wait_send()
                self.relay(k, step, other).wait_send()

        steps(1, self.place.length, lambda step: self.line(k, step).wait_send())
        if self.place.sides == 2:
            steps(0, self.place.length, lambda step: self.side(k, step).wait_send())
        if parts > 1:
            self.each(one)

    def events(self, tiles, urgent, ahead=4):
        made = []
        line = side = across = 0.0
        hop = 8.0
        number = len(self.pieces)
        for k in range(number):
            parts = self.pieces[k][3]
            margin = 8.0 if k < urgent else 30.0
            load = tiles[k] * (2 if parts == 4 else 4)
            line = line + load
            side = max(side + load, line + load / 4 + hop)
            last = side
            made.append((line + hop, k, 0))
            made.append((side + hop, k, 1))
            if parts == 4:
                across = max(across + 3.5 * tiles[k], side + tiles[k] / 2 + hop)
                last = across
                made.append((across + hop + margin, k, 2))
            wait = 0.0 if k < urgent else 2 * margin
            made.append((last + 2 * hop + wait + (margin if parts == 4 else 0.0), k, 3))
        made.sort()

        def action(k, kind):
            if kind == 0:
                self.forward(k)
                if k + ahead < number:
                    self.start(k + ahead)
            else:
                (self.spread, self.exchange, self.arrive)[kind - 1](k)

        return [(when, k, kind, functools.partial(action, k, kind)) for when, k, kind in made]


PACK = (16, 512)


def pack_small(gains, taps):
    count = taps.shape[0]

    def fit(values, rows):
        values = values.reshape(count, -1, values.shape[-1]).astype(bf16)
        return jnp.pad(
            values, ((0, 0), (0, rows - values.shape[1]), (0, PACK[1] - values.shape[2]))
        )

    rows = [fit(gains[0], 1), fit(gains[1], 1), fit(gains[2], 2), fit(taps, PACK[0] - 4)]
    return jnp.concatenate(rows, axis=1).reshape(count * PACK[0], PACK[1])


def unpack_small(packed, shapes):
    packed = packed.reshape(-1, PACK[0], PACK[1])
    gains = [packed[:, row, : shape[0]] for row, shape in enumerate(shapes[:3])]
    return gains + [packed[:, 4 : 4 + shapes[3][0], : shapes[3][1]]]


def place_rows(packed, count, width):
    if width % 128 == 0:
        return jnp.concatenate(
            [packed[s * PACK[0] : (s + 1) * PACK[0], :width] for s in range(count)], axis=1
        )
    total = count * width
    row = lax.broadcasted_iota(jnp.int32, (PACK[1], total), 0)
    col = lax.broadcasted_iota(jnp.int32, (PACK[1], total), 1)
    pick = jnp.where(lax.rem(col, width) == row, 1.0, 0.0).astype(bf16)
    wide = nn(packed.astype(bf16), pick)
    row = lax.broadcasted_iota(jnp.int32, wide.shape, 0)
    col = lax.broadcasted_iota(jnp.int32, wide.shape, 1)
    wide = jnp.where(lax.div(row, PACK[0]) == lax.div(col, width), wide, 0.0).astype(bf16)
    row = lax.broadcasted_iota(jnp.int32, (PACK[0], count * PACK[0]), 0)
    col = lax.broadcasted_iota(jnp.int32, (PACK[0], count * PACK[0]), 1)
    fold = jnp.where(lax.rem(col, PACK[0]) == row, 1.0, 0.0).astype(bf16)
    return nn(fold, wide)


GROUP = 2


def grid_indices():
    row = lax.broadcasted_iota(jnp.int32, (CHUNK, CHUNK), 0)
    col = lax.broadcasted_iota(jnp.int32, (CHUNK, CHUNK), 1)
    return row, col


def conv_pre(wide_ref, taps, rows):
    total = None
    for offset in range(TAPS):
        term = taps[offset : offset + 1, :] * wide_ref[pl.ds(HALO - TAPS + 1 + offset, rows), :]
        total = term if total is None else total + term
    return total


def sigmoid(values):
    return 1.0 / (1.0 + jnp.exp(-values))


def head_column(table, head):
    lane = lax.broadcasted_iota(jnp.int32, table.shape, 1)
    return jnp.sum(jnp.where(lane == head, table, 0.0), axis=1, keepdims=True)


ARRAYS = 7


def forward_kernel(count, pieces, mixed, heads, tap_width, *refs):
    tokens_ref = refs[0]
    shards, refs = refs[1 : 1 + ARRAYS], refs[1 + ARRAYS :]
    gathered, refs = refs[:ARRAYS], refs[ARRAYS:]
    (
        finals_ref,
        normed_ref,
        normed_t_ref,
        signals_ref,
        logit_ref,
        taps_ref,
        out_ref,
        carry_ref,
        fresh_ref,
        inverse_ref,
        starts_ref,
    ), refs = refs[:11], refs[11:]
    (
        tokens,
        weights,
        rates_weight,
        packed,
        all_taps,
        wide,
        level_masks,
        final,
        halo_sem,
        token_sem,
        load_sem,
        final_sem,
        *sems,
    ) = refs
    group = pl.program_id(0)
    groups = heads // GROUP
    rows = out_ref.shape[0]
    size = out_ref.shape[1] // GROUP
    span = GROUP * size
    chunks = rows // CHUNK
    levels = CHUNK.bit_length() - 1
    row, col = grid_indices()
    gather = Gather(count, pieces, shards, gathered, sems)
    place = gather.place
    tiles = [piece[2] / 128 * shards[piece[0]].shape[0] / 128 for piece in pieces]
    events = gather.events(tiles, 2 + groups)

    def halo(arriving):
        return remote(
            tokens_ref.at[pl.ds(rows - HALO, HALO), :],
            tokens.at[pl.ds(0, HALO), :],
            halo_sem.at[0],
            halo_sem.at[1],
            {"seq": lax.rem(place.position + 1, 4), "fsdp": place.index},
        )

    def load(step, slot):
        return pltpu.make_async_copy(
            gathered[mixed].at[:, pl.ds(pl.multiple_of(step * 3 * span, 128), 3 * span)],
            weights.at[slot],
            load_sem.at[slot],
        )

    per_step = 12
    plan = {}
    mark = 0
    for step in range(groups):
        for spot in range(per_step):
            now = 50.0 + (step * per_step + spot) * 5.5
            upto = mark
            for index in range(mark, len(events)):
                when, k, kind, _ = events[index]
                if spot == 0 and kind == 3 and (k == 2 + step or (step == 0 and k < 2)):
                    upto = index + 1
                elif when <= now and upto == index:
                    upto = index + 1
            plan[step, spot] = (mark, upto)
            mark = upto
    remaining = (mark, len(events))

    def run(bounds):
        for _, _, _, action in events[bounds[0] : bounds[1]]:
            action()

    def spot(number):
        for step in range(groups):
            bounds = plan[step, number]
            if bounds[1] > bounds[0]:

                @pl.when(group == step)
                def _():
                    run(bounds)

    @pl.when(group == 0)
    def _():
        own = pltpu.make_async_copy(tokens_ref, tokens.at[pl.ds(HALO, rows), :], token_sem.at[0])
        own.start()
        place.greet_all()

        @pl.when(place.position < 3)
        def _():
            halo(False).start()

        gather.start(0)
        gather.start(1)
        gather.start(2)
        gather.start(3)

        @pl.when(place.position == 0)
        def _():
            tokens[pl.ds(0, HALO), :] = jnp.zeros((HALO, tokens.shape[1]), bf16)

        for level in range(levels):
            same = (row >> (level + 1)) == (col >> (level + 1))
            below = ((row >> level) & 1 == 1) & ((col >> level) & 1 == 0)
            level_masks[level] = jnp.where(same & below, 1.0, 0.0).astype(bf16)

        limit = max(i for i, event in enumerate(events) if event[1] == 0) + 1
        run((0, limit))
        copy = pltpu.make_async_copy(gathered[0], packed, token_sem.at[1])
        copy.start()
        copy.wait()
        small = packed[...].astype(f32)
        gain = place_rows(small, count, tokens.shape[1] // count)[0:1, :]
        all_taps[...] = place_rows(small, count, tap_width)[4 : 4 + TAPS, :]
        own.wait()

        @pl.when(place.position > 0)
        def _():
            halo(True).wait_recv()

        block = 208 if tokens.shape[0] % 208 == 0 else HALO

        def norm(index):
            part = pl.ds(pl.multiple_of(index * block, HALO), block)
            normed_ref[part, :] = rms_scale(tokens[part, :].astype(f32), gain).astype(bf16)

        steps(0, tokens.shape[0] // block, norm)
        for first in range(0, rows, CHUNK):
            part = normed_ref[pl.ds(HALO + first, CHUNK), :]
            normed_t_ref[:, first : first + CHUNK] = part.T
        run((limit, plan[0, 0][1]))
        copy = pltpu.make_async_copy(gathered[1], rates_weight, token_sem.at[1])
        copy.start()
        load(0, 0).start()
        copy.wait()
        logit_ref[...] = nn(normed_ref[pl.ds(HALO, rows), :], rates_weight[...]).astype(bf16)
        load(0, 0).wait()

    for step in range(1, groups):
        bounds = plan[step, 0]

        @pl.when(group == step)
        def _():
            run(bounds)
            load(step, 0).start()
            load(step, 0).wait()

    signals_ref[...] = nn(normed_ref[...], weights[0]).astype(bf16)
    spot(1)

    lows = [[], [], []]
    for inner in range(GROUP):
        for which in range(3):
            first = pl.multiple_of((which * heads + group * GROUP + inner) * size, 128)
            taps = all_taps[:, pl.ds(first, size)]
            taps_ref[inner, which] = taps
            wide[...] = signals_ref[:, pl.ds((inner * 3 + which) * size, size)].astype(f32)
            pre = conv_pre(wide, taps, rows)
            act = pre * sigmoid(pre)
            if which < 2:
                act = act * lax.rsqrt(jnp.sum(act * act, axis=1, keepdims=True) + epsilon)
            lows[which].append(act.astype(bf16))
        if inner == 0:
            spot(2)
    spot(3)
    logits = logit_ref[...].astype(f32)
    rates = [sigmoid(head_column(logits, group * GROUP + inner)) for inner in range(GROUP)]
    scaling = size ** (-0.5)
    eye = jnp.where(row == col, 1.0, 0.0)
    lower = row >= col

    work = [(inner, chunk) for inner in range(GROUP) for chunk in range(chunks)]

    def cut(values, item):
        inner, chunk = item
        return values[inner][chunk * CHUNK : (chunk + 1) * CHUNK]

    queries, keys, values = lows
    stricts = [(cut(rates, i) * nt(cut(keys, i), cut(keys, i))).astype(bf16) for i in work]
    results = [eye - (strict * level_masks[0]).astype(f32) for strict in stricts]
    scores = [jnp.where(lower, nt(cut(queries, i), cut(keys, i)), 0.0).astype(bf16) for i in work]
    for level in range(1, levels):
        mask = level_masks[level]
        lowered = [result.astype(bf16) for result in results]
        inners = [nn(low, strict * mask).astype(bf16) for low, strict in zip(lowered, stricts)]
        results = [
            result - nn(inner, low) for result, inner, low in zip(results, inners, lowered)
        ]
        if level in (2, 4, 6):
            spot(3 + level // 2)
    inverses = [result.astype(bf16) for result in results]
    for (inner, chunk), inverse in zip(work, inverses):
        part = slice(chunk * CHUNK, (chunk + 1) * CHUNK)
        inverse_ref[part, inner * CHUNK : (inner + 1) * CHUNK] = inverse
    spot(7)

    srow = lax.broadcasted_iota(jnp.int32, (size, size), 0)
    scol = lax.broadcasted_iota(jnp.int32, (size, size), 1)
    memories = [
        jnp.concatenate(
            [jnp.zeros((size, size), f32), jnp.where(srow == scol, 1.0, 0.0)], axis=1
        )
    ] * GROUP
    for chunk in range(chunks):
        part = slice(chunk * CHUNK, (chunk + 1) * CHUNK)
        for inner in range(GROUP):
            item = (inner, chunk)
            key_part, query_part, rate_part = cut(keys, item), cut(queries, item), cut(rates, item)
            low_memory = memories[inner].astype(bf16)
            starts_ref[inner, chunk] = low_memory
            seen = nn(key_part, low_memory)
            aim = jnp.concatenate(
                [cut(values, item).astype(f32), jnp.zeros((CHUNK, size), f32)], axis=1
            )
            aim = (rate_part * (aim - seen)).astype(bf16)
            fresh = nn(inverses[work.index(item)], aim).astype(bf16)
            fresh_ref[part, inner * 2 * size : (inner + 1) * 2 * size] = fresh
            both = scaling * (
                nn(query_part, low_memory) + nn(scores[work.index(item)], fresh)
            )
            out_ref[part, inner * size : (inner + 1) * size] = both[:, :size]
            carry_ref[part, inner * size : (inner + 1) * size] = both[:, size:].astype(bf16)
            memories[inner] = memories[inner] + tn(key_part, fresh)
        if chunk < 3:
            spot(8 + chunk)

    def send_final(step, hop):
        position = lax.rem(place.position + hop, 4)
        block = pl.ds(step * GROUP, GROUP)
        return remote(
            final.at[block],
            finals_ref.at[place.position, block],
            final_sem.at[0, step, hop],
            final_sem.at[1, step, hop],
            {"seq": position, "fsdp": place.index},
        )

    def keep_final(step):
        block = pl.ds(step * GROUP, GROUP)
        return pltpu.make_async_copy(
            final.at[block], finals_ref.at[place.position, block], final_sem.at[0, step, 0]
        )

    def take_final(step, hop):
        position = lax.rem(place.position + 4 - hop, 4)
        block = pl.ds(step * GROUP, GROUP)
        return remote(
            final.at[block],
            finals_ref.at[position, block],
            final_sem.at[0, step, hop],
            final_sem.at[1, step, hop],
            {"seq": position, "fsdp": place.index},
        )

    for step in range(groups):

        @pl.when(group == step)
        def _():
            for inner in range(GROUP):
                final[step * GROUP + inner] = memories[inner].astype(bf16)
            for hop in range(1, 4):
                send_final(step, hop).start()
            keep_final(step).start()

    spot(11)

    @pl.when(group == groups - 1)
    def _():
        run(remaining)
        for k in range(len(pieces)):
            gather.sent(k)
        for step in range(groups):
            for hop in range(1, 4):
                send_final(step, hop).wait_send()
                take_final(step, hop).wait_recv()
            keep_final(step).wait()

        @pl.when(place.position < 3)
        def _():
            halo(False).wait_send()


def plan_pieces(depths, widths, span):
    def portions(a, wanted):
        while depths[a] % (16 * wanted) != 0:
            wanted //= 2
        return wanted

    pieces = [(0, 0, widths[0], 1), (1, 0, widths[1], portions(1, 2))]
    for step in range(widths[2] // span):
        pieces.append((2, step * span, span, portions(2, 4)))
    pieces.append((3, 0, widths[3], portions(3, 4)))
    for a in (4, 5, 6):
        half = widths[a] // 2
        for part in range(2):
            wanted = 2 if (a, part) in ((5, 0), (6, 1)) else 4
            pieces.append((a, part * half, half, portions(a, wanted)))
    return pieces


def forward(tokens, shards, heads, tap_width):
    count = lax.axis_size("fsdp")
    rows, width = tokens.shape
    size = width // heads
    span = GROUP * size
    groups = heads // GROUP
    chunks = rows // CHUNK
    wide_rows = rows + HALO
    depths = [shard.shape[0] for shard in shards]
    widths = [shard.shape[1] for shard in shards]
    pieces = plan_pieces(depths, widths, 3 * span)
    anywhere = pl.BlockSpec(memory_space=pl.ANY)
    shape = jax.ShapeDtypeStruct
    return pl.pallas_call(
        functools.partial(forward_kernel, count, pieces, 2, heads, tap_width),
        grid=(groups,),
        in_specs=[anywhere] * (1 + ARRAYS),
        out_specs=[anywhere] * (ARRAYS + 1)
        + [
            pl.BlockSpec((wide_rows, width), lambda g: (0, 0)),
            pl.BlockSpec((width, rows), lambda g: (0, 0)),
            pl.BlockSpec((wide_rows, 3 * span), lambda g: (0, g)),
            pl.BlockSpec((rows, widths[1]), lambda g: (0, 0)),
            pl.BlockSpec((GROUP, 3, TAPS, size), lambda g: (g, 0, 0, 0)),
            pl.BlockSpec((rows, span), lambda g: (0, g)),
            pl.BlockSpec((rows, span), lambda g: (0, g)),
            pl.BlockSpec((rows, 2 * span), lambda g: (0, g)),
            pl.BlockSpec((rows, GROUP * CHUNK), lambda g: (0, g)),
            pl.BlockSpec((GROUP, chunks, size, 2 * size), lambda g: (g, 0, 0, 0)),
        ],
        out_shape=[shape((count * d, w), bf16) for d, w in zip(depths, widths)]
        + [
            shape((4, heads, size, 2 * size), bf16),
            shape((wide_rows, width), bf16),
            shape((width, rows), bf16),
            shape((wide_rows, 3 * width), bf16),
            shape((rows, widths[1]), bf16),
            shape((heads, 3, TAPS, size), f32),
            shape((rows, width), f32),
            shape((rows, width), bf16),
            shape((rows, 2 * width), bf16),
            shape((rows, heads * CHUNK), bf16),
            shape((heads, chunks, size, 2 * size), bf16),
        ],
        scratch_shapes=[
            pltpu.VMEM((wide_rows, width), bf16),
            pltpu.VMEM((1, width, 3 * span), bf16),
            pltpu.VMEM((width, widths[1]), bf16),
            pltpu.VMEM((count * PACK[0], PACK[1]), bf16),
            pltpu.VMEM((TAPS, 3 * width), f32),
            pltpu.VMEM((wide_rows, size), f32),
            pltpu.VMEM((CHUNK.bit_length() - 1, CHUNK, CHUNK), bf16),
            pltpu.VMEM((heads, size, 2 * size), bf16),
            pltpu.SemaphoreType.DMA((2,)),
            pltpu.SemaphoreType.DMA((2,)),
            pltpu.SemaphoreType.DMA((2,)),
            pltpu.SemaphoreType.DMA((2, groups, 4)),
        ]
        + Gather.scratch(pieces, count),
        compiler_params=pltpu.CompilerParams(
            collective_id=0, has_side_effects=True, vmem_limit_bytes=60 * MIB
        ),
    )(tokens, *shards)


def mix_kernel(position_ref, out_ref, carry_ref, finals_ref, gain_ref, mixed_ref, state_ref):
    position = position_ref[0]
    size = out_ref.shape[1]
    state = jnp.zeros((size, size), f32)
    for index in range(finals_ref.shape[0] - 1):
        pair = finals_ref[index, 0]
        later = pair[:, :size].astype(f32) + nn(pair[:, size:], state.astype(bf16))
        state = jnp.where(index < position, later, state)
    state_ref[0] = state
    output = out_ref[...] + nn(carry_ref[...], state.astype(bf16))
    gain = gain_ref[...].astype(f32)
    mixed_ref[...] = rms_scale(output, gain).astype(bf16)


def mix(position, outputs, carries, finals, gain):
    rows, width = outputs.shape
    groups, heads, size, _ = finals.shape
    plain = pl.BlockSpec((rows, size), lambda h: (0, h))
    return pl.pallas_call(
        mix_kernel,
        grid=(heads,),
        in_specs=[
            pl.BlockSpec(memory_space=pltpu.SMEM),
            plain,
            plain,
            pl.BlockSpec((groups, 1, size, 2 * size), lambda h: (0, h, 0, 0)),
            pl.BlockSpec((1, size), lambda h: (0, 0)),
        ],
        out_specs=[plain, pl.BlockSpec((1, size, size), lambda h: (h, 0, 0))],
        out_shape=[
            jax.ShapeDtypeStruct((rows, width), bf16),
            jax.ShapeDtypeStruct((heads, size, size), f32),
        ],
        compiler_params=pltpu.CompilerParams(vmem_limit_bytes=63 * MIB),
    )(position, outputs, carries, finals, gain)


def unmix_kernel(
    heads,
    out_ref,
    carry_ref,
    state_ref,
    gain_ref,
    grad_ref,
    grad_out_ref,
    grad_gain_ref,
    grads_ref,
    grad_states,
    sems,
):
    head = pl.program_id(0)
    position, index = lax.axis_index("seq"), lax.axis_index("fsdp")

    def device(hop):
        return {"seq": lax.rem(position + hop, 4), "fsdp": index}

    def send(one, hop, arriving=False):
        source = lax.rem(position + 4 - hop, 4) if arriving else position
        return remote(
            grad_states.at[one],
            grads_ref.at[source, one],
            sems.at[0, one, hop],
            sems.at[1, one, hop],
            device(hop),
        )

    def keep(one):
        return pltpu.make_async_copy(
            grad_states.at[one], grads_ref.at[position, one], sems.at[0, one, 0]
        )

    @pl.when(head == 0)
    def _():
        barrier = pltpu.get_barrier_semaphore()
        for hop in range(1, 4):
            pl.semaphore_signal(barrier, inc=1, device_id=device(hop), device_id_type=MESH)
        grad_gain_ref[...] = jnp.zeros_like(grad_gain_ref)

    output = out_ref[...] + nn(carry_ref[...], state_ref[0].astype(bf16))
    gain = gain_ref[...].astype(f32)
    grad = grad_ref[...].astype(f32)
    scaling = lax.rsqrt(jnp.mean(output * output, axis=1, keepdims=True) + epsilon)
    unit_rows = output * scaling
    grad_gain_ref[...] += jnp.sum(grad * unit_rows, axis=0, keepdims=True)
    scaled = grad * gain
    grad_out = scaling * (scaled - unit_rows * jnp.mean(scaled * unit_rows, axis=1, keepdims=True))
    low_grad = grad_out.astype(bf16)
    grad_states[head] = tn(carry_ref[...], low_grad).astype(bf16)

    @pl.when(head == 0)
    def _():
        pl.semaphore_wait(pltpu.get_barrier_semaphore(), 3)

    for hop in range(1, 4):
        send(head, hop).start()
    keep(head).start()
    grad_out_ref[...] = (grad_out * output.shape[1] ** (-0.5)).astype(bf16)

    @pl.when(head == heads - 1)
    def _():
        def one(step):
            keep(step).wait()
            for hop in range(1, 4):
                send(step, hop).wait_send()
                send(step, hop, True).wait_recv()

        steps(0, heads, one)


def unmix(outputs, carries, states, gain, grad_heads):
    rows, width = outputs.shape
    heads, size, _ = states.shape
    plain = pl.BlockSpec((rows, size), lambda h: (0, h))
    state = pl.BlockSpec((1, size, size), lambda h: (h, 0, 0))
    vector = pl.BlockSpec((1, size), lambda h: (0, 0))
    return pl.pallas_call(
        functools.partial(unmix_kernel, heads),
        grid=(heads,),
        in_specs=[plain, plain, state, vector, plain],
        out_specs=[plain, vector, pl.BlockSpec(memory_space=pl.ANY)],
        out_shape=[
            jax.ShapeDtypeStruct((rows, width), bf16),
            jax.ShapeDtypeStruct((1, size), f32),
            jax.ShapeDtypeStruct((4, heads, size, size), bf16),
        ],
        scratch_shapes=[
            pltpu.VMEM((heads, size, size), bf16),
            pltpu.SemaphoreType.DMA((2, heads, 4)),
        ],
        compiler_params=pltpu.CompilerParams(
            collective_id=1, has_side_effects=True, vmem_limit_bytes=63 * MIB
        ),
    )(outputs, carries, states, gain, grad_heads)


TILE = 256
SLOTS = 3
DENSE_STRIDE = 4


def dense_kernel(count, shapes, *refs):
    (
        mixed_ref,
        w_out_ref,
        gain_ref,
        cotangent_ref,
        gate_ref,
        up_ref,
        down_ref,
        tokens_ref,
        layer_out_ref,
        grad_gain_ref,
        grad_out_ref,
        grad_attended_ref,
        grad_heads_ref,
        rest_ref,
        sums_ref,
        attended,
        normed,
        normed_t,
        cotangent_t,
        result,
        grad_normed,
        source,
        plain_sem,
        rest_sem,
    ), refs = refs[:24], refs[24:]
    tile = pl.program_id(0)
    rows, width = attended.shape
    depth = width // count
    number = len(shapes)
    tiles = number + rest_ref.shape[3] // (3 * TILE)
    blocks = [slice(first, first + CHUNK) for first in range(0, rows, CHUNK)]
    columns = [slice(first, first + CHUNK) for first in range(0, width, CHUNK)]
    gain = gain_ref[...].astype(f32)

    due, later, reduce = {}, [], None
    if number > 0:
        buffers = [refs[i * number : (i + 1) * number] for i in range(Reduce.BUFFERS)]
        sems = refs[Reduce.BUFFERS * number :]
        sources = [source.at[p % SLOTS] for p in range(number)]
        targets = [sums_ref.at[:, pl.ds(p * 3 * TILE, 3 * TILE)] for p in range(number)]
        reduce = Reduce(count, shapes, sources, targets, buffers, None, sems)
        begin = [2 * p + 3 for p in range(number)]
        due, later = reduce.plan(
            begin, [DENSE_STRIDE] * number, 2 * tiles - 1, [False] * number
        )

    def spot(which):
        for step in range(tiles):
            actions = due.get(2 * step + which, ())
            if actions:

                @pl.when(tile == step)
                def _():
                    for action in actions:
                        action()

    def rest(step):
        slot = lax.rem(step, SLOTS)
        first = pl.multiple_of((step - number) * 3 * TILE, 128)
        return pltpu.make_async_copy(
            source.at[slot], rest_ref.at[:, :, :, pl.ds(first, 3 * TILE)], rest_sem.at[slot]
        )

    def fetch(start, target, slot):
        return pltpu.make_async_copy(start, target, plain_sem.at[slot])

    @pl.when(tile == 0)
    def _():
        load = fetch(tokens_ref, normed, 0)
        load.start()
        if reduce is not None:
            reduce.place.greet_all()
        load.wait()
        for block in blocks:
            values = normed[block, :].astype(f32) + nn(mixed_ref[block, :], w_out_ref[...])
            attended[block, :] = values
            result[block, :] = values
            low = rms_scale(values, gain).astype(bf16)
            normed[block, :] = low
            normed_t[:, block] = low.T
            cotangent_t[:, block] = cotangent_ref[block, :].T
        grad_normed[...] = jnp.zeros_like(grad_normed)

    @pl.when(tile >= number + SLOTS)
    def _():
        rest(tile - SLOTS).wait()

    spot(0)
    gate = nn(normed[...], gate_ref[...])
    up = nn(normed[...], up_ref[...])
    grad_hidden = nn(cotangent_ref[...], down_ref[...])
    sig = sigmoid(gate)
    activated = gate * sig
    hidden = (activated * up).astype(bf16)
    grad_gate = (grad_hidden * up * sig * (1.0 + gate * (1.0 - sig))).astype(bf16)
    grad_up = (grad_hidden * activated).astype(bf16)
    slot = lax.rem(tile, SLOTS)
    for which, (left, right) in enumerate(
        ((normed_t, grad_gate), (normed_t, grad_up), (cotangent_t, hidden))
    ):
        piece = nn(left[...], right).astype(bf16).reshape(count // 2, 2, depth, TILE)
        source[slot, :, :, :, pl.ds(which * TILE, TILE)] = piece

    spot(1)
    for column in columns:
        result[:, column] += nt(hidden, down_ref[column, :])
        grad_normed[:, column] += nt(grad_gate, gate_ref[column, :]) + nt(
            grad_up, up_ref[column, :]
        )

    for p in range(number):

        @pl.when(tile == p)
        def _():
            reduce.start(p, False)

    @pl.when(tile >= number)
    def _():
        rest(tile).start()

    @pl.when(tile == tiles - 1)
    def _():
        gain_grad = jnp.zeros((1, width), f32)
        for block in blocks:
            layer_out_ref[block, :] = result[block, :].astype(bf16)
            values = attended[block, :]
            grad = grad_normed[block, :]
            scaling = lax.rsqrt(jnp.mean(values * values, axis=1, keepdims=True) + epsilon)
            unit = values * scaling
            gain_grad = gain_grad + jnp.sum(grad * unit, axis=0, keepdims=True)
            scaled = grad * gain
            grad = cotangent_ref[block, :].astype(f32) + scaling * (
                scaled - unit * jnp.mean(scaled * unit, axis=1, keepdims=True)
            )
            attended[block, :] = grad
            low = grad.astype(bf16)
            normed[block, :] = low
            normed_t[:, block] = mixed_ref[block, :].T
        fetch(attended, grad_attended_ref, 0).start()
        grad_gain_ref[...] = gain_grad
        for block in blocks:
            cotangent_t[block, :] = nt(normed[block, :], w_out_ref[...]).astype(bf16)
        fetch(cotangent_t, grad_heads_ref, 1).start()
        for action in later[: len(later) // 2]:
            action()
        for column in columns:
            grad_out_ref[column, :] = nn(normed_t[column, :], normed[...]).astype(bf16)
        for action in later[len(later) // 2 :]:
            action()
        for p in range(number):
            reduce.finish(p)
        for step in range(max(number, tiles - SLOTS), tiles):
            rest(step).wait()
        fetch(attended, grad_attended_ref, 0).wait()
        fetch(cotangent_t, grad_heads_ref, 1).wait()


def dense(mixed, tokens, w_out, gain, cotangent, w_gate, w_up, w_down_t, number):
    count = lax.axis_size("fsdp")
    rows, width = tokens.shape
    hidden = w_gate.shape[1]
    tiles = hidden // TILE
    depth = width // count
    shapes = [(depth, 3 * TILE, 2 if p % 2 == 0 else 4) for p in range(number)]
    whole = pl.BlockSpec((rows, width), lambda j: (0, 0))
    square = pl.BlockSpec((width, width), lambda j: (0, 0))
    vector = pl.BlockSpec((1, width), lambda j: (0, 0))
    slab = pl.BlockSpec((width, TILE), lambda j: (0, j))
    anywhere = pl.BlockSpec(memory_space=pl.ANY)
    shape = jax.ShapeDtypeStruct
    more = dict(collective_id=3, has_side_effects=True) if number > 0 else {}
    extra = []
    if number > 0:
        extra = Reduce.buffers(count, shapes) + Reduce.semaphores(count, number)
    return pl.pallas_call(
        functools.partial(dense_kernel, count, shapes),
        grid=(tiles,),
        in_specs=[whole, square, vector, whole, slab, slab, slab, anywhere],
        out_specs=[whole, vector, square] + [anywhere] * 4,
        out_shape=[
            shape((rows, width), bf16),
            shape((1, width), f32),
            shape((width, width), bf16),
            shape((rows, width), f32),
            shape((rows, width), bf16),
            shape((count // 2, 2, depth, (tiles - number) * 3 * TILE), bf16),
            shape((depth, max(number, 1) * 3 * TILE), bf16),
        ],
        scratch_shapes=[
            pltpu.VMEM((rows, width), f32),
            pltpu.VMEM((rows, width), bf16),
            pltpu.VMEM((width, rows), bf16),
            pltpu.VMEM((width, rows), bf16),
            pltpu.VMEM((rows, width), f32),
            pltpu.VMEM((rows, width), f32),
            pltpu.VMEM((SLOTS, count // 2, 2, depth, 3 * TILE), bf16),
            pltpu.SemaphoreType.DMA((2,)),
            pltpu.SemaphoreType.DMA((SLOTS,)),
        ]
        + extra,
        compiler_params=pltpu.CompilerParams(vmem_limit_bytes=63 * MIB, **more),
    )(mixed, w_out, gain, cotangent, w_gate, w_up, w_down_t, tokens)


STRIDE = 4


def backward_kernel(
    count, arrays, shapes, loaded_number, heads, tap_width, gain_width, *refs
):
    (
        signals_ref,
        logit_ref,
        taps_ref,
        grad_ref,
        fresh_ref,
        inverse_ref,
        starts_ref,
        state_ref,
        finals_ref,
        grads_ref,
        weights_ref,
        rates_weight_ref,
        gain_ref,
        grad_mlp_ref,
        grad_gain_ref,
        normed_ref,
        tokens_ref,
    ), refs = refs[:17], refs[17:]
    full, refs = refs[:arrays], refs[arrays:]
    grad_tokens_ref, refs = refs[0], refs[1:]
    outs, refs = refs[: arrays + 3], refs[arrays + 3 :]
    (
        normed_t,
        tokens,
        total,
        grad_signals,
        tails,
        firsts,
        edges,
        wides,
        pres,
        grads,
        padded,
        grad_logits,
        small_rows,
        small_source,
        beta_source,
        mixed_source,
        staging,
        plain_sem,
        edge_sem,
    ), refs = refs[:19], refs[19:]
    number = len(shapes)
    buffers = [refs[i * number : (i + 1) * number] for i in range(Reduce.BUFFERS)]
    sems = refs[Reduce.BUFFERS * number :]

    head = pl.program_id(0)
    rows, size = grad_ref.shape
    width = total.shape[1]
    chunks = rows // CHUNK
    row, col = grid_indices()
    lower, upper = row >= col, row <= col

    sources, targets = [], []
    for a in range(arrays):
        halves = max(full[a].shape[3] // (3 * TILE), 1)
        half = full[a].shape[3] // halves
        for part in range(halves):
            columns = pl.ds(part * half, half)
            sources.append(full[a].at[:, :, :, columns])
            targets.append(outs[a].at[:, columns])
    slots = mixed_source.shape[0]
    for one in range(heads):
        sources.append(mixed_source.at[one % slots])
        targets.append(outs[arrays].at[:, pl.ds(one * 3 * size, 3 * size)])
    sources += [beta_source, small_source]
    targets += [outs[arrays + 1], outs[arrays + 2]]
    reduce = Reduce(count, shapes, sources, targets, buffers, staging, sems)
    place = reduce.place
    position = place.position
    loaded = [p < loaded_number for p in range(number)]
    begin = [1 + 3 * (p // 2) for p in range(loaded_number)]
    begin += [2 * one + 5 for one in range(heads)] + [2 * heads + 5, 2 * heads + 6]
    stride = [STRIDE] * loaded_number + [STRIDE - 1] * (number - loaded_number)
    due, later = reduce.plan(begin, stride, 2 * heads, loaded)

    def spot(which):
        for step in range(heads + 1):
            actions = due.get(2 * step + which, ())
            if actions:

                @pl.when(head == step)
                def _():
                    for action in actions:
                        action()

    def fetch(source, target, slot):
        return pltpu.make_async_copy(source, target, plain_sem.at[slot])

    def edge(one, slot, arriving=False):
        return remote(
            firsts.at[slot],
            edges.at[one],
            edge_sem.at[0, one],
            edge_sem.at[1, one],
            reduce.device(3),
        )

    @pl.when(head == 0)
    def _():
        fetch(normed_ref, normed_t, 0).start()
        fetch(tokens_ref, tokens, 1).start()
        place.greet_all()
        for p in range(min(2, loaded_number)):
            reduce.start(p, True)
        total[...] = jnp.zeros_like(total)
        padded[...] = jnp.zeros_like(padded)
        grad_logits[...] = jnp.zeros_like(grad_logits)
        small_rows[...] = jnp.zeros_like(small_rows)
        fetch(normed_ref, normed_t, 0).wait()
        fetch(tokens_ref, tokens, 1).wait()

    spot(0)

    @pl.when(head < heads)
    def _():
        slot = lax.rem(head, 2)
        lows, scales = [], []
        for which in range(3):
            wides[which] = signals_ref[:, pl.ds(which * size, size)].astype(f32)
            pre = conv_pre(wides.at[which], taps_ref[0, which], rows)
            pres[which] = pre
            act = pre * sigmoid(pre)
            if which < 2:
                scale = lax.rsqrt(jnp.sum(act * act, axis=1, keepdims=True) + epsilon)
                act = act * scale
                scales.append(scale)
            lows.append(act.astype(bf16))
        queries, keys, values = lows
        rates = sigmoid(head_column(logit_ref[...].astype(f32), head))

        state = state_ref[0].astype(bf16)
        first = fresh_ref[:, pl.ds(0, size)].astype(f32)
        fresh_all = (first + nn(fresh_ref[:, pl.ds(size, size)], state)).astype(bf16)

        grad_memory = jnp.zeros((size, size), f32)
        for index in reversed(range(1, 4)):
            later = grads_ref[index, 0].astype(f32) + tn(
                finals_ref[index, 0, :, pl.ds(size, size)], grad_memory.astype(bf16)
            )
            grad_memory = jnp.where(index > position, later, grad_memory)
        grad_rates = [None] * chunks
        for chunk in reversed(range(chunks)):
            part = slice(chunk * CHUNK, (chunk + 1) * CHUNK)
            key, query, value, rate = keys[part], queries[part], values[part], rates[part]
            grad_out = grad_ref[part, :]
            fresh = fresh_all[part]
            start = starts_ref[0, chunk]
            memory = (start[:, :size].astype(f32) + nn(start[:, size:], state)).astype(bf16)
            low_grad = grad_memory.astype(bf16)
            key_f = key.astype(f32)
            rated = (rate * key_f).astype(bf16)

            scores_t = jnp.where(upper, nt(key, query), 0.0).astype(bf16)
            grad_fresh = (nn(scores_t, grad_out) + nn(key, low_grad)).astype(bf16)
            aim = tn(inverse_ref[part, :], grad_fresh)
            low_aim = aim.astype(bf16)
            grad_memory = grad_memory + tn(query, grad_out) - tn(rated, low_aim)

            grad_scores = jnp.where(lower, nt(grad_out, fresh), 0.0).astype(bf16)
            grad_scores_t = jnp.where(upper, nt(fresh, grad_out), 0.0).astype(bf16)
            grad_strict = jnp.where(row > col, nt(low_aim, fresh), 0.0).astype(bf16)
            grad_strict_t = jnp.where(row < col, nt(fresh, low_aim), 0.0).astype(bf16)

            grad_query = nt(grad_out, memory) + nn(grad_scores, key)
            within = -(nn(grad_strict, key) + nt(low_aim, memory))
            grad_rates[chunk] = jnp.sum(
                key_f * within + value.astype(f32) * aim, axis=1, keepdims=True
            )
            grad_key = (
                rate * within
                - nn(grad_strict_t, rated)
                + nn(grad_scores_t, query)
                + nt(fresh, low_grad)
            )
            grads[0, part, :] = grad_query
            grads[1, part, :] = grad_key
            grads[2, part, :] = rate * aim
            if chunk == chunks // 2:
                spot(1)

        lane = lax.broadcasted_iota(jnp.int32, grad_logits.shape, 1)
        grad_rate = jnp.concatenate(grad_rates, axis=0)
        grad_logit = grad_rate * rates * (1.0 - rates)
        grad_logits[...] = jnp.where(lane == head, grad_logit, grad_logits[...])

        @pl.when((head >= 2) & (position > 0))
        def _():
            edge(head - 2, slot).wait_send()

        for which in range(3):
            taps = taps_ref[0, which]
            pre = pres[which]
            sig = sigmoid(pre)
            grad_act = grads[which]
            if which < 2:
                unit = pre * sig * scales[which]
                grad_act = scales[which] * (
                    grad_act - unit * jnp.sum(grad_act * unit, axis=1, keepdims=True)
                )
            grad_pre = grad_act * sig * (1.0 + pre * (1.0 - sig))
            padded[pl.ds(HALO, rows), :] = grad_pre
            sums = []
            for offset in range(TAPS):
                shifted = wides[which, pl.ds(HALO - TAPS + 1 + offset, rows), :]
                sums.append(jnp.sum(grad_pre * shifted, axis=0, keepdims=True))
            where = pl.multiple_of((which * heads + head) * size, 128)
            small_rows[4:8, pl.ds(where, size)] = jnp.concatenate(sums, axis=0)

            def back(start, amount):
                result = None
                for offset in range(TAPS):
                    term = (
                        taps[offset : offset + 1, :]
                        * padded[pl.ds(start + TAPS - 1 - offset, amount), :]
                    )
                    result = term if result is None else result + term
                return result

            columns = pl.ds(which * size, size)
            grad_signal = back(HALO, rows)
            grad_signals[slot, :, columns] = grad_signal.astype(bf16)
            tails[slot, :, columns] = grad_signal[rows - HALO :]
            firsts[slot, :, columns] = back(0, HALO)

        @pl.when(position > 0)
        def _():
            edge(head, slot).start()

    for one in range(heads):

        @pl.when(head == one + 1)
        def _():
            slot = one % 2

            @pl.when(position < 3)
            def _():
                edge(one, slot).wait_recv()
                tails[slot] = tails[slot] + edges[one]

            grad_signals[slot, pl.ds(rows - HALO, HALO), :] = tails[slot].astype(bf16)
            grad = grad_signals[slot]
            source = mixed_source.at[one % slots]
            depth = width // count
            half = count // 4
            for part in range(2):
                piece = nn(normed_t[pl.ds(part * 2 * half * depth, 2 * half * depth), :], grad)
                source[pl.ds(part * half, half)] = piece.astype(bf16).reshape(
                    half, 2, depth, 3 * size
                )
            reduce.start(loaded_number + one, False)
            weights = weights_ref[...]
            for part in range(0, rows, CHUNK):
                block = pl.ds(part, CHUNK)
                total[block, :] += nt(grad[part : part + CHUNK], weights)

    @pl.when(head == heads)
    def _():
        depth = width // count
        low_logits = grad_logits[...].astype(bf16)
        beta_source[...] = (
            nn(normed_t[...], low_logits).astype(bf16).reshape(beta_source.shape)
        )
        reduce.start(number - 2, False)
        gain = gain_ref[...].astype(f32)
        weights = rates_weight_ref[...]
        gain_grad = jnp.zeros((1, width), f32)
        for part in range(0, rows, CHUNK):
            block = pl.ds(part, CHUNK)
            grad = total[block, :] + nt(low_logits[part : part + CHUNK], weights)
            values = tokens[block, :].astype(f32)
            scaling = lax.rsqrt(jnp.mean(values * values, axis=1, keepdims=True) + epsilon)
            unit = values * scaling
            gain_grad = gain_grad + jnp.sum(grad * unit, axis=0, keepdims=True)
            scaled = grad * gain
            total[block, :] = scaling * (
                scaled - unit * jnp.mean(scaled * unit, axis=1, keepdims=True)
            )
        fetch(total, grad_tokens_ref, 0).start()
        small_rows[0:1, pl.ds(0, width)] = gain_grad
        small_rows[1:2, pl.ds(0, width)] = grad_mlp_ref[...]
        small_rows[2:3, pl.ds(0, size)] = grad_gain_ref[...]
        small = small_rows[...]
        gains = gather_rows(small[:, :width], count, gain_width)
        last = gather_rows(small[:, :size], count, size // count)
        taps = gather_rows(small, count, tap_width)
        which = lax.broadcasted_iota(jnp.int32, gains.shape, 1)
        small = jnp.where(which == 2, last, jnp.where(which < 2, gains, taps))
        small_source[...] = small.astype(bf16).reshape(small_source.shape)
        reduce.start(number - 1, False)
        for action in later:
            action()
        for p in range(number):
            reduce.finish(p)
        fetch(total, grad_tokens_ref, 0).wait()
        for one in range(heads - 2, heads):

            @pl.when(position > 0)
            def _():
                edge(one, one % 2).wait_send()


def gather_rows(wide, count, width):
    total = count * width
    rows = wide.shape[0]
    if width % 128 == 0:
        blank = jnp.zeros((rows, PACK[1] - width), f32)
        return jnp.stack(
            [
                jnp.concatenate([wide[:, s * width : (s + 1) * width], blank], axis=1)
                for s in range(count)
            ]
        )
    row = lax.broadcasted_iota(jnp.int32, (count * rows, rows), 0)
    col = lax.broadcasted_iota(jnp.int32, (count * rows, rows), 1)
    spread = jnp.where(lax.rem(row, rows) == col, 1.0, 0.0).astype(bf16)
    tall = nn(spread, wide[:, :total].astype(bf16))
    row = lax.broadcasted_iota(jnp.int32, tall.shape, 0)
    col = lax.broadcasted_iota(jnp.int32, tall.shape, 1)
    tall = jnp.where(lax.div(row, rows) == lax.div(col, width), tall, 0.0).astype(bf16)
    row = lax.broadcasted_iota(jnp.int32, (total, PACK[1]), 0)
    col = lax.broadcasted_iota(jnp.int32, (total, PACK[1]), 1)
    pick = jnp.where(lax.rem(row, width) == col, 1.0, 0.0).astype(bf16)
    return nn(tall, pick).reshape(count, rows, PACK[1])


def backward(
    signals,
    logits,
    taps,
    grad_out,
    fresh,
    inverses,
    starts,
    state,
    finals,
    grad_starts,
    w_mixed,
    w_rates,
    gain,
    grad_mlp,
    grad_gain,
    normed_t,
    tokens,
    full,
    tap_width,
    gain_width,
):
    count = lax.axis_size("fsdp")
    wide_rows = signals.shape[0]
    rows, width = grad_out.shape
    heads, _, _, size = taps.shape
    chunks = rows // CHUNK
    depth = width // count
    views = full

    def portions(depth, wanted):
        while depth % (16 * wanted) != 0:
            wanted //= 2
        return wanted

    shapes = []
    for a, view in enumerate(views):
        halves = max(view.shape[3] // (3 * TILE), 1)
        for part in range(halves):
            shapes.append((depth, view.shape[3] // halves, 4 if (a + part) % 2 else 2))
    loaded = len(shapes)
    for head in range(heads):
        shapes.append((depth, 3 * size, portions(depth, 4 if head % 2 == 0 else 2)))
    shapes.append((depth, logits.shape[1], portions(depth, 2)))
    shapes.append(PACK + (1,))
    staged = max([d // 2 for d, _, _ in shapes[:loaded]] + [16])
    widest = max([w for _, w, _ in shapes[:loaded]] + [128])

    def now(h):
        return jnp.minimum(h, heads - 1)

    def before(h):
        return jnp.maximum(h - 1, 0)

    whole = pl.BlockSpec(logits.shape, lambda h: (0, 0))
    vector = pl.BlockSpec((1, width), lambda h: (0, 0))
    anywhere = pl.BlockSpec(memory_space=pl.ANY)
    shape = jax.ShapeDtypeStruct
    return pl.pallas_call(
        functools.partial(
            backward_kernel, count, len(views), shapes, loaded, heads, tap_width, gain_width
        ),
        grid=(heads + 1,),
        in_specs=[
            pl.BlockSpec((wide_rows, 3 * size), lambda h: (0, now(h))),
            whole,
            pl.BlockSpec((1, 3, TAPS, size), lambda h: (now(h), 0, 0, 0)),
            pl.BlockSpec((rows, size), lambda h: (0, now(h))),
            pl.BlockSpec((rows, 2 * size), lambda h: (0, now(h))),
            pl.BlockSpec((rows, CHUNK), lambda h: (0, now(h))),
            pl.BlockSpec((1, chunks, size, 2 * size), lambda h: (now(h), 0, 0, 0)),
            pl.BlockSpec((1, size, size), lambda h: (now(h), 0, 0)),
            pl.BlockSpec((4, 1, size, 2 * size), lambda h: (0, now(h), 0, 0)),
            pl.BlockSpec((4, 1, size, size), lambda h: (0, now(h), 0, 0)),
            pl.BlockSpec((width, 3 * size), lambda h: (0, before(h))),
            pl.BlockSpec(w_rates.shape, lambda h: (0, 0)),
            vector,
            vector,
            pl.BlockSpec((1, size), lambda h: (0, 0)),
        ]
        + [anywhere] * (2 + len(views)),
        out_specs=[anywhere] * (4 + len(views)),
        out_shape=[shape((rows, width), f32)]
        + [shape(view.shape[2:], bf16) for view in views]
        + [
            shape((depth, 3 * width), bf16),
            shape((depth, logits.shape[1]), bf16),
            shape(PACK, bf16),
        ],
        scratch_shapes=[
            pltpu.VMEM((width, rows), bf16),
            pltpu.VMEM((rows, width), bf16),
            pltpu.VMEM((rows, width), f32),
            pltpu.VMEM((2, rows, 3 * size), bf16),
            pltpu.VMEM((2, HALO, 3 * size), f32),
            pltpu.VMEM((2, HALO, 3 * size), f32),
            pltpu.VMEM((heads, HALO, 3 * size), f32),
            pltpu.VMEM((3, wide_rows, size), f32),
            pltpu.VMEM((3, rows, size), f32),
            pltpu.VMEM((3, rows, size), f32),
            pltpu.VMEM((rows + 2 * HALO, size), f32),
            pltpu.VMEM(logits.shape, f32),
            pltpu.VMEM((PACK[0], 3 * width), f32),
            pltpu.VMEM((count // 2, 2) + PACK, bf16),
            pltpu.VMEM((count // 2, 2, depth, logits.shape[1]), bf16),
            pltpu.VMEM((SLOTS, count // 2, 2, depth, 3 * size), bf16),
            pltpu.VMEM((2, count // 2, 2, staged, widest), bf16),
            pltpu.SemaphoreType.DMA((2,)),
            pltpu.SemaphoreType.DMA((2, heads)),
        ]
        + Reduce.buffers(count, shapes)
        + Reduce.semaphores(count, len(shapes)),
        compiler_params=pltpu.CompilerParams(
            collective_id=2, has_side_effects=True, vmem_limit_bytes=63 * MIB
        ),
    )(
        signals,
        logits,
        taps,
        grad_out,
        fresh,
        inverses,
        starts,
        state,
        finals,
        grad_starts,
        w_mixed,
        w_rates,
        gain,
        grad_mlp,
        grad_gain,
        normed_t,
        tokens,
        *views,
    )


def arrange_kernel(q_ref, k_ref, v_ref, down_ref, mixed_ref, down_t_ref):
    size = q_ref.shape[1]
    for which, ref in enumerate((q_ref, k_ref, v_ref)):
        mixed_ref[:, which * size : (which + 1) * size] = ref[...]
    down_t_ref[...] = down_ref[...].T


def arrange(w_query, w_key, w_value, w_down, heads):
    depth, width = w_query.shape
    size = width // heads
    tiles = w_down.shape[0] // TILE
    column = pl.BlockSpec((depth, size), lambda j: (0, jnp.minimum(j, heads - 1)))
    return pl.pallas_call(
        arrange_kernel,
        grid=(tiles,),
        in_specs=[column, column, column, pl.BlockSpec((TILE, depth), lambda j: (j, 0))],
        out_specs=[
            pl.BlockSpec((depth, 3 * size), lambda j: (0, jnp.minimum(j, heads - 1))),
            pl.BlockSpec((depth, TILE), lambda j: (0, j)),
        ],
        out_shape=[
            jax.ShapeDtypeStruct((depth, 3 * width), bf16),
            jax.ShapeDtypeStruct((depth, w_down.shape[0]), bf16),
        ],
        compiler_params=pltpu.CompilerParams(vmem_limit_bytes=63 * MIB),
    )(w_query, w_key, w_value, w_down)


def deliver_kernel(
    number,
    sums_ref,
    rest_ref,
    mixed_ref,
    out_ref,
    attended_ref,
    tokens_ref,
    gate_out,
    up_out,
    down_out,
    query_out,
    key_out,
    value_out,
    out_out,
    tokens_out,
):
    tile = pl.program_id(0)
    packed = jnp.where(tile < number, sums_ref[...], rest_ref[...]).astype(f32)
    gate_out[...] = packed[:, :TILE]
    up_out[...] = packed[:, TILE : 2 * TILE]
    down_out[...] = packed[:, 2 * TILE :].T
    size = query_out.shape[1]
    for which, ref in enumerate((query_out, key_out, value_out)):
        ref[...] = mixed_ref[:, which * size : (which + 1) * size].astype(f32)
    out_out[...] = out_ref[...].astype(f32)
    tokens_out[...] = attended_ref[...] + tokens_ref[...]


def deliver(number, sums, rest, mixed, out, grad_attended, grad_tokens, heads):
    depth, width = out.shape
    size = width // heads
    rows = grad_tokens.shape[0] // heads
    tiles = number + rest.shape[1] // (3 * TILE)

    def head(j):
        return jnp.minimum(j, heads - 1)

    column = pl.BlockSpec((depth, size), lambda j: (0, head(j)))
    block = pl.BlockSpec((rows, width), lambda j: (head(j), 0))
    tile = pl.BlockSpec((depth, TILE), lambda j: (0, j))
    shape = jax.ShapeDtypeStruct
    return pl.pallas_call(
        functools.partial(deliver_kernel, number),
        grid=(tiles,),
        in_specs=[
            pl.BlockSpec((depth, 3 * TILE), lambda j: (0, jnp.minimum(j, number - 1))),
            pl.BlockSpec((depth, 3 * TILE), lambda j: (0, jnp.maximum(j - number, 0))),
            pl.BlockSpec((depth, 3 * size), lambda j: (0, head(j))),
            column,
            block,
            block,
        ],
        out_specs=[
            tile,
            tile,
            pl.BlockSpec((TILE, depth), lambda j: (j, 0)),
            column,
            column,
            column,
            column,
            block,
        ],
        out_shape=[
            shape((depth, tiles * TILE), f32),
            shape((depth, tiles * TILE), f32),
            shape((tiles * TILE, depth), f32),
            shape((depth, width), f32),
            shape((depth, width), f32),
            shape((depth, width), f32),
            shape((depth, width), f32),
            shape(grad_tokens.shape, f32),
        ],
        compiler_params=pltpu.CompilerParams(vmem_limit_bytes=63 * MIB),
    )(sums, rest, mixed, out, grad_attended, grad_tokens)


def local(
    inputs,
    g_attn,
    w_query,
    w_key,
    w_value,
    w_beta,
    conv_taps,
    o_gain,
    w_out,
    g_mlp,
    w_gate,
    w_up,
    w_down,
    cotangent,
):
    count = lax.axis_size("fsdp")
    position = lax.axis_index("seq")
    groups = lax.axis_size("seq")
    tokens_low = inputs[0]
    rows, width = tokens_low.shape
    heads = w_beta.shape[1]
    size = width // heads
    depth = w_query.shape[0]
    small = (g_attn.shape, g_mlp.shape, o_gain.shape, conv_taps.shape)
    packed = pack_small((g_attn[None], g_mlp[None], o_gain[None]), conv_taps[None])
    if depth % 128 == 0:
        mixed, down_t = arrange(w_query, w_key, w_value, w_down, heads)
    else:
        mixed = jnp.stack([w.reshape(depth, -1, size) for w in (w_query, w_key, w_value)], axis=2)
        mixed, down_t = mixed.reshape(depth, 3 * width), jnp.transpose(w_down)
    shards = (
        packed,
        jnp.pad(w_beta, ((0, 0), (0, 128 - heads))),
        mixed,
        w_out,
        w_gate,
        w_up,
        down_t,
    )
    results = forward(tokens_low, shards, heads, conv_taps.shape[1])
    packed, w_beta, w_mixed, w_out, w_gate, w_up, w_down_t = results[:ARRAYS]
    finals, _, normed_t, signals, logits, taps = results[ARRAYS : ARRAYS + 6]
    outputs, carries, fresh, inverses, starts = results[ARRAYS + 6 :]
    g_attn, g_mlp, o_gain, _ = unpack_small(packed, small)
    g_attn, g_mlp, o_gain = g_attn.reshape(-1), g_mlp.reshape(-1), o_gain.reshape(-1)

    gain_out = o_gain.reshape(1, size)
    head_rows, state_in = mix(position.reshape(1), outputs, carries, finals, gain_out)
    tiles = w_gate.shape[1] // TILE
    beside = depth % 64 == 0
    number = tiles - 4 if beside else 0
    layer_out, grad_gain_mlp, grad_out_matrix, grad_attended, grad_heads, rest, sums = dense(
        head_rows,
        tokens_low,
        w_out,
        g_mlp.reshape(1, -1),
        cotangent[0],
        w_gate,
        w_up,
        w_down_t,
        number,
    )
    grad_delta, grad_gain_out, grad_starts = unmix(
        outputs, carries, state_in, gain_out, grad_heads
    )
    full = (rest, grad_out_matrix.reshape(count // 2, 2, depth, width))
    results = backward(
        signals,
        logits,
        taps,
        grad_delta,
        fresh,
        inverses,
        starts,
        state_in,
        finals,
        grad_starts,
        w_mixed,
        w_beta,
        g_attn.reshape(1, -1),
        grad_gain_mlp,
        grad_gain_out,
        normed_t,
        tokens_low,
        full if beside else (),
        small[3][1],
        small[0][0],
    )
    grad_from_attn, full_sums = results[0], results[1:-3]
    grad_mixed_matrix, grad_beta_matrix, packed = results[-3:]
    if beside and depth % 128 == 0:
        (
            grad_gate_matrix,
            grad_up_matrix,
            grad_down_matrix,
            grad_query_matrix,
            grad_key_matrix,
            grad_value_matrix,
            grad_out_matrix,
            grad_inputs,
        ) = deliver(
            number,
            sums,
            full_sums[0],
            grad_mixed_matrix,
            full_sums[1],
            grad_attended,
            grad_from_attn,
            heads,
        )
    else:
        if beside:
            sums, grad_out_matrix = jnp.concatenate([sums, full_sums[0]], axis=1), full_sums[1]
        else:
            sums, grad_out_matrix = (
                lax.psum(
                    lax.psum_scatter(
                        g.reshape((count,) + g.shape[2:]), "fsdp", scatter_dimension=0
                    ),
                    "seq",
                )
                for g in full
            )
        sums = sums.astype(f32).reshape(depth, tiles, 3, TILE)
        grad_gate_matrix, grad_up_matrix, grad_down_t = (
            sums[:, :, which].reshape(depth, tiles * TILE) for which in range(3)
        )
        grad_down_matrix = jnp.transpose(grad_down_t)
        grad_mixed_matrix = grad_mixed_matrix.astype(f32).reshape(depth, heads, 3, size)
        grad_query_matrix, grad_key_matrix, grad_value_matrix = (
            grad_mixed_matrix[:, :, which].reshape(depth, width) for which in range(3)
        )
        grad_out_matrix = grad_out_matrix.astype(f32)
        grad_inputs = grad_attended + grad_from_attn
    parts = [part[0].astype(f32) for part in unpack_small(packed, small)]
    grad_gain_attn, grad_gain_mlp, grad_gain_out, grad_taps = parts
    return (
        layer_out[None],
        grad_inputs[None],
        grad_gain_attn,
        grad_query_matrix,
        grad_key_matrix,
        grad_value_matrix,
        grad_beta_matrix[:, :heads].astype(f32),
        grad_taps,
        grad_gain_out,
        grad_out_matrix,
        grad_gain_mlp,
        grad_gate_matrix,
        grad_up_matrix,
        grad_down_matrix,
    )


def solution(mesh):
    vector = P("fsdp")
    rows = P("fsdp", None)
    columns = P(None, "fsdp")
    tokens = P("fsdp", "seq", None)
    return jax.shard_map(
        local,
        mesh=mesh,
        in_specs=(
            tokens,
            vector,
            rows,
            rows,
            rows,
            rows,
            columns,
            vector,
            rows,
            vector,
            rows,
            rows,
            columns,
            tokens,
        ),
        out_specs=(
            tokens,
            tokens,
            vector,
            rows,
            rows,
            rows,
            rows,
            columns,
            vector,
            rows,
            vector,
            rows,
            rows,
            columns,
        ),
        check_vma=False,
    )
```

```python
import functools

import jax
import jax.numpy as jnp
from jax import lax
from jax.experimental import pallas as pl
from jax.experimental.pallas import tpu as pltpu
from jax.sharding import PartitionSpec as P

CHUNK = 256
HALO = 16
TAPS = 4
MIB = 1024 * 1024

highest = lax.Precision.HIGHEST
epsilon = 1e-06
f32 = jnp.float32
bf16 = jnp.bfloat16


def nn(left_side, right_side):
    return lax.dot_general(
        left_side, right_side, (((1,), (0,)), ((), ())), preferred_element_type=f32
    )


def nt(left_side, right_side):
    return lax.dot_general(
        left_side, right_side, (((1,), (1,)), ((), ())), preferred_element_type=f32
    )


def tn(left_side, right_side):
    return lax.dot_general(
        left_side, right_side, (((0,), (0,)), ((), ())), preferred_element_type=f32
    )


def rms_scale(values, gain_vec):
    return (
        values * lax.rsqrt(jnp.mean(values * values, axis=-1, keepdims=True) + epsilon) * gain_vec
    )


def norm_backward(values, gain_vec, grad_out):
    scaling = lax.rsqrt(jnp.mean(values * values, axis=-1, keepdims=True) + epsilon)
    unit_rows = values * scaling
    gain_grad = jnp.sum(grad_out * unit_rows, axis=0)
    scaled_grad = grad_out * gain_vec
    input_grad = scaling * (
        scaled_grad - unit_rows * jnp.mean(scaled_grad * unit_rows, axis=-1, keepdims=True)
    )
    return (input_grad, gain_grad)


MESH = pl.DeviceIdType.MESH


class Place:
    def __init__(self, count):
        self.count = count
        self.sides = 2 if count % 2 == 0 else 1
        self.length = count // self.sides
        self.position = lax.axis_index("seq")
        self.index = lax.axis_index("fsdp")
        self.core = lax.rem(self.position, 2)
        self.chip = lax.div(self.position, 2)
        self.side = lax.rem(self.index, self.sides)
        self.spot = lax.div(self.index, self.sides)

    def sibling(self):
        return {"seq": self.position + 1 - 2 * self.core, "fsdp": self.index}

    def across(self):
        return {"seq": lax.rem(self.position + 2, 4), "fsdp": self.index}

    def partner(self):
        return {"seq": self.position, "fsdp": self.spot * 2 + 1 - self.side}

    def ahead(self, step):
        spot = lax.rem(self.spot + step, self.length)
        return {"seq": self.position, "fsdp": spot * self.sides + self.side}

    def shard(self, spot, side):
        return spot * self.sides + side

    def behind(self, step):
        return lax.rem(self.spot + self.length - step, self.length)

    def greet_all(self):
        self.greet(False, True)

    def greet(self, across, sequence=False):
        barrier = pltpu.get_barrier_semaphore()
        total = self.length - 1

        def signal(device):
            pl.semaphore_signal(barrier, inc=1, device_id=device, device_id_type=MESH)

        def one(step, carry):
            signal(self.ahead(step))
            return carry

        lax.fori_loop(1, self.length, one, 0)
        if sequence:
            for hop in range(1, 4):
                signal({"seq": lax.rem(self.position + hop, 4), "fsdp": self.index})
            total += 3
        else:
            signal(self.sibling())
            total += 1
        if self.sides == 2:
            signal(self.partner())
            total += 1
        if across:
            signal(self.across())
            total += 1
        pl.semaphore_wait(barrier, total)


def remote(source, target, send, recv, device):
    return pltpu.make_async_remote_copy(
        src_ref=source,
        dst_ref=target,
        send_sem=send,
        recv_sem=recv,
        device_id=device,
        device_id_type=MESH,
    )


def steps(first, last, body):
    def one(step, carry):
        body(step)
        return carry

    lax.fori_loop(first, last, one, 0)


class Reduce:
    BUFFERS = 6

    def __init__(self, count, pieces, sources, targets, buffers, staging, sems):
        self.place = Place(count)
        self.pieces, self.sources, self.targets, self.staging = pieces, sources, targets, staging
        self.acc, self.x_in, self.y_in, self.z_in, self.parts_in, self.result = buffers
        (
            self.core_sem,
            self.load_sem,
            self.x_sem,
            self.y_sem,
            self.z_sem,
            self.share_sem,
            self.final_sem,
            self.store_sem,
        ) = sems

    @staticmethod
    def buffers(count, pieces):
        length = count // 2
        acc, x_in, y_in, z_in, parts_in, result = [], [], [], [], [], []
        for depth, width, parts in pieces:
            rows = depth // parts
            acc.append(pltpu.VMEM((length, 2, depth // min(parts, 2), width), bf16))
            x_in.append(
                pltpu.VMEM((length, 2, rows, width) if parts == 4 else (1, 1, 16, 128), bf16)
            )
            y_in.append(pltpu.VMEM((length, rows, width), bf16))
            z_in.append(pltpu.VMEM((length, rows, width), bf16))
            parts_in.append(
                pltpu.VMEM((4 // parts, rows, width) if parts < 4 else (1, 16, 128), bf16)
            )
            result.append(pltpu.VMEM((rows, width), bf16))
        return acc + x_in + y_in + z_in + parts_in + result

    @staticmethod
    def semaphores(count, number):
        pair = pltpu.SemaphoreType.DMA((number, 2))
        one = pltpu.SemaphoreType.DMA((number,))
        hops = pltpu.SemaphoreType.DMA((number, 2, 4))
        return [pair, one, pair, pair, pair, hops, hops, one]

    def half(self, p, core):
        depth, _, parts = self.pieces[p]
        rows = depth // min(parts, 2)
        return pl.ds(pl.multiple_of(core * rows, 16) if parts > 1 else 0, rows)

    def quarter(self, p, chip):
        depth, _, parts = self.pieces[p]
        rows = depth // parts
        return pl.ds(pl.multiple_of(chip * rows, 16) if parts == 4 else 0, rows)

    def device(self, hop):
        return {"seq": lax.rem(self.place.position + hop, 4), "fsdp": self.place.index}

    def to_sibling(self, p):
        return remote(
            self.sources[p].at[:, :, self.half(p, 1 - self.place.core), :],
            self.acc[p],
            self.core_sem.at[p, 0],
            self.core_sem.at[p, 1],
            self.place.sibling(),
        )

    def stage(self, p):
        depth, width, parts = self.pieces[p]
        return self.staging.at[p % 2, :, :, pl.ds(0, depth // 2), pl.ds(0, width)]

    def load(self, p):
        return pltpu.make_async_copy(
            self.sources[p].at[:, :, self.half(p, self.place.core), :],
            self.stage(p),
            self.load_sem.at[p],
        )

    def to_x(self, p):
        return remote(
            self.acc[p].at[:, :, self.quarter(p, 1 - self.place.chip), :],
            self.x_in[p],
            self.x_sem.at[p, 0],
            self.x_sem.at[p, 1],
            self.place.across(),
        )

    def to_y(self, p):
        place = self.place
        return remote(
            self.acc[p].at[:, 1 - place.side, self.quarter(p, place.chip), :],
            self.y_in[p],
            self.y_sem.at[p, 0],
            self.y_sem.at[p, 1],
            place.partner(),
        )

    def to_z(self, p, step):
        place = self.place
        spot = lax.rem(place.spot + step, place.length)
        return remote(
            self.acc[p].at[spot, place.side, self.quarter(p, place.chip), :],
            self.z_in[p].at[step],
            self.z_sem.at[p, 0],
            self.z_sem.at[p, 1],
            place.ahead(step),
        )

    def all_z(self, p):
        both = self.z_in[p].at[pl.ds(1, self.place.length - 1)]
        return remote(
            both, both, self.z_sem.at[p, 0], self.z_sem.at[p, 1], self.place.ahead(1)
        )

    def sharers(self, p):
        return {1: (1, 2, 3), 2: (2,), 4: ()}[self.pieces[p][2]]

    def receivers(self, p):
        return {1: (), 2: (0,), 4: (1, 2, 3)}[self.pieces[p][2]]

    def sharer(self, p, position):
        return position if self.pieces[p][2] == 1 else lax.div(position, 2)

    def to_share(self, p, hop, arriving=False):
        position = self.place.position
        source = lax.rem(position + 4 - hop, 4) if arriving else position
        buffer = self.parts_in[p].at[self.sharer(p, source)]
        return remote(
            buffer,
            buffer,
            self.share_sem.at[p, 0, hop],
            self.share_sem.at[p, 1, hop],
            self.device(hop),
        )

    def target(self, p, position):
        depth, _, parts = self.pieces[p]
        rows = depth // parts
        core, chip = lax.rem(position, 2), lax.div(position, 2)
        first = {1: 0, 2: core * rows, 4: (core * 2 + chip) * rows}[parts]
        return self.targets[p].at[pl.ds(pl.multiple_of(first, 16) if parts > 1 else 0, rows), :]

    def to_result(self, p, hop, arriving=False):
        place = self.place
        if hop == 0:
            other = place.position + 1 - 2 * place.core
            device = place.sibling()
        else:
            other = lax.rem(place.position + 4 - hop, 4)
            device = self.device(hop)
        return remote(
            self.result[p],
            self.target(p, other if arriving else place.position),
            self.final_sem.at[p, 0, hop],
            self.final_sem.at[p, 1, hop],
            device,
        )

    def store(self, p):
        return pltpu.make_async_copy(
            self.result[p], self.target(p, self.place.position), self.store_sem.at[p]
        )

    def start(self, p, loaded):
        if self.pieces[p][2] > 1:
            self.to_sibling(p).start()
        if loaded:
            self.load(p).start()

    def on_core(self, p, loaded):
        parts = self.pieces[p][2]
        acc = self.acc[p]
        half = self.half(p, self.place.core)
        rows, width = acc.shape[2], acc.shape[3]
        if loaded:
            self.load(p).wait()
        if parts == 1:
            acc[...] = self.sources[p][...]
        else:
            self.to_sibling(p).wait_recv()

            def add(spot):
                if loaded:
                    own = self.staging[p % 2, spot, :, pl.ds(0, rows), pl.ds(0, width)]
                else:
                    own = self.sources[p][spot, :, half, :]
                acc[spot] = acc[spot] + own

            steps(0, self.place.length, add)
        (self.to_x if parts == 4 else self.to_y)(p).start()
        if parts > 1:
            self.to_sibling(p).wait_send()

    def on_x(self, p):
        acc, side = self.acc[p], 1 - self.place.side
        rows = self.quarter(p, self.place.chip)
        self.to_x(p).wait_recv()

        def add(spot):
            acc[spot, side, rows, :] = acc[spot, side, rows, :] + self.x_in[p][spot, side]

        steps(0, self.place.length, add)
        self.to_y(p).start()

    def on_y(self, p):
        place = self.place
        acc = self.acc[p]
        rows = self.quarter(p, place.chip)
        self.to_y(p).wait_recv()

        def one(step):
            spot = lax.rem(place.spot + step, place.length)
            total = acc[spot, place.side, rows, :].astype(f32) + self.y_in[p][spot].astype(f32)
            if self.pieces[p][2] == 4:
                total = total + self.x_in[p][spot, place.side].astype(f32)
            acc[spot, place.side, rows, :] = total.astype(bf16)

        def send(step):
            one(step)
            self.to_z(p, step).start()

        steps(1, place.length, send)
        one(0)

    def on_z(self, p):
        place = self.place
        rows = self.quarter(p, place.chip)
        self.all_z(p).wait_recv()
        total = self.acc[p][place.spot, place.side, rows, :].astype(f32)
        if place.length <= 8:
            for step in range(1, place.length):
                total = total + self.z_in[p][step].astype(f32)
        else:
            total = lax.fori_loop(
                1,
                place.length,
                lambda step, carry: carry + self.z_in[p][step].astype(f32),
                total,
            )
        if self.pieces[p][2] == 4:
            self.result[p][...] = total.astype(bf16)
            self.publish(p)
        else:
            self.parts_in[p][self.sharer(p, place.position)] = total.astype(bf16)
            for hop in self.sharers(p):
                self.to_share(p, hop).start()

    def on_share(self, p):
        total = None
        for hop in self.sharers(p):
            self.to_share(p, hop, True).wait_recv()
        for index in range(4 // self.pieces[p][2]):
            term = self.parts_in[p][index].astype(f32)
            total = term if total is None else total + term
        self.result[p][...] = total.astype(bf16)
        self.publish(p)

    def publish(self, p):
        for hop in self.receivers(p):
            self.to_result(p, hop).start()
        self.store(p).start()

    def finish(self, p):
        if self.pieces[p][2] == 4:
            self.to_x(p).wait_send()
        self.to_y(p).wait_send()
        self.all_z(p).wait_send()
        for hop in self.sharers(p):
            self.to_share(p, hop).wait_send()
        for hop in self.receivers(p):
            self.to_result(p, hop).wait_send()
            self.to_result(p, hop, True).wait_recv()
        self.store(p).wait()

    def plan(self, begin, stride, last, loaded, idle=()):
        due = []
        for p, (_, _, parts) in enumerate(self.pieces):
            for index, kind in enumerate((0, 1, 2, 3) if parts == 4 else (0, 2, 3, 4)):
                half = begin[p] + stride[p] * index
                while half in idle:
                    half += 1
                due.append((half, -index, p, kind))
        due.sort()

        def action(p, kind):
            if kind == 0:
                self.on_core(p, loaded[p])
                if loaded[p] and p + 2 < len(self.pieces) and loaded[p + 2]:
                    self.start(p + 2, True)
            else:
                (self.on_x, self.on_y, self.on_z, self.on_share)[kind - 1](p)

        def at(test):
            return [functools.partial(action, p, kind) for half, _, p, kind in due if test(half)]

        return (
            {half: at(lambda when: when == half) for half in range(last + 1)},
            at(lambda when: when > last),
        )


class Gather:
    SEMS = 6

    def __init__(self, count, pieces, shards, outs, sems):
        self.place = Place(count)
        self.pieces, self.shards, self.outs = pieces, shards, outs
        self.line_sem, self.side_sem, self.core_sem, self.across_sem, self.relay_sem, self.own = (
            sems
        )

    @staticmethod
    def scratch(pieces, count):
        length = count // 2 if count % 2 == 0 else count
        number = len(pieces)
        slots = 2 * length if max(piece[3] for piece in pieces) > 1 else 1
        return [
            pltpu.SemaphoreType.DMA((number, 2, length)),
            pltpu.SemaphoreType.DMA((number, 2, length)),
            pltpu.SemaphoreType.DMA((number, 2, slots)),
            pltpu.SemaphoreType.DMA((number, 2, slots)),
            pltpu.SemaphoreType.DMA((number, 2, slots)),
            pltpu.SemaphoreType.DMA((number,)),
        ]

    def portion(self, k, core, chip):
        parts = self.pieces[k][3]
        if parts == 1:
            return 0
        return core if parts == 2 else 2 * chip + core

    def region(self, k, shard, core, chip):
        a, offset, width, parts = self.pieces[k]
        depth = self.shards[a].shape[0]
        rows = depth // parts
        first = shard * depth + self.portion(k, core, chip) * rows
        return self.outs[a].at[pl.ds(pl.multiple_of(first, 16), rows), pl.ds(offset, width)]

    def source(self, k):
        p = self.place
        a, offset, width, parts = self.pieces[k]
        rows = self.shards[a].shape[0] // parts
        first = self.portion(k, p.core, p.chip) * rows
        return self.shards[a].at[pl.ds(pl.multiple_of(first, 16), rows), pl.ds(offset, width)]

    def line(self, k, step, arriving=False):
        p = self.place
        shard = p.shard(p.behind(step), p.side) if arriving else p.index
        target = self.region(k, shard, p.core, p.chip)
        return remote(
            target if arriving else self.source(k),
            target,
            self.line_sem.at[k, 0, step],
            self.line_sem.at[k, 1, step],
            p.ahead(step),
        )

    def side(self, k, step, arriving=False, own=False):
        p = self.place
        shard = p.shard(p.behind(step), 1 - p.side if arriving else p.side)
        target = self.region(k, shard, p.core, p.chip)
        return remote(
            self.source(k) if own else target,
            target,
            self.side_sem.at[k, 0, step],
            self.side_sem.at[k, 1, step],
            p.partner(),
        )

    def cross(self, k, step, other, sems, core, chip, device):
        p = self.place
        shard = p.shard(p.behind(step), 1 - p.side if other else p.side)
        target = self.region(k, shard, core, chip)
        slot = 2 * step + (1 if other else 0)
        return remote(target, target, sems.at[k, 0, slot], sems.at[k, 1, slot], device)

    def core(self, k, step, other, arriving=False):
        p = self.place
        core = 1 - p.core if arriving else p.core
        return self.cross(k, step, other, self.core_sem, core, p.chip, p.sibling())

    def across(self, k, step, other, arriving=False):
        p = self.place
        chip = 1 - p.chip if arriving else p.chip
        return self.cross(k, step, other, self.across_sem, p.core, chip, p.across())

    def relay(self, k, step, other, arriving=False):
        p = self.place
        core = 1 - p.core if arriving else p.core
        return self.cross(k, step, other, self.relay_sem, core, 1 - p.chip, p.sibling())

    def keep(self, k):
        a, offset, width, _ = self.pieces[k]
        depth = self.shards[a].shape[0]
        rows = pl.ds(pl.multiple_of(self.place.index * depth, 16), depth)
        columns = pl.ds(offset, width)
        return pltpu.make_async_copy(
            self.shards[a].at[:, columns], self.outs[a].at[rows, columns], self.own.at[k]
        )

    def hand(self, k, step, other):
        parts = self.pieces[k][3]
        if parts == 4:
            self.across(k, step, other).start()
        if parts > 1:
            self.core(k, step, other).start()

    def start(self, k):
        steps(1, self.place.length, lambda step: self.line(k, step).start())
        if self.place.sides == 2:
            self.side(k, 0, own=True).start()
        self.keep(k).start()

    def forward(self, k):
        def one(step):
            self.line(k, step, True).wait_recv()
            if self.place.sides == 2:
                self.side(k, step).start()
            self.hand(k, step, False)

        steps(1, self.place.length, one)

    def spread(self, k):
        def one(step):
            self.side(k, step, True).wait_recv()
            self.hand(k, step, True)

        if self.place.sides == 2:
            steps(0, self.place.length, one)

    def each(self, body):
        steps(1, self.place.length, lambda step: body(step, False))
        if self.place.sides == 2:
            steps(0, self.place.length, lambda step: body(step, True))

    def exchange(self, k):
        def one(step, other):
            self.across(k, step, other, True).wait_recv()
            self.relay(k, step, other).start()

        if self.pieces[k][3] == 4:
            self.each(one)

    def arrive(self, k):
        parts = self.pieces[k][3]

        def one(step, other):
            self.core(k, step, other, True).wait_recv()
            if parts == 4:
                self.relay(k, step, other, True).wait_recv()

        self.keep(k).wait()
        if parts > 1:
            self.each(one)

    def sent(self, k):
        parts = self.pieces[k][3]

        def one(step, other):
            self.core(k, step, other).wait_send()
            if parts == 4:
                self.across(k, step, other).wait_send()
                self.relay(k, step, other).wait_send()

        steps(1, self.place.length, lambda step: self.line(k, step).wait_send())
        if self.place.sides == 2:
            steps(0, self.place.length, lambda step: self.side(k, step).wait_send())
        if parts > 1:
            self.each(one)

    def events(self, tiles, urgent, ahead=4):
        made = []
        line = side = across = 0.0
        hop = 8.0
        number = len(self.pieces)
        for k in range(number):
            parts = self.pieces[k][3]
            margin = 8.0 if k < urgent else 30.0
            load = tiles[k] * (2 if parts == 4 else 4)
            line = line + load
            side = max(side + load, line + load / 4 + hop)
            last = side
            made.append((line + hop, k, 0))
            made.append((side + hop, k, 1))
            if parts == 4:
                across = max(across + 3.5 * tiles[k], side + tiles[k] / 2 + hop)
                last = across
                made.append((across + hop + margin, k, 2))
            wait = 0.0 if k < urgent else 2 * margin
            made.append((last + 2 * hop + wait + (margin if parts == 4 else 0.0), k, 3))
        made.sort()

        def action(k, kind):
            if kind == 0:
                self.forward(k)
                if k + ahead < number:
                    self.start(k + ahead)
            else:
                (self.spread, self.exchange, self.arrive)[kind - 1](k)

        return [(when, k, kind, functools.partial(action, k, kind)) for when, k, kind in made]


PACK = (16, 512)


def pack_small(gains, taps):
    count = taps.shape[0]

    def fit(values, rows):
        values = values.reshape(count, -1, values.shape[-1]).astype(bf16)
        return jnp.pad(
            values, ((0, 0), (0, rows - values.shape[1]), (0, PACK[1] - values.shape[2]))
        )

    rows = [fit(gains[0], 1), fit(gains[1], 1), fit(gains[2], 2), fit(taps, PACK[0] - 4)]
    return jnp.concatenate(rows, axis=1).reshape(count * PACK[0], PACK[1])


def unpack_small(packed, shapes):
    packed = packed.reshape(-1, PACK[0], PACK[1])
    gains = [packed[:, row, : shape[0]] for row, shape in enumerate(shapes[:3])]
    return gains + [packed[:, 4 : 4 + shapes[3][0], : shapes[3][1]]]


def place_rows(packed, count, width):
    if width % 128 == 0:
        return jnp.concatenate(
            [packed[s * PACK[0] : (s + 1) * PACK[0], :width] for s in range(count)], axis=1
        )
    total = count * width
    row = lax.broadcasted_iota(jnp.int32, (PACK[1], total), 0)
    col = lax.broadcasted_iota(jnp.int32, (PACK[1], total), 1)
    pick = jnp.where(lax.rem(col, width) == row, 1.0, 0.0).astype(bf16)
    wide = nn(packed.astype(bf16), pick)
    row = lax.broadcasted_iota(jnp.int32, wide.shape, 0)
    col = lax.broadcasted_iota(jnp.int32, wide.shape, 1)
    wide = jnp.where(lax.div(row, PACK[0]) == lax.div(col, width), wide, 0.0).astype(bf16)
    row = lax.broadcasted_iota(jnp.int32, (PACK[0], count * PACK[0]), 0)
    col = lax.broadcasted_iota(jnp.int32, (PACK[0], count * PACK[0]), 1)
    fold = jnp.where(lax.rem(col, PACK[0]) == row, 1.0, 0.0).astype(bf16)
    return nn(fold, wide)


GROUP = 2


def grid_indices():
    row = lax.broadcasted_iota(jnp.int32, (CHUNK, CHUNK), 0)
    col = lax.broadcasted_iota(jnp.int32, (CHUNK, CHUNK), 1)
    return row, col


def conv_pre(wide_ref, taps, rows):
    total = None
    for offset in range(TAPS):
        term = taps[offset : offset + 1, :] * wide_ref[pl.ds(HALO - TAPS + 1 + offset, rows), :]
        total = term if total is None else total + term
    return total


def sigmoid(values):
    return 1.0 / (1.0 + jnp.exp(-values))


def head_column(table, head):
    lane = lax.broadcasted_iota(jnp.int32, table.shape, 1)
    return jnp.sum(jnp.where(lane == head, table, 0.0), axis=1, keepdims=True)


ARRAYS = 7


def forward_kernel(count, pieces, mixed, heads, tap_width, *refs):
    tokens_ref = refs[0]
    shards, refs = refs[1 : 1 + ARRAYS], refs[1 + ARRAYS :]
    gathered, refs = refs[:ARRAYS], refs[ARRAYS:]
    (
        finals_ref,
        normed_ref,
        normed_t_ref,
        signals_ref,
        logit_ref,
        taps_ref,
        out_ref,
        carry_ref,
        fresh_ref,
        inverse_ref,
        starts_ref,
    ), refs = refs[:11], refs[11:]
    (
        tokens,
        weights,
        rates_weight,
        packed,
        all_taps,
        wide,
        level_masks,
        final,
        halo_sem,
        token_sem,
        load_sem,
        final_sem,
        *sems,
    ) = refs
    group = pl.program_id(0)
    groups = heads // GROUP
    rows = out_ref.shape[0]
    size = out_ref.shape[1] // GROUP
    span = GROUP * size
    chunks = rows // CHUNK
    levels = CHUNK.bit_length() - 1
    row, col = grid_indices()
    gather = Gather(count, pieces, shards, gathered, sems)
    place = gather.place
    tiles = [piece[2] / 128 * shards[piece[0]].shape[0] / 128 for piece in pieces]
    events = gather.events(tiles, 2 + groups)

    def halo(arriving):
        return remote(
            tokens_ref.at[pl.ds(rows - HALO, HALO), :],
            tokens.at[pl.ds(0, HALO), :],
            halo_sem.at[0],
            halo_sem.at[1],
            {"seq": lax.rem(place.position + 1, 4), "fsdp": place.index},
        )

    def load(step, slot):
        return pltpu.make_async_copy(
            gathered[mixed].at[:, pl.ds(pl.multiple_of(step * 3 * span, 128), 3 * span)],
            weights.at[slot],
            load_sem.at[slot],
        )

    per_step = 12
    plan = {}
    mark = 0
    for step in range(groups):
        for spot in range(per_step):
            now = 50.0 + (step * per_step + spot) * 5.5
            upto = mark
            for index in range(mark, len(events)):
                when, k, kind, _ = events[index]
                if spot == 0 and kind == 3 and (k == 2 + step or (step == 0 and k < 2)):
                    upto = index + 1
                elif when <= now and upto == index:
                    upto = index + 1
            plan[step, spot] = (mark, upto)
            mark = upto
    remaining = (mark, len(events))

    def run(bounds):
        for _, _, _, action in events[bounds[0] : bounds[1]]:
            action()

    def spot(number):
        for step in range(groups):
            bounds = plan[step, number]
            if bounds[1] > bounds[0]:

                @pl.when(group == step)
                def _():
                    run(bounds)

    @pl.when(group == 0)
    def _():
        own = pltpu.make_async_copy(tokens_ref, tokens.at[pl.ds(HALO, rows), :], token_sem.at[0])
        own.start()
        place.greet_all()

        @pl.when(place.position < 3)
        def _():
            halo(False).start()

        gather.start(0)
        gather.start(1)
        gather.start(2)
        gather.start(3)

        @pl.when(place.position == 0)
        def _():
            tokens[pl.ds(0, HALO), :] = jnp.zeros((HALO, tokens.shape[1]), bf16)

        for level in range(levels):
            same = (row >> (level + 1)) == (col >> (level + 1))
            below = ((row >> level) & 1 == 1) & ((col >> level) & 1 == 0)
            level_masks[level] = jnp.where(same & below, 1.0, 0.0).astype(bf16)

        limit = max(i for i, event in enumerate(events) if event[1] == 0) + 1
        run((0, limit))
        copy = pltpu.make_async_copy(gathered[0], packed, token_sem.at[1])
        copy.start()
        copy.wait()
        small = packed[...].astype(f32)
        gain = place_rows(small, count, tokens.shape[1] // count)[0:1, :]
        all_taps[...] = place_rows(small, count, tap_width)[4 : 4 + TAPS, :]
        own.wait()

        @pl.when(place.position > 0)
        def _():
            halo(True).wait_recv()

        block = 208 if tokens.shape[0] % 208 == 0 else HALO

        def norm(index):
            part = pl.ds(pl.multiple_of(index * block, HALO), block)
            normed_ref[part, :] = rms_scale(tokens[part, :].astype(f32), gain).astype(bf16)

        steps(0, tokens.shape[0] // block, norm)
        for first in range(0, rows, CHUNK):
            part = normed_ref[pl.ds(HALO + first, CHUNK), :]
            normed_t_ref[:, first : first + CHUNK] = part.T
        run((limit, plan[0, 0][1]))
        copy = pltpu.make_async_copy(gathered[1], rates_weight, token_sem.at[1])
        copy.start()
        load(0, 0).start()
        copy.wait()
        logit_ref[...] = nn(normed_ref[pl.ds(HALO, rows), :], rates_weight[...]).astype(bf16)
        load(0, 0).wait()

    for step in range(1, groups):
        bounds = plan[step, 0]

        @pl.when(group == step)
        def _():
            run(bounds)
            load(step, 0).start()
            load(step, 0).wait()

    signals_ref[...] = nn(normed_ref[...], weights[0]).astype(bf16)
    spot(1)

    lows = [[], [], []]
    for inner in range(GROUP):
        for which in range(3):
            first = pl.multiple_of((which * heads + group * GROUP + inner) * size, 128)
            taps = all_taps[:, pl.ds(first, size)]
            taps_ref[inner, which] = taps
            wide[...] = signals_ref[:, pl.ds((inner * 3 + which) * size, size)].astype(f32)
            pre = conv_pre(wide, taps, rows)
            act = pre * sigmoid(pre)
            if which < 2:
                act = act * lax.rsqrt(jnp.sum(act * act, axis=1, keepdims=True) + epsilon)
            lows[which].append(act.astype(bf16))
        if inner == 0:
            spot(2)
    spot(3)
    logits = logit_ref[...].astype(f32)
    rates = [sigmoid(head_column(logits, group * GROUP + inner)) for inner in range(GROUP)]
    scaling = size ** (-0.5)
    eye = jnp.where(row == col, 1.0, 0.0)
    lower = row >= col

    work = [(inner, chunk) for inner in range(GROUP) for chunk in range(chunks)]

    def cut(values, item):
        inner, chunk = item
        return values[inner][chunk * CHUNK : (chunk + 1) * CHUNK]

    queries, keys, values = lows
    stricts = [(cut(rates, i) * nt(cut(keys, i), cut(keys, i))).astype(bf16) for i in work]
    results = [eye - (strict * level_masks[0]).astype(f32) for strict in stricts]
    scores = [jnp.where(lower, nt(cut(queries, i), cut(keys, i)), 0.0).astype(bf16) for i in work]
    for level in range(1, levels):
        mask = level_masks[level]
        lowered = [result.astype(bf16) for result in results]
        inners = [nn(low, strict * mask).astype(bf16) for low, strict in zip(lowered, stricts)]
        results = [
            result - nn(inner, low) for result, inner, low in zip(results, inners, lowered)
        ]
        if level in (2, 4, 6):
            spot(3 + level // 2)
    inverses = [result.astype(bf16) for result in results]
    for (inner, chunk), inverse in zip(work, inverses):
        part = slice(chunk * CHUNK, (chunk + 1) * CHUNK)
        inverse_ref[part, inner * CHUNK : (inner + 1) * CHUNK] = inverse
    spot(7)

    srow = lax.broadcasted_iota(jnp.int32, (size, size), 0)
    scol = lax.broadcasted_iota(jnp.int32, (size, size), 1)
    memories = [
        jnp.concatenate(
            [jnp.zeros((size, size), f32), jnp.where(srow == scol, 1.0, 0.0)], axis=1
        )
    ] * GROUP
    for chunk in range(chunks):
        part = slice(chunk * CHUNK, (chunk + 1) * CHUNK)
        for inner in range(GROUP):
            item = (inner, chunk)
            key_part, query_part, rate_part = cut(keys, item), cut(queries, item), cut(rates, item)
            low_memory = memories[inner].astype(bf16)
            starts_ref[inner, chunk] = low_memory
            seen = nn(key_part, low_memory)
            aim = jnp.concatenate(
                [cut(values, item).astype(f32), jnp.zeros((CHUNK, size), f32)], axis=1
            )
            aim = (rate_part * (aim - seen)).astype(bf16)
            fresh = nn(inverses[work.index(item)], aim).astype(bf16)
            fresh_ref[part, inner * 2 * size : (inner + 1) * 2 * size] = fresh
            both = scaling * (
                nn(query_part, low_memory) + nn(scores[work.index(item)], fresh)
            )
            out_ref[part, inner * size : (inner + 1) * size] = both[:, :size]
            carry_ref[part, inner * size : (inner + 1) * size] = both[:, size:].astype(bf16)
            memories[inner] = memories[inner] + tn(key_part, fresh)
        if chunk < 3:
            spot(8 + chunk)

    def send_final(step, hop):
        position = lax.rem(place.position + hop, 4)
        block = pl.ds(step * GROUP, GROUP)
        return remote(
            final.at[block],
            finals_ref.at[place.position, block],
            final_sem.at[0, step, hop],
            final_sem.at[1, step, hop],
            {"seq": position, "fsdp": place.index},
        )

    def keep_final(step):
        block = pl.ds(step * GROUP, GROUP)
        return pltpu.make_async_copy(
            final.at[block], finals_ref.at[place.position, block], final_sem.at[0, step, 0]
        )

    def take_final(step, hop):
        position = lax.rem(place.position + 4 - hop, 4)
        block = pl.ds(step * GROUP, GROUP)
        return remote(
            final.at[block],
            finals_ref.at[position, block],
            final_sem.at[0, step, hop],
            final_sem.at[1, step, hop],
            {"seq": position, "fsdp": place.index},
        )

    for step in range(groups):

        @pl.when(group == step)
        def _():
            for inner in range(GROUP):
                final[step * GROUP + inner] = memories[inner].astype(bf16)
            for hop in range(1, 4):
                send_final(step, hop).start()
            keep_final(step).start()

    spot(11)

    @pl.when(group == groups - 1)
    def _():
        run(remaining)
        for k in range(len(pieces)):
            gather.sent(k)
        for step in range(groups):
            for hop in range(1, 4):
                send_final(step, hop).wait_send()
                take_final(step, hop).wait_recv()
            keep_final(step).wait()

        @pl.when(place.position < 3)
        def _():
            halo(False).wait_send()


def plan_pieces(depths, widths, span):
    def portions(a, wanted):
        while depths[a] % (16 * wanted) != 0:
            wanted //= 2
        return wanted

    pieces = [(0, 0, widths[0], 1), (1, 0, widths[1], portions(1, 2))]
    for step in range(widths[2] // span):
        pieces.append((2, step * span, span, portions(2, 4)))
    pieces.append((3, 0, widths[3], portions(3, 4)))
    for a in (4, 5, 6):
        half = widths[a] // 2
        for part in range(2):
            wanted = 2 if (a, part) in ((5, 0), (6, 1)) else 4
            pieces.append((a, part * half, half, portions(a, wanted)))
    return pieces


def forward(tokens, shards, heads, tap_width):
    count = lax.axis_size("fsdp")
    rows, width = tokens.shape
    size = width // heads
    span = GROUP * size
    groups = heads // GROUP
    chunks = rows // CHUNK
    wide_rows = rows + HALO
    depths = [shard.shape[0] for shard in shards]
    widths = [shard.shape[1] for shard in shards]
    pieces = plan_pieces(depths, widths, 3 * span)
    anywhere = pl.BlockSpec(memory_space=pl.ANY)
    shape = jax.ShapeDtypeStruct
    return pl.pallas_call(
        functools.partial(forward_kernel, count, pieces, 2, heads, tap_width),
        grid=(groups,),
        in_specs=[anywhere] * (1 + ARRAYS),
        out_specs=[anywhere] * (ARRAYS + 1)
        + [
            pl.BlockSpec((wide_rows, width), lambda g: (0, 0)),
            pl.BlockSpec((width, rows), lambda g: (0, 0)),
            pl.BlockSpec((wide_rows, 3 * span), lambda g: (0, g)),
            pl.BlockSpec((rows, widths[1]), lambda g: (0, 0)),
            pl.BlockSpec((GROUP, 3, TAPS, size), lambda g: (g, 0, 0, 0)),
            pl.BlockSpec((rows, span), lambda g: (0, g)),
            pl.BlockSpec((rows, span), lambda g: (0, g)),
            pl.BlockSpec((rows, 2 * span), lambda g: (0, g)),
            pl.BlockSpec((rows, GROUP * CHUNK), lambda g: (0, g)),
            pl.BlockSpec((GROUP, chunks, size, 2 * size), lambda g: (g, 0, 0, 0)),
        ],
        out_shape=[shape((count * d, w), bf16) for d, w in zip(depths, widths)]
        + [
            shape((4, heads, size, 2 * size), bf16),
            shape((wide_rows, width), bf16),
            shape((width, rows), bf16),
            shape((wide_rows, 3 * width), bf16),
            shape((rows, widths[1]), bf16),
            shape((heads, 3, TAPS, size), f32),
            shape((rows, width), f32),
            shape((rows, width), bf16),
            shape((rows, 2 * width), bf16),
            shape((rows, heads * CHUNK), bf16),
            shape((heads, chunks, size, 2 * size), bf16),
        ],
        scratch_shapes=[
            pltpu.VMEM((wide_rows, width), bf16),
            pltpu.VMEM((1, width, 3 * span), bf16),
            pltpu.VMEM((width, widths[1]), bf16),
            pltpu.VMEM((count * PACK[0], PACK[1]), bf16),
            pltpu.VMEM((TAPS, 3 * width), f32),
            pltpu.VMEM((wide_rows, size), f32),
            pltpu.VMEM((CHUNK.bit_length() - 1, CHUNK, CHUNK), bf16),
            pltpu.VMEM((heads, size, 2 * size), bf16),
            pltpu.SemaphoreType.DMA((2,)),
            pltpu.SemaphoreType.DMA((2,)),
            pltpu.SemaphoreType.DMA((2,)),
            pltpu.SemaphoreType.DMA((2, groups, 4)),
        ]
        + Gather.scratch(pieces, count),
        compiler_params=pltpu.CompilerParams(
            collective_id=0, has_side_effects=True, vmem_limit_bytes=60 * MIB
        ),
    )(tokens, *shards)


def mix_kernel(position_ref, out_ref, carry_ref, finals_ref, gain_ref, mixed_ref, state_ref):
    position = position_ref[0]
    size = out_ref.shape[1]
    state = jnp.zeros((size, size), f32)
    for index in range(finals_ref.shape[0] - 1):
        pair = finals_ref[index, 0]
        later = pair[:, :size].astype(f32) + nn(pair[:, size:], state.astype(bf16))
        state = jnp.where(index < position, later, state)
    state_ref[0] = state
    output = out_ref[...] + nn(carry_ref[...], state.astype(bf16))
    gain = gain_ref[...].astype(f32)
    mixed_ref[...] = rms_scale(output, gain).astype(bf16)


def mix(position, outputs, carries, finals, gain):
    rows, width = outputs.shape
    groups, heads, size, _ = finals.shape
    plain = pl.BlockSpec((rows, size), lambda h: (0, h))
    return pl.pallas_call(
        mix_kernel,
        grid=(heads,),
        in_specs=[
            pl.BlockSpec(memory_space=pltpu.SMEM),
            plain,
            plain,
            pl.BlockSpec((groups, 1, size, 2 * size), lambda h: (0, h, 0, 0)),
            pl.BlockSpec((1, size), lambda h: (0, 0)),
        ],
        out_specs=[plain, pl.BlockSpec((1, size, size), lambda h: (h, 0, 0))],
        out_shape=[
            jax.ShapeDtypeStruct((rows, width), bf16),
            jax.ShapeDtypeStruct((heads, size, size), f32),
        ],
        compiler_params=pltpu.CompilerParams(vmem_limit_bytes=63 * MIB),
    )(position, outputs, carries, finals, gain)


def unmix_kernel(
    heads,
    out_ref,
    carry_ref,
    state_ref,
    gain_ref,
    grad_ref,
    grad_out_ref,
    grad_gain_ref,
    grads_ref,
    grad_states,
    sems,
):
    head = pl.program_id(0)
    position, index = lax.axis_index("seq"), lax.axis_index("fsdp")

    def device(hop):
        return {"seq": lax.rem(position + hop, 4), "fsdp": index}

    def send(one, hop, arriving=False):
        source = lax.rem(position + 4 - hop, 4) if arriving else position
        return remote(
            grad_states.at[one],
            grads_ref.at[source, one],
            sems.at[0, one, hop],
            sems.at[1, one, hop],
            device(hop),
        )

    def keep(one):
        return pltpu.make_async_copy(
            grad_states.at[one], grads_ref.at[position, one], sems.at[0, one, 0]
        )

    @pl.when(head == 0)
    def _():
        barrier = pltpu.get_barrier_semaphore()
        for hop in range(1, 4):
            pl.semaphore_signal(barrier, inc=1, device_id=device(hop), device_id_type=MESH)
        grad_gain_ref[...] = jnp.zeros_like(grad_gain_ref)

    output = out_ref[...] + nn(carry_ref[...], state_ref[0].astype(bf16))
    gain = gain_ref[...].astype(f32)
    grad = grad_ref[...].astype(f32)
    scaling = lax.rsqrt(jnp.mean(output * output, axis=1, keepdims=True) + epsilon)
    unit_rows = output * scaling
    grad_gain_ref[...] += jnp.sum(grad * unit_rows, axis=0, keepdims=True)
    scaled = grad * gain
    grad_out = scaling * (scaled - unit_rows * jnp.mean(scaled * unit_rows, axis=1, keepdims=True))
    low_grad = grad_out.astype(bf16)
    grad_states[head] = tn(carry_ref[...], low_grad).astype(bf16)

    @pl.when(head == 0)
    def _():
        pl.semaphore_wait(pltpu.get_barrier_semaphore(), 3)

    for hop in range(1, 4):
        send(head, hop).start()
    keep(head).start()
    grad_out_ref[...] = (grad_out * output.shape[1] ** (-0.5)).astype(bf16)

    @pl.when(head == heads - 1)
    def _():
        def one(step):
            keep(step).wait()
            for hop in range(1, 4):
                send(step, hop).wait_send()
                send(step, hop, True).wait_recv()

        steps(0, heads, one)


def unmix(outputs, carries, states, gain, grad_heads):
    rows, width = outputs.shape
    heads, size, _ = states.shape
    plain = pl.BlockSpec((rows, size), lambda h: (0, h))
    state = pl.BlockSpec((1, size, size), lambda h: (h, 0, 0))
    vector = pl.BlockSpec((1, size), lambda h: (0, 0))
    return pl.pallas_call(
        functools.partial(unmix_kernel, heads),
        grid=(heads,),
        in_specs=[plain, plain, state, vector, plain],
        out_specs=[plain, vector, pl.BlockSpec(memory_space=pl.ANY)],
        out_shape=[
            jax.ShapeDtypeStruct((rows, width), bf16),
            jax.ShapeDtypeStruct((1, size), f32),
            jax.ShapeDtypeStruct((4, heads, size, size), bf16),
        ],
        scratch_shapes=[
            pltpu.VMEM((heads, size, size), bf16),
            pltpu.SemaphoreType.DMA((2, heads, 4)),
        ],
        compiler_params=pltpu.CompilerParams(
            collective_id=1, has_side_effects=True, vmem_limit_bytes=63 * MIB
        ),
    )(outputs, carries, states, gain, grad_heads)


TILE = 256
SLOTS = 3
DENSE_STRIDE = 4


def dense_kernel(count, shapes, *refs):
    (
        mixed_ref,
        w_out_ref,
        gain_ref,
        cotangent_ref,
        gate_ref,
        up_ref,
        down_ref,
        tokens_ref,
        layer_out_ref,
        grad_gain_ref,
        grad_out_ref,
        grad_attended_ref,
        grad_heads_ref,
        rest_ref,
        sums_ref,
        attended,
        normed,
        normed_t,
        cotangent_t,
        result,
        grad_normed,
        source,
        plain_sem,
        rest_sem,
    ), refs = refs[:24], refs[24:]
    tile = pl.program_id(0)
    rows, width = attended.shape
    depth = width // count
    number = len(shapes)
    tiles = number + rest_ref.shape[3] // (3 * TILE)
    blocks = [slice(first, first + CHUNK) for first in range(0, rows, CHUNK)]
    columns = [slice(first, first + CHUNK) for first in range(0, width, CHUNK)]
    gain = gain_ref[...].astype(f32)

    due, later, reduce = {}, [], None
    if number > 0:
        buffers = [refs[i * number : (i + 1) * number] for i in range(Reduce.BUFFERS)]
        sems = refs[Reduce.BUFFERS * number :]
        sources = [source.at[p % SLOTS] for p in range(number)]
        targets = [sums_ref.at[:, pl.ds(p * 3 * TILE, 3 * TILE)] for p in range(number)]
        reduce = Reduce(count, shapes, sources, targets, buffers, None, sems)
        begin = [2 * p + 3 for p in range(number)]
        due, later = reduce.plan(
            begin, [DENSE_STRIDE] * number, 2 * tiles - 1, [False] * number
        )

    def spot(which):
        for step in range(tiles):
            actions = due.get(2 * step + which, ())
            if actions:

                @pl.when(tile == step)
                def _():
                    for action in actions:
                        action()

    def rest(step):
        slot = lax.rem(step, SLOTS)
        first = pl.multiple_of((step - number) * 3 * TILE, 128)
        return pltpu.make_async_copy(
            source.at[slot], rest_ref.at[:, :, :, pl.ds(first, 3 * TILE)], rest_sem.at[slot]
        )

    def fetch(start, target, slot):
        return pltpu.make_async_copy(start, target, plain_sem.at[slot])

    @pl.when(tile == 0)
    def _():
        load = fetch(tokens_ref, normed, 0)
        load.start()
        if reduce is not None:
            reduce.place.greet_all()
        load.wait()
        for block in blocks:
            values = normed[block, :].astype(f32) + nn(mixed_ref[block, :], w_out_ref[...])
            attended[block, :] = values
            result[block, :] = values
            low = rms_scale(values, gain).astype(bf16)
            normed[block, :] = low
            normed_t[:, block] = low.T
            cotangent_t[:, block] = cotangent_ref[block, :].T
        grad_normed[...] = jnp.zeros_like(grad_normed)

    @pl.when(tile >= number + SLOTS)
    def _():
        rest(tile - SLOTS).wait()

    spot(0)
    gate = nn(normed[...], gate_ref[...])
    up = nn(normed[...], up_ref[...])
    grad_hidden = nn(cotangent_ref[...], down_ref[...])
    sig = sigmoid(gate)
    activated = gate * sig
    hidden = (activated * up).astype(bf16)
    grad_gate = (grad_hidden * up * sig * (1.0 + gate * (1.0 - sig))).astype(bf16)
    grad_up = (grad_hidden * activated).astype(bf16)
    slot = lax.rem(tile, SLOTS)
    for which, (left, right) in enumerate(
        ((normed_t, grad_gate), (normed_t, grad_up), (cotangent_t, hidden))
    ):
        piece = nn(left[...], right).astype(bf16).reshape(count // 2, 2, depth, TILE)
        source[slot, :, :, :, pl.ds(which * TILE, TILE)] = piece

    spot(1)
    for column in columns:
        result[:, column] += nt(hidden, down_ref[column, :])
        grad_normed[:, column] += nt(grad_gate, gate_ref[column, :]) + nt(
            grad_up, up_ref[column, :]
        )

    for p in range(number):

        @pl.when(tile == p)
        def _():
            reduce.start(p, False)

    @pl.when(tile >= number)
    def _():
        rest(tile).start()

    @pl.when(tile == tiles - 1)
    def _():
        gain_grad = jnp.zeros((1, width), f32)
        for block in blocks:
            layer_out_ref[block, :] = result[block, :].astype(bf16)
            values = attended[block, :]
            grad = grad_normed[block, :]
            scaling = lax.rsqrt(jnp.mean(values * values, axis=1, keepdims=True) + epsilon)
            unit = values * scaling
            gain_grad = gain_grad + jnp.sum(grad * unit, axis=0, keepdims=True)
            scaled = grad * gain
            grad = cotangent_ref[block, :].astype(f32) + scaling * (
                scaled - unit * jnp.mean(scaled * unit, axis=1, keepdims=True)
            )
            attended[block, :] = grad
            low = grad.astype(bf16)
            normed[block, :] = low
            normed_t[:, block] = mixed_ref[block, :].T
        fetch(attended, grad_attended_ref, 0).start()
        grad_gain_ref[...] = gain_grad
        for block in blocks:
            cotangent_t[block, :] = nt(normed[block, :], w_out_ref[...]).astype(bf16)
        fetch(cotangent_t, grad_heads_ref, 1).start()
        for action in later[: len(later) // 2]:
            action()
        for column in columns:
            grad_out_ref[column, :] = nn(normed_t[column, :], normed[...]).astype(bf16)
        for action in later[len(later) // 2 :]:
            action()
        for p in range(number):
            reduce.finish(p)
        for step in range(max(number, tiles - SLOTS), tiles):
            rest(step).wait()
        fetch(attended, grad_attended_ref, 0).wait()
        fetch(cotangent_t, grad_heads_ref, 1).wait()


def dense(mixed, tokens, w_out, gain, cotangent, w_gate, w_up, w_down_t, number):
    count = lax.axis_size("fsdp")
    rows, width = tokens.shape
    hidden = w_gate.shape[1]
    tiles = hidden // TILE
    depth = width // count
    shapes = [(depth, 3 * TILE, 2 if p % 2 == 0 else 4) for p in range(number)]
    whole = pl.BlockSpec((rows, width), lambda j: (0, 0))
    square = pl.BlockSpec((width, width), lambda j: (0, 0))
    vector = pl.BlockSpec((1, width), lambda j: (0, 0))
    slab = pl.BlockSpec((width, TILE), lambda j: (0, j))
    anywhere = pl.BlockSpec(memory_space=pl.ANY)
    shape = jax.ShapeDtypeStruct
    more = dict(collective_id=3, has_side_effects=True) if number > 0 else {}
    extra = []
    if number > 0:
        extra = Reduce.buffers(count, shapes) + Reduce.semaphores(count, number)
    return pl.pallas_call(
        functools.partial(dense_kernel, count, shapes),
        grid=(tiles,),
        in_specs=[whole, square, vector, whole, slab, slab, slab, anywhere],
        out_specs=[whole, vector, square] + [anywhere] * 4,
        out_shape=[
            shape((rows, width), bf16),
            shape((1, width), f32),
            shape((width, width), bf16),
            shape((rows, width), f32),
            shape((rows, width), bf16),
            shape((count // 2, 2, depth, (tiles - number) * 3 * TILE), bf16),
            shape((depth, max(number, 1) * 3 * TILE), bf16),
        ],
        scratch_shapes=[
            pltpu.VMEM((rows, width), f32),
            pltpu.VMEM((rows, width), bf16),
            pltpu.VMEM((width, rows), bf16),
            pltpu.VMEM((width, rows), bf16),
            pltpu.VMEM((rows, width), f32),
            pltpu.VMEM((rows, width), f32),
            pltpu.VMEM((SLOTS, count // 2, 2, depth, 3 * TILE), bf16),
            pltpu.SemaphoreType.DMA((2,)),
            pltpu.SemaphoreType.DMA((SLOTS,)),
        ]
        + extra,
        compiler_params=pltpu.CompilerParams(vmem_limit_bytes=63 * MIB, **more),
    )(mixed, w_out, gain, cotangent, w_gate, w_up, w_down_t, tokens)


STRIDE = 4


def backward_kernel(
    count, arrays, shapes, loaded_number, heads, tap_width, gain_width, *refs
):
    (
        signals_ref,
        logit_ref,
        taps_ref,
        grad_ref,
        fresh_ref,
        inverse_ref,
        starts_ref,
        state_ref,
        finals_ref,
        grads_ref,
        weights_ref,
        rates_weight_ref,
        gain_ref,
        grad_mlp_ref,
        grad_gain_ref,
        normed_ref,
        tokens_ref,
    ), refs = refs[:17], refs[17:]
    full, refs = refs[:arrays], refs[arrays:]
    grad_tokens_ref, refs = refs[0], refs[1:]
    outs, refs = refs[: arrays + 3], refs[arrays + 3 :]
    (
        normed_t,
        tokens,
        total,
        grad_signals,
        tails,
        firsts,
        edges,
        wides,
        pres,
        grads,
        padded,
        grad_logits,
        small_rows,
        small_source,
        beta_source,
        mixed_source,
        staging,
        plain_sem,
        edge_sem,
    ), refs = refs[:19], refs[19:]
    number = len(shapes)
    buffers = [refs[i * number : (i + 1) * number] for i in range(Reduce.BUFFERS)]
    sems = refs[Reduce.BUFFERS * number :]

    head = pl.program_id(0)
    rows, size = grad_ref.shape
    width = total.shape[1]
    chunks = rows // CHUNK
    row, col = grid_indices()
    lower, upper = row >= col, row <= col

    sources, targets = [], []
    for a in range(arrays):
        halves = max(full[a].shape[3] // (3 * TILE), 1)
        half = full[a].shape[3] // halves
        for part in range(halves):
            columns = pl.ds(part * half, half)
            sources.append(full[a].at[:, :, :, columns])
            targets.append(outs[a].at[:, columns])
    slots = mixed_source.shape[0]
    for one in range(heads):
        sources.append(mixed_source.at[one % slots])
        targets.append(outs[arrays].at[:, pl.ds(one * 3 * size, 3 * size)])
    sources += [beta_source, small_source]
    targets += [outs[arrays + 1], outs[arrays + 2]]
    reduce = Reduce(count, shapes, sources, targets, buffers, staging, sems)
    place = reduce.place
    position = place.position
    loaded = [p < loaded_number for p in range(number)]
    begin = [1 + 3 * (p // 2) for p in range(loaded_number)]
    begin += [2 * one + 5 for one in range(heads)] + [2 * heads + 5, 2 * heads + 6]
    stride = [STRIDE] * loaded_number + [STRIDE - 1] * (number - loaded_number)
    due, later = reduce.plan(begin, stride, 2 * heads, loaded)

    def spot(which):
        for step in range(heads + 1):
            actions = due.get(2 * step + which, ())
            if actions:

                @pl.when(head == step)
                def _():
                    for action in actions:
                        action()

    def fetch(source, target, slot):
        return pltpu.make_async_copy(source, target, plain_sem.at[slot])

    def edge(one, slot, arriving=False):
        return remote(
            firsts.at[slot],
            edges.at[one],
            edge_sem.at[0, one],
            edge_sem.at[1, one],
            reduce.device(3),
        )

    @pl.when(head == 0)
    def _():
        fetch(normed_ref, normed_t, 0).start()
        fetch(tokens_ref, tokens, 1).start()
        place.greet_all()
        for p in range(min(2, loaded_number)):
            reduce.start(p, True)
        total[...] = jnp.zeros_like(total)
        padded[...] = jnp.zeros_like(padded)
        grad_logits[...] = jnp.zeros_like(grad_logits)
        small_rows[...] = jnp.zeros_like(small_rows)
        fetch(normed_ref, normed_t, 0).wait()
        fetch(tokens_ref, tokens, 1).wait()

    spot(0)

    @pl.when(head < heads)
    def _():
        slot = lax.rem(head, 2)
        lows, scales = [], []
        for which in range(3):
            wides[which] = signals_ref[:, pl.ds(which * size, size)].astype(f32)
            pre = conv_pre(wides.at[which], taps_ref[0, which], rows)
            pres[which] = pre
            act = pre * sigmoid(pre)
            if which < 2:
                scale = lax.rsqrt(jnp.sum(act * act, axis=1, keepdims=True) + epsilon)
                act = act * scale
                scales.append(scale)
            lows.append(act.astype(bf16))
        queries, keys, values = lows
        rates = sigmoid(head_column(logit_ref[...].astype(f32), head))

        state = state_ref[0].astype(bf16)
        first = fresh_ref[:, pl.ds(0, size)].astype(f32)
        fresh_all = (first + nn(fresh_ref[:, pl.ds(size, size)], state)).astype(bf16)

        grad_memory = jnp.zeros((size, size), f32)
        for index in reversed(range(1, 4)):
            later = grads_ref[index, 0].astype(f32) + tn(
                finals_ref[index, 0, :, pl.ds(size, size)], grad_memory.astype(bf16)
            )
            grad_memory = jnp.where(index > position, later, grad_memory)
        grad_rates = [None] * chunks
        for chunk in reversed(range(chunks)):
            part = slice(chunk * CHUNK, (chunk + 1) * CHUNK)
            key, query, value, rate = keys[part], queries[part], values[part], rates[part]
            grad_out = grad_ref[part, :]
            fresh = fresh_all[part]
            start = starts_ref[0, chunk]
            memory = (start[:, :size].astype(f32) + nn(start[:, size:], state)).astype(bf16)
            low_grad = grad_memory.astype(bf16)
            key_f = key.astype(f32)
            rated = (rate * key_f).astype(bf16)

            scores_t = jnp.where(upper, nt(key, query), 0.0).astype(bf16)
            grad_fresh = (nn(scores_t, grad_out) + nn(key, low_grad)).astype(bf16)
            aim = tn(inverse_ref[part, :], grad_fresh)
            low_aim = aim.astype(bf16)
            grad_memory = grad_memory + tn(query, grad_out) - tn(rated, low_aim)

            grad_scores = jnp.where(lower, nt(grad_out, fresh), 0.0).astype(bf16)
            grad_scores_t = jnp.where(upper, nt(fresh, grad_out), 0.0).astype(bf16)
            grad_strict = jnp.where(row > col, nt(low_aim, fresh), 0.0).astype(bf16)
            grad_strict_t = jnp.where(row < col, nt(fresh, low_aim), 0.0).astype(bf16)

            grad_query = nt(grad_out, memory) + nn(grad_scores, key)
            within = -(nn(grad_strict, key) + nt(low_aim, memory))
            grad_rates[chunk] = jnp.sum(
                key_f * within + value.astype(f32) * aim, axis=1, keepdims=True
            )
            grad_key = (
                rate * within
                - nn(grad_strict_t, rated)
                + nn(grad_scores_t, query)
                + nt(fresh, low_grad)
            )
            grads[0, part, :] = grad_query
            grads[1, part, :] = grad_key
            grads[2, part, :] = rate * aim
            if chunk == chunks // 2:
                spot(1)

        lane = lax.broadcasted_iota(jnp.int32, grad_logits.shape, 1)
        grad_rate = jnp.concatenate(grad_rates, axis=0)
        grad_logit = grad_rate * rates * (1.0 - rates)
        grad_logits[...] = jnp.where(lane == head, grad_logit, grad_logits[...])

        @pl.when((head >= 2) & (position > 0))
        def _():
            edge(head - 2, slot).wait_send()

        for which in range(3):
            taps = taps_ref[0, which]
            pre = pres[which]
            sig = sigmoid(pre)
            grad_act = grads[which]
            if which < 2:
                unit = pre * sig * scales[which]
                grad_act = scales[which] * (
                    grad_act - unit * jnp.sum(grad_act * unit, axis=1, keepdims=True)
                )
            grad_pre = grad_act * sig * (1.0 + pre * (1.0 - sig))
            padded[pl.ds(HALO, rows), :] = grad_pre
            sums = []
            for offset in range(TAPS):
                shifted = wides[which, pl.ds(HALO - TAPS + 1 + offset, rows), :]
                sums.append(jnp.sum(grad_pre * shifted, axis=0, keepdims=True))
            where = pl.multiple_of((which * heads + head) * size, 128)
            small_rows[4:8, pl.ds(where, size)] = jnp.concatenate(sums, axis=0)

            def back(start, amount):
                result = None
                for offset in range(TAPS):
                    term = (
                        taps[offset : offset + 1, :]
                        * padded[pl.ds(start + TAPS - 1 - offset, amount), :]
                    )
                    result = term if result is None else result + term
                return result

            columns = pl.ds(which * size, size)
            grad_signal = back(HALO, rows)
            grad_signals[slot, :, columns] = grad_signal.astype(bf16)
            tails[slot, :, columns] = grad_signal[rows - HALO :]
            firsts[slot, :, columns] = back(0, HALO)

        @pl.when(position > 0)
        def _():
            edge(head, slot).start()

    for one in range(heads):

        @pl.when(head == one + 1)
        def _():
            slot = one % 2

            @pl.when(position < 3)
            def _():
                edge(one, slot).wait_recv()
                tails[slot] = tails[slot] + edges[one]

            grad_signals[slot, pl.ds(rows - HALO, HALO), :] = tails[slot].astype(bf16)
            grad = grad_signals[slot]
            source = mixed_source.at[one % slots]
            depth = width // count
            half = count // 4
            for part in range(2):
                piece = nn(normed_t[pl.ds(part * 2 * half * depth, 2 * half * depth), :], grad)
                source[pl.ds(part * half, half)] = piece.astype(bf16).reshape(
                    half, 2, depth, 3 * size
                )
            reduce.start(loaded_number + one, False)
            weights = weights_ref[...]
            for part in range(0, rows, CHUNK):
                block = pl.ds(part, CHUNK)
                total[block, :] += nt(grad[part : part + CHUNK], weights)

    @pl.when(head == heads)
    def _():
        depth = width // count
        low_logits = grad_logits[...].astype(bf16)
        beta_source[...] = (
            nn(normed_t[...], low_logits).astype(bf16).reshape(beta_source.shape)
        )
        reduce.start(number - 2, False)
        gain = gain_ref[...].astype(f32)
        weights = rates_weight_ref[...]
        gain_grad = jnp.zeros((1, width), f32)
        for part in range(0, rows, CHUNK):
            block = pl.ds(part, CHUNK)
            grad = total[block, :] + nt(low_logits[part : part + CHUNK], weights)
            values = tokens[block, :].astype(f32)
            scaling = lax.rsqrt(jnp.mean(values * values, axis=1, keepdims=True) + epsilon)
            unit = values * scaling
            gain_grad = gain_grad + jnp.sum(grad * unit, axis=0, keepdims=True)
            scaled = grad * gain
            total[block, :] = scaling * (
                scaled - unit * jnp.mean(scaled * unit, axis=1, keepdims=True)
            )
        fetch(total, grad_tokens_ref, 0).start()
        small_rows[0:1, pl.ds(0, width)] = gain_grad
        small_rows[1:2, pl.ds(0, width)] = grad_mlp_ref[...]
        small_rows[2:3, pl.ds(0, size)] = grad_gain_ref[...]
        small = small_rows[...]
        gains = gather_rows(small[:, :width], count, gain_width)
        last = gather_rows(small[:, :size], count, size // count)
        taps = gather_rows(small, count, tap_width)
        which = lax.broadcasted_iota(jnp.int32, gains.shape, 1)
        small = jnp.where(which == 2, last, jnp.where(which < 2, gains, taps))
        small_source[...] = small.astype(bf16).reshape(small_source.shape)
        reduce.start(number - 1, False)
        for action in later:
            action()
        for p in range(number):
            reduce.finish(p)
        fetch(total, grad_tokens_ref, 0).wait()
        for one in range(heads - 2, heads):

            @pl.when(position > 0)
            def _():
                edge(one, one % 2).wait_send()


def gather_rows(wide, count, width):
    total = count * width
    rows = wide.shape[0]
    if width % 128 == 0:
        blank = jnp.zeros((rows, PACK[1] - width), f32)
        return jnp.stack(
            [
                jnp.concatenate([wide[:, s * width : (s + 1) * width], blank], axis=1)
                for s in range(count)
            ]
        )
    row = lax.broadcasted_iota(jnp.int32, (count * rows, rows), 0)
    col = lax.broadcasted_iota(jnp.int32, (count * rows, rows), 1)
    spread = jnp.where(lax.rem(row, rows) == col, 1.0, 0.0).astype(bf16)
    tall = nn(spread, wide[:, :total].astype(bf16))
    row = lax.broadcasted_iota(jnp.int32, tall.shape, 0)
    col = lax.broadcasted_iota(jnp.int32, tall.shape, 1)
    tall = jnp.where(lax.div(row, rows) == lax.div(col, width), tall, 0.0).astype(bf16)
    row = lax.broadcasted_iota(jnp.int32, (total, PACK[1]), 0)
    col = lax.broadcasted_iota(jnp.int32, (total, PACK[1]), 1)
    pick = jnp.where(lax.rem(row, width) == col, 1.0, 0.0).astype(bf16)
    return nn(tall, pick).reshape(count, rows, PACK[1])


def backward(
    signals,
    logits,
    taps,
    grad_out,
    fresh,
    inverses,
    starts,
    state,
    finals,
    grad_starts,
    w_mixed,
    w_rates,
    gain,
    grad_mlp,
    grad_gain,
    normed_t,
    tokens,
    full,
    tap_width,
    gain_width,
):
    count = lax.axis_size("fsdp")
    wide_rows = signals.shape[0]
    rows, width = grad_out.shape
    heads, _, _, size = taps.shape
    chunks = rows // CHUNK
    depth = width // count
    views = full

    def portions(depth, wanted):
        while depth % (16 * wanted) != 0:
            wanted //= 2
        return wanted

    shapes = []
    for a, view in enumerate(views):
        halves = max(view.shape[3] // (3 * TILE), 1)
        for part in range(halves):
            shapes.append((depth, view.shape[3] // halves, 4 if (a + part) % 2 else 2))
    loaded = len(shapes)
    for head in range(heads):
        shapes.append((depth, 3 * size, portions(depth, 4 if head % 2 == 0 else 2)))
    shapes.append((depth, logits.shape[1], portions(depth, 2)))
    shapes.append(PACK + (1,))
    staged = max([d // 2 for d, _, _ in shapes[:loaded]] + [16])
    widest = max([w for _, w, _ in shapes[:loaded]] + [128])

    def now(h):
        return jnp.minimum(h, heads - 1)

    def before(h):
        return jnp.maximum(h - 1, 0)

    whole = pl.BlockSpec(logits.shape, lambda h: (0, 0))
    vector = pl.BlockSpec((1, width), lambda h: (0, 0))
    anywhere = pl.BlockSpec(memory_space=pl.ANY)
    shape = jax.ShapeDtypeStruct
    return pl.pallas_call(
        functools.partial(
            backward_kernel, count, len(views), shapes, loaded, heads, tap_width, gain_width
        ),
        grid=(heads + 1,),
        in_specs=[
            pl.BlockSpec((wide_rows, 3 * size), lambda h: (0, now(h))),
            whole,
            pl.BlockSpec((1, 3, TAPS, size), lambda h: (now(h), 0, 0, 0)),
            pl.BlockSpec((rows, size), lambda h: (0, now(h))),
            pl.BlockSpec((rows, 2 * size), lambda h: (0, now(h))),
            pl.BlockSpec((rows, CHUNK), lambda h: (0, now(h))),
            pl.BlockSpec((1, chunks, size, 2 * size), lambda h: (now(h), 0, 0, 0)),
            pl.BlockSpec((1, size, size), lambda h: (now(h), 0, 0)),
            pl.BlockSpec((4, 1, size, 2 * size), lambda h: (0, now(h), 0, 0)),
            pl.BlockSpec((4, 1, size, size), lambda h: (0, now(h), 0, 0)),
            pl.BlockSpec((width, 3 * size), lambda h: (0, before(h))),
            pl.BlockSpec(w_rates.shape, lambda h: (0, 0)),
            vector,
            vector,
            pl.BlockSpec((1, size), lambda h: (0, 0)),
        ]
        + [anywhere] * (2 + len(views)),
        out_specs=[anywhere] * (4 + len(views)),
        out_shape=[shape((rows, width), f32)]
        + [shape(view.shape[2:], bf16) for view in views]
        + [
            shape((depth, 3 * width), bf16),
            shape((depth, logits.shape[1]), bf16),
            shape(PACK, bf16),
        ],
        scratch_shapes=[
            pltpu.VMEM((width, rows), bf16),
            pltpu.VMEM((rows, width), bf16),
            pltpu.VMEM((rows, width), f32),
            pltpu.VMEM((2, rows, 3 * size), bf16),
            pltpu.VMEM((2, HALO, 3 * size), f32),
            pltpu.VMEM((2, HALO, 3 * size), f32),
            pltpu.VMEM((heads, HALO, 3 * size), f32),
            pltpu.VMEM((3, wide_rows, size), f32),
            pltpu.VMEM((3, rows, size), f32),
            pltpu.VMEM((3, rows, size), f32),
            pltpu.VMEM((rows + 2 * HALO, size), f32),
            pltpu.VMEM(logits.shape, f32),
            pltpu.VMEM((PACK[0], 3 * width), f32),
            pltpu.VMEM((count // 2, 2) + PACK, bf16),
            pltpu.VMEM((count // 2, 2, depth, logits.shape[1]), bf16),
            pltpu.VMEM((SLOTS, count // 2, 2, depth, 3 * size), bf16),
            pltpu.VMEM((2, count // 2, 2, staged, widest), bf16),
            pltpu.SemaphoreType.DMA((2,)),
            pltpu.SemaphoreType.DMA((2, heads)),
        ]
        + Reduce.buffers(count, shapes)
        + Reduce.semaphores(count, len(shapes)),
        compiler_params=pltpu.CompilerParams(
            collective_id=2, has_side_effects=True, vmem_limit_bytes=63 * MIB
        ),
    )(
        signals,
        logits,
        taps,
        grad_out,
        fresh,
        inverses,
        starts,
        state,
        finals,
        grad_starts,
        w_mixed,
        w_rates,
        gain,
        grad_mlp,
        grad_gain,
        normed_t,
        tokens,
        *views,
    )


def arrange_kernel(heads, q_ref, k_ref, v_ref, down_ref, mixed_ref, down_t_ref):
    size = q_ref.shape[1] // heads
    for head in range(heads):
        for which, ref in enumerate((q_ref, k_ref, v_ref)):
            first = (head * 3 + which) * size
            mixed_ref[:, first : first + size] = ref[:, head * size : (head + 1) * size]
    for first in range(0, down_ref.shape[0], TILE):
        down_t_ref[:, first : first + TILE] = down_ref[first : first + TILE, :].T


def arrange(w_query, w_key, w_value, w_down, heads):
    depth, width = w_query.shape
    return pl.pallas_call(
        functools.partial(arrange_kernel, heads),
        out_shape=[
            jax.ShapeDtypeStruct((depth, 3 * width), bf16),
            jax.ShapeDtypeStruct((depth, w_down.shape[0]), bf16),
        ],
        compiler_params=pltpu.CompilerParams(vmem_limit_bytes=63 * MIB),
    )(w_query, w_key, w_value, w_down)


def deliver_kernel(
    number,
    sums_ref,
    rest_ref,
    mixed_ref,
    out_ref,
    attended_ref,
    tokens_ref,
    gate_out,
    up_out,
    down_out,
    query_out,
    key_out,
    value_out,
    out_out,
    tokens_out,
):
    tile = pl.program_id(0)
    packed = jnp.where(tile < number, sums_ref[...], rest_ref[...]).astype(f32)
    gate_out[...] = packed[:, :TILE]
    up_out[...] = packed[:, TILE : 2 * TILE]
    down_out[...] = packed[:, 2 * TILE :].T
    size = query_out.shape[1]
    for which, ref in enumerate((query_out, key_out, value_out)):
        ref[...] = mixed_ref[:, which * size : (which + 1) * size].astype(f32)
    out_out[...] = out_ref[...].astype(f32)
    tokens_out[...] = attended_ref[...] + tokens_ref[...]


def deliver(number, sums, rest, mixed, out, grad_attended, grad_tokens, heads):
    depth, width = out.shape
    size = width // heads
    rows = grad_tokens.shape[0] // heads
    tiles = number + rest.shape[1] // (3 * TILE)

    def head(j):
        return jnp.minimum(j, heads - 1)

    column = pl.BlockSpec((depth, size), lambda j: (0, head(j)))
    block = pl.BlockSpec((rows, width), lambda j: (head(j), 0))
    tile = pl.BlockSpec((depth, TILE), lambda j: (0, j))
    shape = jax.ShapeDtypeStruct
    return pl.pallas_call(
        functools.partial(deliver_kernel, number),
        grid=(tiles,),
        in_specs=[
            pl.BlockSpec((depth, 3 * TILE), lambda j: (0, jnp.minimum(j, number - 1))),
            pl.BlockSpec((depth, 3 * TILE), lambda j: (0, jnp.maximum(j - number, 0))),
            pl.BlockSpec((depth, 3 * size), lambda j: (0, head(j))),
            column,
            block,
            block,
        ],
        out_specs=[
            tile,
            tile,
            pl.BlockSpec((TILE, depth), lambda j: (j, 0)),
            column,
            column,
            column,
            column,
            block,
        ],
        out_shape=[
            shape((depth, tiles * TILE), f32),
            shape((depth, tiles * TILE), f32),
            shape((tiles * TILE, depth), f32),
            shape((depth, width), f32),
            shape((depth, width), f32),
            shape((depth, width), f32),
            shape((depth, width), f32),
            shape(grad_tokens.shape, f32),
        ],
        compiler_params=pltpu.CompilerParams(vmem_limit_bytes=63 * MIB),
    )(sums, rest, mixed, out, grad_attended, grad_tokens)


def local(
    inputs,
    g_attn,
    w_query,
    w_key,
    w_value,
    w_beta,
    conv_taps,
    o_gain,
    w_out,
    g_mlp,
    w_gate,
    w_up,
    w_down,
    cotangent,
):
    count = lax.axis_size("fsdp")
    position = lax.axis_index("seq")
    groups = lax.axis_size("seq")
    tokens_low = inputs[0]
    rows, width = tokens_low.shape
    heads = w_beta.shape[1]
    size = width // heads
    depth = w_query.shape[0]
    small = (g_attn.shape, g_mlp.shape, o_gain.shape, conv_taps.shape)
    packed = pack_small((g_attn[None], g_mlp[None], o_gain[None]), conv_taps[None])
    if depth % 128 == 0:
        mixed, down_t = arrange(w_query, w_key, w_value, w_down, heads)
    else:
        mixed = jnp.stack([w.reshape(depth, -1, size) for w in (w_query, w_key, w_value)], axis=2)
        mixed, down_t = mixed.reshape(depth, 3 * width), jnp.transpose(w_down)
    shards = (
        packed,
        jnp.pad(w_beta, ((0, 0), (0, 128 - heads))),
        mixed,
        w_out,
        w_gate,
        w_up,
        down_t,
    )
    results = forward(tokens_low, shards, heads, conv_taps.shape[1])
    packed, w_beta, w_mixed, w_out, w_gate, w_up, w_down_t = results[:ARRAYS]
    finals, _, normed_t, signals, logits, taps = results[ARRAYS : ARRAYS + 6]
    outputs, carries, fresh, inverses, starts = results[ARRAYS + 6 :]
    g_attn, g_mlp, o_gain, _ = unpack_small(packed, small)
    g_attn, g_mlp, o_gain = g_attn.reshape(-1), g_mlp.reshape(-1), o_gain.reshape(-1)

    gain_out = o_gain.reshape(1, size)
    head_rows, state_in = mix(position.reshape(1), outputs, carries, finals, gain_out)
    tiles = w_gate.shape[1] // TILE
    beside = depth % 64 == 0
    number = tiles - 4 if beside else 0
    layer_out, grad_gain_mlp, grad_out_matrix, grad_attended, grad_heads, rest, sums = dense(
        head_rows,
        tokens_low,
        w_out,
        g_mlp.reshape(1, -1),
        cotangent[0],
        w_gate,
        w_up,
        w_down_t,
        number,
    )
    grad_delta, grad_gain_out, grad_starts = unmix(
        outputs, carries, state_in, gain_out, grad_heads
    )
    full = (rest, grad_out_matrix.reshape(count // 2, 2, depth, width))
    results = backward(
        signals,
        logits,
        taps,
        grad_delta,
        fresh,
        inverses,
        starts,
        state_in,
        finals,
        grad_starts,
        w_mixed,
        w_beta,
        g_attn.reshape(1, -1),
        grad_gain_mlp,
        grad_gain_out,
        normed_t,
        tokens_low,
        full if beside else (),
        small[3][1],
        small[0][0],
    )
    grad_from_attn, full_sums = results[0], results[1:-3]
    grad_mixed_matrix, grad_beta_matrix, packed = results[-3:]
    if beside and depth % 128 == 0:
        (
            grad_gate_matrix,
            grad_up_matrix,
            grad_down_matrix,
            grad_query_matrix,
            grad_key_matrix,
            grad_value_matrix,
            grad_out_matrix,
            grad_inputs,
        ) = deliver(
            number,
            sums,
            full_sums[0],
            grad_mixed_matrix,
            full_sums[1],
            grad_attended,
            grad_from_attn,
            heads,
        )
    else:
        if beside:
            sums, grad_out_matrix = jnp.concatenate([sums, full_sums[0]], axis=1), full_sums[1]
        else:
            sums, grad_out_matrix = (
                lax.psum(
                    lax.psum_scatter(
                        g.reshape((count,) + g.shape[2:]), "fsdp", scatter_dimension=0
                    ),
                    "seq",
                )
                for g in full
            )
        sums = sums.astype(f32).reshape(depth, tiles, 3, TILE)
        grad_gate_matrix, grad_up_matrix, grad_down_t = (
            sums[:, :, which].reshape(depth, tiles * TILE) for which in range(3)
        )
        grad_down_matrix = jnp.transpose(grad_down_t)
        grad_mixed_matrix = grad_mixed_matrix.astype(f32).reshape(depth, heads, 3, size)
        grad_query_matrix, grad_key_matrix, grad_value_matrix = (
            grad_mixed_matrix[:, :, which].reshape(depth, width) for which in range(3)
        )
        grad_out_matrix = grad_out_matrix.astype(f32)
        grad_inputs = grad_attended + grad_from_attn
    parts = [part[0].astype(f32) for part in unpack_small(packed, small)]
    grad_gain_attn, grad_gain_mlp, grad_gain_out, grad_taps = parts
    return (
        layer_out[None],
        grad_inputs[None],
        grad_gain_attn,
        grad_query_matrix,
        grad_key_matrix,
        grad_value_matrix,
        grad_beta_matrix[:, :heads].astype(f32),
        grad_taps,
        grad_gain_out,
        grad_out_matrix,
        grad_gain_mlp,
        grad_gate_matrix,
        grad_up_matrix,
        grad_down_matrix,
    )


def solution(mesh):
    vector = P("fsdp")
    rows = P("fsdp", None)
    columns = P(None, "fsdp")
    tokens = P("fsdp", "seq", None)
    return jax.shard_map(
        local,
        mesh=mesh,
        in_specs=(
            tokens,
            vector,
            rows,
            rows,
            rows,
            rows,
            columns,
            vector,
            rows,
            vector,
            rows,
            rows,
            columns,
            tokens,
        ),
        out_specs=(
            tokens,
            tokens,
            vector,
            rows,
            rows,
            rows,
            rows,
            columns,
            vector,
            rows,
            vector,
            rows,
            rows,
            columns,
        ),
        check_vma=False,
    )
```
